128 devices in a mesh: expert: 16 (over z, y), tensor: 8 (over x, core).
Axes of the slice: x: 4, y: 4, z: 4, core: 2. Of those that a mesh axis runs over, the one named last changes fastest.
Arguments:
- tokens: bfloat16 [4096, 2048], P('expert', 'tensor'), may hold values from -6 to 6
- cotangent: bfloat16 [4096, 2048], P('expert', 'tensor'), may hold values from -6 to 6
- attn_gain: bfloat16 [2048], replicated, may hold values from 0.5 to 1.5
- w_query: bfloat16 [2048, 3072], P(None, 'tensor'), may hold values from -0.125 to 0.125
- w_latent: bfloat16 [2048, 576], replicated, may hold values from -0.125 to 0.125
- latent_gain: bfloat16 [512], replicated, may hold values from 0.5 to 1.5
- w_expand: bfloat16 [512, 4096], P(None, 'tensor'), may hold values from -0.25 to 0.25
- w_out: bfloat16 [2048, 2048], P('tensor'), may hold values from -0.5 to 0.5
- ffn_gain: bfloat16 [2048], replicated, may hold values from 0.5 to 1.5
- shared_gate: bfloat16 [2048, 2816], P(None, 'tensor'), may hold values from -0.125 to 0.125
- shared_up: bfloat16 [2048, 2816], P(None, 'tensor'), may hold values from -0.125 to 0.125
- shared_down: bfloat16 [2816, 2048], P('tensor'), may hold values from -0.109375 to 0.109375
- expert_gate: bfloat16 [64, 2048, 1408], P('expert', None, 'tensor'), may hold values from -0.125 to 0.125
- expert_up: bfloat16 [64, 2048, 1408], P('expert', None, 'tensor'), may hold values from -0.125 to 0.125
- expert_down: bfloat16 [64, 1408, 2048], P('expert', 'tensor'), may hold values from -0.21875 to 0.21875
- seq_lengths: int32 [64], replicated, may hold values from 1 to 253, as said below
- seq_order: int32 [64], replicated, may hold values from 0 to 63, as said below
- routes: int32 [4096, 6], P('expert'), may hold values from 0 to 63, all different within a row
- gate_weights: float32 [4096, 6], P('expert'), may hold values from 0.25 to 1
Outputs:
- output: bfloat16 [4096, 2048], P('expert', 'tensor')
- input_grad: bfloat16 [4096, 2048], P('expert', 'tensor')
- grad_attn_gain: float32 [2048], P('expert')
- grad_query: float32 [2048, 3072], P('expert', 'tensor')
- grad_latent: float32 [2048, 576], P('expert')
- grad_latent_gain: float32 [512], P('expert')
- grad_expand: float32 [512, 4096], P('expert', 'tensor')
- grad_out: float32 [2048, 2048], P('tensor', 'expert')
- feedforward_gain_gradient: float32 [2048], P('expert')
- grad_shared_gate: float32 [2048, 2816], P('expert', 'tensor')
- grad_shared_up: float32 [2048, 2816], P('expert', 'tensor')
- grad_shared_down: float32 [2816, 2048], P('tensor', 'expert')
- grad_expert_gate: float32 [64, 2048, 1408], P('expert', None, 'tensor')
- grad_expert_up: float32 [64, 2048, 1408], P('expert', None, 'tensor')
- grad_expert_down: float32 [64, 1408, 2048], P('expert', 'tensor')
The draws below stay inside these ranges and needn't reach their ends.
Inputs may be any that keep to these rules, and one draw needn't show every extreme that they name: `seq_lengths`: in dealt order (sequence seq_order[j] at place j) every 4 consecutive places hold 256 tokens in all. `seq_order`: A permutation of the 64 sequences.
All inputs are finite; a program needn't handle non-finite values.
Results may differ from the reference program's by a relative error of at most 0.03.
Values may be sent and summed in bfloat16 or wider, within the bound.
A program may use at most 256 MiB of HBM per device.

```python
import math
import jax
import jax.numpy as jnp
from jax import lax

D = 2048
HEADS = 16
NOPE = 128
ROPE = 64
LATENT = 512
VDIM = 128
FF = 1408
SHARED_FF = 2816
TOP = 6
SEQ_GROUP = 4
GROUP_TOK = 256
EXPERTS = 64
TOKENS = 4096
CAPACITY = 27
N_TENSOR = 8


def deal_draw(key):
    token_groups = TOKENS // GROUP_TOK
    group_keys = jax.random.split(jax.random.fold_in(key, 11), token_groups)

    def one_group(subkey):
        cuts = jax.random.permutation(subkey, GROUP_TOK - 1)[:SEQ_GROUP - 1].astype(jnp.int32) + 1
        cuts = jnp.sort(cuts)
        edges = jnp.concatenate([jnp.zeros((1,), jnp.int32), cuts, jnp.full((1,), GROUP_TOK, jnp.int32)])
        return edges[1:] - edges[:-1]
    spread = jax.vmap(one_group)(group_keys)
    chosen = jax.random.randint(jax.random.fold_in(key, 13), (), 0, token_groups).astype(jnp.int32)
    slot_pick = jax.random.randint(jax.random.fold_in(key, 14), (), 0, SEQ_GROUP).astype(jnp.int32)
    seats = jnp.arange(SEQ_GROUP, dtype=jnp.int32)
    longest = jnp.where(seats == slot_pick, GROUP_TOK - SEQ_GROUP + 1, 1).astype(jnp.int32)
    rows = jnp.arange(token_groups, dtype=jnp.int32)[:, None]
    dealt = jnp.where(rows == chosen, longest[None, :], spread).reshape(-1).astype(jnp.int32)
    order = jax.random.permutation(jax.random.fold_in(key, 12), token_groups * SEQ_GROUP).astype(jnp.int32)
    lengths = jnp.zeros((token_groups * SEQ_GROUP,), jnp.int32).at[order].set(dealt)
    return (lengths, order)


def draw_seq_lengths(key, part):
    shared = deal_draw(key)
    return shared[0]


def draw_seq_order(key, part):
    shared = deal_draw(key)
    return shared[1]


def block_levels(own_key, shape, shards, smallest, high):
    def one(dim, shards_of):
        draws = jax.random.uniform(jax.random.fold_in(jax.random.fold_in(own_key, 6), dim), (shards_of,), jnp.float32, smallest / len(shards), high / len(shards))
        return jnp.repeat(jnp.exp(draws), shape[dim] // shards_of).reshape((-1,) + (1,) * (len(shape) - dim - 1))

    loudness = one(*shards[0])
    for cut in shards[1:]:
        loudness = loudness * one(*cut)
    return loudness


def distinct(rng, rows, count, top, lift):
    order = jax.random.permutation(jax.random.fold_in(rng, 1), count)
    boost = order
    for power in range(3):
        boost = boost * boost // count
    boost = boost * lift // count
    lots = jax.random.randint(jax.random.fold_in(rng, 2), (rows, count), 0, 4096) + boost
    sure = jax.random.permutation(jax.random.fold_in(rng, 3), rows)[jnp.arange(count) % rows]
    lots = jnp.where(jnp.arange(rows)[:, None] == sure[None, :], 1 << 14, lots)
    merit = lots * count + jnp.arange(count)
    return lax.top_k(merit.astype(jnp.int32), top)[1].astype(jnp.int32)


def centred(stream_key, extent, scale, most, pieces=(), kind=jnp.bfloat16):
    array = jax.random.normal(stream_key, extent, jnp.float32) * scale
    if len(pieces) > 0:
        array = block_levels(stream_key, extent, pieces, -0.22, 0.18) * array
    return jnp.clip(array, min=-most, max=most).astype(kind)


def setup_inputs(seed: int = 0) -> dict:
    seeds = jax.random.split(jax.random.key(seed), 20)
    return {
        "tokens": centred(seeds[0], (TOKENS, D), 1.0, 6.0, ((0, 16), (1, 8))),
        "cotangent": centred(seeds[1], (TOKENS, D), 1.0, 6.0, ((0, 16), (1, 8))),
        "attn_gain": jnp.clip(1.0 + 0.1 * jax.random.normal(seeds[2], (D,), jnp.float32), 0.5, 1.5).astype(jnp.bfloat16),
        "w_query": centred(seeds[3], (D, HEADS * (NOPE + ROPE)), D ** -0.5, 0.125, ((1, 8),)),
        "w_latent": centred(seeds[4], (D, LATENT + ROPE), D ** -0.5, 0.125),
        "latent_gain": jnp.clip(1.0 + 0.1 * jax.random.normal(seeds[5], (LATENT,), jnp.float32), 0.5, 1.5).astype(jnp.bfloat16),
        "w_expand": centred(seeds[6], (LATENT, HEADS * (NOPE + VDIM)), LATENT ** -0.5, 0.25, ((1, 8),)),
        "w_out": centred(seeds[7], (HEADS * VDIM, D), (HEADS * VDIM // 16) ** -0.5, 0.5, ((0, 8),)),
        "ffn_gain": jnp.clip(1.0 + 0.1 * jax.random.normal(seeds[8], (D,), jnp.float32), 0.5, 1.5).astype(jnp.bfloat16),
        "shared_gate": centred(seeds[9], (D, SHARED_FF), D ** -0.5, 0.125, ((1, 8),)),
        "shared_up": centred(seeds[10], (D, SHARED_FF), D ** -0.5, 0.125, ((1, 8),)),
        "shared_down": centred(seeds[11], (SHARED_FF, D), SHARED_FF ** -0.5, 0.109375, ((0, 8),)),
        "expert_gate": centred(seeds[12], (EXPERTS, D, FF), D ** -0.5, 0.125, ((0, 16), (2, 8))),
        "expert_up": centred(seeds[13], (EXPERTS, D, FF), D ** -0.5, 0.125, ((0, 16), (2, 8))),
        "expert_down": centred(seeds[14], (EXPERTS, FF, D), (FF // 2) ** -0.5, 0.21875, ((0, 16), (1, 8))),
        "seq_lengths": draw_seq_lengths(jax.random.fold_in(seeds[19], 71), 0),
        "seq_order": draw_seq_order(jax.random.fold_in(seeds[19], 71), 0),
        "routes": distinct(seeds[17], TOKENS, EXPERTS, TOP, 768),
        "gate_weights": jnp.clip(jnp.exp(math.log(1.0) - 1.3862944 * jax.random.uniform(seeds[18], (TOKENS, TOP), jnp.float32) ** block_levels(seeds[18], (TOKENS, TOP), ((0, 16),), -0.2, 0.2)), 0.25, 1.0),
    }


@jax.custom_vjp
def low(v):
    return lax.optimization_barrier(v.astype(jnp.bfloat16)).astype(jnp.float32)

@jax.custom_vjp
def low_back(v):
    return v

def low_keep(v):
    return (low(v), None)

def low_pass(kept, grad):
    return (grad,)

def back_keep(v):
    return (v, None)

def back_low(kept, grad):
    return (low(grad),)
low.defvjp(low_keep, low_pass)
low_back.defvjp(back_keep, back_low)
EPS = 1e-06
HIGH = lax.Precision.HIGHEST

def matmul(left, right):
    return jnp.dot(left, right, precision=HIGH, preferred_element_type=jnp.float32)

def rms_scale(value, gain):
    return value * lax.rsqrt(lax.optimization_barrier(jnp.mean(value * value, axis=-1, keepdims=True)) + EPS) * gain

def rotate(value, offsets):
    half = value.shape[-1] // 2
    freqs = jnp.exp(-jnp.log(10000.0) * jnp.arange(half, dtype=jnp.float32) / half)
    angles = offsets.astype(jnp.float32)[:, None] * freqs[None, :]
    angles = angles.reshape((angles.shape[0],) + (1,) * (value.ndim - 2) + (half,))
    cosine = jnp.cos(angles)
    sine = jnp.sin(angles)
    first = value[..., :half]
    second = value[..., half:]
    return jnp.concatenate([first * cosine - second * sine, second * cosine + first * sine], axis=-1)

def deal_layout(lengths, order, total):
    count = lengths.shape[0]
    begins = jnp.cumsum(lengths) - lengths
    dealt_lengths = lengths[order]
    dispatched_starts = jnp.cumsum(dealt_lengths) - dealt_lengths
    places = jnp.arange(total, dtype=jnp.int32)
    which = lax.optimization_barrier(jnp.sum((places[:, None] >= dispatched_starts[None, :]).astype(jnp.int32), axis=1)) - 1
    offsets = places - dispatched_starts[which]
    source = begins[order[which]] + offsets
    numbers = jnp.arange(count, dtype=jnp.int32)
    inverse_seq = lax.optimization_barrier(jnp.sum(jnp.where(order[None, :] == numbers[:, None], numbers[None, :], 0), axis=1))
    owner = lax.optimization_barrier(jnp.sum((places[:, None] >= begins[None, :]).astype(jnp.int32), axis=1)) - 1
    target = dispatched_starts[inverse_seq[owner]] + places - begins[owner]
    return (source, target, offsets, which)

def softmax_rows(scores):
    peak = lax.optimization_barrier(jnp.max(scores, axis=-1, keepdims=True))
    expo = jnp.exp(scores - peak)
    return expo / lax.optimization_barrier(jnp.sum(expo, axis=-1, keepdims=True))

def reference(tokens, cotangent, attn_gain, w_query, w_latent, latent_gain, w_expand, w_out, ffn_gain, shared_gate, shared_up, shared_down, expert_gate, expert_up, expert_down, seq_lengths, seq_order, routes, gate_weights):
    source, target, offsets, which = deal_layout(seq_lengths, seq_order, TOKENS)
    token_groups = TOKENS // GROUP_TOK
    pairs = GROUP_TOK * TOP
    grouped = routes.reshape(token_groups, pairs)
    onehot = (grouped[:, :, None] == jnp.arange(EXPERTS, dtype=jnp.int32)[None, None, :]).astype(jnp.int32)
    slots = lax.optimization_barrier(jnp.sum(onehot * jnp.cumsum(onehot, axis=1), axis=2)) - 1
    kept = slots < CAPACITY
    group_ids = jnp.arange(token_groups, dtype=jnp.int32)[:, None]
    entries = EXPERTS * token_groups * CAPACITY
    flat_place = jnp.where(kept, grouped * (token_groups * CAPACITY) + group_ids * CAPACITY + slots, entries).reshape(-1).astype(jnp.int32)
    pair_token = (jnp.arange(TOKENS * TOP, dtype=jnp.int32) // TOP).astype(jnp.int32)
    table = jnp.full((entries + 1,), TOKENS, jnp.int32).at[flat_place].set(pair_token)[:entries]
    gate_flat = gate_weights.reshape(-1).astype(jnp.float32)
    head_width = NOPE + ROPE
    slice_width = FF // N_TENSOR

    def forward(inputs, g_attn, wq, wlat, g_lat, wexp, wo, g_ffn, wsg, wsu, wsd, weg, weu, wed):
        dealt = inputs[source]
        normed = low(rms_scale(dealt, g_attn))

        def attend(block):
            rows_in, offs, segs = block
            query_pre = low_back(matmul(rows_in, wq)).reshape(GROUP_TOK, HEADS, head_width)
            query = low(jnp.concatenate([query_pre[..., :NOPE], rotate(query_pre[..., NOPE:], offs)], axis=-1))
            latent = low_back(matmul(rows_in, wlat))
            key_rope = low(rotate(latent[:, LATENT:], offs))
            compressed = low(rms_scale(latent[:, :LATENT], g_lat))
            expanded = low(low_back(matmul(compressed, wexp))).reshape(GROUP_TOK, HEADS, NOPE + VDIM)
            keys = jnp.concatenate([expanded[..., :NOPE], jnp.broadcast_to(key_rope[:, None, :], (GROUP_TOK, HEADS, ROPE))], axis=-1)
            values = expanded[..., NOPE:]
            scores = low_back(jnp.einsum('qhd,khd->hqk', query, keys, precision=HIGH) * head_width ** (-0.5))
            here = jnp.arange(GROUP_TOK, dtype=jnp.int32)
            allowed = (segs[:, None] == segs[None, :]) & (here[:, None] >= here[None, :])
            probs = softmax_rows(jnp.where(allowed[None], scores, -1e+30))
            mixed = low_back(low(jnp.einsum('hqk,khd->qhd', low(probs), values, precision=HIGH)))
            return low_back(matmul(mixed.reshape(GROUP_TOK, HEADS * VDIM), wo))
        attn = lax.map(jax.checkpoint(attend), (normed.reshape(token_groups, GROUP_TOK, D), offsets.reshape(token_groups, GROUP_TOK), which.reshape(token_groups, GROUP_TOK))).reshape(TOKENS, D)
        middle = dealt + attn
        normed_two = low(rms_scale(middle, g_ffn))
        shared_g = low_back(matmul(normed_two, wsg))
        shared_u = low_back(matmul(normed_two, wsu))
        shared_out = matmul(low(shared_g * jax.nn.sigmoid(shared_g) * shared_u), wsd)
        padded = jnp.concatenate([normed_two, jnp.zeros((1, D), jnp.float32)], axis=0)
        received_rows = padded[table].reshape(EXPERTS, token_groups * CAPACITY, D)

        def expert(block):
            rows_in, wg, wu, wd = block
            summed = jnp.zeros((rows_in.shape[0], D), jnp.float32)
            for piece in range(N_TENSOR):
                lower = piece * slice_width
                upper = lower + slice_width
                copied = low_back(rows_in)
                gate_pre = low_back(matmul(copied, wg[:, lower:upper]))
                up_pre = low_back(matmul(copied, wu[:, lower:upper]))
                hidden = low(gate_pre * jax.nn.sigmoid(gate_pre) * up_pre)
                summed = summed + low_back(low(matmul(hidden, wd[lower:upper, :])))
            return summed
        produced = lax.map(jax.checkpoint(expert), (received_rows, weg, weu, wed)).reshape(entries, D)
        produced = jnp.concatenate([produced, jnp.zeros((1, D), jnp.float32)], axis=0)
        routed = lax.optimization_barrier(jnp.sum((gate_flat[:, None] * produced[flat_place]).reshape(TOKENS, TOP, D), axis=1))
        return (middle + shared_out + routed)[target]
    f32 = jnp.float32
    result, pullback = jax.vjp(forward, tokens.astype(f32), attn_gain.astype(f32), w_query.astype(f32), w_latent.astype(f32), latent_gain.astype(f32), w_expand.astype(f32), w_out.astype(f32), ffn_gain.astype(f32), shared_gate.astype(f32), shared_up.astype(f32), shared_down.astype(f32), expert_gate.astype(f32), expert_up.astype(f32), expert_down.astype(f32))
    grads = pullback(cotangent.astype(f32))
    return (result.astype(jnp.bfloat16), grads[0].astype(jnp.bfloat16), grads[1], grads[2], grads[3], grads[4], grads[5], grads[6], grads[7], grads[8], grads[9], grads[10], grads[11], grads[12], grads[13])
```

```python
import functools

import jax
import jax.numpy as jnp
from jax import lax
from jax.experimental import pallas as pl
from jax.experimental.pallas import tpu as pltpu
from jax.sharding import PartitionSpec as P

NOPE = 128
ROPE = 64
HEAD = NOPE + ROPE
LATENT = 512
VDIM = 128
D = 2048
GROUP = 256
TOP = 6
EXPERTS = 64
GROUPS = 16
LOCAL = 4
CAP = 27
PADCAP = 32
TENSOR = 8
COLS = D // TENSOR
EPS = 1e-06

XN = 4
YN = 4
ZN = 4
CORES = 2

F32 = jnp.float32
BF16 = jnp.bfloat16
MESH = pl.DeviceIdType.MESH
ANY = pl.BlockSpec(memory_space=pl.ANY)
VM = pl.BlockSpec(memory_space=pltpu.VMEM)
DMA = pltpu.SemaphoreType.DMA
MIB = 1024 * 1024


def remote(src, dst, ssem, rsem, axis, index):
    return pltpu.make_async_remote_copy(
        src_ref=src,
        dst_ref=dst,
        send_sem=ssem,
        recv_sem=rsem,
        device_id={axis: index},
        device_id_type=MESH,
    )


def greet(peers):
    barrier = pltpu.get_barrier_semaphore()
    for axis, index in peers:
        pl.semaphore_signal(barrier, inc=1, device_id={axis: index}, device_id_type=MESH)
    pl.semaphore_wait(barrier, len(peers))


def params(cid, vmem=48):
    return pltpu.CompilerParams(
        collective_id=cid, has_side_effects=True, vmem_limit_bytes=vmem * MIB
    )


def x_peers():
    t = lax.axis_index("tensor")
    x = t // CORES
    c = lax.rem(t, CORES)
    right = lax.rem(x + 1, XN) * CORES + c
    left = lax.rem(x + XN - 1, XN) * CORES + c
    far = lax.rem(x + 2, XN) * CORES + c
    twin = x * CORES + (1 - c)
    return t, right, left, far, twin


def greet_x():
    t, right, left, far, twin = x_peers()
    greet([("tensor", right), ("tensor", left), ("tensor", twin)])


def greet_tensor():
    t = lax.axis_index("tensor")
    greet([("tensor", lax.rem(t + j, TENSOR)) for j in range(1, TENSOR)])


def cols(index, width):
    return pl.ds(pl.multiple_of(index * width, width), width)


def gather_tensor(nch, src, out_ref, ssem, rsem):
    t, right, left, far, twin = x_peers()
    flip = twin - t
    rows, width = src.shape
    rc = rows // nch
    h = rc // 2

    def block(k, owner, part=None):
        if part is None:
            return out_ref.at[pl.ds(k * rc, rc), cols(owner, width)]
        return out_ref.at[pl.ds(k * rc + part * h, h), cols(owner, width)]

    sends = []

    def send(k, j, ref, dst, target):
        c = remote(ref, dst, ssem.at[k, j], rsem.at[k, j], "tensor", target)
        c.start()
        sends.append(c)

    def arrived(k, j, ref):
        remote(ref, ref, ssem.at[k, j], rsem.at[k, j], "tensor", twin).wait_recv()

    for k in range(nch):
        part = src.at[pl.ds(k * rc, rc), :]
        send(k, 0, part, block(k, t), right)
        send(k, 1, part, block(k, t), left)
        send(k, 4, part, block(k, t), twin)
    for k in range(nch):
        arrived(k, 0, block(k, left))
        send(k, 2, block(k, left, 0), block(k, left, 0), right)
        send(k, 5, block(k, left), block(k, left), twin)
        arrived(k, 1, block(k, right))
        send(k, 3, block(k, right, 1), block(k, right, 1), left)
        send(k, 6, block(k, right), block(k, right), twin)
    for k in range(nch):
        arrived(k, 2, block(k, far, 0))
        send(k, 7, block(k, far, 0), block(k, far, 0), twin)
        arrived(k, 3, block(k, far, 1))
        send(k, 8, block(k, far, 1), block(k, far, 1), twin)
    for k in range(nch):
        arrived(k, 4, block(k, twin))
        arrived(k, 5, block(k, left + flip))
        arrived(k, 6, block(k, right + flip))
        arrived(k, 7, block(k, far + flip, 0))
        arrived(k, 8, block(k, far + flip, 1))
    for s in sends:
        s.wait_send()


def gather_sems(nch):
    return [DMA((nch, 9)), DMA((nch, 9))]


def scatter_tensor(nch, view, rows, width, emit, own, sib, half, full, ssem, rsem, lsem):
    t, right, left, far, twin = x_peers()
    flip = twin - t
    rc = rows // nch
    h = rc // 2
    order = (far, right, left, t)
    sends = []

    def send(k, j, src, dst, target):
        c = remote(src, dst, ssem.at[k, j], rsem.at[k, j], "tensor", target)
        c.start()
        sends.append(c)

    def arrived(k, j, ref):
        remote(ref, ref, ssem.at[k, j], rsem.at[k, j], "tensor", twin).wait_recv()

    loads = {}
    for k in range(nch):
        r = pl.ds(k * rc, rc)
        for j, owner in enumerate(order):
            send(k, j, view(r, owner + flip), sib.at[j, r], twin)
            c = pltpu.make_async_copy(view(r, owner), own.at[j, r], lsem.at[k, j])
            c.start()
            loads[k, j] = c

    def pair(k, j):
        loads[k, j].wait()
        arrived(k, j, sib.at[j, pl.ds(k * rc, rc)])

    def add(j, r):
        return own[j, r].astype(F32) + sib[j, r].astype(F32)

    for k in range(nch):
        r0, r1 = pl.ds(k * rc, h), pl.ds(k * rc + h, h)
        r, hk = pl.ds(k * rc, rc), pl.ds(k * h, h)
        pair(k, 0)
        own[0, r] = add(0, r).astype(own.dtype)
        send(k, 4, own.at[0, r0], half.at[0, hk], right)
        send(k, 5, own.at[0, r1], half.at[1, hk], left)
    for k in range(nch):
        r0, r1 = pl.ds(k * rc, h), pl.ds(k * rc + h, h)
        r, hk = pl.ds(k * rc, rc), pl.ds(k * h, h)
        pair(k, 1)
        pair(k, 2)
        arrived(k, 4, half.at[0, hk])
        own[1, r1] = add(1, r1).astype(own.dtype)
        own[1, r0] = (add(1, r0) + half[0, hk].astype(F32)).astype(own.dtype)
        send(k, 6, own.at[1, r], full.at[0, r], right)
        arrived(k, 5, half.at[1, hk])
        own[2, r0] = add(2, r0).astype(own.dtype)
        own[2, r1] = (add(2, r1) + half[1, hk].astype(F32)).astype(own.dtype)
        send(k, 7, own.at[2, r], full.at[1, r], left)
    for k in range(nch):
        r = pl.ds(k * rc, rc)
        pair(k, 3)
        arrived(k, 6, full.at[0, r])
        arrived(k, 7, full.at[1, r])
        emit(r, add(3, r) + full[0, r].astype(F32) + full[1, r].astype(F32))
    for s in sends:
        s.wait_send()


def scatter_scratch(nch, rows, width, dtype):
    return [
        pltpu.VMEM((4, rows, width), dtype),
        pltpu.VMEM((4, rows, width), dtype),
        pltpu.VMEM((2, rows // 2, width), dtype),
        pltpu.VMEM((2, rows, width), dtype),
        DMA((nch, 8)),
        DMA((nch, 8)),
        DMA((nch, 4)),
    ]


def sum_rows_tensor(value, buf, ssem, rsem):
    t = lax.axis_index("tensor")
    rows = value.shape[0]
    mine = jnp.broadcast_to(jnp.sum(value, axis=1, keepdims=True), (rows, 128))
    buf[t] = jnp.transpose(mine)[:8]
    sends = []
    for j in range(1, TENSOR):
        to = lax.rem(t + j, TENSOR)
        c = remote(buf.at[t], buf.at[t], ssem.at[j], rsem.at[j], "tensor", to)
        c.start()
        sends.append(c)
    for j in range(1, TENSOR):
        ref = buf.at[lax.rem(t + TENSOR - j, TENSOR)]
        remote(ref, ref, ssem.at[j], rsem.at[j], "tensor", t).wait_recv()
    total = jnp.sum(buf[...], axis=0)
    for s in sends:
        s.wait_send()
    return jnp.transpose(total)[:, :1]


def sum_rows_scratch():
    return [pltpu.VMEM((TENSOR, 8, GROUP), F32), DMA((TENSOR,)), DMA((TENSOR,))]


def ag_tensor_kernel(nch, in_ref, out_ref, ssem, rsem, lsem):
    t = lax.axis_index("tensor")
    greet_x()
    own = pltpu.make_async_copy(in_ref, out_ref.at[:, cols(t, in_ref.shape[1])], lsem)
    own.start()
    gather_tensor(nch, in_ref, out_ref, ssem, rsem)
    own.wait()


def ag_tensor(value, cid, nch=1):
    rows, width = value.shape
    return pl.pallas_call(
        functools.partial(ag_tensor_kernel, nch),
        out_shape=jax.ShapeDtypeStruct((rows, width * TENSOR), value.dtype),
        in_specs=[ANY],
        out_specs=ANY,
        scratch_shapes=gather_sems(nch) + [DMA],
        compiler_params=params(cid),
        name="ag_tensor",
    )(value)


def rs_tensor_kernel(nch, in_ref, out_ref, *scratch):
    rows = in_ref.shape[0]
    width = in_ref.shape[1] // TENSOR
    greet_x()

    def emit(r, value):
        out_ref[r] = value.astype(out_ref.dtype)

    scatter_tensor(
        nch, lambda r, owner: in_ref.at[r, cols(owner, width)], rows, width, emit, *scratch
    )


def rs_tensor(value, cid, nch=1, dtype=None):
    rows, total = value.shape
    width = total // TENSOR
    return pl.pallas_call(
        functools.partial(rs_tensor_kernel, nch),
        out_shape=jax.ShapeDtypeStruct((rows, width), dtype or value.dtype),
        in_specs=[ANY],
        out_specs=VM,
        scratch_shapes=scatter_scratch(nch, rows, width, value.dtype),
        compiler_params=params(cid),
        name="rs_tensor",
    )(value)


def middle_kernel(
    part_ref, x_ref, gain_ref, mid_ref, inv_ref, low_ref, full_ref, *scratch
):
    rs, ag, st, lsem = scratch[:7], scratch[7:9], scratch[9:12], scratch[12]
    t = lax.axis_index("tensor")
    greet_tensor()

    def emit(r, value):
        mid_ref[r] = x_ref[r].astype(F32) + value

    scatter_tensor(1, lambda r, owner: part_ref.at[r, cols(owner, COLS)], GROUP, COLS, emit, *rs)
    mid = mid_ref[...]
    inv = lax.rsqrt(sum_rows_tensor(mid * mid, *st) * (1.0 / D) + EPS)
    inv_ref[...] = inv
    low_ref[...] = (mid * inv * gain_ref[...].astype(F32)).astype(BF16)
    own = pltpu.make_async_copy(low_ref, full_ref.at[:, cols(t, COLS)], lsem)
    own.start()
    gather_tensor(1, low_ref, full_ref, *ag)
    own.wait()


def middle_step(part, x_cols, gain, cid):
    return pl.pallas_call(
        middle_kernel,
        out_shape=(
            jax.ShapeDtypeStruct((GROUP, COLS), F32),
            jax.ShapeDtypeStruct((GROUP, 1), F32),
            jax.ShapeDtypeStruct((GROUP, COLS), BF16),
            jax.ShapeDtypeStruct((GROUP, D), BF16),
        ),
        in_specs=[ANY, VM, VM],
        out_specs=(VM, VM, VM, ANY),
        scratch_shapes=scatter_scratch(1, GROUP, COLS, F32)
        + gather_sems(1)
        + sum_rows_scratch()
        + [DMA],
        compiler_params=params(cid),
        name="middle_step",
    )(part, x_cols, gain)


def back_middle_kernel(
    routed_ref, shared_ref, mid_ref, inv_ref, gain_ref, dy_ref,
    dmid_ref, dgain_ref, full_ref, low, buf, ssem, rsem, agss, agrs, lsem
):
    t = lax.axis_index("tensor")
    greet_tensor()
    dn = routed_ref[...] + shared_ref[...]
    mid = mid_ref[...]
    inv = inv_ref[...]
    u = dn * gain_ref[...].astype(F32)
    total = sum_rows_tensor(u * mid, buf, ssem, rsem)
    dmid = dy_ref[...].astype(F32) + inv * u - mid * (inv * inv * inv * total * (1.0 / D))
    dmid_ref[...] = dmid
    low[...] = dmid.astype(BF16)
    own = pltpu.make_async_copy(low, full_ref.at[:, cols(t, COLS)], lsem)
    own.start()
    dgain_ref[...] = jnp.sum(dn * mid * inv, axis=0, keepdims=True)
    gather_tensor(1, low, full_ref, agss, agrs)
    own.wait()


def back_middle(routed, shared, mid, inv, gain, dy, cid):
    return pl.pallas_call(
        back_middle_kernel,
        out_shape=(
            jax.ShapeDtypeStruct((GROUP, COLS), F32),
            jax.ShapeDtypeStruct((1, COLS), F32),
            jax.ShapeDtypeStruct((GROUP, D), BF16),
        ),
        in_specs=[VM] * 6,
        out_specs=(VM, VM, ANY),
        scratch_shapes=[pltpu.VMEM((GROUP, COLS), BF16)]
        + sum_rows_scratch()
        + gather_sems(1)
        + [DMA],
        compiler_params=params(cid),
        name="back_middle",
    )(routed, shared, mid, inv, gain, dy)


def back_input_kernel(
    part_ref, lat_ref, x_ref, inv_ref, gain_ref, dmid_ref, ffn_ref, dx_ref, gains_ref, low, dn, *scratch
):
    rs, st, ag, lsem = scratch[:7], scratch[7:10], scratch[10:12], scratch[12]
    t = lax.axis_index("tensor")
    greet_tensor()

    def emit(r, value):
        dn[r] = value + lat_ref[r]

    scatter_tensor(1, lambda r, owner: part_ref.at[r, cols(owner, COLS)], GROUP, COLS, emit, *rs)
    xd = x_ref[...].astype(F32)
    inv = inv_ref[...]
    d = dn[...]
    u = d * gain_ref[...].astype(F32)
    row = jnp.sum(d * xd * inv, axis=0, keepdims=True)
    place = lax.broadcasted_iota(jnp.int32, (16, COLS), 0)
    both = jnp.where(place == 0, row, jnp.where(place == 1, ffn_ref[...], 0.0))
    low[...] = both.astype(BF16)
    own = pltpu.make_async_copy(low, gains_ref.at[:, cols(t, COLS)], lsem)
    own.start()
    total = sum_rows_tensor(u * xd, *st)
    dx_ref[...] = dmid_ref[...] + inv * u - xd * (inv * inv * inv * total * (1.0 / D))
    for j in range(1, TENSOR):
        to = lax.rem(t + j, TENSOR)
        dst = gains_ref.at[:, cols(t, COLS)]
        remote(low, dst, ag[0].at[j], ag[1].at[j], "tensor", to).start()
    for j in range(1, TENSOR):
        dst = gains_ref.at[:, cols(lax.rem(t + TENSOR - j, TENSOR), COLS)]
        c = remote(low, dst, ag[0].at[j], ag[1].at[j], "tensor", t)
        c.wait_recv()
        c.wait_send()
    own.wait()


def back_input(part, lat, x, inv, gain, dmid, ffn, cid):
    return pl.pallas_call(
        back_input_kernel,
        out_shape=(
            jax.ShapeDtypeStruct((GROUP, COLS), F32),
            jax.ShapeDtypeStruct((16, D), BF16),
        ),
        in_specs=[ANY] + [VM] * 6,
        out_specs=(VM, ANY),
        scratch_shapes=[pltpu.VMEM((16, COLS), BF16), pltpu.VMEM((GROUP, COLS), F32)]
        + scatter_scratch(1, GROUP, COLS, BF16)
        + sum_rows_scratch()
        + [DMA((TENSOR,)), DMA((TENSOR,)), DMA],
        compiler_params=params(cid),
        name="back_input",
    )(part, lat, x, inv, gain, dmid, ffn)


def ar_kernel(in_ref, out_ref, acc, got, ssem, rsem, ssem2, rsem2):
    t = lax.axis_index("tensor")
    greet_tensor()
    for j in range(1, TENSOR):
        to = lax.rem(t + j, TENSOR)
        remote(in_ref.at[to], got.at[t], ssem.at[j], rsem.at[j], "tensor", to).start()
    total = in_ref[t].astype(F32)
    for j in range(1, TENSOR):
        frm = lax.rem(t + TENSOR - j, TENSOR)
        c = remote(in_ref.at[t], got.at[frm], ssem.at[j], rsem.at[j], "tensor", t)
        c.wait_recv()
        c.wait_send()
        total = total + got[frm].astype(F32)
    acc[...] = total.astype(BF16)
    out_ref[t] = acc[...]
    for j in range(1, TENSOR):
        to = lax.rem(t + j, TENSOR)
        remote(acc, out_ref.at[t], ssem2.at[j], rsem2.at[j], "tensor", to).start()
    for j in range(1, TENSOR):
        frm = lax.rem(t + TENSOR - j, TENSOR)
        c = remote(acc, out_ref.at[frm], ssem2.at[j], rsem2.at[j], "tensor", t)
        c.wait_recv()
        c.wait_send()


def ar_tensor(value, cid):
    rows, n = value.shape
    part = rows // TENSOR
    out = pl.pallas_call(
        ar_kernel,
        out_shape=jax.ShapeDtypeStruct((TENSOR, part, n), value.dtype),
        in_specs=[VM],
        out_specs=VM,
        scratch_shapes=[
            pltpu.VMEM((part, n), value.dtype),
            pltpu.VMEM((TENSOR, part, n), value.dtype),
        ]
        + [DMA((TENSOR,))] * 4,
        compiler_params=params(cid),
        name="ar_tensor",
    )(value.reshape(TENSOR, part, n))
    return out.reshape(rows, n)


def a2a_expert_kernel(in_ref, out_ref, ssem, rsem, lsem):
    e = lax.axis_index("expert")
    z = e // YN
    y = lax.rem(e, YN)
    peers = []
    for dz in range(ZN):
        for dy in range(YN):
            if dz or dy:
                to = lax.rem(z + dz, ZN) * YN + lax.rem(y + dy, YN)
                frm = lax.rem(z + ZN - dz, ZN) * YN + lax.rem(y + YN - dy, YN)
                peers.append((to, frm))
    greet([("expert", to) for to, frm in peers])
    own = pltpu.make_async_copy(in_ref.at[e], out_ref.at[e], lsem)
    own.start()
    sends = []
    for j, (to, frm) in enumerate(peers):
        c = remote(in_ref.at[to], out_ref.at[e], ssem.at[j], rsem.at[j], "expert", to)
        c.start()
        sends.append(c)
    for j, (to, frm) in enumerate(peers):
        remote(out_ref.at[frm], out_ref.at[frm], ssem.at[j], rsem.at[j], "expert", to).wait_recv()
    for s in sends:
        s.wait_send()
    own.wait()


def a2a_expert(value, cid):
    n = value.shape[0]
    return pl.pallas_call(
        a2a_expert_kernel,
        out_shape=jax.ShapeDtypeStruct(value.shape, value.dtype),
        in_specs=[ANY],
        out_specs=ANY,
        scratch_shapes=[DMA((n - 1,)), DMA((n - 1,)), DMA],
        compiler_params=params(cid),
        name="a2a_expert",
    )(value)


def ag_expert_kernel(a_ref, b_ref, ao_ref, bo_ref, ssem, rsem, lsem):
    e = lax.axis_index("expert")
    z = e // YN
    y = lax.rem(e, YN)
    yr, yl, yf = lax.rem(y + 1, YN), lax.rem(y + 3, YN), lax.rem(y + 2, YN)
    zr, zl, zf = lax.rem(z + 1, ZN), lax.rem(z + 3, ZN), lax.rem(z + 2, ZN)
    y_right, y_left = z * YN + yr, z * YN + yl
    z_right, z_left = zr * YN + y, zl * YN + y
    greet([("expert", p) for p in (y_right, y_left, z_right, z_left)])
    h = a_ref.shape[0] // 2
    own_a = pltpu.make_async_copy(a_ref, ao_ref.at[z, y], lsem.at[0])
    own_b = pltpu.make_async_copy(b_ref, bo_ref.at[z, y], lsem.at[1])
    own_a.start()
    own_b.start()
    sends = []

    def send(j, src, dst, to):
        c = remote(src, dst, ssem.at[j], rsem.at[j], "expert", to)
        c.start()
        sends.append(c)

    def arrived(j, ref):
        remote(ref, ref, ssem.at[j], rsem.at[j], "expert", y_right).wait_recv()

    first, second = pl.ds(0, h), pl.ds(h, h)
    send(0, a_ref, ao_ref.at[z, y], y_right)
    send(1, a_ref, ao_ref.at[z, y], y_left)
    send(2, b_ref, bo_ref.at[z, y], z_right)
    send(3, b_ref, bo_ref.at[z, y], z_left)
    arrived(0, ao_ref.at[z, yl])
    send(4, ao_ref.at[z, yl, first], ao_ref.at[z, yl, first], y_right)
    arrived(1, ao_ref.at[z, yr])
    send(5, ao_ref.at[z, yr, second], ao_ref.at[z, yr, second], y_left)
    arrived(2, bo_ref.at[zl, y])
    send(6, bo_ref.at[zl, y, first], bo_ref.at[zl, y, first], z_right)
    arrived(3, bo_ref.at[zr, y])
    send(7, bo_ref.at[zr, y, second], bo_ref.at[zr, y, second], z_left)
    ys = (y, yl, yr, yf)
    zs = (z, zl, zr, zf)
    for i in range(4):
        if i == 3:
            arrived(4, ao_ref.at[z, yf, first])
            arrived(5, ao_ref.at[z, yf, second])
            arrived(6, bo_ref.at[zf, y, first])
            arrived(7, bo_ref.at[zf, y, second])
        sa, sb = ao_ref.at[z, ys[i]], bo_ref.at[zs[i], y]
        src_a, src_b = (a_ref, b_ref) if i == 0 else (sa, sb)
        send(8 + 4 * i, src_a, sa, z_right)
        send(9 + 4 * i, src_a, sa, z_left)
        send(10 + 4 * i, src_b, sb, y_right)
        send(11 + 4 * i, src_b, sb, y_left)
    for i in range(4):
        arrived(8 + 4 * i, ao_ref.at[zl, ys[i]])
        send(24 + 4 * i, ao_ref.at[zl, ys[i], first], ao_ref.at[zl, ys[i], first], z_right)
        arrived(9 + 4 * i, ao_ref.at[zr, ys[i]])
        send(25 + 4 * i, ao_ref.at[zr, ys[i], second], ao_ref.at[zr, ys[i], second], z_left)
        arrived(10 + 4 * i, bo_ref.at[zs[i], yl])
        send(26 + 4 * i, bo_ref.at[zs[i], yl, first], bo_ref.at[zs[i], yl, first], y_right)
        arrived(11 + 4 * i, bo_ref.at[zs[i], yr])
        send(27 + 4 * i, bo_ref.at[zs[i], yr, second], bo_ref.at[zs[i], yr, second], y_left)
    for i in range(4):
        arrived(24 + 4 * i, ao_ref.at[zf, ys[i], first])
        arrived(25 + 4 * i, ao_ref.at[zf, ys[i], second])
        arrived(26 + 4 * i, bo_ref.at[zs[i], yf, first])
        arrived(27 + 4 * i, bo_ref.at[zs[i], yf, second])
    for s in sends:
        s.wait_send()
    own_a.wait()
    own_b.wait()


def ag_expert(a, b, cid):
    shape = jax.ShapeDtypeStruct((ZN, YN) + a.shape, a.dtype)
    ao, bo = pl.pallas_call(
        ag_expert_kernel,
        out_shape=(shape, shape),
        in_specs=[ANY, ANY],
        out_specs=(ANY, ANY),
        scratch_shapes=[DMA((40,)), DMA((40,)), DMA((2,))],
        compiler_params=params(cid),
        name="ag_expert",
    )(a, b)
    return ao.reshape((GROUPS,) + a.shape), bo.reshape((GROUPS,) + a.shape)


def dot_nn(a, b):
    return lax.dot_general(a, b, (((1,), (0,)), ((), ())), preferred_element_type=F32)


def dot_nt(a, b):
    return lax.dot_general(a, b, (((1,), (1,)), ((), ())), preferred_element_type=F32)


def dot_tn(a, b):
    return lax.dot_general(a, b, (((0,), (0,)), ((), ())), preferred_element_type=F32)


def expert_kernel(rows_ref, grad_ref, wg_ref, wu_ref, wd_ref, part_ref, drows_ref, gg_ref, gu_ref, gd_ref):
    n = GROUPS * PADCAP
    rows = rows_ref[...].reshape(n, D)
    grad = grad_ref[...].reshape(n, D)
    wg, wu, wd = wg_ref[0], wu_ref[0], wd_ref[0]
    gate = dot_nt(rows, wg)
    up = dot_nt(rows, wu)
    sig = jax.nn.sigmoid(gate)
    silu = gate * sig
    hidden = (silu * up).astype(BF16)
    part_ref[...] = dot_nn(hidden, wd).astype(BF16).reshape(part_ref.shape)
    gd_ref[0] = dot_tn(hidden, grad)
    dh = dot_nt(grad, wd)
    dg = (dh * up * (sig * (1.0 + gate * (1.0 - sig)))).astype(BF16)
    du = (dh * silu).astype(BF16)
    gg_ref[0] = dot_tn(dg, rows)
    gu_ref[0] = dot_tn(du, rows)
    drows_ref[...] = (dot_nn(dg, wg) + dot_nn(du, wu)).astype(BF16).reshape(drows_ref.shape)


def expert_step(rows, grads, wg, wu, wd):
    hid = wd.shape[1]
    block = pl.BlockSpec((GROUPS, 1, PADCAP, D), lambda i: (0, i, 0, 0))
    weight = pl.BlockSpec((1, hid, D), lambda i: (i, 0, 0))
    shape = jax.ShapeDtypeStruct((GROUPS, LOCAL, PADCAP, D), BF16)
    wshape = jax.ShapeDtypeStruct((LOCAL, hid, D), F32)
    return pl.pallas_call(
        expert_kernel,
        grid=(LOCAL,),
        out_shape=(shape, shape, wshape, wshape, wshape),
        in_specs=[block, block, weight, weight, weight],
        out_specs=(block, block, weight, weight, weight),
        compiler_params=pltpu.CompilerParams(vmem_limit_bytes=60 * MIB),
        cost_estimate=pl.CostEstimate(
            flops=9 * 2 * 2048 * 2048 * hid, bytes_accessed=60 * MIB, transcendentals=0
        ),
        name="expert_step",
    )(
        rows.reshape(GROUPS, LOCAL, PADCAP, D),
        grads.reshape(GROUPS, LOCAL, PADCAP, D),
        wg,
        wu,
        wd,
    )


def rms_scale(value, gain):
    return value * lax.rsqrt(jnp.mean(value * value, axis=-1, keepdims=True) + EPS) * gain


def rotate(value, cosine, sine):
    half = value.shape[-1] // 2
    first = value[..., :half]
    second = value[..., half:]
    return jnp.concatenate(
        [first * cosine - second * sine, second * cosine + first * sine], axis=-1
    )


def pick(index, table):
    numbers = jnp.arange(table.shape[0], dtype=jnp.int32)
    return jnp.sum(jnp.where(index[:, None] == numbers[None, :], table[None, :], 0), axis=1)


def exclusive(values):
    numbers = jnp.arange(values.shape[0], dtype=jnp.int32)
    return jnp.sum(jnp.where(numbers[:, None] > numbers[None, :], values[None, :], 0), axis=1)


def deal_rows(lengths, order, group):
    begins = exclusive(lengths)
    dealt_begins = exclusive(pick(order, lengths))
    dealt_source = pick(order, begins)
    numbers = jnp.arange(lengths.shape[0], dtype=jnp.int32)
    inverse = jnp.sum(jnp.where(order[None, :] == numbers[:, None], numbers[None, :], 0), axis=1)
    given_target = pick(inverse, dealt_begins)
    rows = group * GROUP + jnp.arange(GROUP, dtype=jnp.int32)
    which = jnp.sum((rows[:, None] >= dealt_begins[None, :]).astype(jnp.int32), axis=1) - 1
    offsets = rows - pick(which, dealt_begins)
    source = pick(which, dealt_source) + offsets
    owner = jnp.sum((rows[:, None] >= begins[None, :]).astype(jnp.int32), axis=1) - 1
    target = pick(owner, given_target - begins) + rows
    return source, target, offsets, which


def one_hot_rows(index, count):
    numbers = jnp.arange(count, dtype=jnp.int32)
    return (index[:, None] == numbers[None, :]).astype(BF16)


def per_device(
    tokens,
    cotangent,
    attn_gain,
    w_query,
    w_latent,
    latent_gain,
    w_expand,
    w_out,
    ffn_gain,
    shared_gate,
    shared_up,
    shared_down,
    expert_gate,
    expert_up,
    expert_down,
    seq_lengths,
    seq_order,
    routes,
    gate_weights,
):
    group = lax.axis_index("expert")
    column = lax.axis_index("tensor")
    total = GROUP * GROUPS
    source, target, offsets, which = deal_rows(seq_lengths, seq_order, group)

    all_x, all_dy = ag_expert(tokens, cotangent, 0)
    take = one_hot_rows(source, total)
    x_cols = dot_nn(take, all_x.reshape(total, COLS)).astype(BF16)
    dy_cols = dot_nn(take, all_dy.reshape(total, COLS)).astype(BF16)
    x_full = ag_tensor(x_cols, 1)
    dy_full = lax.all_gather(dy_cols, "tensor", axis=1, tiled=True)

    chosen = routes.T
    gates = gate_weights.T
    experts = jnp.arange(EXPERTS, dtype=jnp.int32)
    hit = chosen[:, None, :] == experts[None, :, None]
    member = jnp.sum(hit.astype(F32), axis=0)
    gate_of = jnp.sum(jnp.where(hit, gates[:, None, :], 0.0), axis=0)
    token = jnp.arange(GROUP, dtype=jnp.int32)
    earlier = (token[:, None] < token[None, :]).astype(BF16)
    count = dot_nn(member.astype(BF16), earlier)
    slot = jnp.where((member > 0.5) & (count < CAP - 0.5), count, -1.0).astype(jnp.int32)
    seats = jnp.arange(PADCAP, dtype=jnp.int32)
    match = slot[:, None, :] == seats[None, :, None]
    place = match.astype(BF16).reshape(EXPERTS * PADCAP, GROUP)
    weight = jnp.where(match, gate_of[:, None, :], 0.0)
    slot_gate = jnp.sum(weight, axis=2).reshape(EXPERTS * PADCAP, 1)
    weight = weight.reshape(EXPERTS * PADCAP, GROUP)
    weight_high = lax.reduce_precision(weight, 8, 7)
    weight_low = (weight - weight_high).astype(BF16)
    weight_high = weight_high.astype(BF16)

    slot_grad = (slot_gate * dot_nn(place, dy_cols)).astype(BF16)
    slot_grad = slot_grad.reshape(GROUPS, LOCAL * PADCAP, COLS)
    slot_grad = lax.all_to_all(slot_grad, "expert", split_axis=0, concat_axis=0, tiled=True)
    grad_rows = lax.all_gather(slot_grad.reshape(-1, COLS), "tensor", axis=1, tiled=True)

    attn_gainf = attn_gain.astype(F32)
    latent_gainf = latent_gain.astype(F32)
    half = ROPE // 2
    freqs = jnp.exp(-jnp.log(10000.0) * jnp.arange(half, dtype=F32) / half)
    angles = offsets.astype(F32)[:, None] * freqs[None, :]
    cosine, sine = jnp.cos(angles), jnp.sin(angles)
    dealt = x_full.astype(F32)
    inv_one = lax.rsqrt(jnp.mean(dealt * dealt, axis=-1, keepdims=True) + EPS)
    normed = (dealt * inv_one * attn_gainf).astype(BF16)
    heads = w_query.shape[1] // HEAD
    scale = HEAD ** (-0.5)
    query_pre = dot_nn(normed, w_query).reshape(GROUP, heads, HEAD)
    cos_h, sin_h = cosine[:, None, :], sine[:, None, :]
    query = jnp.concatenate(
        [query_pre[..., :NOPE], rotate(query_pre[..., NOPE:], cos_h, sin_h)], axis=-1
    ).astype(BF16)
    latent = dot_nn(normed, w_latent)
    key_rope = rotate(latent[:, LATENT:], cosine, sine).astype(BF16)
    latent_main = latent[:, :LATENT]
    compressed = rms_scale(latent_main, latent_gainf).astype(BF16)
    expanded = dot_nn(compressed, w_expand).astype(BF16).reshape(GROUP, heads, NOPE + VDIM)
    keys = jnp.concatenate(
        [expanded[..., :NOPE], jnp.broadcast_to(key_rope[:, None, :], (GROUP, heads, ROPE))],
        axis=-1,
    )
    values = expanded[..., NOPE:]
    allowed = (which[:, None] == which[None, :]) & (token[:, None] >= token[None, :])
    raw = jnp.einsum("qhd,khd->hqk", query, keys, preferred_element_type=F32) * scale
    scores = jnp.where(allowed[None], raw, -1e30)
    peak = jnp.max(scores, axis=-1, keepdims=True)
    expo = jnp.exp(scores - peak)
    probs = expo / jnp.sum(expo, axis=-1, keepdims=True)
    probs_low = probs.astype(BF16)
    mixed = jnp.einsum("hqk,khd->qhd", probs_low, values, preferred_element_type=F32)
    mixed = mixed.astype(BF16).reshape(GROUP, heads * VDIM)
    attn_part = dot_nn(mixed, w_out)

    def own_cols(vector):
        return lax.dynamic_slice_in_dim(vector, column * COLS, COLS, 0).reshape(1, COLS)

    middle, inv_two, normed_two_cols, normed_two = middle_step(
        attn_part, x_cols, own_cols(ffn_gain), 2
    )

    outgoing = dot_nn(place, normed_two_cols).astype(BF16)
    received = a2a_expert(outgoing.reshape(GROUPS, LOCAL * PADCAP, COLS), 3)
    rows = ag_tensor(received.reshape(-1, COLS), 4, 4)

    sg_t, su_t = shared_gate.T, shared_up.T
    shared_g = dot_nt(normed_two, sg_t)
    shared_u = dot_nt(normed_two, su_t)
    shared_sig = jax.nn.sigmoid(shared_g)
    shared_silu = shared_g * shared_sig
    shared_h = (shared_silu * shared_u).astype(BF16)
    shared_part = dot_nn(shared_h, shared_down).astype(BF16)
    grad_sh = dot_nt(dy_full, shared_down)
    grad_sg = (
        grad_sh * shared_u * (shared_sig * (1.0 + shared_g * (1.0 - shared_sig)))
    ).astype(BF16)
    grad_su = (grad_sh * shared_silu).astype(BF16)
    shared_grad = (dot_nn(grad_sg, sg_t) + dot_nn(grad_su, su_t)).astype(BF16)
    shared_sum = rs_tensor(jnp.concatenate([shared_part, shared_grad], axis=0), 5, 1, F32)
    shared_weights = jnp.concatenate(
        [
            dot_tn(normed_two, grad_sg).astype(BF16),
            dot_tn(normed_two, grad_su).astype(BF16),
            dot_tn(dy_full, shared_h).astype(BF16),
        ],
        axis=1,
    )
    shared_weights = lax.psum_scatter(
        shared_weights, "expert", scatter_dimension=0, tiled=True
    ).astype(F32)
    wide = shared_g.shape[1]
    grad_sgate = shared_weights[:, :wide]
    grad_sup = shared_weights[:, wide : 2 * wide]
    grad_sdown = shared_weights[:, 2 * wide :].T

    part, drows, grad_eg, grad_eu, grad_ed = expert_step(
        rows,
        grad_rows,
        jnp.swapaxes(expert_gate, 1, 2),
        jnp.swapaxes(expert_up, 1, 2),
        expert_down,
    )
    back = rs_tensor(drows.reshape(-1, D), 6, 4)
    back = a2a_expert(back.reshape(GROUPS, LOCAL * PADCAP, COLS), 7)
    routed_grad = dot_tn(place, back.reshape(-1, COLS))

    returned = lax.psum_scatter(part.reshape(-1, D), "tensor", scatter_dimension=1, tiled=True)
    returned = lax.all_to_all(
        returned.reshape(GROUPS, LOCAL * PADCAP, COLS),
        "expert",
        split_axis=0,
        concat_axis=0,
        tiled=True,
    ).reshape(-1, COLS)
    routed = dot_tn(weight_high, returned) + dot_tn(weight_low, returned)
    output_cols = (middle + shared_sum[:GROUP] + routed).astype(BF16)
    all_out = lax.all_gather(output_cols, "expert", axis=0, tiled=True)

    dmid, dgain_ffn, d_attn = back_middle(
        routed_grad, shared_sum[GROUP:], middle, inv_two, own_cols(ffn_gain), dy_cols, 8
    )

    grad_wout = dot_tn(d_attn, mixed).astype(BF16)
    grad_mixed = dot_nt(d_attn, w_out).astype(BF16).reshape(GROUP, heads, VDIM)
    grad_values = jnp.einsum("hqk,qhd->khd", probs_low, grad_mixed, preferred_element_type=F32)
    grad_probs = jnp.einsum("qhd,khd->hqk", grad_mixed, values, preferred_element_type=F32)
    grad_scores = (
        probs * (grad_probs - jnp.sum(grad_probs * probs, axis=-1, keepdims=True))
    ).astype(BF16)
    grad_query = jnp.einsum("hqk,khd->qhd", grad_scores, keys, preferred_element_type=F32) * scale
    grad_keys = jnp.einsum("hqk,qhd->khd", grad_scores, query, preferred_element_type=F32) * scale
    grad_qpre = jnp.concatenate(
        [grad_query[..., :NOPE], rotate(grad_query[..., NOPE:], cos_h, -sin_h)], axis=-1
    )
    grad_qpre = grad_qpre.astype(BF16).reshape(GROUP, heads * HEAD)
    rope_part = jnp.sum(grad_keys[..., NOPE:], axis=1)
    grad_expanded = jnp.concatenate([grad_keys[..., :NOPE], grad_values], axis=-1)
    grad_expanded = grad_expanded.astype(BF16).reshape(GROUP, heads * (NOPE + VDIM))
    grad_wexp = dot_tn(compressed, grad_expanded).astype(BF16)
    compressed_part = dot_nt(grad_expanded, w_expand)
    summed = ar_tensor(
        jnp.concatenate(
            [compressed_part, rope_part, jnp.zeros((GROUP, ROPE), F32)], axis=1
        ).astype(BF16),
        9,
    ).astype(F32)
    grad_wq = dot_tn(normed, grad_qpre).astype(BF16)
    normed_part = dot_nt(grad_qpre, w_query).astype(BF16)
    unused, latent_norm_back = jax.vjp(rms_scale, latent_main, latent_gainf)
    grad_lmain, grad_lgain = latent_norm_back(summed[:, :LATENT])
    grad_lrope = rotate(summed[:, LATENT : LATENT + ROPE], cosine, -sine)
    grad_latent_low = jnp.concatenate([grad_lmain, grad_lrope], axis=-1).astype(BF16)
    grad_wlat = dot_tn(normed, grad_latent_low).astype(BF16)
    own_latent = lax.dynamic_slice_in_dim(w_latent, column * COLS, COLS, 0)
    latent_cols = dot_nt(grad_latent_low, own_latent)
    dx_cols, gains = back_input(
        normed_part, latent_cols, x_cols, inv_one, own_cols(attn_gain), dmid, dgain_ffn, 10
    )

    def sum_groups(value):
        moved = lax.all_to_all(value, "expert", split_axis=0, concat_axis=0, tiled=True)
        return jnp.sum(
            moved.reshape(GROUPS, moved.shape[0] // GROUPS, moved.shape[1]).astype(F32), axis=0
        )

    grad_wq = sum_groups(grad_wq)
    grad_wlat = sum_groups(grad_wlat)
    grad_wexp = sum_groups(grad_wexp)
    grad_wout = sum_groups(grad_wout).T

    extra = jnp.concatenate(
        [gains[:2].reshape(16, COLS), grad_lgain.astype(BF16).reshape(2, COLS)], axis=0
    )
    bundle = jnp.concatenate(
        [dx_cols.astype(BF16), extra, jnp.zeros((14, COLS), BF16)], axis=0
    )
    left, right = ag_expert(bundle[:, : COLS // 2], bundle[:, COLS // 2 :], 11)
    back_take = one_hot_rows(target, total)
    output = dot_nn(back_take, all_out).astype(BF16)
    input_grad = jnp.concatenate(
        [
            dot_nn(back_take, side[:, :GROUP].reshape(total, COLS // 2)).astype(BF16)
            for side in (left, right)
        ],
        axis=1,
    )
    sums = jnp.concatenate(
        [
            jnp.sum(side[:, GROUP : GROUP + 18].astype(F32), axis=0)
            for side in (left, right)
        ],
        axis=1,
    )
    gain_grads = sums[:16].reshape(2, D)
    lgain_grad = sums[16:].reshape(LATENT)
    own = lax.dynamic_slice_in_dim(gain_grads, group * (D // GROUPS), D // GROUPS, 1)
    own_l = lax.dynamic_slice_in_dim(lgain_grad, group * (LATENT // GROUPS), LATENT // GROUPS, 0)
    return (
        output,
        input_grad,
        own[0],
        grad_wq,
        grad_wlat,
        own_l,
        grad_wexp,
        grad_wout,
        own[1],
        grad_sgate,
        grad_sup,
        grad_sdown,
        jnp.swapaxes(grad_eg, 1, 2),
        jnp.swapaxes(grad_eu, 1, 2),
        grad_ed,
    )


def solution(mesh):
    return jax.shard_map(
        per_device,
        mesh=mesh,
        in_specs=(
            P("expert", "tensor"),
            P("expert", "tensor"),
            P(),
            P(None, "tensor"),
            P(),
            P(),
            P(None, "tensor"),
            P("tensor", None),
            P(),
            P(None, "tensor"),
            P(None, "tensor"),
            P("tensor", None),
            P("expert", None, "tensor"),
            P("expert", None, "tensor"),
            P("expert", "tensor", None),
            P(),
            P(),
            P("expert", None),
            P("expert", None),
        ),
        out_specs=(
            P("expert", "tensor"),
            P("expert", "tensor"),
            P("expert"),
            P("expert", "tensor"),
            P("expert", None),
            P("expert"),
            P("expert", "tensor"),
            P("tensor", "expert"),
            P("expert"),
            P("expert", "tensor"),
            P("expert", "tensor"),
            P("tensor", "expert"),
            P("expert", None, "tensor"),
            P("expert", None, "tensor"),
            P("expert", "tensor", None),
        ),
        check_vma=False,
    )
```

```python
import functools

import jax
import jax.numpy as jnp
from jax import lax
from jax.experimental import pallas as pl
from jax.experimental.pallas import tpu as pltpu
from jax.sharding import PartitionSpec as P

NOPE = 128
ROPE = 64
HEAD = NOPE + ROPE
LATENT = 512
VDIM = 128
D = 2048
GROUP = 256
TOP = 6
EXPERTS = 64
GROUPS = 16
LOCAL = 4
CAP = 27
PADCAP = 32
TENSOR = 8
COLS = D // TENSOR
EPS = 1e-06

XN = 4
YN = 4
ZN = 4
CORES = 2

F32 = jnp.float32
BF16 = jnp.bfloat16
MESH = pl.DeviceIdType.MESH
ANY = pl.BlockSpec(memory_space=pl.ANY)
VM = pl.BlockSpec(memory_space=pltpu.VMEM)
DMA = pltpu.SemaphoreType.DMA
MIB = 1024 * 1024


def remote(src, dst, ssem, rsem, axis, index):
    return pltpu.make_async_remote_copy(
        src_ref=src,
        dst_ref=dst,
        send_sem=ssem,
        recv_sem=rsem,
        device_id={axis: index},
        device_id_type=MESH,
    )


def greet(peers):
    barrier = pltpu.get_barrier_semaphore()
    for axis, index in peers:
        pl.semaphore_signal(barrier, inc=1, device_id={axis: index}, device_id_type=MESH)
    pl.semaphore_wait(barrier, len(peers))


def params(cid, vmem=48):
    return pltpu.CompilerParams(
        collective_id=cid, has_side_effects=True, vmem_limit_bytes=vmem * MIB
    )


def x_peers():
    t = lax.axis_index("tensor")
    x = t // CORES
    c = lax.rem(t, CORES)
    right = lax.rem(x + 1, XN) * CORES + c
    left = lax.rem(x + XN - 1, XN) * CORES + c
    far = lax.rem(x + 2, XN) * CORES + c
    twin = x * CORES + (1 - c)
    return t, right, left, far, twin


def greet_x():
    t, right, left, far, twin = x_peers()
    greet([("tensor", right), ("tensor", left), ("tensor", twin)])


def greet_tensor():
    t = lax.axis_index("tensor")
    greet([("tensor", lax.rem(t + j, TENSOR)) for j in range(1, TENSOR)])


def cols(index, width):
    return pl.ds(pl.multiple_of(index * width, width), width)


def gather_tensor(nch, src, out_ref, ssem, rsem):
    t, right, left, far, twin = x_peers()
    flip = twin - t
    rows, width = src.shape
    rc = rows // nch
    h = rc // 2

    def block(k, owner, part=None):
        if part is None:
            return out_ref.at[pl.ds(k * rc, rc), cols(owner, width)]
        return out_ref.at[pl.ds(k * rc + part * h, h), cols(owner, width)]

    sends = []

    def send(k, j, ref, dst, target):
        c = remote(ref, dst, ssem.at[k, j], rsem.at[k, j], "tensor", target)
        c.start()
        sends.append(c)

    def arrived(k, j, ref):
        remote(ref, ref, ssem.at[k, j], rsem.at[k, j], "tensor", twin).wait_recv()

    for k in range(nch):
        part = src.at[pl.ds(k * rc, rc), :]
        send(k, 0, part, block(k, t), right)
        send(k, 1, part, block(k, t), left)
        send(k, 4, part, block(k, t), twin)
    for k in range(nch):
        arrived(k, 0, block(k, left))
        send(k, 2, block(k, left, 0), block(k, left, 0), right)
        send(k, 5, block(k, left), block(k, left), twin)
        arrived(k, 1, block(k, right))
        send(k, 3, block(k, right, 1), block(k, right, 1), left)
        send(k, 6, block(k, right), block(k, right), twin)
    for k in range(nch):
        arrived(k, 2, block(k, far, 0))
        send(k, 7, block(k, far, 0), block(k, far, 0), twin)
        arrived(k, 3, block(k, far, 1))
        send(k, 8, block(k, far, 1), block(k, far, 1), twin)
    for k in range(nch):
        arrived(k, 4, block(k, twin))
        arrived(k, 5, block(k, left + flip))
        arrived(k, 6, block(k, right + flip))
        arrived(k, 7, block(k, far + flip, 0))
        arrived(k, 8, block(k, far + flip, 1))
    for s in sends:
        s.wait_send()


def gather_sems(nch):
    return [DMA((nch, 9)), DMA((nch, 9))]


def scatter_tensor(nch, view, rows, width, emit, own, sib, half, full, ssem, rsem, lsem):
    t, right, left, far, twin = x_peers()
    flip = twin - t
    rc = rows // nch
    h = rc // 2
    order = (far, right, left, t)
    sends = []

    def send(k, j, src, dst, target):
        c = remote(src, dst, ssem.at[k, j], rsem.at[k, j], "tensor", target)
        c.start()
        sends.append(c)

    def arrived(k, j, ref):
        remote(ref, ref, ssem.at[k, j], rsem.at[k, j], "tensor", twin).wait_recv()

    loads = {}
    for k in range(nch):
        r = pl.ds(k * rc, rc)
        for j, owner in enumerate(order):
            send(k, j, view(r, owner + flip), sib.at[j, r], twin)
            c = pltpu.make_async_copy(view(r, owner), own.at[j, r], lsem.at[k, j])
            c.start()
            loads[k, j] = c

    def pair(k, j):
        loads[k, j].wait()
        arrived(k, j, sib.at[j, pl.ds(k * rc, rc)])

    def add(j, r):
        return own[j, r].astype(F32) + sib[j, r].astype(F32)

    for k in range(nch):
        r0, r1 = pl.ds(k * rc, h), pl.ds(k * rc + h, h)
        r, hk = pl.ds(k * rc, rc), pl.ds(k * h, h)
        pair(k, 0)
        own[0, r] = add(0, r).astype(own.dtype)
        send(k, 4, own.at[0, r0], half.at[0, hk], right)
        send(k, 5, own.at[0, r1], half.at[1, hk], left)
    for k in range(nch):
        r0, r1 = pl.ds(k * rc, h), pl.ds(k * rc + h, h)
        r, hk = pl.ds(k * rc, rc), pl.ds(k * h, h)
        pair(k, 1)
        pair(k, 2)
        arrived(k, 4, half.at[0, hk])
        own[1, r1] = add(1, r1).astype(own.dtype)
        own[1, r0] = (add(1, r0) + half[0, hk].astype(F32)).astype(own.dtype)
        send(k, 6, own.at[1, r], full.at[0, r], right)
        arrived(k, 5, half.at[1, hk])
        own[2, r0] = add(2, r0).astype(own.dtype)
        own[2, r1] = (add(2, r1) + half[1, hk].astype(F32)).astype(own.dtype)
        send(k, 7, own.at[2, r], full.at[1, r], left)
    for k in range(nch):
        r = pl.ds(k * rc, rc)
        pair(k, 3)
        arrived(k, 6, full.at[0, r])
        arrived(k, 7, full.at[1, r])
        emit(r, add(3, r) + full[0, r].astype(F32) + full[1, r].astype(F32))
    for s in sends:
        s.wait_send()


def scatter_scratch(nch, rows, width, dtype):
    return [
        pltpu.VMEM((4, rows, width), dtype),
        pltpu.VMEM((4, rows, width), dtype),
        pltpu.VMEM((2, rows // 2, width), dtype),
        pltpu.VMEM((2, rows, width), dtype),
        DMA((nch, 8)),
        DMA((nch, 8)),
        DMA((nch, 4)),
    ]


def sum_rows_tensor(value, buf, ssem, rsem):
    t = lax.axis_index("tensor")
    rows = value.shape[0]
    mine = jnp.broadcast_to(jnp.sum(value, axis=1, keepdims=True), (rows, 128))
    buf[t] = jnp.transpose(mine)[:8]
    sends = []
    for j in range(1, TENSOR):
        to = lax.rem(t + j, TENSOR)
        c = remote(buf.at[t], buf.at[t], ssem.at[j], rsem.at[j], "tensor", to)
        c.start()
        sends.append(c)
    for j in range(1, TENSOR):
        ref = buf.at[lax.rem(t + TENSOR - j, TENSOR)]
        remote(ref, ref, ssem.at[j], rsem.at[j], "tensor", t).wait_recv()
    total = jnp.sum(buf[...], axis=0)
    for s in sends:
        s.wait_send()
    return jnp.transpose(total)[:, :1]


def sum_rows_scratch():
    return [pltpu.VMEM((TENSOR, 8, GROUP), F32), DMA((TENSOR,)), DMA((TENSOR,))]


def ag_tensor_kernel(nch, in_ref, out_ref, ssem, rsem, lsem):
    t = lax.axis_index("tensor")
    greet_x()
    own = pltpu.make_async_copy(in_ref, out_ref.at[:, cols(t, in_ref.shape[1])], lsem)
    own.start()
    gather_tensor(nch, in_ref, out_ref, ssem, rsem)
    own.wait()


def ag_tensor(value, cid, nch=1):
    rows, width = value.shape
    return pl.pallas_call(
        functools.partial(ag_tensor_kernel, nch),
        out_shape=jax.ShapeDtypeStruct((rows, width * TENSOR), value.dtype),
        in_specs=[ANY],
        out_specs=ANY,
        scratch_shapes=gather_sems(nch) + [DMA],
        compiler_params=params(cid),
        name="ag_tensor",
    )(value)


def middle_kernel(
    part_ref, x_ref, gain_ref, mid_ref, inv_ref, low_ref, full_ref, *scratch
):
    rs, ag, st, lsem = scratch[:7], scratch[7:9], scratch[9:12], scratch[12]
    t = lax.axis_index("tensor")
    greet_tensor()

    def emit(r, value):
        mid_ref[r] = x_ref[r].astype(F32) + value

    scatter_tensor(1, lambda r, owner: part_ref.at[r, cols(owner, COLS)], GROUP, COLS, emit, *rs)
    mid = mid_ref[...]
    inv = lax.rsqrt(sum_rows_tensor(mid * mid, *st) * (1.0 / D) + EPS)
    inv_ref[...] = inv
    low_ref[...] = (mid * inv * gain_ref[...].astype(F32)).astype(BF16)
    own = pltpu.make_async_copy(low_ref, full_ref.at[:, cols(t, COLS)], lsem)
    own.start()
    gather_tensor(1, low_ref, full_ref, *ag)
    own.wait()


def middle_step(part, x_cols, gain, cid):
    return pl.pallas_call(
        middle_kernel,
        out_shape=(
            jax.ShapeDtypeStruct((GROUP, COLS), F32),
            jax.ShapeDtypeStruct((GROUP, 1), F32),
            jax.ShapeDtypeStruct((GROUP, COLS), BF16),
            jax.ShapeDtypeStruct((GROUP, D), BF16),
        ),
        in_specs=[ANY, VM, VM],
        out_specs=(VM, VM, VM, ANY),
        scratch_shapes=scatter_scratch(1, GROUP, COLS, F32)
        + gather_sems(1)
        + sum_rows_scratch()
        + [DMA],
        compiler_params=params(cid),
        name="middle_step",
    )(part, x_cols, gain)


def back_input_kernel(
    part_ref, lat_ref, x_ref, inv_ref, gain_ref, dmid_ref, ffn_ref, dx_ref, gains_ref, low, dn, *scratch
):
    rs, st, ag, lsem = scratch[:7], scratch[7:10], scratch[10:12], scratch[12]
    t = lax.axis_index("tensor")
    greet_tensor()

    def emit(r, value):
        dn[r] = value + lat_ref[r]

    scatter_tensor(1, lambda r, owner: part_ref.at[r, cols(owner, COLS)], GROUP, COLS, emit, *rs)
    xd = x_ref[...].astype(F32)
    inv = inv_ref[...]
    d = dn[...]
    u = d * gain_ref[...].astype(F32)
    row = jnp.sum(d * xd * inv, axis=0, keepdims=True)
    place = lax.broadcasted_iota(jnp.int32, (16, COLS), 0)
    both = jnp.where(place == 0, row, jnp.where(place == 1, ffn_ref[...], 0.0))
    low[...] = both.astype(BF16)
    own = pltpu.make_async_copy(low, gains_ref.at[:, cols(t, COLS)], lsem)
    own.start()
    total = sum_rows_tensor(u * xd, *st)
    dx_ref[...] = dmid_ref[...] + inv * u - xd * (inv * inv * inv * total * (1.0 / D))
    for j in range(1, TENSOR):
        to = lax.rem(t + j, TENSOR)
        dst = gains_ref.at[:, cols(t, COLS)]
        remote(low, dst, ag[0].at[j], ag[1].at[j], "tensor", to).start()
    for j in range(1, TENSOR):
        dst = gains_ref.at[:, cols(lax.rem(t + TENSOR - j, TENSOR), COLS)]
        c = remote(low, dst, ag[0].at[j], ag[1].at[j], "tensor", t)
        c.wait_recv()
        c.wait_send()
    own.wait()


def back_input(part, lat, x, inv, gain, dmid, ffn, cid):
    return pl.pallas_call(
        back_input_kernel,
        out_shape=(
            jax.ShapeDtypeStruct((GROUP, COLS), F32),
            jax.ShapeDtypeStruct((16, D), BF16),
        ),
        in_specs=[ANY] + [VM] * 6,
        out_specs=(VM, ANY),
        scratch_shapes=[pltpu.VMEM((16, COLS), BF16), pltpu.VMEM((GROUP, COLS), F32)]
        + scatter_scratch(1, GROUP, COLS, BF16)
        + sum_rows_scratch()
        + [DMA((TENSOR,)), DMA((TENSOR,)), DMA],
        compiler_params=params(cid),
        name="back_input",
    )(part, lat, x, inv, gain, dmid, ffn)


def ar_kernel(in_ref, out_ref, acc, got, ssem, rsem, ssem2, rsem2):
    t = lax.axis_index("tensor")
    greet_tensor()
    for j in range(1, TENSOR):
        to = lax.rem(t + j, TENSOR)
        remote(in_ref.at[to], got.at[t], ssem.at[j], rsem.at[j], "tensor", to).start()
    total = in_ref[t].astype(F32)
    for j in range(1, TENSOR):
        frm = lax.rem(t + TENSOR - j, TENSOR)
        c = remote(in_ref.at[t], got.at[frm], ssem.at[j], rsem.at[j], "tensor", t)
        c.wait_recv()
        c.wait_send()
        total = total + got[frm].astype(F32)
    acc[...] = total.astype(BF16)
    out_ref[t] = acc[...]
    for j in range(1, TENSOR):
        to = lax.rem(t + j, TENSOR)
        remote(acc, out_ref.at[t], ssem2.at[j], rsem2.at[j], "tensor", to).start()
    for j in range(1, TENSOR):
        frm = lax.rem(t + TENSOR - j, TENSOR)
        c = remote(acc, out_ref.at[frm], ssem2.at[j], rsem2.at[j], "tensor", t)
        c.wait_recv()
        c.wait_send()


def ar_tensor(value, cid):
    rows, n = value.shape
    part = rows // TENSOR
    out = pl.pallas_call(
        ar_kernel,
        out_shape=jax.ShapeDtypeStruct((TENSOR, part, n), value.dtype),
        in_specs=[VM],
        out_specs=VM,
        scratch_shapes=[
            pltpu.VMEM((part, n), value.dtype),
            pltpu.VMEM((TENSOR, part, n), value.dtype),
        ]
        + [DMA((TENSOR,))] * 4,
        compiler_params=params(cid),
        name="ar_tensor",
    )(value.reshape(TENSOR, part, n))
    return out.reshape(rows, n)


def ag_expert_kernel(a_ref, b_ref, ao_ref, bo_ref, ssem, rsem, lsem):
    e = lax.axis_index("expert")
    z = e // YN
    y = lax.rem(e, YN)
    yr, yl, yf = lax.rem(y + 1, YN), lax.rem(y + 3, YN), lax.rem(y + 2, YN)
    zr, zl, zf = lax.rem(z + 1, ZN), lax.rem(z + 3, ZN), lax.rem(z + 2, ZN)
    y_right, y_left = z * YN + yr, z * YN + yl
    z_right, z_left = zr * YN + y, zl * YN + y
    greet([("expert", p) for p in (y_right, y_left, z_right, z_left)])
    h = a_ref.shape[0] // 2
    own_a = pltpu.make_async_copy(a_ref, ao_ref.at[z, y], lsem.at[0])
    own_b = pltpu.make_async_copy(b_ref, bo_ref.at[z, y], lsem.at[1])
    own_a.start()
    own_b.start()
    sends = []

    def send(j, src, dst, to):
        c = remote(src, dst, ssem.at[j], rsem.at[j], "expert", to)
        c.start()
        sends.append(c)

    def arrived(j, ref):
        remote(ref, ref, ssem.at[j], rsem.at[j], "expert", y_right).wait_recv()

    first, second = pl.ds(0, h), pl.ds(h, h)
    send(0, a_ref, ao_ref.at[z, y], y_right)
    send(1, a_ref, ao_ref.at[z, y], y_left)
    send(2, b_ref, bo_ref.at[z, y], z_right)
    send(3, b_ref, bo_ref.at[z, y], z_left)
    arrived(0, ao_ref.at[z, yl])
    send(4, ao_ref.at[z, yl, first], ao_ref.at[z, yl, first], y_right)
    arrived(1, ao_ref.at[z, yr])
    send(5, ao_ref.at[z, yr, second], ao_ref.at[z, yr, second], y_left)
    arrived(2, bo_ref.at[zl, y])
    send(6, bo_ref.at[zl, y, first], bo_ref.at[zl, y, first], z_right)
    arrived(3, bo_ref.at[zr, y])
    send(7, bo_ref.at[zr, y, second], bo_ref.at[zr, y, second], z_left)
    ys = (y, yl, yr, yf)
    zs = (z, zl, zr, zf)
    for i in range(4):
        if i == 3:
            arrived(4, ao_ref.at[z, yf, first])
            arrived(5, ao_ref.at[z, yf, second])
            arrived(6, bo_ref.at[zf, y, first])
            arrived(7, bo_ref.at[zf, y, second])
        sa, sb = ao_ref.at[z, ys[i]], bo_ref.at[zs[i], y]
        src_a, src_b = (a_ref, b_ref) if i == 0 else (sa, sb)
        send(8 + 4 * i, src_a, sa, z_right)
        send(9 + 4 * i, src_a, sa, z_left)
        send(10 + 4 * i, src_b, sb, y_right)
        send(11 + 4 * i, src_b, sb, y_left)
    for i in range(4):
        arrived(8 + 4 * i, ao_ref.at[zl, ys[i]])
        send(24 + 4 * i, ao_ref.at[zl, ys[i], first], ao_ref.at[zl, ys[i], first], z_right)
        arrived(9 + 4 * i, ao_ref.at[zr, ys[i]])
        send(25 + 4 * i, ao_ref.at[zr, ys[i], second], ao_ref.at[zr, ys[i], second], z_left)
        arrived(10 + 4 * i, bo_ref.at[zs[i], yl])
        send(26 + 4 * i, bo_ref.at[zs[i], yl, first], bo_ref.at[zs[i], yl, first], y_right)
        arrived(11 + 4 * i, bo_ref.at[zs[i], yr])
        send(27 + 4 * i, bo_ref.at[zs[i], yr, second], bo_ref.at[zs[i], yr, second], y_left)
    for i in range(4):
        arrived(24 + 4 * i, ao_ref.at[zf, ys[i], first])
        arrived(25 + 4 * i, ao_ref.at[zf, ys[i], second])
        arrived(26 + 4 * i, bo_ref.at[zs[i], yf, first])
        arrived(27 + 4 * i, bo_ref.at[zs[i], yf, second])
    for s in sends:
        s.wait_send()
    own_a.wait()
    own_b.wait()


def ag_expert(a, b, cid):
    shape = jax.ShapeDtypeStruct((ZN, YN) + a.shape, a.dtype)
    ao, bo = pl.pallas_call(
        ag_expert_kernel,
        out_shape=(shape, shape),
        in_specs=[ANY, ANY],
        out_specs=(ANY, ANY),
        scratch_shapes=[DMA((40,)), DMA((40,)), DMA((2,))],
        compiler_params=params(cid),
        name="ag_expert",
    )(a, b)
    return ao.reshape((GROUPS,) + a.shape), bo.reshape((GROUPS,) + a.shape)


def dot_nn(a, b):
    return lax.dot_general(a, b, (((1,), (0,)), ((), ())), preferred_element_type=F32)


def dot_nt(a, b):
    return lax.dot_general(a, b, (((1,), (1,)), ((), ())), preferred_element_type=F32)


def dot_tn(a, b):
    return lax.dot_general(a, b, (((0,), (0,)), ((), ())), preferred_element_type=F32)


ROWS = GROUPS * PADCAP


def expert_peers():
    e = lax.axis_index("expert")
    z = e // YN
    y = lax.rem(e, YN)
    peers = []
    for dz in range(ZN):
        for dy in range(YN):
            if dz or dy:
                to = lax.rem(z + dz, ZN) * YN + lax.rem(y + dy, YN)
                frm = lax.rem(z + ZN - dz, ZN) * YN + lax.rem(y + YN - dy, YN)
                peers.append((to, frm))
    return e, peers


def seat_rows(index):
    return pl.ds(pl.multiple_of(index * PADCAP, PADCAP), PADCAP)


def moe_kernel(
    place_ref, ncols_ref, nfull_hbm, dy_hbm, sg_hbm, su_hbm, sd_hbm, wg_hbm, wu_hbm, wd_hbm, grads_hbm,
    mid_ref, inv_ref, gain_ref, dyc_ref,
    part_hbm, gg_hbm, gu_hbm, gd_hbm, shout_ref, sh_ref, dsg_ref, dsu_ref, dmid_ref, dgain_ref, dattn_hbm,
    nfull, dyf, sgv, suv, sdv, outbuf, rows, drows, sib, half, full, wbuf, gbuf, gout, pbuf, res, back, shsum, low,
    d_s, d_r, a_s, a_r, r_s, r_r, b_s, b_r, f_s, f_r, st_buf, st_s, st_r, l_in, l_w, l_g, l_out, l_own,
):
    t, right, left, far, twin = x_peers()
    flip = twin - t
    e, peers = expert_peers()
    greet(
        [("tensor", lax.rem(t + j, TENSOR)) for j in range(1, TENSOR)]
        + [("expert", to) for to, frm in peers]
    )
    sends = []

    def send(src, dst, ssem, rsem, axis, to):
        c = remote(src, dst, ssem, rsem, axis, to)
        c.start()
        sends.append(c)

    def got(ref, ssem, rsem):
        remote(ref, ref, ssem, rsem, "tensor", twin).wait_recv()

    early = [
        pltpu.make_async_copy(src, dst, l_in.at[i])
        for i, (src, dst) in enumerate(
            [(nfull_hbm, nfull), (sg_hbm, sgv), (su_hbm, suv), (sd_hbm, sdv), (dy_hbm, dyf)]
        )
    ]
    for c in early:
        c.start()

    def load(k):
        s = k % 2
        copies = [
            pltpu.make_async_copy(ref.at[k], wbuf.at[s, i], l_w.at[s, i])
            for i, ref in enumerate((wg_hbm, wu_hbm, wd_hbm))
        ]
        copies.append(pltpu.make_async_copy(grads_hbm.at[k], gbuf.at[s], l_g.at[s]))
        for c in copies:
            c.start()
        return copies

    loads = {0: load(0), 1: load(1)}

    own_copies = []
    for k in range(LOCAL):
        outbuf[k] = dot_nn(place_ref[k], ncols_ref[...]).astype(BF16)
        c = pltpu.make_async_copy(
            outbuf.at[k, seat_rows(e)], rows.at[k, seat_rows(e), cols(t, COLS)], l_own.at[k]
        )
        c.start()
        own_copies.append(c)
        for j, (to, frm) in enumerate(peers):
            send(
                outbuf.at[k, seat_rows(to)], rows.at[k, seat_rows(e), cols(t, COLS)],
                d_s.at[k, j], d_r.at[k, j], "expert", to,
            )

    h = ROWS // 2

    def block(k, owner, part=None):
        if part is None:
            return rows.at[k, :, cols(owner, COLS)]
        return rows.at[k, pl.ds(part * h, h), cols(owner, COLS)]

    def asend(k, j, ref, to):
        send(ref, ref, a_s.at[k, j], a_r.at[k, j], "tensor", to)

    def agot(k, j, ref):
        got(ref, a_s.at[k, j], a_r.at[k, j])

    def gather_1(k):
        own_copies[k].wait()
        for j, (to, frm) in enumerate(peers):
            ref = rows.at[k, seat_rows(frm), cols(t, COLS)]
            got(ref, d_s.at[k, j], d_r.at[k, j])
        asend(k, 0, block(k, t), right)
        asend(k, 1, block(k, t), left)
        asend(k, 4, block(k, t), twin)

    def gather_2(k):
        agot(k, 0, block(k, left))
        asend(k, 2, block(k, left, 0), right)
        asend(k, 5, block(k, left), twin)
        agot(k, 1, block(k, right))
        asend(k, 3, block(k, right, 1), left)
        asend(k, 6, block(k, right), twin)

    def gather_3(k):
        agot(k, 2, block(k, far, 0))
        asend(k, 7, block(k, far, 0), twin)
        agot(k, 3, block(k, far, 1))
        asend(k, 8, block(k, far, 1), twin)

    def gather_4(k):
        agot(k, 4, block(k, twin))
        agot(k, 5, block(k, left + flip))
        agot(k, 6, block(k, right + flip))
        agot(k, 7, block(k, far + flip, 0))
        agot(k, 8, block(k, far + flip, 1))

    order = (far, right, left, t)

    def slot(k):
        return 3 if k == LOCAL else k % 3

    def rsend(k, j, src, dst, to):
        send(src, dst, r_s.at[k, j], r_r.at[k, j], "tensor", to)

    def rgot(k, j, ref):
        got(ref, r_s.at[k, j], r_r.at[k, j])

    def mine(k, j):
        return drows[slot(k), :, cols(order[j], COLS)].astype(F32)

    twin_sends = {}

    def sum_1(k):
        first = len(sends)
        for j, owner in enumerate(order):
            rsend(k, j, drows.at[slot(k), :, cols(owner + flip, COLS)], sib.at[k, j], twin)
        twin_sends[k] = sends[first:]
        del sends[first:]

    def sum_2(k):
        rgot(k, 0, sib.at[k, 0])
        sib[k, 0] = (mine(k, 0) + sib[k, 0].astype(F32)).astype(BF16)
        rsend(k, 4, sib.at[k, 0, pl.ds(0, h)], half.at[k, 0], right)
        rsend(k, 5, sib.at[k, 0, pl.ds(h, h)], half.at[k, 1], left)

    def sum_3(k):
        for j, to in ((1, right), (2, left)):
            rgot(k, j, sib.at[k, j])
            rgot(k, 3 + j, half.at[k, j - 1])
            both = mine(k, j) + sib[k, j].astype(F32)
            extra = half[k, j - 1].astype(F32)
            if j == 1:
                sib[k, j, :h] = (both[:h] + extra).astype(BF16)
                sib[k, j, h:] = both[h:].astype(BF16)
            else:
                sib[k, j, :h] = both[:h].astype(BF16)
                sib[k, j, h:] = (both[h:] + extra).astype(BF16)
            rsend(k, 5 + j, sib.at[k, j], full.at[k, j - 1], to)

    def sum_4(k):
        rgot(k, 3, sib.at[k, 3])
        rgot(k, 6, full.at[k, 0])
        rgot(k, 7, full.at[k, 1])
        value = mine(k, 3) + sib[k, 3].astype(F32) + full[k, 0].astype(F32) + full[k, 1].astype(F32)
        for c in twin_sends[k]:
            c.wait_send()
        if k == LOCAL:
            shsum[...] = value
            return
        res[k] = value.astype(BF16)
        c = pltpu.make_async_copy(res.at[k, seat_rows(e)], back.at[k, seat_rows(e)], l_own.at[k])
        c.start()
        own_copies[k] = c
        for j, (to, frm) in enumerate(peers):
            send(res.at[k, seat_rows(to)], back.at[k, seat_rows(e)], b_s.at[k, j], b_r.at[k, j], "expert", to)

    def shared_forward():
        for c in early[:4]:
            c.wait()
        n = nfull[...]
        g = dot_nt(n, sgv[...])
        u = dot_nt(n, suv[...])
        sig = jax.nn.sigmoid(g)
        silu = g * sig
        sh_ref[...] = (silu * u).astype(BF16)
        return g, u, sig, silu

    def shared_backward(g, u, sig, silu):
        early[4].wait()
        dh = dot_nt(dyf[...], sdv[...])
        dsg_ref[...] = (dh * u * (sig * (1.0 + g * (1.0 - sig)))).astype(BF16)
        dsu_ref[...] = (dh * silu).astype(BF16)

    tiles = [pl.ds(i * 512, 512) for i in range(D // 512)]

    def shared_rows():
        hid = sh_ref[...]
        dsg, dsu = dsg_ref[...], dsu_ref[...]
        for n in tiles:
            drows[3, :GROUP, n] = dot_nn(hid, sdv[:, n]).astype(BF16)
            drows[3, GROUP:, n] = (dot_nn(dsg, sgv[:, n]) + dot_nn(dsu, suv[:, n])).astype(BF16)

    out_copies = {}

    def compute_1(k):
        s = k % 2
        for c in loads[k]:
            c.wait()
        r = rows[k]
        gate = dot_nt(r, wbuf[s, 0])
        up = dot_nt(r, wbuf[s, 1])
        dh = dot_nt(gbuf[s], wbuf[s, 2])
        sig = jax.nn.sigmoid(gate)
        silu = gate * sig
        hidden = (silu * up).astype(BF16)
        dg = (dh * up * (sig * (1.0 + gate * (1.0 - sig)))).astype(BF16)
        du = (dh * silu).astype(BF16)
        for n in tiles:
            drows[slot(k), :, n] = (
                dot_nn(dg, wbuf[s, 0, :, n]) + dot_nn(du, wbuf[s, 1, :, n])
            ).astype(BF16)
        return hidden, dg, du

    def compute_2(k, hidden, dg, du):
        s = k % 2
        if k:
            for c in out_copies[k - 1]:
                c.wait()
        for n in tiles:
            pbuf[:, n] = dot_nn(hidden, wbuf[s, 2, :, n]).astype(BF16)
            gout[0, :, n] = dot_tn(dg, rows[k, :, n])
            gout[1, :, n] = dot_tn(du, rows[k, :, n])
            gout[2, :, n] = dot_tn(hidden, gbuf[s, :, n])
        out_copies[k] = [
            pltpu.make_async_copy(src, dst.at[k], l_out.at[i])
            for i, (src, dst) in enumerate(
                [(pbuf, part_hbm), (gout.at[0], gg_hbm), (gout.at[1], gu_hbm), (gout.at[2], gd_hbm)]
            )
        ]
        for c in out_copies[k]:
            c.start()
        if k + 2 < LOCAL:
            loads[k + 2] = load(k + 2)

    state = shared_forward()
    gather_1(0)
    shared_backward(*state)
    gather_1(1)
    gather_2(0)
    shared_rows()
    sum_1(4)
    gather_1(2)
    gather_2(1)
    gather_3(0)
    gather_1(3)
    gather_4(0)
    c0 = compute_1(0)
    sum_1(0)
    gather_2(2)
    gather_3(1)
    sum_2(4)
    compute_2(0, *c0)
    gather_4(1)
    sum_2(0)
    c1 = compute_1(1)
    sum_1(1)
    gather_2(3)
    gather_3(2)
    sum_3(0)
    compute_2(1, *c1)
    gather_4(2)
    sum_2(1)
    c2 = compute_1(2)
    sum_1(2)
    gather_3(3)
    sum_3(1)
    sum_4(0)
    sum_3(4)
    compute_2(2, *c2)
    gather_4(3)
    sum_2(2)
    c3 = compute_1(3)
    sum_1(3)
    sum_3(2)
    sum_4(1)
    sum_2(3)
    compute_2(3, *c3)
    sum_4(2)
    sum_3(3)
    sum_4(4)
    shout_ref[...] = shsum[:GROUP]
    sum_4(3)

    dn = shsum[GROUP:]
    for k in range(LOCAL):
        own_copies[k].wait()
        for j, (to, frm) in enumerate(peers):
            got(back.at[k, seat_rows(frm)], b_s.at[k, j], b_r.at[k, j])
        dn = dn + dot_tn(place_ref[k], back[k])

    mid = mid_ref[...]
    inv = inv_ref[...]
    u = dn * gain_ref[...].astype(F32)
    total = sum_rows_tensor(u * mid, st_buf, st_s, st_r)
    dmid = dyc_ref[...].astype(F32) + inv * u - mid * (inv * inv * inv * total * (1.0 / D))
    dmid_ref[...] = dmid
    low[...] = dmid.astype(BF16)
    own = pltpu.make_async_copy(low, dattn_hbm.at[:, cols(t, COLS)], l_own.at[0])
    own.start()
    dgain_ref[...] = jnp.sum(dn * mid * inv, axis=0, keepdims=True)
    gather_tensor(1, low, dattn_hbm, f_s, f_r)
    own.wait()
    for c in out_copies[LOCAL - 1]:
        c.wait()
    for c in sends:
        c.wait_send()


def moe_step(place, ncols, nfull, dy, sg, su, sd, wg, wu, wd, grads, mid, inv, gain, dyc, cid):
    hid = wd.shape[1]
    wide = sd.shape[0]
    wshape = jax.ShapeDtypeStruct((LOCAL, hid, D), F32)
    vmem = pltpu.VMEM
    return pl.pallas_call(
        moe_kernel,
        out_shape=(
            jax.ShapeDtypeStruct((LOCAL, ROWS, D), BF16),
            wshape,
            wshape,
            wshape,
            jax.ShapeDtypeStruct((GROUP, COLS), F32),
            jax.ShapeDtypeStruct((GROUP, wide), BF16),
            jax.ShapeDtypeStruct((GROUP, wide), BF16),
            jax.ShapeDtypeStruct((GROUP, wide), BF16),
            jax.ShapeDtypeStruct((GROUP, COLS), F32),
            jax.ShapeDtypeStruct((1, COLS), F32),
            jax.ShapeDtypeStruct((GROUP, D), BF16),
        ),
        in_specs=[VM, VM] + [ANY] * 9 + [VM] * 4,
        out_specs=(ANY, ANY, ANY, ANY, VM, VM, VM, VM, VM, VM, ANY),
        scratch_shapes=[
            vmem((GROUP, D), BF16),
            vmem((GROUP, D), BF16),
            vmem((wide, D), BF16),
            vmem((wide, D), BF16),
            vmem((wide, D), BF16),
            vmem((LOCAL, ROWS, COLS), BF16),
            vmem((LOCAL, ROWS, D), BF16),
            vmem((4, ROWS, D), BF16),
            vmem((LOCAL + 1, 4, ROWS, COLS), BF16),
            vmem((LOCAL + 1, 2, ROWS // 2, COLS), BF16),
            vmem((LOCAL + 1, 2, ROWS, COLS), BF16),
            vmem((2, 3, hid, D), BF16),
            vmem((2, ROWS, D), BF16),
            vmem((3, hid, D), F32),
            vmem((ROWS, D), BF16),
            vmem((LOCAL, ROWS, COLS), BF16),
            vmem((LOCAL, ROWS, COLS), BF16),
            vmem((2 * GROUP, COLS), F32),
            vmem((GROUP, COLS), BF16),
            DMA((LOCAL, 15)),
            DMA((LOCAL, 15)),
            DMA((LOCAL, 9)),
            DMA((LOCAL, 9)),
            DMA((LOCAL + 1, 8)),
            DMA((LOCAL + 1, 8)),
            DMA((LOCAL, 15)),
            DMA((LOCAL, 15)),
            DMA((1, 9)),
            DMA((1, 9)),
            vmem((TENSOR, 8, GROUP), F32),
            DMA((TENSOR,)),
            DMA((TENSOR,)),
            DMA((5,)),
            DMA((2, 3)),
            DMA((2,)),
            DMA((4,)),
            DMA((LOCAL,)),
        ],
        compiler_params=params(cid, 63),
        cost_estimate=pl.CostEstimate(
            flops=40 * 10**9, bytes_accessed=100 * MIB, transcendentals=0
        ),
        name="moe_step",
    )(place, ncols, nfull, dy, sg, su, sd, wg, wu, wd, grads, mid, inv, gain, dyc)


def rms_scale(value, gain):
    return value * lax.rsqrt(jnp.mean(value * value, axis=-1, keepdims=True) + EPS) * gain


def rotate(value, cosine, sine):
    half = value.shape[-1] // 2
    first = value[..., :half]
    second = value[..., half:]
    return jnp.concatenate(
        [first * cosine - second * sine, second * cosine + first * sine], axis=-1
    )


def pick(index, table):
    numbers = jnp.arange(table.shape[0], dtype=jnp.int32)
    return jnp.sum(jnp.where(index[:, None] == numbers[None, :], table[None, :], 0), axis=1)


def exclusive(values):
    numbers = jnp.arange(values.shape[0], dtype=jnp.int32)
    return jnp.sum(jnp.where(numbers[:, None] > numbers[None, :], values[None, :], 0), axis=1)


def deal_rows(lengths, order, group):
    begins = exclusive(lengths)
    dealt_begins = exclusive(pick(order, lengths))
    dealt_source = pick(order, begins)
    numbers = jnp.arange(lengths.shape[0], dtype=jnp.int32)
    inverse = jnp.sum(jnp.where(order[None, :] == numbers[:, None], numbers[None, :], 0), axis=1)
    given_target = pick(inverse, dealt_begins)
    rows = group * GROUP + jnp.arange(GROUP, dtype=jnp.int32)
    which = jnp.sum((rows[:, None] >= dealt_begins[None, :]).astype(jnp.int32), axis=1) - 1
    offsets = rows - pick(which, dealt_begins)
    source = pick(which, dealt_source) + offsets
    owner = jnp.sum((rows[:, None] >= begins[None, :]).astype(jnp.int32), axis=1) - 1
    target = pick(owner, given_target - begins) + rows
    return source, target, offsets, which


def one_hot_rows(index, count):
    numbers = jnp.arange(count, dtype=jnp.int32)
    return (index[:, None] == numbers[None, :]).astype(BF16)


def per_device(
    tokens,
    cotangent,
    attn_gain,
    w_query,
    w_latent,
    latent_gain,
    w_expand,
    w_out,
    ffn_gain,
    shared_gate,
    shared_up,
    shared_down,
    expert_gate,
    expert_up,
    expert_down,
    seq_lengths,
    seq_order,
    routes,
    gate_weights,
):
    group = lax.axis_index("expert")
    column = lax.axis_index("tensor")
    total = GROUP * GROUPS
    source, target, offsets, which = deal_rows(seq_lengths, seq_order, group)

    all_x, all_dy = ag_expert(tokens, cotangent, 0)
    take = one_hot_rows(source, total)
    x_cols = dot_nn(take, all_x.reshape(total, COLS)).astype(BF16)
    dy_cols = dot_nn(take, all_dy.reshape(total, COLS)).astype(BF16)
    x_full = ag_tensor(x_cols, 1)
    dy_full = lax.all_gather(dy_cols, "tensor", axis=1, tiled=True)

    chosen = routes.T
    gates = gate_weights.T
    numbers = jnp.arange(EXPERTS, dtype=jnp.int32)
    experts = lax.rem(numbers, GROUPS) * LOCAL + numbers // GROUPS
    hit = chosen[:, None, :] == experts[None, :, None]
    member = jnp.sum(hit.astype(F32), axis=0)
    gate_of = jnp.sum(jnp.where(hit, gates[:, None, :], 0.0), axis=0)
    token = jnp.arange(GROUP, dtype=jnp.int32)
    earlier = (token[:, None] < token[None, :]).astype(BF16)
    count = dot_nn(member.astype(BF16), earlier)
    slot = jnp.where((member > 0.5) & (count < CAP - 0.5), count, -1.0).astype(jnp.int32)
    seats = jnp.arange(PADCAP, dtype=jnp.int32)
    match = slot[:, None, :] == seats[None, :, None]
    place = match.astype(BF16).reshape(EXPERTS * PADCAP, GROUP)
    weight = jnp.where(match, gate_of[:, None, :], 0.0)
    slot_gate = jnp.sum(weight, axis=2).reshape(EXPERTS * PADCAP, 1)
    weight = weight.reshape(EXPERTS * PADCAP, GROUP)
    weight_high = lax.reduce_precision(weight, 8, 7)
    weight_low = (weight - weight_high).astype(BF16)
    weight_high = weight_high.astype(BF16)

    slot_grad = (slot_gate * dot_nn(place, dy_cols)).astype(BF16)
    slot_grad = slot_grad.reshape(LOCAL, GROUPS, PADCAP, COLS)
    slot_grad = lax.all_to_all(slot_grad, "expert", split_axis=1, concat_axis=1, tiled=True)
    grad_rows = lax.all_gather(slot_grad.reshape(-1, COLS), "tensor", axis=1, tiled=True)

    attn_gainf = attn_gain.astype(F32)
    latent_gainf = latent_gain.astype(F32)
    half = ROPE // 2
    freqs = jnp.exp(-jnp.log(10000.0) * jnp.arange(half, dtype=F32) / half)
    angles = offsets.astype(F32)[:, None] * freqs[None, :]
    cosine, sine = jnp.cos(angles), jnp.sin(angles)
    dealt = x_full.astype(F32)
    inv_one = lax.rsqrt(jnp.mean(dealt * dealt, axis=-1, keepdims=True) + EPS)
    normed = (dealt * inv_one * attn_gainf).astype(BF16)
    heads = w_query.shape[1] // HEAD
    scale = HEAD ** (-0.5)
    query_pre = dot_nn(normed, w_query).reshape(GROUP, heads, HEAD)
    cos_h, sin_h = cosine[:, None, :], sine[:, None, :]
    query = jnp.concatenate(
        [query_pre[..., :NOPE], rotate(query_pre[..., NOPE:], cos_h, sin_h)], axis=-1
    ).astype(BF16)
    latent = dot_nn(normed, w_latent)
    key_rope = rotate(latent[:, LATENT:], cosine, sine).astype(BF16)
    latent_main = latent[:, :LATENT]
    compressed = rms_scale(latent_main, latent_gainf).astype(BF16)
    expanded = dot_nn(compressed, w_expand).astype(BF16).reshape(GROUP, heads, NOPE + VDIM)
    keys = jnp.concatenate(
        [expanded[..., :NOPE], jnp.broadcast_to(key_rope[:, None, :], (GROUP, heads, ROPE))],
        axis=-1,
    )
    values = expanded[..., NOPE:]
    allowed = (which[:, None] == which[None, :]) & (token[:, None] >= token[None, :])
    raw = jnp.einsum("qhd,khd->hqk", query, keys, preferred_element_type=F32) * scale
    scores = jnp.where(allowed[None], raw, -1e30)
    peak = jnp.max(scores, axis=-1, keepdims=True)
    expo = jnp.exp(scores - peak)
    probs = expo / jnp.sum(expo, axis=-1, keepdims=True)
    probs_low = probs.astype(BF16)
    mixed = jnp.einsum("hqk,khd->qhd", probs_low, values, preferred_element_type=F32)
    mixed = mixed.astype(BF16).reshape(GROUP, heads * VDIM)
    attn_part = dot_nn(mixed, w_out)

    def own_cols(vector):
        return lax.dynamic_slice_in_dim(vector, column * COLS, COLS, 0).reshape(1, COLS)

    middle, inv_two, normed_two_cols, normed_two = middle_step(
        attn_part, x_cols, own_cols(ffn_gain), 2
    )

    (
        part, grad_eg, grad_eu, grad_ed, shared_out, shared_h, grad_sg, grad_su, dmid, dgain_ffn, d_attn
    ) = moe_step(
        place.reshape(LOCAL, ROWS, GROUP),
        normed_two_cols,
        normed_two,
        dy_full,
        shared_gate.T,
        shared_up.T,
        shared_down,
        jnp.swapaxes(expert_gate, 1, 2),
        jnp.swapaxes(expert_up, 1, 2),
        expert_down,
        grad_rows.reshape(LOCAL, ROWS, D),
        middle,
        inv_two,
        own_cols(ffn_gain),
        dy_cols,
        3,
    )
    shared_weights = jnp.concatenate(
        [
            dot_tn(normed_two, grad_sg).astype(BF16),
            dot_tn(normed_two, grad_su).astype(BF16),
            dot_tn(dy_full, shared_h).astype(BF16),
        ],
        axis=1,
    )
    shared_weights = lax.psum_scatter(
        shared_weights, "expert", scatter_dimension=0, tiled=True
    ).astype(F32)
    wide = shared_h.shape[1]
    grad_sgate = shared_weights[:, :wide]
    grad_sup = shared_weights[:, wide : 2 * wide]
    grad_sdown = shared_weights[:, 2 * wide :].T

    returned = lax.psum_scatter(part.reshape(-1, D), "tensor", scatter_dimension=1, tiled=True)
    returned = lax.all_to_all(
        returned.reshape(LOCAL, GROUPS, PADCAP, COLS),
        "expert",
        split_axis=1,
        concat_axis=1,
        tiled=True,
    ).reshape(-1, COLS)
    routed = dot_tn(weight_high, returned) + dot_tn(weight_low, returned)
    output_cols = (middle + shared_out + routed).astype(BF16)
    all_out = lax.all_gather(output_cols, "expert", axis=0, tiled=True)

    grad_wout = dot_tn(d_attn, mixed).astype(BF16)
    grad_mixed = dot_nt(d_attn, w_out).astype(BF16).reshape(GROUP, heads, VDIM)
    grad_values = jnp.einsum("hqk,qhd->khd", probs_low, grad_mixed, preferred_element_type=F32)
    grad_probs = jnp.einsum("qhd,khd->hqk", grad_mixed, values, preferred_element_type=F32)
    grad_scores = (
        probs * (grad_probs - jnp.sum(grad_probs * probs, axis=-1, keepdims=True))
    ).astype(BF16)
    grad_query = jnp.einsum("hqk,khd->qhd", grad_scores, keys, preferred_element_type=F32) * scale
    grad_keys = jnp.einsum("hqk,qhd->khd", grad_scores, query, preferred_element_type=F32) * scale
    grad_qpre = jnp.concatenate(
        [grad_query[..., :NOPE], rotate(grad_query[..., NOPE:], cos_h, -sin_h)], axis=-1
    )
    grad_qpre = grad_qpre.astype(BF16).reshape(GROUP, heads * HEAD)
    rope_part = jnp.sum(grad_keys[..., NOPE:], axis=1)
    grad_expanded = jnp.concatenate([grad_keys[..., :NOPE], grad_values], axis=-1)
    grad_expanded = grad_expanded.astype(BF16).reshape(GROUP, heads * (NOPE + VDIM))
    grad_wexp = dot_tn(compressed, grad_expanded).astype(BF16)
    compressed_part = dot_nt(grad_expanded, w_expand)
    summed = ar_tensor(
        jnp.concatenate(
            [compressed_part, rope_part, jnp.zeros((GROUP, ROPE), F32)], axis=1
        ).astype(BF16),
        9,
    ).astype(F32)
    grad_wq = dot_tn(normed, grad_qpre).astype(BF16)
    normed_part = dot_nt(grad_qpre, w_query).astype(BF16)
    unused, latent_norm_back = jax.vjp(rms_scale, latent_main, latent_gainf)
    grad_lmain, grad_lgain = latent_norm_back(summed[:, :LATENT])
    grad_lrope = rotate(summed[:, LATENT : LATENT + ROPE], cosine, -sine)
    grad_latent_low = jnp.concatenate([grad_lmain, grad_lrope], axis=-1).astype(BF16)
    grad_wlat = dot_tn(normed, grad_latent_low).astype(BF16)
    own_latent = lax.dynamic_slice_in_dim(w_latent, column * COLS, COLS, 0)
    latent_cols = dot_nt(grad_latent_low, own_latent)
    dx_cols, gains = back_input(
        normed_part, latent_cols, x_cols, inv_one, own_cols(attn_gain), dmid, dgain_ffn, 10
    )

    def sum_groups(value):
        moved = lax.all_to_all(value, "expert", split_axis=0, concat_axis=0, tiled=True)
        return jnp.sum(
            moved.reshape(GROUPS, moved.shape[0] // GROUPS, moved.shape[1]).astype(F32), axis=0
        )

    grad_wq = sum_groups(grad_wq)
    grad_wlat = sum_groups(grad_wlat)
    grad_wexp = sum_groups(grad_wexp)
    grad_wout = sum_groups(grad_wout).T

    extra = jnp.concatenate(
        [gains[:2].reshape(16, COLS), grad_lgain.astype(BF16).reshape(2, COLS)], axis=0
    )
    bundle = jnp.concatenate(
        [dx_cols.astype(BF16), extra, jnp.zeros((14, COLS), BF16)], axis=0
    )
    left, right = ag_expert(bundle[:, : COLS // 2], bundle[:, COLS // 2 :], 11)
    back_take = one_hot_rows(target, total)
    output = dot_nn(back_take, all_out).astype(BF16)
    input_grad = jnp.concatenate(
        [
            dot_nn(back_take, side[:, :GROUP].reshape(total, COLS // 2)).astype(BF16)
            for side in (left, right)
        ],
        axis=1,
    )
    sums = jnp.concatenate(
        [
            jnp.sum(side[:, GROUP : GROUP + 18].astype(F32), axis=0)
            for side in (left, right)
        ],
        axis=1,
    )
    gain_grads = sums[:16].reshape(2, D)
    lgain_grad = sums[16:].reshape(LATENT)
    own = lax.dynamic_slice_in_dim(gain_grads, group * (D // GROUPS), D // GROUPS, 1)
    own_l = lax.dynamic_slice_in_dim(lgain_grad, group * (LATENT // GROUPS), LATENT // GROUPS, 0)
    return (
        output,
        input_grad,
        own[0],
        grad_wq,
        grad_wlat,
        own_l,
        grad_wexp,
        grad_wout,
        own[1],
        grad_sgate,
        grad_sup,
        grad_sdown,
        jnp.swapaxes(grad_eg, 1, 2),
        jnp.swapaxes(grad_eu, 1, 2),
        grad_ed,
    )


def solution(mesh):
    return jax.shard_map(
        per_device,
        mesh=mesh,
        in_specs=(
            P("expert", "tensor"),
            P("expert", "tensor"),
            P(),
            P(None, "tensor"),
            P(),
            P(),
            P(None, "tensor"),
            P("tensor", None),
            P(),
            P(None, "tensor"),
            P(None, "tensor"),
            P("tensor", None),
            P("expert", None, "tensor"),
            P("expert", None, "tensor"),
            P("expert", "tensor", None),
            P(),
            P(),
            P("expert", None),
            P("expert", None),
        ),
        out_specs=(
            P("expert", "tensor"),
            P("expert", "tensor"),
            P("expert"),
            P("expert", "tensor"),
            P("expert", None),
            P("expert"),
            P("expert", "tensor"),
            P("tensor", "expert"),
            P("expert"),
            P("expert", "tensor"),
            P("expert", "tensor"),
            P("tensor", "expert"),
            P("expert", None, "tensor"),
            P("expert", None, "tensor"),
            P("expert", "tensor", None),
        ),
        check_vma=False,
    )
```

```python
import functools

import jax
import jax.numpy as jnp
from jax import lax
from jax.experimental import pallas as pl
from jax.experimental.pallas import tpu as pltpu
from jax.sharding import PartitionSpec as P

NOPE = 128
ROPE = 64
HEAD = NOPE + ROPE
LATENT = 512
VDIM = 128
D = 2048
GROUP = 256
TOP = 6
EXPERTS = 64
GROUPS = 16
LOCAL = 4
CAP = 27
PADCAP = 32
TENSOR = 8
COLS = D // TENSOR
EPS = 1e-06

XN = 4
YN = 4
ZN = 4
CORES = 2

F32 = jnp.float32
BF16 = jnp.bfloat16
MESH = pl.DeviceIdType.MESH
ANY = pl.BlockSpec(memory_space=pl.ANY)
VM = pl.BlockSpec(memory_space=pltpu.VMEM)
DMA = pltpu.SemaphoreType.DMA
MIB = 1024 * 1024


def remote(src, dst, ssem, rsem, axis, index):
    return pltpu.make_async_remote_copy(
        src_ref=src,
        dst_ref=dst,
        send_sem=ssem,
        recv_sem=rsem,
        device_id={axis: index},
        device_id_type=MESH,
    )


def greet(peers):
    barrier = pltpu.get_barrier_semaphore()
    for axis, index in peers:
        pl.semaphore_signal(barrier, inc=1, device_id={axis: index}, device_id_type=MESH)
    pl.semaphore_wait(barrier, len(peers))


def params(cid, vmem=48):
    return pltpu.CompilerParams(
        collective_id=cid, has_side_effects=True, vmem_limit_bytes=vmem * MIB
    )


def x_peers():
    t = lax.axis_index("tensor")
    x = t // CORES
    c = lax.rem(t, CORES)
    right = lax.rem(x + 1, XN) * CORES + c
    left = lax.rem(x + XN - 1, XN) * CORES + c
    far = lax.rem(x + 2, XN) * CORES + c
    twin = x * CORES + (1 - c)
    return t, right, left, far, twin


def greet_x():
    t, right, left, far, twin = x_peers()
    greet([("tensor", right), ("tensor", left), ("tensor", twin)])


def greet_tensor():
    t = lax.axis_index("tensor")
    greet([("tensor", lax.rem(t + j, TENSOR)) for j in range(1, TENSOR)])


def cols(index, width):
    return pl.ds(pl.multiple_of(index * width, width), width)


def gather_tensor(nch, src, out_ref, ssem, rsem):
    t, right, left, far, twin = x_peers()
    flip = twin - t
    rows, width = src.shape
    rc = rows // nch
    h = rc // 2

    def block(k, owner, part=None):
        if part is None:
            return out_ref.at[pl.ds(k * rc, rc), cols(owner, width)]
        return out_ref.at[pl.ds(k * rc + part * h, h), cols(owner, width)]

    sends = []

    def send(k, j, ref, dst, target):
        c = remote(ref, dst, ssem.at[k, j], rsem.at[k, j], "tensor", target)
        c.start()
        sends.append(c)

    def arrived(k, j, ref):
        remote(ref, ref, ssem.at[k, j], rsem.at[k, j], "tensor", twin).wait_recv()

    for k in range(nch):
        part = src.at[pl.ds(k * rc, rc), :]
        send(k, 0, part, block(k, t), right)
        send(k, 1, part, block(k, t), left)
        send(k, 4, part, block(k, t), twin)
    for k in range(nch):
        arrived(k, 0, block(k, left))
        send(k, 2, block(k, left, 0), block(k, left, 0), right)
        send(k, 5, block(k, left), block(k, left), twin)
        arrived(k, 1, block(k, right))
        send(k, 3, block(k, right, 1), block(k, right, 1), left)
        send(k, 6, block(k, right), block(k, right), twin)
    for k in range(nch):
        arrived(k, 2, block(k, far, 0))
        send(k, 7, block(k, far, 0), block(k, far, 0), twin)
        arrived(k, 3, block(k, far, 1))
        send(k, 8, block(k, far, 1), block(k, far, 1), twin)
    for k in range(nch):
        arrived(k, 4, block(k, twin))
        arrived(k, 5, block(k, left + flip))
        arrived(k, 6, block(k, right + flip))
        arrived(k, 7, block(k, far + flip, 0))
        arrived(k, 8, block(k, far + flip, 1))
    for s in sends:
        s.wait_send()


def gather_sems(nch):
    return [DMA((nch, 9)), DMA((nch, 9))]


def scatter_tensor(nch, view, rows, width, emit, own, sib, half, full, ssem, rsem, lsem):
    t, right, left, far, twin = x_peers()
    flip = twin - t
    rc = rows // nch
    h = rc // 2
    order = (far, right, left, t)
    sends = []

    def send(k, j, src, dst, target):
        c = remote(src, dst, ssem.at[k, j], rsem.at[k, j], "tensor", target)
        c.start()
        sends.append(c)

    def arrived(k, j, ref):
        remote(ref, ref, ssem.at[k, j], rsem.at[k, j], "tensor", twin).wait_recv()

    loads = {}
    for k in range(nch):
        r = pl.ds(k * rc, rc)
        for j, owner in enumerate(order):
            send(k, j, view(r, owner + flip), sib.at[j, r], twin)
            c = pltpu.make_async_copy(view(r, owner), own.at[j, r], lsem.at[k, j])
            c.start()
            loads[k, j] = c

    def pair(k, j):
        loads[k, j].wait()
        arrived(k, j, sib.at[j, pl.ds(k * rc, rc)])

    def add(j, r):
        return own[j, r].astype(F32) + sib[j, r].astype(F32)

    for k in range(nch):
        r0, r1 = pl.ds(k * rc, h), pl.ds(k * rc + h, h)
        r, hk = pl.ds(k * rc, rc), pl.ds(k * h, h)
        pair(k, 0)
        own[0, r] = add(0, r).astype(own.dtype)
        send(k, 4, own.at[0, r0], half.at[0, hk], right)
        send(k, 5, own.at[0, r1], half.at[1, hk], left)
    for k in range(nch):
        r0, r1 = pl.ds(k * rc, h), pl.ds(k * rc + h, h)
        r, hk = pl.ds(k * rc, rc), pl.ds(k * h, h)
        pair(k, 1)
        pair(k, 2)
        arrived(k, 4, half.at[0, hk])
        own[1, r1] = add(1, r1).astype(own.dtype)
        own[1, r0] = (add(1, r0) + half[0, hk].astype(F32)).astype(own.dtype)
        send(k, 6, own.at[1, r], full.at[0, r], right)
        arrived(k, 5, half.at[1, hk])
        own[2, r0] = add(2, r0).astype(own.dtype)
        own[2, r1] = (add(2, r1) + half[1, hk].astype(F32)).astype(own.dtype)
        send(k, 7, own.at[2, r], full.at[1, r], left)
    for k in range(nch):
        r = pl.ds(k * rc, rc)
        pair(k, 3)
        arrived(k, 6, full.at[0, r])
        arrived(k, 7, full.at[1, r])
        emit(r, add(3, r) + full[0, r].astype(F32) + full[1, r].astype(F32))
    for s in sends:
        s.wait_send()


def scatter_scratch(nch, rows, width, dtype):
    return [
        pltpu.VMEM((4, rows, width), dtype),
        pltpu.VMEM((4, rows, width), dtype),
        pltpu.VMEM((2, rows // 2, width), dtype),
        pltpu.VMEM((2, rows, width), dtype),
        DMA((nch, 8)),
        DMA((nch, 8)),
        DMA((nch, 4)),
    ]


def sum_rows_tensor(value, buf, ssem, rsem):
    t = lax.axis_index("tensor")
    rows = value.shape[0]
    mine = jnp.broadcast_to(jnp.sum(value, axis=1, keepdims=True), (rows, 128))
    buf[t] = jnp.transpose(mine)[:8]
    sends = []
    for j in range(1, TENSOR):
        to = lax.rem(t + j, TENSOR)
        c = remote(buf.at[t], buf.at[t], ssem.at[j], rsem.at[j], "tensor", to)
        c.start()
        sends.append(c)
    for j in range(1, TENSOR):
        ref = buf.at[lax.rem(t + TENSOR - j, TENSOR)]
        remote(ref, ref, ssem.at[j], rsem.at[j], "tensor", t).wait_recv()
    total = jnp.sum(buf[...], axis=0)
    for s in sends:
        s.wait_send()
    return jnp.transpose(total)[:, :1]


def sum_rows_scratch():
    return [pltpu.VMEM((TENSOR, 8, GROUP), F32), DMA((TENSOR,)), DMA((TENSOR,))]


def ag_tensor_kernel(nch, in_ref, out_ref, ssem, rsem, lsem):
    t = lax.axis_index("tensor")
    greet_x()
    own = pltpu.make_async_copy(in_ref, out_ref.at[:, cols(t, in_ref.shape[1])], lsem)
    own.start()
    gather_tensor(nch, in_ref, out_ref, ssem, rsem)
    own.wait()


def ag_tensor(value, cid, nch=1):
    rows, width = value.shape
    return pl.pallas_call(
        functools.partial(ag_tensor_kernel, nch),
        out_shape=jax.ShapeDtypeStruct((rows, width * TENSOR), value.dtype),
        in_specs=[ANY],
        out_specs=ANY,
        scratch_shapes=gather_sems(nch) + [DMA],
        compiler_params=params(cid),
        name="ag_tensor",
    )(value)


def middle_kernel(
    part_ref, x_ref, gain_ref, mid_ref, inv_ref, low_ref, full_ref, *scratch
):
    rs, ag, st, lsem = scratch[:7], scratch[7:9], scratch[9:12], scratch[12]
    t = lax.axis_index("tensor")
    greet_tensor()

    def emit(r, value):
        mid_ref[r] = x_ref[r].astype(F32) + value

    scatter_tensor(1, lambda r, owner: part_ref.at[r, cols(owner, COLS)], GROUP, COLS, emit, *rs)
    mid = mid_ref[...]
    inv = lax.rsqrt(sum_rows_tensor(mid * mid, *st) * (1.0 / D) + EPS)
    inv_ref[...] = inv
    low_ref[...] = (mid * inv * gain_ref[...].astype(F32)).astype(BF16)
    own = pltpu.make_async_copy(low_ref, full_ref.at[:, cols(t, COLS)], lsem)
    own.start()
    gather_tensor(1, low_ref, full_ref, *ag)
    own.wait()


def middle_step(part, x_cols, gain, cid):
    return pl.pallas_call(
        middle_kernel,
        out_shape=(
            jax.ShapeDtypeStruct((GROUP, COLS), F32),
            jax.ShapeDtypeStruct((GROUP, 1), F32),
            jax.ShapeDtypeStruct((GROUP, COLS), BF16),
            jax.ShapeDtypeStruct((GROUP, D), BF16),
        ),
        in_specs=[ANY, VM, VM],
        out_specs=(VM, VM, VM, ANY),
        scratch_shapes=scatter_scratch(1, GROUP, COLS, F32)
        + gather_sems(1)
        + sum_rows_scratch()
        + [DMA],
        compiler_params=params(cid),
        name="middle_step",
    )(part, x_cols, gain)


def ag_expert_kernel(a_ref, b_ref, ao_ref, bo_ref, ssem, rsem, lsem):
    e = lax.axis_index("expert")
    z = e // YN
    y = lax.rem(e, YN)
    yr, yl, yf = lax.rem(y + 1, YN), lax.rem(y + 3, YN), lax.rem(y + 2, YN)
    zr, zl, zf = lax.rem(z + 1, ZN), lax.rem(z + 3, ZN), lax.rem(z + 2, ZN)
    y_right, y_left = z * YN + yr, z * YN + yl
    z_right, z_left = zr * YN + y, zl * YN + y
    greet([("expert", p) for p in (y_right, y_left, z_right, z_left)])
    h = a_ref.shape[0] // 2
    own_a = pltpu.make_async_copy(a_ref, ao_ref.at[z, y], lsem.at[0])
    own_b = pltpu.make_async_copy(b_ref, bo_ref.at[z, y], lsem.at[1])
    own_a.start()
    own_b.start()
    sends = []

    def send(j, src, dst, to):
        c = remote(src, dst, ssem.at[j], rsem.at[j], "expert", to)
        c.start()
        sends.append(c)

    def arrived(j, ref):
        remote(ref, ref, ssem.at[j], rsem.at[j], "expert", y_right).wait_recv()

    first, second = pl.ds(0, h), pl.ds(h, h)
    send(0, a_ref, ao_ref.at[z, y], y_right)
    send(1, a_ref, ao_ref.at[z, y], y_left)
    send(2, b_ref, bo_ref.at[z, y], z_right)
    send(3, b_ref, bo_ref.at[z, y], z_left)
    arrived(0, ao_ref.at[z, yl])
    send(4, ao_ref.at[z, yl, first], ao_ref.at[z, yl, first], y_right)
    arrived(1, ao_ref.at[z, yr])
    send(5, ao_ref.at[z, yr, second], ao_ref.at[z, yr, second], y_left)
    arrived(2, bo_ref.at[zl, y])
    send(6, bo_ref.at[zl, y, first], bo_ref.at[zl, y, first], z_right)
    arrived(3, bo_ref.at[zr, y])
    send(7, bo_ref.at[zr, y, second], bo_ref.at[zr, y, second], z_left)
    ys = (y, yl, yr, yf)
    zs = (z, zl, zr, zf)
    for i in range(4):
        if i == 3:
            arrived(4, ao_ref.at[z, yf, first])
            arrived(5, ao_ref.at[z, yf, second])
            arrived(6, bo_ref.at[zf, y, first])
            arrived(7, bo_ref.at[zf, y, second])
        sa, sb = ao_ref.at[z, ys[i]], bo_ref.at[zs[i], y]
        src_a, src_b = (a_ref, b_ref) if i == 0 else (sa, sb)
        send(8 + 4 * i, src_a, sa, z_right)
        send(9 + 4 * i, src_a, sa, z_left)
        send(10 + 4 * i, src_b, sb, y_right)
        send(11 + 4 * i, src_b, sb, y_left)
    for i in range(4):
        arrived(8 + 4 * i, ao_ref.at[zl, ys[i]])
        send(24 + 4 * i, ao_ref.at[zl, ys[i], first], ao_ref.at[zl, ys[i], first], z_right)
        arrived(9 + 4 * i, ao_ref.at[zr, ys[i]])
        send(25 + 4 * i, ao_ref.at[zr, ys[i], second], ao_ref.at[zr, ys[i], second], z_left)
        arrived(10 + 4 * i, bo_ref.at[zs[i], yl])
        send(26 + 4 * i, bo_ref.at[zs[i], yl, first], bo_ref.at[zs[i], yl, first], y_right)
        arrived(11 + 4 * i, bo_ref.at[zs[i], yr])
        send(27 + 4 * i, bo_ref.at[zs[i], yr, second], bo_ref.at[zs[i], yr, second], y_left)
    for i in range(4):
        arrived(24 + 4 * i, ao_ref.at[zf, ys[i], first])
        arrived(25 + 4 * i, ao_ref.at[zf, ys[i], second])
        arrived(26 + 4 * i, bo_ref.at[zs[i], yf, first])
        arrived(27 + 4 * i, bo_ref.at[zs[i], yf, second])
    for s in sends:
        s.wait_send()
    own_a.wait()
    own_b.wait()


def ag_expert(a, b, cid):
    shape = jax.ShapeDtypeStruct((ZN, YN) + a.shape, a.dtype)
    ao, bo = pl.pallas_call(
        ag_expert_kernel,
        out_shape=(shape, shape),
        in_specs=[ANY, ANY],
        out_specs=(ANY, ANY),
        scratch_shapes=[DMA((40,)), DMA((40,)), DMA((2,))],
        compiler_params=params(cid),
        name="ag_expert",
    )(a, b)
    return ao.reshape((GROUPS,) + a.shape), bo.reshape((GROUPS,) + a.shape)


def dot_nn(a, b):
    return lax.dot_general(a, b, (((1,), (0,)), ((), ())), preferred_element_type=F32)


def dot_nt(a, b):
    return lax.dot_general(a, b, (((1,), (1,)), ((), ())), preferred_element_type=F32)


def dot_tn(a, b):
    return lax.dot_general(a, b, (((0,), (0,)), ((), ())), preferred_element_type=F32)


ROWS = GROUPS * PADCAP


def expert_peers():
    e = lax.axis_index("expert")
    z = e // YN
    y = lax.rem(e, YN)
    peers = []
    for dz in range(ZN):
        for dy in range(YN):
            if dz or dy:
                to = lax.rem(z + dz, ZN) * YN + lax.rem(y + dy, YN)
                frm = lax.rem(z + ZN - dz, ZN) * YN + lax.rem(y + YN - dy, YN)
                peers.append((to, frm))
    return e, peers


def seat_rows(index):
    return pl.ds(pl.multiple_of(index * PADCAP, PADCAP), PADCAP)


def moe_kernel(
    place_ref, ncols_ref, nfull_hbm, dy_hbm, sg_hbm, su_hbm, sd_hbm, wg_hbm, wu_hbm, wd_hbm, grads_hbm,
    mid_ref, inv_ref, gain_ref, dyc_ref,
    part_hbm, gg_hbm, gu_hbm, gd_hbm, shout_ref, dmid_ref, dgain_ref, dattn_hbm, wsend_hbm, wgot_hbm,
    sh_ref, dsg_ref, dsu_ref, nfull, dyf, sgv, suv, sdv, outbuf, rows, drows, sib, half, full, wbuf, gbuf, gout, pbuf, res, back, shsum, low,
    d_s, d_r, a_s, a_r, r_s, r_r, b_s, b_r, f_s, f_r, w_s, w_r, st_buf, st_s, st_r, l_in, l_w, l_g, l_out, l_own, l_sh,
):
    t, right, left, far, twin = x_peers()
    flip = twin - t
    e, peers = expert_peers()
    greet(
        [("tensor", lax.rem(t + j, TENSOR)) for j in range(1, TENSOR)]
        + [("expert", to) for to, frm in peers]
    )
    sends = []

    def send(src, dst, ssem, rsem, axis, to):
        c = remote(src, dst, ssem, rsem, axis, to)
        c.start()
        sends.append(c)

    def got(ref, ssem, rsem):
        remote(ref, ref, ssem, rsem, "tensor", twin).wait_recv()

    early = [
        pltpu.make_async_copy(src, dst, l_in.at[i])
        for i, (src, dst) in enumerate(
            [(nfull_hbm, nfull), (sg_hbm, sgv), (su_hbm, suv), (sd_hbm, sdv), (dy_hbm, dyf)]
        )
    ]
    for c in early:
        c.start()

    def load(k):
        s = k % 2
        copies = [
            pltpu.make_async_copy(ref.at[k], wbuf.at[s, i], l_w.at[s, i])
            for i, ref in enumerate((wg_hbm, wu_hbm, wd_hbm))
        ]
        copies.append(pltpu.make_async_copy(grads_hbm.at[k], gbuf.at[s], l_g.at[s]))
        for c in copies:
            c.start()
        return copies

    loads = {0: load(0), 1: load(1)}

    own_copies = []
    for k in range(LOCAL):
        outbuf[k] = dot_nn(place_ref[k], ncols_ref[...]).astype(BF16)
        c = pltpu.make_async_copy(
            outbuf.at[k, seat_rows(e)], rows.at[k, seat_rows(e), cols(t, COLS)], l_own.at[k]
        )
        c.start()
        own_copies.append(c)
        for j, (to, frm) in enumerate(peers):
            send(
                outbuf.at[k, seat_rows(to)], rows.at[k, seat_rows(e), cols(t, COLS)],
                d_s.at[k, j], d_r.at[k, j], "expert", to,
            )

    h = ROWS // 2

    def block(k, owner, part=None):
        if part is None:
            return rows.at[k, :, cols(owner, COLS)]
        return rows.at[k, pl.ds(part * h, h), cols(owner, COLS)]

    def asend(k, j, ref, to):
        send(ref, ref, a_s.at[k, j], a_r.at[k, j], "tensor", to)

    def agot(k, j, ref):
        got(ref, a_s.at[k, j], a_r.at[k, j])

    def gather_1(k):
        own_copies[k].wait()
        for j, (to, frm) in enumerate(peers):
            ref = rows.at[k, seat_rows(frm), cols(t, COLS)]
            got(ref, d_s.at[k, j], d_r.at[k, j])
        asend(k, 0, block(k, t), right)
        asend(k, 1, block(k, t), left)
        asend(k, 4, block(k, t), twin)

    def gather_2(k):
        agot(k, 0, block(k, left))
        asend(k, 2, block(k, left, 0), right)
        asend(k, 5, block(k, left), twin)
        agot(k, 1, block(k, right))
        asend(k, 3, block(k, right, 1), left)
        asend(k, 6, block(k, right), twin)

    def gather_3(k):
        agot(k, 2, block(k, far, 0))
        asend(k, 7, block(k, far, 0), twin)
        agot(k, 3, block(k, far, 1))
        asend(k, 8, block(k, far, 1), twin)

    def gather_4(k):
        agot(k, 4, block(k, twin))
        agot(k, 5, block(k, left + flip))
        agot(k, 6, block(k, right + flip))
        agot(k, 7, block(k, far + flip, 0))
        agot(k, 8, block(k, far + flip, 1))

    order = (far, right, left, t)

    def slot(k):
        return 3 if k == LOCAL else k % 3

    def rsend(k, j, src, dst, to):
        send(src, dst, r_s.at[k, j], r_r.at[k, j], "tensor", to)

    def rgot(k, j, ref):
        got(ref, r_s.at[k, j], r_r.at[k, j])

    def mine(k, j):
        return drows[slot(k), :, cols(order[j], COLS)].astype(F32)

    twin_sends = {}

    def sum_1(k):
        first = len(sends)
        for j, owner in enumerate(order):
            rsend(k, j, drows.at[slot(k), :, cols(owner + flip, COLS)], sib.at[k, j], twin)
        twin_sends[k] = sends[first:]
        del sends[first:]

    def sum_2(k):
        rgot(k, 0, sib.at[k, 0])
        sib[k, 0] = (mine(k, 0) + sib[k, 0].astype(F32)).astype(BF16)
        rsend(k, 4, sib.at[k, 0, pl.ds(0, h)], half.at[k, 0], right)
        rsend(k, 5, sib.at[k, 0, pl.ds(h, h)], half.at[k, 1], left)

    def sum_3(k):
        for j, to in ((1, right), (2, left)):
            rgot(k, j, sib.at[k, j])
            rgot(k, 3 + j, half.at[k, j - 1])
            both = mine(k, j) + sib[k, j].astype(F32)
            extra = half[k, j - 1].astype(F32)
            if j == 1:
                sib[k, j, :h] = (both[:h] + extra).astype(BF16)
                sib[k, j, h:] = both[h:].astype(BF16)
            else:
                sib[k, j, :h] = both[:h].astype(BF16)
                sib[k, j, h:] = (both[h:] + extra).astype(BF16)
            rsend(k, 5 + j, sib.at[k, j], full.at[k, j - 1], to)

    def sum_4(k):
        rgot(k, 3, sib.at[k, 3])
        rgot(k, 6, full.at[k, 0])
        rgot(k, 7, full.at[k, 1])
        value = mine(k, 3) + sib[k, 3].astype(F32) + full[k, 0].astype(F32) + full[k, 1].astype(F32)
        for c in twin_sends[k]:
            c.wait_send()
        if k == LOCAL:
            shsum[...] = value
            return
        res[k] = value.astype(BF16)
        c = pltpu.make_async_copy(res.at[k, seat_rows(e)], back.at[k, seat_rows(e)], l_own.at[k])
        c.start()
        own_copies[k] = c
        for j, (to, frm) in enumerate(peers):
            send(res.at[k, seat_rows(to)], back.at[k, seat_rows(e)], b_s.at[k, j], b_r.at[k, j], "expert", to)

    def shared_forward():
        for c in early[:4]:
            c.wait()
        n = nfull[...]
        g = dot_nt(n, sgv[...])
        u = dot_nt(n, suv[...])
        sig = jax.nn.sigmoid(g)
        silu = g * sig
        sh_ref[...] = (silu * u).astype(BF16)
        return g, u, sig, silu

    def shared_backward(g, u, sig, silu):
        early[4].wait()
        dh = dot_nt(dyf[...], sdv[...])
        dsg_ref[...] = (dh * u * (sig * (1.0 + g * (1.0 - sig)))).astype(BF16)
        dsu_ref[...] = (dh * silu).astype(BF16)

    tiles = [pl.ds(i * 512, 512) for i in range(D // 512)]

    def shared_rows():
        hid = sh_ref[...]
        dsg, dsu = dsg_ref[...], dsu_ref[...]
        for n in tiles:
            drows[3, :GROUP, n] = dot_nn(hid, sdv[:, n]).astype(BF16)
            drows[3, GROUP:, n] = (dot_nn(dsg, sgv[:, n]) + dot_nn(dsu, suv[:, n])).astype(BF16)

    stages = (drows.at[1], drows.at[2], pbuf)
    staged = []

    def shared_weights():
        pairs = ((dsg_ref, nfull), (dsu_ref, nfull), (sh_ref, dyf))
        wide = sd_hbm.shape[0]
        for i, (lhs, rhs) in enumerate(pairs):
            for n in tiles:
                stages[i][:wide, n] = dot_tn(lhs[...], rhs[:, n]).astype(BF16)
            c = pltpu.make_async_copy(stages[i].at[pl.ds(0, wide)], wsend_hbm.at[i], l_sh.at[i])
            c.start()
            staged.append(c)

    def shared_send():
        for i in range(3):
            staged[i].wait()
            for j, (to, frm) in enumerate(peers):
                send(wsend_hbm.at[i, :, cols(to, 128)], wgot_hbm.at[e, i], w_s.at[i, j], w_r.at[i, j], "expert", to)
            c = pltpu.make_async_copy(wsend_hbm.at[i, :, cols(e, 128)], wgot_hbm.at[e, i], l_sh.at[i])
            c.start()
            staged[i] = c

    out_copies = {}

    def compute_1(k):
        s = k % 2
        for c in loads[k]:
            c.wait()
        r = rows[k]
        gate = dot_nt(r, wbuf[s, 0])
        up = dot_nt(r, wbuf[s, 1])
        dh = dot_nt(gbuf[s], wbuf[s, 2])
        sig = jax.nn.sigmoid(gate)
        silu = gate * sig
        hidden = (silu * up).astype(BF16)
        dg = (dh * up * (sig * (1.0 + gate * (1.0 - sig)))).astype(BF16)
        du = (dh * silu).astype(BF16)
        for n in tiles:
            drows[slot(k), :, n] = (
                dot_nn(dg, wbuf[s, 0, :, n]) + dot_nn(du, wbuf[s, 1, :, n])
            ).astype(BF16)
        return hidden, dg, du

    def compute_2(k, hidden, dg, du):
        s = k % 2
        if k:
            for c in out_copies[k - 1]:
                c.wait()
        for n in tiles:
            pbuf[:, n] = dot_nn(hidden, wbuf[s, 2, :, n]).astype(BF16)
            gout[0, :, n] = dot_tn(dg, rows[k, :, n])
            gout[1, :, n] = dot_tn(du, rows[k, :, n])
            gout[2, :, n] = dot_tn(hidden, gbuf[s, :, n])
        out_copies[k] = [
            pltpu.make_async_copy(src, dst.at[k], l_out.at[i])
            for i, (src, dst) in enumerate(
                [(pbuf, part_hbm), (gout.at[0], gg_hbm), (gout.at[1], gu_hbm), (gout.at[2], gd_hbm)]
            )
        ]
        for c in out_copies[k]:
            c.start()
        if k + 2 < LOCAL:
            loads[k + 2] = load(k + 2)

    state = shared_forward()
    gather_1(0)
    shared_backward(*state)
    gather_1(1)
    gather_2(0)
    shared_rows()
    sum_1(4)
    shared_weights()
    gather_1(2)
    gather_2(1)
    gather_3(0)
    gather_1(3)
    shared_send()
    gather_4(0)
    c0 = compute_1(0)
    sum_1(0)
    gather_2(2)
    gather_3(1)
    sum_2(4)
    compute_2(0, *c0)
    gather_4(1)
    sum_2(0)
    c1 = compute_1(1)
    sum_1(1)
    gather_2(3)
    gather_3(2)
    sum_3(0)
    compute_2(1, *c1)
    gather_4(2)
    sum_2(1)
    c2 = compute_1(2)
    sum_1(2)
    gather_3(3)
    sum_3(1)
    sum_4(0)
    sum_3(4)
    compute_2(2, *c2)
    gather_4(3)
    sum_2(2)
    c3 = compute_1(3)
    sum_1(3)
    sum_3(2)
    sum_4(1)
    sum_2(3)
    compute_2(3, *c3)
    sum_4(2)
    sum_3(3)
    sum_4(4)
    shout_ref[...] = shsum[:GROUP]
    sum_4(3)

    dn = shsum[GROUP:]
    for k in range(LOCAL):
        own_copies[k].wait()
        for j, (to, frm) in enumerate(peers):
            got(back.at[k, seat_rows(frm)], b_s.at[k, j], b_r.at[k, j])
        dn = dn + dot_tn(place_ref[k], back[k])

    mid = mid_ref[...]
    inv = inv_ref[...]
    u = dn * gain_ref[...].astype(F32)
    total = sum_rows_tensor(u * mid, st_buf, st_s, st_r)
    dmid = dyc_ref[...].astype(F32) + inv * u - mid * (inv * inv * inv * total * (1.0 / D))
    dmid_ref[...] = dmid
    low[...] = dmid.astype(BF16)
    own = pltpu.make_async_copy(low, dattn_hbm.at[:, cols(t, COLS)], l_own.at[0])
    own.start()
    dgain_ref[...] = jnp.sum(dn * mid * inv, axis=0, keepdims=True)
    gather_tensor(1, low, dattn_hbm, f_s, f_r)
    own.wait()
    for c in out_copies[LOCAL - 1]:
        c.wait()
    for i in range(3):
        staged[i].wait()
        for j, (to, frm) in enumerate(peers):
            got(wgot_hbm.at[frm, i], w_s.at[i, j], w_r.at[i, j])
    for c in sends:
        c.wait_send()


def moe_step(place, ncols, nfull, dy, sg, su, sd, wg, wu, wd, grads, mid, inv, gain, dyc, cid):
    hid = wd.shape[1]
    wide = sd.shape[0]
    wshape = jax.ShapeDtypeStruct((LOCAL, hid, D), F32)
    vmem = pltpu.VMEM
    return pl.pallas_call(
        moe_kernel,
        out_shape=(
            jax.ShapeDtypeStruct((LOCAL, ROWS, D), BF16),
            wshape,
            wshape,
            wshape,
            jax.ShapeDtypeStruct((GROUP, COLS), F32),
            jax.ShapeDtypeStruct((GROUP, COLS), F32),
            jax.ShapeDtypeStruct((1, COLS), F32),
            jax.ShapeDtypeStruct((GROUP, D), BF16),
            jax.ShapeDtypeStruct((3, wide, D), BF16),
            jax.ShapeDtypeStruct((GROUPS, 3, wide, D // GROUPS), BF16),
        ),
        in_specs=[VM, VM] + [ANY] * 9 + [VM] * 4,
        out_specs=(ANY, ANY, ANY, ANY, VM, VM, VM, ANY, ANY, ANY),
        scratch_shapes=[
            vmem((GROUP, wide), BF16),
            vmem((GROUP, wide), BF16),
            vmem((GROUP, wide), BF16),
            vmem((GROUP, D), BF16),
            vmem((GROUP, D), BF16),
            vmem((wide, D), BF16),
            vmem((wide, D), BF16),
            vmem((wide, D), BF16),
            vmem((LOCAL, ROWS, COLS), BF16),
            vmem((LOCAL, ROWS, D), BF16),
            vmem((4, ROWS, D), BF16),
            vmem((LOCAL + 1, 4, ROWS, COLS), BF16),
            vmem((LOCAL + 1, 2, ROWS // 2, COLS), BF16),
            vmem((LOCAL + 1, 2, ROWS, COLS), BF16),
            vmem((2, 3, hid, D), BF16),
            vmem((2, ROWS, D), BF16),
            vmem((3, hid, D), F32),
            vmem((ROWS, D), BF16),
            vmem((LOCAL, ROWS, COLS), BF16),
            vmem((LOCAL, ROWS, COLS), BF16),
            vmem((2 * GROUP, COLS), F32),
            vmem((GROUP, COLS), BF16),
            DMA((LOCAL, 15)),
            DMA((LOCAL, 15)),
            DMA((LOCAL, 9)),
            DMA((LOCAL, 9)),
            DMA((LOCAL + 1, 8)),
            DMA((LOCAL + 1, 8)),
            DMA((LOCAL, 15)),
            DMA((LOCAL, 15)),
            DMA((1, 9)),
            DMA((1, 9)),
            DMA((3, 15)),
            DMA((3, 15)),
            vmem((TENSOR, 8, GROUP), F32),
            DMA((TENSOR,)),
            DMA((TENSOR,)),
            DMA((5,)),
            DMA((2, 3)),
            DMA((2,)),
            DMA((4,)),
            DMA((LOCAL,)),
            DMA((3,)),
        ],
        compiler_params=params(cid, 63),
        cost_estimate=pl.CostEstimate(
            flops=40 * 10**9, bytes_accessed=100 * MIB, transcendentals=0
        ),
        name="moe_step",
    )(place, ncols, nfull, dy, sg, su, sd, wg, wu, wd, grads, mid, inv, gain, dyc)


def swap_halves(value):
    return pltpu.roll(value, 64, 1)


def turn(value, cosine, sine):
    return value * cosine + swap_halves(value) * sine


def lane_head(shape):
    lane = lax.broadcasted_iota(jnp.int32, shape, 1)
    return lax.rem(lane // (ROPE // 2), 2)


def regroup(dtype):
    n = 2 * HEAD
    given = lax.broadcasted_iota(jnp.int32, (n, n), 0)
    made = lax.broadcasted_iota(jnp.int32, (n, n), 1)
    r = made - 2 * NOPE
    q = r // (ROPE // 2)
    turned = lax.rem(q, 2) * HEAD + NOPE + (q // 2) * (ROPE // 2) + lax.rem(r, ROPE // 2)
    source = jnp.where(made < NOPE, made, jnp.where(made < 2 * NOPE, made + ROPE, turned))
    return jnp.where(given == source, 1.0, 0.0).astype(dtype)


def attention_kernel(
    x_ref, gain_ref, wq_ref, wl_ref, lgain_ref, wexp_ref, wout_ref, cos_ref, sin_ref, wcol_ref, wrow_ref,
    part_ref, normed_ref, inv_ref, q_ref, exp_ref, kr_ref, comp_ref, lat_ref, linv_ref, probs_ref, mixed_ref,
    wrope,
):
    xd = x_ref[...].astype(F32)
    inv = lax.rsqrt(jnp.sum(xd * xd, axis=1, keepdims=True) * (1.0 / D) + EPS)
    inv_ref[...] = inv
    normed = (xd * inv * gain_ref[...].astype(F32)).astype(BF16)
    normed_ref[...] = normed
    half = ROPE // 2
    for i in range(4):
        row = LATENT + (i // 2) * half
        wrope[i * half : (i + 1) * half] = wl_ref[row : row + half]
    cosine, sine = cos_ref[...], sin_ref[...]
    lat = dot_nt(normed, wl_ref[:LATENT])
    lat_ref[...] = lat
    linv = lax.rsqrt(jnp.sum(lat * lat, axis=1, keepdims=True) * (1.0 / LATENT) + EPS)
    linv_ref[...] = linv
    kr = turn(dot_nt(normed, wrope[...]), cosine, sine).astype(BF16)
    kr_ref[...] = kr
    comp = (lat * linv * lgain_ref[...].astype(F32)).astype(BF16)
    comp_ref[...] = comp
    expanded = dot_nn(comp, wexp_ref[...]).astype(BF16)
    exp_ref[...] = expanded
    pre = lax.dot_general(
        dot_nn(normed, wq_ref[...]),
        regroup(F32),
        (((1,), (0,)), ((), ())),
        precision=lax.Precision.HIGHEST,
        preferred_element_type=F32,
    )
    q_ref[:, : 2 * NOPE] = pre[:, : 2 * NOPE].astype(BF16)
    qr = turn(pre[:, 2 * NOPE :], cosine, sine)
    q_ref[:, 2 * NOPE :] = qr.astype(BF16)
    head = lane_head((GROUP, 2 * ROPE))
    key = lax.broadcasted_iota(jnp.int32, (GROUP, GROUP), 1)
    at = lax.broadcasted_iota(jnp.int32, (GROUP, GROUP), 0)
    allowed = (wcol_ref[...] == wrow_ref[...]) & (at >= key)
    scale = HEAD ** (-0.5)
    for h in range(2):
        q = q_ref[:, h * NOPE : (h + 1) * NOPE]
        k = expanded[:, 256 * h : 256 * h + NOPE]
        v = expanded[:, 256 * h + NOPE : 256 * h + NOPE + VDIM]
        turned = jnp.where(head == h, qr, 0.0).astype(BF16)
        raw = (dot_nt(q, k) + dot_nt(turned, kr)) * scale
        scores = jnp.where(allowed, raw, -1e30)
        expo = jnp.exp(scores - jnp.max(scores, axis=1, keepdims=True))
        probs = expo / jnp.sum(expo, axis=1, keepdims=True)
        probs_ref[h] = probs
        mixed_ref[:, h * VDIM : (h + 1) * VDIM] = dot_nn(probs.astype(BF16), v).astype(BF16)
    mixed = mixed_ref[...]
    for n in range(4):
        s = slice(n * 512, (n + 1) * 512)
        part_ref[:, s] = dot_nn(mixed, wout_ref[:, s])


def attention_step(x, gain, wq, wl, lgain, wexp, wout, cosine, sine, wcol, wrow):
    def out(*shape, dtype=BF16):
        return jax.ShapeDtypeStruct(shape, dtype)

    return pl.pallas_call(
        attention_kernel,
        out_shape=(
            out(GROUP, D, dtype=F32),
            out(GROUP, D),
            out(GROUP, 1, dtype=F32),
            out(GROUP, 2 * HEAD),
            out(GROUP, 512),
            out(GROUP, 2 * ROPE),
            out(GROUP, LATENT),
            out(GROUP, LATENT, dtype=F32),
            out(GROUP, 1, dtype=F32),
            out(2, GROUP, GROUP, dtype=F32),
            out(GROUP, 2 * VDIM),
        ),
        in_specs=[VM] * 11,
        out_specs=(VM,) * 11,
        scratch_shapes=[pltpu.VMEM((2 * ROPE, D), BF16)],
        compiler_params=pltpu.CompilerParams(vmem_limit_bytes=48 * MIB),
        name="attention_step",
    )(x, gain, wq, wl, lgain, wexp, wout, cosine, sine, wcol, wrow)


def gather_expert_stages(a, b, ss, rs, send):
    e = lax.axis_index("expert")
    z = e // YN
    y = lax.rem(e, YN)
    yr, yl, yf = lax.rem(y + 1, YN), lax.rem(y + 3, YN), lax.rem(y + 2, YN)
    zr, zl, zf = lax.rem(z + 1, ZN), lax.rem(z + 3, ZN), lax.rem(z + 2, ZN)
    y_right, y_left = z * YN + yr, z * YN + yl
    z_right, z_left = zr * YN + y, zl * YN + y
    h = a.shape[2] // 2
    first, second = pl.ds(0, h), pl.ds(h, h)
    ys = (y, yl, yr, yf)
    zs = (z, zl, zr, zf)

    def put(j, ref, to):
        send(ref, ref, ss.at[j], rs.at[j], "expert", to)

    def arrived(j, ref):
        remote(ref, ref, ss.at[j], rs.at[j], "expert", y_right).wait_recv()

    def second_phase(i):
        put(8 + 4 * i, a.at[z, ys[i]], z_right)
        put(9 + 4 * i, a.at[z, ys[i]], z_left)
        put(10 + 4 * i, b.at[zs[i], y], y_right)
        put(11 + 4 * i, b.at[zs[i], y], y_left)

    def stage_0():
        put(0, a.at[z, y], y_right)
        put(1, a.at[z, y], y_left)
        put(2, b.at[z, y], z_right)
        put(3, b.at[z, y], z_left)
        second_phase(0)

    def stage_1():
        arrived(0, a.at[z, yl])
        put(4, a.at[z, yl, first], y_right)
        arrived(1, a.at[z, yr])
        put(5, a.at[z, yr, second], y_left)
        arrived(2, b.at[zl, y])
        put(6, b.at[zl, y, first], z_right)
        arrived(3, b.at[zr, y])
        put(7, b.at[zr, y, second], z_left)
        second_phase(1)
        second_phase(2)

    def stage_2():
        arrived(4, a.at[z, yf, first])
        arrived(5, a.at[z, yf, second])
        arrived(6, b.at[zf, y, first])
        arrived(7, b.at[zf, y, second])
        second_phase(3)
        for i in range(4):
            arrived(8 + 4 * i, a.at[zl, ys[i]])
            put(24 + 4 * i, a.at[zl, ys[i], first], z_right)
            arrived(9 + 4 * i, a.at[zr, ys[i]])
            put(25 + 4 * i, a.at[zr, ys[i], second], z_left)
            arrived(10 + 4 * i, b.at[zs[i], yl])
            put(26 + 4 * i, b.at[zs[i], yl, first], y_right)
            arrived(11 + 4 * i, b.at[zs[i], yr])
            put(27 + 4 * i, b.at[zs[i], yr, second], y_left)

    def stage_3():
        for i in range(4):
            arrived(24 + 4 * i, a.at[zf, ys[i], first])
            arrived(25 + 4 * i, a.at[zf, ys[i], second])
            arrived(26 + 4 * i, b.at[zs[i], yf, first])
            arrived(27 + 4 * i, b.at[zs[i], yf, second])

    return stage_0, stage_1, stage_2, stage_3


def sum_stages(theirs, mine, rows, sib, half, full, ss, rs, send):
    t, right, left, far, twin = x_peers()
    flip = twin - t
    order = (far, right, left, t)
    h = rows // 2

    def put(j, src, dst, to):
        send(src, dst, ss.at[j], rs.at[j], "tensor", to)

    def arrived(j, ref):
        remote(ref, ref, ss.at[j], rs.at[j], "tensor", twin).wait_recv()

    def stage_1():
        for j, owner in enumerate(order):
            put(j, theirs(owner + flip), sib.at[j], twin)

    def stage_2():
        arrived(0, sib.at[0])
        sib[0] = (mine(0) + sib[0].astype(F32)).astype(sib.dtype)
        put(4, sib.at[0, pl.ds(0, h)], half.at[0], right)
        put(5, sib.at[0, pl.ds(h, h)], half.at[1], left)

    def stage_3():
        for j, to in ((1, right), (2, left)):
            arrived(j, sib.at[j])
            arrived(3 + j, half.at[j - 1])
            both = mine(j) + sib[j].astype(F32)
            extra = half[j - 1].astype(F32)
            if j == 1:
                sib[j, :h] = (both[:h] + extra).astype(sib.dtype)
                sib[j, h:] = both[h:].astype(sib.dtype)
            else:
                sib[j, :h] = both[:h].astype(sib.dtype)
                sib[j, h:] = (both[h:] + extra).astype(sib.dtype)
            put(5 + j, sib.at[j], full.at[j - 1], to)

    def stage_4():
        arrived(3, sib.at[3])
        arrived(6, full.at[0])
        arrived(7, full.at[1])
        return mine(3) + sib[3].astype(F32) + full[0].astype(F32) + full[1].astype(F32)

    return stage_1, stage_2, stage_3, stage_4


SLICE = 80
WIDE_LAT = LATENT + 2 * ROPE


def back_kernel(
    dattn_ref, mixed_ref, wout_ref, q_ref, exp_ref, kr_ref, probs_ref, cos_ref, sin_ref, lat_ref, linv_ref,
    lgain_ref, x_ref, inv_ref, gain_ref, dmid_ref, ffn_ref, mid_ref, shout_ref, gate_ref, target_ref,
    place_hbm, normed_hbm, wq_hbm, wexp_hbm, comp_hbm, wl_hbm, part_hbm,
    out_ref, dx_ref, gwq_ref, gwexp_ref, gwout_ref, gwlat_ref, gains_ref,
    normed, wq, wexp, comp, wl, place,
    own, sib, half, full, res, fback,
    npart, nsib, nhalf, nfull,
    swq, swexp, swout, swlat, rwq, rwexp, rwout, rwlat, lowlat,
    cbuf, cgot, dlat, gm, gin, oa, ob, xa, xb,
    st_buf, st_s, st_r,
    p_s, p_r, fb_s, fb_r, n_s, n_r, w_s, w_r, c_s, c_r, dl_s, dl_r, gm_s, gm_r, gt_s, gt_r, wl_s, wl_r,
    o_s, o_r, x_s, x_r, l_in, l_own,
):
    t, right, left, far, twin = x_peers()
    e, peers = expert_peers()
    others = [(lax.rem(t + j, TENSOR), lax.rem(t + TENSOR - j, TENSOR)) for j in range(1, TENSOR)]
    z, y = e // YN, lax.rem(e, YN)
    greet([("tensor", to) for to, frm in others] + [("expert", to) for to, frm in peers])
    sends = []

    def send(src, dst, ssem, rsem, axis, to):
        c = remote(src, dst, ssem, rsem, axis, to)
        c.start()
        sends.append(c)

    def got(ref, ssem, rsem):
        remote(ref, ref, ssem, rsem, "tensor", twin).wait_recv()

    half_rope = ROPE // 2
    for i in (1, 3):
        wl[LATENT + i * half_rope : LATENT + (i + 1) * half_rope] = jnp.zeros((half_rope, COLS), BF16)
    wide = [
        (wq_hbm, wq),
        (wexp_hbm, wexp),
        (normed_hbm, normed),
        (comp_hbm, comp),
        (place_hbm, place),
        (wl_hbm.at[pl.ds(0, LATENT), cols(t, COLS)], wl.at[pl.ds(0, LATENT)]),
        (
            wl_hbm.at[pl.ds(LATENT, half_rope), cols(t, COLS)],
            wl.at[pl.ds(LATENT, half_rope)],
        ),
        (
            wl_hbm.at[pl.ds(LATENT + half_rope, half_rope), cols(t, COLS)],
            wl.at[pl.ds(LATENT + 2 * half_rope, half_rope)],
        ),
    ]
    early = [pltpu.make_async_copy(src, dst, l_in.at[i]) for i, (src, dst) in enumerate(wide)]
    for c in early:
        c.start()

    order = (far, right, left, t)
    chunks = []
    for k in range(LOCAL):

        def theirs(owner, k=k):
            return part_hbm.at[k, :, cols(owner, COLS)]

        def mine(j, k=k):
            return own[k, j].astype(F32)

        chunks.append(
            sum_stages(
                theirs, mine, ROWS, sib.at[k], half.at[k], full.at[k], p_s.at[k], p_r.at[k], send
            )
        )
    own_loads = {}
    for k in range(LOCAL):
        for j, owner in enumerate(order):
            c = pltpu.make_async_copy(part_hbm.at[k, :, cols(owner, COLS)], own.at[k, j], l_own.at[k, j])
            c.start()
            own_loads[k, j] = c
        chunks[k][0]()

    def forward_2(k):
        for j in range(4):
            own_loads[k, j].wait()
        chunks[k][1]()

    def forward_4(k):
        res[k] = chunks[k][3]().astype(BF16)
        fback[k, seat_rows(e)] = res[k, seat_rows(e)]
        for j, (to, frm) in enumerate(peers):
            send(
                res.at[k, seat_rows(to)], fback.at[k, seat_rows(e)], fb_s.at[k, j], fb_r.at[k, j], "expert", to
            )

    scale = HEAD ** (-0.5)
    cosine, sine = cos_ref[...], sin_ref[...]
    head = lane_head((GROUP, 2 * ROPE))
    dattn = dattn_ref[...]
    dmix = dot_nt(dattn, wout_ref[...]).astype(BF16)
    kr = kr_ref[...]
    qr = q_ref[:, 2 * NOPE :]
    turned = jnp.zeros((GROUP, 2 * ROPE), F32)
    rope_sum = jnp.zeros((GROUP, 2 * ROPE), F32)
    dq_parts = []
    dexp_parts = []
    for h in range(2):
        p = probs_ref[h]
        dm = dmix[:, h * VDIM : (h + 1) * VDIM]
        k = exp_ref[:, 256 * h : 256 * h + NOPE]
        v = exp_ref[:, 256 * h + NOPE : 256 * h + NOPE + VDIM]
        dv = dot_tn(p.astype(BF16), dm)
        dp = dot_nt(dm, v)
        ds = (p * (dp - jnp.sum(dp * p, axis=1, keepdims=True))).astype(BF16)
        dq_parts.append((dot_nn(ds, k) * scale).astype(BF16))
        turned = turned + jnp.where(head == h, dot_nn(ds, kr) * scale, 0.0)
        dk = dot_tn(ds, q_ref[:, h * NOPE : (h + 1) * NOPE]) * scale
        rope_sum = rope_sum + jnp.where(head == h, dot_tn(ds, qr) * scale, 0.0)
        dexp_parts += [dk.astype(BF16), dv.astype(BF16)]
    dexp = jnp.concatenate(dexp_parts, axis=1)
    dq_parts.append(turn(turned, cosine, -sine).astype(BF16))
    dq = dot_nt(jnp.concatenate(dq_parts, axis=1), regroup(BF16)).astype(BF16)

    early[1].wait()
    cpart = dot_nt(dexp, wexp[...])
    share = GROUP // TENSOR
    for i in range(TENSOR):
        r = slice(i * share, (i + 1) * share)
        cbuf[i, :, :LATENT] = cpart[r].astype(BF16)
        cbuf[i, :, LATENT:] = rope_sum[r].astype(BF16)
    for j, (to, frm) in enumerate(others):
        send(cbuf.at[to], cgot.at[t], c_s.at[j], c_r.at[j], "tensor", to)

    early[0].wait()
    for n in range(TENSOR):
        npart[n] = dot_nt(dq, wq[n * COLS : (n + 1) * COLS, :]).astype(BF16)
    n1, n2, n3, n4 = sum_stages(
        lambda owner: npart.at[owner],
        lambda j: npart[order[j]].astype(F32),
        GROUP, nsib, nhalf, nfull, n_s, n_r, send,
    )
    n1()
    forward_2(0)

    def spread(i, source, landed):
        for j, (to, frm) in enumerate(peers):
            send(source(to), landed.at[e], w_s.at[i, j], w_r.at[i, j], "expert", to)

    def collect(i, landed, mine):
        total = mine
        for j, (to, frm) in enumerate(peers):
            got(landed.at[frm], w_s.at[i, j], w_r.at[i, j])
            total = total + landed[frm].astype(F32)
        return total

    mixed = mixed_ref[...]
    for n in range(4):
        s = slice(n * 512, (n + 1) * 512)
        swout[:, s] = dot_tn(mixed, dattn_ref[:, s]).astype(BF16)
    spread(0, lambda to: swout.at[:, cols(to, 128)], rwout)

    total = cbuf[t].astype(F32)
    for j, (to, frm) in enumerate(others):
        got(cgot.at[frm], c_s.at[j], c_r.at[j])
        total = total + cgot[frm].astype(F32)
    mine_rows = pl.ds(pl.multiple_of(t * share, share), share)
    dc = total[:, :LATENT]
    lat = lat_ref[mine_rows, :]
    linv = linv_ref[mine_rows, :]
    lu = dc * lgain_ref[...].astype(F32)
    dot = jnp.sum(lu * lat, axis=1, keepdims=True)
    dlat[t, :, :LATENT] = (linv * lu - lat * (linv * linv * linv * dot * (1.0 / LATENT))).astype(BF16)
    both = total[:, LATENT:]
    both = both + pltpu.roll(both, 2 * ROPE - ROPE // 2, 1)
    both = jnp.where(lane_head((share, 2 * ROPE)) == 0, both, 0.0)
    dlat[t, :, LATENT:] = turn(both, cos_ref[mine_rows, :], -sin_ref[mine_rows, :]).astype(BF16)
    for j, (to, frm) in enumerate(others):
        send(dlat.at[t], dlat.at[t], dl_s.at[j], dl_r.at[j], "tensor", to)
    lgain_row = jnp.sum(dc * lat * linv, axis=0, keepdims=True)

    n2()
    early[2].wait()
    for n in range(4):
        s = slice(n * 512, (n + 1) * 512)
        swq[:, s] = dot_tn(dq, normed[:, s]).astype(BF16)
    spread(1, lambda to: swq.at[:, cols(to, 128)], rwq)
    n3()
    forward_2(1)
    chunks[0][2]()

    for j, (to, frm) in enumerate(others):
        got(dlat.at[frm], dl_s.at[j], dl_r.at[j])
    for i in (5, 6, 7):
        early[i].wait()
    dl = dlat[...].reshape(GROUP, WIDE_LAT)
    dn = dot_nn(dl, wl[...]) + n4()
    xd = x_ref[...].astype(F32)
    inv = inv_ref[...]
    u = dn * gain_ref[...].astype(F32)
    total = sum_rows_tensor(u * xd, st_buf, st_s, st_r)
    dx = (dmid_ref[...] + inv * u - xd * (inv * inv * inv * total * (1.0 / D))).astype(BF16)
    xa[z, y] = dx[:, : COLS // 2]
    xb[z, y] = dx[:, COLS // 2 :]
    x0, x1, x2, x3 = gather_expert_stages(xa, xb, x_s, x_r, send)
    x0()
    gm[...] = jnp.zeros(gm.shape, F32)
    gm[0:1] = jnp.sum(dn * xd * inv, axis=0, keepdims=True)
    gm[1:2] = ffn_ref[...]
    gm[2:3] = lgain_row[:, :COLS]
    gm[3:4] = lgain_row[:, COLS:]
    for j, (to, frm) in enumerate(peers):
        send(gm, gin.at[e], gm_s.at[j], gm_r.at[j], "expert", to)

    pick_rows = lax.broadcasted_iota(jnp.int32, (WIDE_LAT, 128), 0)
    pick_cols = lax.broadcasted_iota(jnp.int32, (WIDE_LAT, 128), 1)
    pick_own = jnp.where((pick_rows == pick_cols + t * SLICE) & (pick_cols < SLICE), 1.0, 0.0).astype(BF16)
    dl_own = dot_nn(dl, pick_own).astype(BF16)
    for n in range(4):
        s = slice(n * 512, (n + 1) * 512)
        swlat[:, s] = dot_tn(dl_own, normed[:, s])[:SLICE].astype(BF16)
    spread(2, lambda to: swlat.at[:, cols(to, 128)], rwlat)
    early[3].wait()
    gwexp = dot_tn(comp[...], dexp)
    for i in range(GROUPS):
        swexp[i] = gwexp[32 * i : 32 * (i + 1)].astype(BF16)
    spread(3, lambda to: swexp.at[to], rwexp)

    chunks[1][2]()
    forward_2(2)
    forward_4(0)
    x1()
    chunks[2][2]()
    forward_2(3)
    forward_4(1)
    chunks[3][2]()
    forward_4(2)
    x2()
    forward_4(3)
    early[4].wait()
    routed = mid_ref[...] + shout_ref[...]
    for k in range(LOCAL):
        for j, (to, frm) in enumerate(peers):
            got(fback.at[k, seat_rows(frm)], fb_s.at[k, j], fb_r.at[k, j])
        gates = jnp.broadcast_to(gate_ref[k][:, None, :], (GROUPS, PADCAP, GROUP)).reshape(ROWS, GROUP)
        weight = place[k].astype(F32) * gates
        high = weight.astype(BF16)
        low = (weight - high.astype(F32)).astype(BF16)
        routed = routed + dot_tn(high, fback[k]) + dot_tn(low, fback[k])
    out = routed.astype(BF16)
    oa[z, y] = out[:, : COLS // 2]
    ob[z, y] = out[:, COLS // 2 :]
    o0, o1, o2, o3 = gather_expert_stages(oa, ob, o_s, o_r, send)
    o0()

    gsum = gm[...]
    for j, (to, frm) in enumerate(peers):
        got(gin.at[frm], gm_s.at[j], gm_r.at[j])
        gsum = gsum + gin[frm]
    gains_ref[t] = gsum
    for j, (to, frm) in enumerate(others):
        send(gains_ref.at[t], gains_ref.at[t], gt_s.at[j], gt_r.at[j], "tensor", to)
    lat_sum = collect(2, rwlat, swlat[:, cols(e, 128)].astype(F32))
    lowlat[...] = lat_sum.astype(BF16)
    gwlat_ref[t] = lowlat[...]
    for j, (to, frm) in enumerate(others):
        send(lowlat, gwlat_ref.at[t], wl_s.at[j], wl_r.at[j], "tensor", to)
    o1()
    gwout_ref[...] = collect(0, rwout, swout[:, cols(e, 128)].astype(F32))
    gwq_ref[...] = jnp.transpose(collect(1, rwq, swq[:, cols(e, 128)].astype(F32)))
    gwexp_ref[...] = collect(3, rwexp, swexp[e].astype(F32))
    x3()
    o2()

    where = target_ref[...]
    lane = lax.broadcasted_iota(jnp.int32, (GROUP, GROUP), 1)

    def undeal(a, b):
        acc = [jnp.zeros((GROUP, COLS // 2), F32) for i in range(2)]
        for g in range(GROUPS):
            hot = jnp.where(where == lane + g * GROUP, 1.0, 0.0).astype(BF16)
            acc = [v + dot_nn(hot, ref[g // YN, g % YN]) for v, ref in zip(acc, (a, b))]
        return jnp.concatenate(acc, axis=1).astype(BF16)

    dx_ref[...] = undeal(xa, xb)
    o3()
    out_ref[...] = undeal(oa, ob)
    for j, (to, frm) in enumerate(others):
        got(gains_ref.at[frm], gt_s.at[j], gt_r.at[j])
        got(gwlat_ref.at[frm], wl_s.at[j], wl_r.at[j])
    for c in sends:
        c.wait_send()


def back_step(small, large, cid):
    vmem = pltpu.VMEM

    def out(*shape, dtype=BF16):
        return jax.ShapeDtypeStruct(shape, dtype)

    pair = lambda n: [DMA((n,)), DMA((n,))]
    grid_pair = lambda m, n: [DMA((m, n)), DMA((m, n))]
    return pl.pallas_call(
        back_kernel,
        out_shape=(
            out(GROUP, COLS),
            out(GROUP, COLS),
            out(D // GROUPS, 2 * HEAD, dtype=F32),
            out(LATENT // GROUPS, 512, dtype=F32),
            out(2 * VDIM, D // GROUPS, dtype=F32),
            out(TENSOR, SLICE, D // GROUPS),
            out(TENSOR, 8, COLS, dtype=F32),
        ),
        in_specs=[VM] * len(small) + [ANY] * len(large),
        out_specs=(VM,) * 7,
        scratch_shapes=[
            vmem((GROUP, D), BF16),
            vmem((D, 2 * HEAD), BF16),
            vmem((LATENT, 512), BF16),
            vmem((GROUP, LATENT), BF16),
            vmem((WIDE_LAT, COLS), BF16),
            vmem((LOCAL, ROWS, GROUP), BF16),
            vmem((LOCAL, 4, ROWS, COLS), BF16),
            vmem((LOCAL, 4, ROWS, COLS), BF16),
            vmem((LOCAL, 2, ROWS // 2, COLS), BF16),
            vmem((LOCAL, 2, ROWS, COLS), BF16),
            vmem((LOCAL, ROWS, COLS), BF16),
            vmem((LOCAL, ROWS, COLS), BF16),
            vmem((TENSOR, GROUP, COLS), BF16),
            vmem((4, GROUP, COLS), BF16),
            vmem((2, GROUP // 2, COLS), BF16),
            vmem((2, GROUP, COLS), BF16),
            vmem((2 * HEAD, D), BF16),
            vmem((GROUPS, LATENT // GROUPS, 512), BF16),
            vmem((2 * VDIM, D), BF16),
            vmem((SLICE, D), BF16),
            vmem((GROUPS, 2 * HEAD, D // GROUPS), BF16),
            vmem((GROUPS, LATENT // GROUPS, 512), BF16),
            vmem((GROUPS, 2 * VDIM, D // GROUPS), BF16),
            vmem((GROUPS, SLICE, D // GROUPS), BF16),
            vmem((SLICE, D // GROUPS), BF16),
            vmem((TENSOR, GROUP // TENSOR, WIDE_LAT), BF16),
            vmem((TENSOR, GROUP // TENSOR, WIDE_LAT), BF16),
            vmem((TENSOR, GROUP // TENSOR, WIDE_LAT), BF16),
            vmem((8, COLS), F32),
            vmem((GROUPS, 8, COLS), F32),
            vmem((ZN, YN, GROUP, COLS // 2), BF16),
            vmem((ZN, YN, GROUP, COLS // 2), BF16),
            vmem((ZN, YN, GROUP, COLS // 2), BF16),
            vmem((ZN, YN, GROUP, COLS // 2), BF16),
        ]
        + sum_rows_scratch()
        + grid_pair(LOCAL, 8)
        + grid_pair(LOCAL, 15)
        + pair(8)
        + grid_pair(4, 15)
        + pair(7)
        + pair(7)
        + pair(15)
        + pair(7)
        + pair(7)
        + pair(40)
        + pair(40)
        + [DMA((8,)), DMA((LOCAL, 4))],
        compiler_params=params(cid, 63),
        name="back_step",
    )(*small, *large)


def pick(index, table):
    numbers = jnp.arange(table.shape[0], dtype=jnp.int32)
    return jnp.sum(jnp.where(index[:, None] == numbers[None, :], table[None, :], 0), axis=1)


def exclusive(values):
    numbers = jnp.arange(values.shape[0], dtype=jnp.int32)
    return jnp.sum(jnp.where(numbers[:, None] > numbers[None, :], values[None, :], 0), axis=1)


def deal_rows(lengths, order, group):
    begins = exclusive(lengths)
    dealt_begins = exclusive(pick(order, lengths))
    dealt_source = pick(order, begins)
    numbers = jnp.arange(lengths.shape[0], dtype=jnp.int32)
    inverse = jnp.sum(jnp.where(order[None, :] == numbers[:, None], numbers[None, :], 0), axis=1)
    given_target = pick(inverse, dealt_begins)
    rows = group * GROUP + jnp.arange(GROUP, dtype=jnp.int32)
    which = jnp.sum((rows[:, None] >= dealt_begins[None, :]).astype(jnp.int32), axis=1) - 1
    offsets = rows - pick(which, dealt_begins)
    source = pick(which, dealt_source) + offsets
    owner = jnp.sum((rows[:, None] >= begins[None, :]).astype(jnp.int32), axis=1) - 1
    target = pick(owner, given_target - begins) + rows
    return source, target, offsets, which


def one_hot_rows(index, count):
    numbers = jnp.arange(count, dtype=jnp.int32)
    return (index[:, None] == numbers[None, :]).astype(BF16)


def per_device(
    tokens,
    cotangent,
    attn_gain,
    w_query,
    w_latent,
    latent_gain,
    w_expand,
    w_out,
    ffn_gain,
    shared_gate,
    shared_up,
    shared_down,
    expert_gate,
    expert_up,
    expert_down,
    seq_lengths,
    seq_order,
    routes,
    gate_weights,
):
    group = lax.axis_index("expert")
    column = lax.axis_index("tensor")
    total = GROUP * GROUPS
    source, target, offsets, which = deal_rows(seq_lengths, seq_order, group)

    all_x, all_dy = ag_expert(tokens, cotangent, 0)
    take = one_hot_rows(source, total)
    x_cols = dot_nn(take, all_x.reshape(total, COLS)).astype(BF16)
    dy_cols = dot_nn(take, all_dy.reshape(total, COLS)).astype(BF16)
    x_full = ag_tensor(x_cols, 1)
    dy_full = lax.all_gather(dy_cols, "tensor", axis=1, tiled=True)

    chosen = routes.T
    gates = gate_weights.T
    numbers = jnp.arange(EXPERTS, dtype=jnp.int32)
    experts = lax.rem(numbers, GROUPS) * LOCAL + numbers // GROUPS
    hit = chosen[:, None, :] == experts[None, :, None]
    member = jnp.sum(hit.astype(F32), axis=0)
    gate_of = jnp.sum(jnp.where(hit, gates[:, None, :], 0.0), axis=0)
    token = jnp.arange(GROUP, dtype=jnp.int32)
    earlier = (token[:, None] < token[None, :]).astype(BF16)
    count = dot_nn(member.astype(BF16), earlier)
    slot = jnp.where((member > 0.5) & (count < CAP - 0.5), count, -1.0).astype(jnp.int32)
    seats = jnp.arange(PADCAP, dtype=jnp.int32)
    match = slot[:, None, :] == seats[None, :, None]
    place = match.astype(BF16).reshape(EXPERTS * PADCAP, GROUP)
    slot_gate = jnp.sum(jnp.where(match, gate_of[:, None, :], 0.0), axis=2)
    slot_gate = slot_gate.reshape(EXPERTS * PADCAP, 1)

    slot_grad = (slot_gate * dot_nn(place, dy_cols)).astype(BF16)
    slot_grad = slot_grad.reshape(LOCAL, GROUPS, PADCAP, COLS)
    slot_grad = lax.all_to_all(slot_grad, "expert", split_axis=1, concat_axis=1, tiled=True)
    grad_rows = lax.all_gather(slot_grad.reshape(-1, COLS), "tensor", axis=1, tiled=True)

    half = ROPE // 2
    freqs = jnp.exp(-jnp.log(10000.0) * jnp.arange(half, dtype=F32) / half)
    angles = offsets.astype(F32)[:, None] * freqs[None, :]
    cosine, sine = jnp.cos(angles), jnp.sin(angles)
    cosine = jnp.concatenate([cosine] * 4, axis=1)
    sine = jnp.concatenate([-sine, -sine, sine, sine], axis=1)
    wlat_t = w_latent.T
    lgain = latent_gain.reshape(1, LATENT)
    attn_part, normed, inv_one, query, expanded, key_rope, compressed, latent, inv_lat, probs, mixed = (
        attention_step(
            x_full,
            attn_gain.reshape(1, D),
            w_query,
            wlat_t,
            lgain,
            w_expand,
            w_out,
            cosine,
            sine,
            which.reshape(GROUP, 1),
            which.reshape(1, GROUP),
        )
    )

    def own_cols(vector):
        return lax.dynamic_slice_in_dim(vector, column * COLS, COLS, 0).reshape(1, COLS)

    middle, inv_two, normed_two_cols, normed_two = middle_step(
        attn_part, x_cols, own_cols(ffn_gain), 2
    )

    (
        part, grad_eg, grad_eu, grad_ed, shared_out, dmid, dgain_ffn, d_attn, unused, shared_weights
    ) = moe_step(
        place.reshape(LOCAL, ROWS, GROUP),
        normed_two_cols,
        normed_two,
        dy_full,
        shared_gate.T,
        shared_up.T,
        shared_down,
        jnp.swapaxes(expert_gate, 1, 2),
        jnp.swapaxes(expert_up, 1, 2),
        expert_down,
        grad_rows.reshape(LOCAL, ROWS, D),
        middle,
        inv_two,
        own_cols(ffn_gain),
        dy_cols,
        3,
    )
    shared_weights = jnp.sum(shared_weights.astype(F32), axis=0)

    output, input_grad, grad_wq, grad_wexp, grad_wout, grad_wlat, gains = back_step(
        (
            d_attn,
            mixed,
            w_out,
            query,
            expanded,
            key_rope,
            probs,
            cosine,
            sine,
            latent,
            inv_lat,
            lgain,
            x_cols,
            inv_one,
            own_cols(attn_gain),
            dmid,
            dgain_ffn,
            middle,
            shared_out,
            gate_of.reshape(LOCAL, GROUPS, GROUP),
            target.reshape(GROUP, 1),
        ),
        (place.reshape(LOCAL, ROWS, GROUP), normed, w_query, w_expand, compressed, wlat_t, part),
        4,
    )
    grad_wlat = grad_wlat.reshape(WIDE_LAT, D // GROUPS)
    grad_wlat = jnp.concatenate(
        [grad_wlat[: LATENT + half], grad_wlat[LATENT + ROPE : LATENT + ROPE + half]], axis=0
    ).T.astype(F32)
    gain_grads = jnp.swapaxes(gains[:, :2], 0, 1).reshape(2, D)
    lgain_grad = jnp.sum(gains[:, 2:4], axis=0).reshape(LATENT)
    own = lax.dynamic_slice_in_dim(gain_grads, group * (D // GROUPS), D // GROUPS, 1)
    own_l = lax.dynamic_slice_in_dim(lgain_grad, group * (LATENT // GROUPS), LATENT // GROUPS, 0)
    return (
        output,
        input_grad,
        own[0],
        grad_wq,
        grad_wlat,
        own_l,
        grad_wexp,
        grad_wout,
        own[1],
        shared_weights[0].T,
        shared_weights[1].T,
        shared_weights[2],
        jnp.swapaxes(grad_eg, 1, 2),
        jnp.swapaxes(grad_eu, 1, 2),
        grad_ed,
    )


def solution(mesh):
    return jax.shard_map(
        per_device,
        mesh=mesh,
        in_specs=(
            P("expert", "tensor"),
            P("expert", "tensor"),
            P(),
            P(None, "tensor"),
            P(),
            P(),
            P(None, "tensor"),
            P("tensor", None),
            P(),
            P(None, "tensor"),
            P(None, "tensor"),
            P("tensor", None),
            P("expert", None, "tensor"),
            P("expert", None, "tensor"),
            P("expert", "tensor", None),
            P(),
            P(),
            P("expert", None),
            P("expert", None),
        ),
        out_specs=(
            P("expert", "tensor"),
            P("expert", "tensor"),
            P("expert"),
            P("expert", "tensor"),
            P("expert", None),
            P("expert"),
            P("expert", "tensor"),
            P("tensor", "expert"),
            P("expert"),
            P("expert", "tensor"),
            P("expert", "tensor"),
            P("tensor", "expert"),
            P("expert", None, "tensor"),
            P("expert", None, "tensor"),
            P("expert", "tensor", None),
        ),
        check_vma=False,
    )
```

```python
import math

import jax
import jax.numpy as jnp
from jax import lax
from jax.experimental import pallas as pl
from jax.experimental.pallas import tpu as pltpu
from jax.sharding import PartitionSpec as P

NOPE = 128
ROPE = 64
HEAD = NOPE + ROPE
LATENT = 512
VDIM = 128
D = 2048
GROUP = 256
TOP = 6
EXPERTS = 64
GROUPS = 16
LOCAL = 4
CAP = 27
PADCAP = 32
TENSOR = 8
COLS = D // TENSOR
EPS = 1e-06

XN = 4
YN = 4
ZN = 4
CORES = 2

F32 = jnp.float32
BF16 = jnp.bfloat16
MESH = pl.DeviceIdType.MESH
ANY = pl.BlockSpec(memory_space=pl.ANY)
VM = pl.BlockSpec(memory_space=pltpu.VMEM)
DMA = pltpu.SemaphoreType.DMA
MIB = 1024 * 1024


def remote(src, dst, ssem, rsem, axis, index):
    return pltpu.make_async_remote_copy(
        src_ref=src,
        dst_ref=dst,
        send_sem=ssem,
        recv_sem=rsem,
        device_id={axis: index},
        device_id_type=MESH,
    )


def greet(peers):
    barrier = pltpu.get_barrier_semaphore()
    for axis, index in peers:
        pl.semaphore_signal(barrier, inc=1, device_id={axis: index}, device_id_type=MESH)
    pl.semaphore_wait(barrier, len(peers))


def params(cid, vmem=48):
    return pltpu.CompilerParams(
        collective_id=cid, has_side_effects=True, vmem_limit_bytes=vmem * MIB
    )


def x_peers():
    t = lax.axis_index("tensor")
    x = t // CORES
    c = lax.rem(t, CORES)
    right = lax.rem(x + 1, XN) * CORES + c
    left = lax.rem(x + XN - 1, XN) * CORES + c
    far = lax.rem(x + 2, XN) * CORES + c
    twin = x * CORES + (1 - c)
    return t, right, left, far, twin


def greet_x():
    t, right, left, far, twin = x_peers()
    greet([("tensor", right), ("tensor", left), ("tensor", twin)])


def greet_tensor():
    t = lax.axis_index("tensor")
    greet([("tensor", lax.rem(t + j, TENSOR)) for j in range(1, TENSOR)])


def cols(index, width):
    return pl.ds(pl.multiple_of(index * width, width), width)


def gather_tensor(nch, src, out_ref, ssem, rsem):
    t, right, left, far, twin = x_peers()
    flip = twin - t
    rows, width = src.shape
    rc = rows // nch
    h = rc // 2

    def block(k, owner, part=None):
        if part is None:
            return out_ref.at[pl.ds(k * rc, rc), cols(owner, width)]
        return out_ref.at[pl.ds(k * rc + part * h, h), cols(owner, width)]

    sends = []

    def send(k, j, ref, dst, target):
        c = remote(ref, dst, ssem.at[k, j], rsem.at[k, j], "tensor", target)
        c.start()
        sends.append(c)

    def arrived(k, j, ref):
        remote(ref, ref, ssem.at[k, j], rsem.at[k, j], "tensor", twin).wait_recv()

    for k in range(nch):
        part = src.at[pl.ds(k * rc, rc), :]
        send(k, 0, part, block(k, t), right)
        send(k, 1, part, block(k, t), left)
        send(k, 4, part, block(k, t), twin)
    for k in range(nch):
        arrived(k, 0, block(k, left))
        send(k, 2, block(k, left, 0), block(k, left, 0), right)
        send(k, 5, block(k, left), block(k, left), twin)
        arrived(k, 1, block(k, right))
        send(k, 3, block(k, right, 1), block(k, right, 1), left)
        send(k, 6, block(k, right), block(k, right), twin)
    for k in range(nch):
        arrived(k, 2, block(k, far, 0))
        send(k, 7, block(k, far, 0), block(k, far, 0), twin)
        arrived(k, 3, block(k, far, 1))
        send(k, 8, block(k, far, 1), block(k, far, 1), twin)
    for k in range(nch):
        arrived(k, 4, block(k, twin))
        arrived(k, 5, block(k, left + flip))
        arrived(k, 6, block(k, right + flip))
        arrived(k, 7, block(k, far + flip, 0))
        arrived(k, 8, block(k, far + flip, 1))
    for s in sends:
        s.wait_send()


def gather_sems(nch):
    return [DMA((nch, 9)), DMA((nch, 9))]


def sum_rows_tensor(value, buf, ssem, rsem):
    t = lax.axis_index("tensor")
    rows = value.shape[0]
    mine = jnp.broadcast_to(jnp.sum(value, axis=1, keepdims=True), (rows, 128))
    buf[t] = jnp.transpose(mine)[:8]
    sends = []
    for j in range(1, TENSOR):
        to = lax.rem(t + j, TENSOR)
        c = remote(buf.at[t], buf.at[t], ssem.at[j], rsem.at[j], "tensor", to)
        c.start()
        sends.append(c)
    for j in range(1, TENSOR):
        ref = buf.at[lax.rem(t + TENSOR - j, TENSOR)]
        remote(ref, ref, ssem.at[j], rsem.at[j], "tensor", t).wait_recv()
    total = jnp.sum(buf[...], axis=0)
    for s in sends:
        s.wait_send()
    return jnp.transpose(total)[:, :1]


def sum_rows_scratch():
    return [pltpu.VMEM((TENSOR, 8, GROUP), F32), DMA((TENSOR,)), DMA((TENSOR,))]


def dot_nn(a, b):
    return lax.dot_general(a, b, (((1,), (0,)), ((), ())), preferred_element_type=F32)


def dot_nt(a, b):
    return lax.dot_general(a, b, (((1,), (1,)), ((), ())), preferred_element_type=F32)


def dot_tn(a, b):
    return lax.dot_general(a, b, (((0,), (0,)), ((), ())), preferred_element_type=F32)


ROWS = GROUPS * PADCAP


def expert_peers():
    e = lax.axis_index("expert")
    z = e // YN
    y = lax.rem(e, YN)
    peers = []
    for dz in range(ZN):
        for dy in range(YN):
            if dz or dy:
                to = lax.rem(z + dz, ZN) * YN + lax.rem(y + dy, YN)
                frm = lax.rem(z + ZN - dz, ZN) * YN + lax.rem(y + YN - dy, YN)
                peers.append((to, frm))
    return e, peers


def seat_rows(index):
    return pl.ds(pl.multiple_of(index * PADCAP, PADCAP), PADCAP)


def moe_kernel(
    place_ref, ncols_ref, nfull_hbm, dy_hbm, sg_hbm, su_hbm, sd_hbm, wg_hbm, wu_hbm, wd_hbm, grads_hbm,
    mid_ref, inv_ref, gain_ref, dyc_ref,
    part_hbm, gg_hbm, gu_hbm, gd_hbm, shout_ref, dmid_ref, dgain_ref, dattn_hbm, wsend_hbm, wgot_hbm,
    sh_ref, dsg_ref, dsu_ref, nfull, dyf, sgv, suv, sdv, outbuf, rows, drows, sib, half, full, wbuf, gbuf, gout, pbuf, res, back, shsum, low,
    d_s, d_r, a_s, a_r, r_s, r_r, b_s, b_r, f_s, f_r, w_s, w_r, st_buf, st_s, st_r, l_in, l_w, l_g, l_out, l_own, l_sh, l_first,
):
    t, right, left, far, twin = x_peers()
    flip = twin - t
    e, peers = expert_peers()
    greet(
        [("tensor", lax.rem(t + j, TENSOR)) for j in range(1, TENSOR)]
        + [("expert", to) for to, frm in peers]
    )
    sends = []

    def send(src, dst, ssem, rsem, axis, to):
        c = remote(src, dst, ssem, rsem, axis, to)
        c.start()
        sends.append(c)

    def got(ref, ssem, rsem):
        remote(ref, ref, ssem, rsem, "tensor", twin).wait_recv()

    early = [
        pltpu.make_async_copy(src, dst, l_in.at[i])
        for i, (src, dst) in enumerate(
            [(nfull_hbm, nfull), (sg_hbm, sgv), (su_hbm, suv), (sd_hbm, sdv), (dy_hbm, dyf)]
        )
    ]
    for c in early:
        c.start()

    def load(k):
        s = k % 2
        copies = [
            pltpu.make_async_copy(ref.at[k], wbuf.at[s, i], l_w.at[s, i])
            for i, ref in enumerate((wg_hbm, wu_hbm, wd_hbm))
        ]
        copies.append(pltpu.make_async_copy(grads_hbm.at[k], gbuf.at[s], l_g.at[s]))
        for c in copies:
            c.start()
        return copies

    loads = {0: load(0), 1: load(1)}

    own_copies = []
    blocks = (t, far)
    for k in range(LOCAL):
        for b in range(2):
            if b == 0:
                outbuf[b, k] = dot_nn(place_ref[k], ncols_ref[...]).astype(BF16)
            else:
                if k == 0:
                    early[0].wait()
                outbuf[b, k] = dot_nn(place_ref[k], nfull[:, cols(far, COLS)]).astype(BF16)
            landed = rows.at[k, seat_rows(e), cols(blocks[b], COLS)]
            c = pltpu.make_async_copy(outbuf.at[b, k, seat_rows(e)], landed, l_first.at[k, b])
            c.start()
            own_copies.append(c)
            for j, (to, frm) in enumerate(peers):
                send(
                    outbuf.at[b, k, seat_rows(to)], landed, d_s.at[k, b, j], d_r.at[k, b, j], "expert", to
                )

    h = ROWS // 2

    def row_block(k):
        return lambda owner: rows.at[k, :, cols(owner, COLS)]

    near = [near_stages(row_block(k), a_s.at[k], a_r.at[k], send) for k in range(LOCAL)]

    def gather_1(k):
        for b in range(2):
            own_copies[2 * k + b].wait()
            for j, (to, frm) in enumerate(peers):
                ref = rows.at[k, seat_rows(frm), cols(blocks[b], COLS)]
                got(ref, d_s.at[k, b, j], d_r.at[k, b, j])
            near[k][b]()

    def gather_2(k):
        near[k][2]()

    def gather_4(k):
        near[k][3]()

    back_copies = {}

    order = (far, right, left, t)

    def slot(k):
        return 3 if k == LOCAL else k % 3

    def rsend(k, j, src, dst, to):
        send(src, dst, r_s.at[k, j], r_r.at[k, j], "tensor", to)

    def rgot(k, j, ref):
        got(ref, r_s.at[k, j], r_r.at[k, j])

    def mine(k, j):
        return drows[slot(k), :, cols(order[j], COLS)].astype(F32)

    twin_sends = {}

    def sum_1(k):
        first = len(sends)
        for j, owner in enumerate(order):
            rsend(k, j, drows.at[slot(k), :, cols(owner + flip, COLS)], sib.at[k, j], twin)
        twin_sends[k] = sends[first:]
        del sends[first:]

    def sum_2(k):
        rgot(k, 0, sib.at[k, 0])
        sib[k, 0] = (mine(k, 0) + sib[k, 0].astype(F32)).astype(BF16)
        rsend(k, 4, sib.at[k, 0, pl.ds(0, h)], half.at[k, 0], right)
        rsend(k, 5, sib.at[k, 0, pl.ds(h, h)], half.at[k, 1], left)

    def sum_3(k):
        for j, to in ((1, right), (2, left)):
            rgot(k, j, sib.at[k, j])
            rgot(k, 3 + j, half.at[k, j - 1])
            both = mine(k, j) + sib[k, j].astype(F32)
            extra = half[k, j - 1].astype(F32)
            if j == 1:
                sib[k, j, :h] = (both[:h] + extra).astype(BF16)
                sib[k, j, h:] = both[h:].astype(BF16)
            else:
                sib[k, j, :h] = both[:h].astype(BF16)
                sib[k, j, h:] = (both[h:] + extra).astype(BF16)
            rsend(k, 5 + j, sib.at[k, j], full.at[k, j - 1], to)

    def sum_4(k):
        rgot(k, 3, sib.at[k, 3])
        rgot(k, 6, full.at[k, 0])
        rgot(k, 7, full.at[k, 1])
        value = mine(k, 3) + sib[k, 3].astype(F32) + full[k, 0].astype(F32) + full[k, 1].astype(F32)
        for c in twin_sends[k]:
            c.wait_send()
        if k == LOCAL:
            shsum[...] = value
            return
        res[k] = value.astype(BF16)
        c = pltpu.make_async_copy(res.at[k, seat_rows(e)], back.at[k, seat_rows(e)], l_own.at[k])
        c.start()
        back_copies[k] = c
        for j, (to, frm) in enumerate(peers):
            send(res.at[k, seat_rows(to)], back.at[k, seat_rows(e)], b_s.at[k, j], b_r.at[k, j], "expert", to)

    def shared_forward():
        for c in early[1:4]:
            c.wait()
        n = nfull[...]
        g = dot_nt(n, sgv[...])
        u = dot_nt(n, suv[...])
        sig = jax.nn.sigmoid(g)
        silu = g * sig
        sh_ref[...] = (silu * u).astype(BF16)
        return g, u, sig, silu

    def shared_backward(g, u, sig, silu):
        early[4].wait()
        dh = dot_nt(dyf[...], sdv[...])
        dsg_ref[...] = (dh * u * (sig * (1.0 + g * (1.0 - sig)))).astype(BF16)
        dsu_ref[...] = (dh * silu).astype(BF16)

    tiles = [pl.ds(i * 512, 512) for i in range(D // 512)]

    def shared_rows():
        hid = sh_ref[...]
        dsg, dsu = dsg_ref[...], dsu_ref[...]
        for n in tiles:
            drows[3, :GROUP, n] = dot_nn(hid, sdv[:, n]).astype(BF16)
            drows[3, GROUP:, n] = (dot_nn(dsg, sgv[:, n]) + dot_nn(dsu, suv[:, n])).astype(BF16)

    stages = (drows.at[1], drows.at[2], pbuf)
    staged = []

    def shared_weights():
        pairs = ((dsg_ref, nfull), (dsu_ref, nfull), (sh_ref, dyf))
        wide = sd_hbm.shape[0]
        for i, (lhs, rhs) in enumerate(pairs):
            for n in tiles:
                stages[i][:wide, n] = dot_tn(lhs[...], rhs[:, n]).astype(BF16)
            c = pltpu.make_async_copy(stages[i].at[pl.ds(0, wide)], wsend_hbm.at[i], l_sh.at[i])
            c.start()
            staged.append(c)

    def shared_send():
        for i in range(3):
            for j, (to, frm) in enumerate(peers):
                send(wsend_hbm.at[i, :, cols(to, 128)], wgot_hbm.at[e, i], w_s.at[i, j], w_r.at[i, j], "expert", to)
            c = pltpu.make_async_copy(wsend_hbm.at[i, :, cols(e, 128)], wgot_hbm.at[e, i], l_sh.at[i])
            c.start()
            staged[i] = c

    out_copies = {}

    def compute_1(k):
        s = k % 2
        for c in loads[k]:
            c.wait()
        r = rows[k]
        gate = dot_nt(r, wbuf[s, 0])
        up = dot_nt(r, wbuf[s, 1])
        dh = dot_nt(gbuf[s], wbuf[s, 2])
        sig = jax.nn.sigmoid(gate)
        silu = gate * sig
        hidden = (silu * up).astype(BF16)
        dg = (dh * up * (sig * (1.0 + gate * (1.0 - sig)))).astype(BF16)
        du = (dh * silu).astype(BF16)
        for n in tiles:
            drows[slot(k), :, n] = (
                dot_nn(dg, wbuf[s, 0, :, n]) + dot_nn(du, wbuf[s, 1, :, n])
            ).astype(BF16)
        return hidden, dg, du

    def compute_2(k, hidden, dg, du):
        s = k % 2
        if k:
            for c in out_copies[k - 1]:
                c.wait()
        for n in tiles:
            pbuf[:, n] = dot_nn(hidden, wbuf[s, 2, :, n]).astype(BF16)
            gout[0, :, n] = dot_tn(dg, rows[k, :, n])
            gout[1, :, n] = dot_tn(du, rows[k, :, n])
            gout[2, :, n] = dot_tn(hidden, gbuf[s, :, n])
        out_copies[k] = [
            pltpu.make_async_copy(src, dst.at[k], l_out.at[i])
            for i, (src, dst) in enumerate(
                [(pbuf, part_hbm), (gout.at[0], gg_hbm), (gout.at[1], gu_hbm), (gout.at[2], gd_hbm)]
            )
        ]
        for c in out_copies[k]:
            c.start()
        if k + 2 < LOCAL:
            loads[k + 2] = load(k + 2)

    state = shared_forward()
    gather_1(0)
    shared_backward(*state)
    shared_rows()
    sum_1(4)
    gather_1(1)
    gather_2(0)
    shared_weights()
    gather_4(0)
    c0 = compute_1(0)
    sum_1(0)
    gather_1(2)
    gather_2(1)
    for i in range(3):
        staged[i].wait()
    gather_4(1)
    c1 = compute_1(1)
    sum_1(1)
    gather_1(3)
    shared_send()
    gather_2(2)
    sum_2(0)
    compute_2(0, *c0)
    gather_2(3)
    sum_3(0)
    sum_2(1)
    gather_4(2)
    c2 = compute_1(2)
    sum_1(2)
    sum_4(0)
    sum_3(1)
    compute_2(1, *c1)
    sum_2(2)
    sum_4(1)
    gather_4(3)
    c3 = compute_1(3)
    sum_1(3)
    sum_2(4)
    sum_3(2)
    sum_2(3)
    sum_3(4)
    compute_2(2, *c2)
    sum_4(2)
    sum_3(3)
    compute_2(3, *c3)
    sum_4(4)
    shout_ref[...] = shsum[:GROUP]
    sum_4(3)

    dn = shsum[GROUP:]
    for k in range(LOCAL):
        back_copies[k].wait()
        for j, (to, frm) in enumerate(peers):
            got(back.at[k, seat_rows(frm)], b_s.at[k, j], b_r.at[k, j])
        dn = dn + dot_tn(place_ref[k], back[k])

    mid = mid_ref[...]
    inv = inv_ref[...]
    u = dn * gain_ref[:, cols(t, COLS)].astype(F32)
    total = sum_rows_tensor(u * mid, st_buf, st_s, st_r)
    dmid = dyc_ref[...].astype(F32) + inv * u - mid * (inv * inv * inv * total * (1.0 / D))
    dmid_ref[...] = dmid
    low[...] = dmid.astype(BF16)
    own = pltpu.make_async_copy(low, dattn_hbm.at[:, cols(t, COLS)], l_own.at[0])
    own.start()
    dgain_ref[...] = jnp.sum(dn * mid * inv, axis=0, keepdims=True)
    gather_tensor(1, low, dattn_hbm, f_s, f_r)
    own.wait()
    for c in out_copies[LOCAL - 1]:
        c.wait()
    for i in range(3):
        staged[i].wait()
        for j, (to, frm) in enumerate(peers):
            got(wgot_hbm.at[frm, i], w_s.at[i, j], w_r.at[i, j])
    for c in sends:
        c.wait_send()


def moe_step(place, ncols, nfull, dy, sg, su, sd, wg, wu, wd, grads, mid, inv, gain, dyc, cid):
    hid = wd.shape[1]
    wide = sd.shape[0]
    wshape = jax.ShapeDtypeStruct((LOCAL, hid, D), F32)
    vmem = pltpu.VMEM
    return pl.pallas_call(
        moe_kernel,
        out_shape=(
            jax.ShapeDtypeStruct((LOCAL, ROWS, D), BF16),
            wshape,
            wshape,
            wshape,
            jax.ShapeDtypeStruct((GROUP, COLS), F32),
            jax.ShapeDtypeStruct((GROUP, COLS), F32),
            jax.ShapeDtypeStruct((1, COLS), F32),
            jax.ShapeDtypeStruct((GROUP, D), BF16),
            jax.ShapeDtypeStruct((3, wide, D), BF16),
            jax.ShapeDtypeStruct((GROUPS, 3, wide, D // GROUPS), BF16),
        ),
        in_specs=[VM, VM] + [ANY] * 9 + [VM] * 4,
        out_specs=(ANY, ANY, ANY, ANY, VM, VM, VM, ANY, ANY, ANY),
        scratch_shapes=[
            vmem((GROUP, wide), BF16),
            vmem((GROUP, wide), BF16),
            vmem((GROUP, wide), BF16),
            vmem((GROUP, D), BF16),
            vmem((GROUP, D), BF16),
            vmem((wide, D), BF16),
            vmem((wide, D), BF16),
            vmem((wide, D), BF16),
            vmem((2, LOCAL, ROWS, COLS), BF16),
            vmem((LOCAL, ROWS, D), BF16),
            vmem((4, ROWS, D), BF16),
            vmem((LOCAL + 1, 4, ROWS, COLS), BF16),
            vmem((LOCAL + 1, 2, ROWS // 2, COLS), BF16),
            vmem((LOCAL + 1, 2, ROWS, COLS), BF16),
            vmem((2, 3, hid, D), BF16),
            vmem((2, ROWS, D), BF16),
            vmem((3, hid, D), F32),
            vmem((ROWS, D), BF16),
            vmem((LOCAL, ROWS, COLS), BF16),
            vmem((LOCAL, ROWS, COLS), BF16),
            vmem((2 * GROUP, COLS), F32),
            vmem((GROUP, COLS), BF16),
            DMA((LOCAL, 2, 15)),
            DMA((LOCAL, 2, 15)),
            DMA((LOCAL, 6)),
            DMA((LOCAL, 6)),
            DMA((LOCAL + 1, 8)),
            DMA((LOCAL + 1, 8)),
            DMA((LOCAL, 15)),
            DMA((LOCAL, 15)),
            DMA((1, 9)),
            DMA((1, 9)),
            DMA((3, 15)),
            DMA((3, 15)),
            vmem((TENSOR, 8, GROUP), F32),
            DMA((TENSOR,)),
            DMA((TENSOR,)),
            DMA((5,)),
            DMA((2, 3)),
            DMA((2,)),
            DMA((4,)),
            DMA((LOCAL,)),
            DMA((3,)),
            DMA((LOCAL, 2)),
        ],
        compiler_params=params(cid, 63),
        cost_estimate=pl.CostEstimate(
            flops=40 * 10**9, bytes_accessed=100 * MIB, transcendentals=0
        ),
        name="moe_step",
    )(place, ncols, nfull, dy, sg, su, sd, wg, wu, wd, grads, mid, inv, gain, dyc)


def swap_halves(value):
    return pltpu.roll(value, 64, 1)


def turn(value, cosine, sine):
    return value * cosine + swap_halves(value) * sine


def lane_head(shape):
    lane = lax.broadcasted_iota(jnp.int32, shape, 1)
    return (lane >> 5) & 1


def regroup(dtype):
    n = 2 * HEAD
    given = lax.broadcasted_iota(jnp.int32, (n, n), 0)
    made = lax.broadcasted_iota(jnp.int32, (n, n), 1)
    r = made - 2 * NOPE
    turned = ((r >> 5) & 1) * HEAD + NOPE + (r >> 6) * (ROPE // 2) + (r & 31)
    source = jnp.where(made < NOPE, made, jnp.where(made < 2 * NOPE, made + ROPE, turned))
    return jnp.where(given == source, 1.0, 0.0).astype(dtype)


def band(index, rows):
    return pl.ds(pl.multiple_of(index * rows, rows), rows)


def hop_start(src, dst, rows, ss, rs, send):
    e, peers = expert_peers()
    dst[band(e, rows)] = src[band(e, rows)]
    for j, (to, frm) in enumerate(peers):
        send(src.at[band(to, rows)], dst.at[band(e, rows)], ss.at[j], rs.at[j], "expert", to)


def hop_wait(dst, rows, ss, rs):
    e, peers = expert_peers()
    for j, (to, frm) in enumerate(peers):
        ref = dst.at[band(frm, rows)]
        remote(ref, ref, ss.at[j], rs.at[j], "expert", to).wait_recv()


def one_hot(test):
    return jnp.where(test, 1.0, 0.0).astype(BF16)


def by_sixteen():
    made, given = iota((GROUP, GROUP), 0), iota((GROUP, GROUP), 1)
    return one_hot(given == (made & 15) * GROUPS + (made >> 4))


def seat_of_row(index):
    return one_hot(iota((GROUP, ROWS), 1).astype(F32) == index)


def row_of_seat(index):
    return one_hot(iota((ROWS, GROUP), 0).astype(F32) == index)


def near_stages(block, ss, rs, send):
    t, right, left, far, twin = x_peers()
    flip = twin - t

    def put(j, owner, to):
        send(block(owner), block(owner), ss.at[j], rs.at[j], "tensor", to)

    def arrived(j, owner):
        ref = block(owner)
        remote(ref, ref, ss.at[j], rs.at[j], "tensor", twin).wait_recv()

    def stage_1():
        put(0, t, right)
        put(1, t, left)
        put(2, t, twin)

    def stage_far():
        put(3, far, twin)

    def stage_2():
        arrived(0, left)
        put(4, left, twin)
        arrived(1, right)
        put(5, right, twin)

    def stage_3():
        arrived(2, twin)
        arrived(3, far + flip)
        arrived(4, left + flip)
        arrived(5, right + flip)

    return stage_1, stage_far, stage_2, stage_3


def sum_stages(theirs, mine, rows, sib, half, full, ss, rs, send):
    t, right, left, far, twin = x_peers()
    flip = twin - t
    order = (far, right, left, t)
    h = rows // 2

    def put(j, src, dst, to):
        send(src, dst, ss.at[j], rs.at[j], "tensor", to)

    def arrived(j, ref):
        remote(ref, ref, ss.at[j], rs.at[j], "tensor", twin).wait_recv()

    def stage_1():
        for j, owner in enumerate(order):
            put(j, theirs(owner + flip), sib.at[j], twin)

    def stage_2():
        arrived(0, sib.at[0])
        sib[0] = (mine(0) + sib[0].astype(F32)).astype(sib.dtype)
        put(4, sib.at[0, pl.ds(0, h)], half.at[0], right)
        put(5, sib.at[0, pl.ds(h, h)], half.at[1], left)

    def stage_3():
        for j, to in ((1, right), (2, left)):
            arrived(j, sib.at[j])
            arrived(3 + j, half.at[j - 1])
            both = mine(j) + sib[j].astype(F32)
            extra = half[j - 1].astype(F32)
            if j == 1:
                sib[j, :h] = (both[:h] + extra).astype(sib.dtype)
                sib[j, h:] = both[h:].astype(sib.dtype)
            else:
                sib[j, :h] = both[:h].astype(sib.dtype)
                sib[j, h:] = (both[h:] + extra).astype(sib.dtype)
            put(5 + j, sib.at[j], full.at[j - 1], to)

    def stage_4():
        arrived(3, sib.at[3])
        arrived(6, full.at[0])
        arrived(7, full.at[1])
        return mine(3) + sib[3].astype(F32) + full[0].astype(F32) + full[1].astype(F32)

    return stage_1, stage_2, stage_3, stage_4


SLICE = 80
WIDE_LAT = LATENT + 2 * ROPE


def back_kernel(
    dattn_ref, mixed_ref, wout_ref, q_ref, exp_ref, kr_ref, probs_ref, cos_ref, sin_ref, lat_ref, linv_ref,
    lgain_ref, x_ref, inv_ref, gain_ref, dmid_ref, ffn_ref, mid_ref, shout_ref, gate_ref, seat_ref, seat_row_ref,
    place_hbm, normed_hbm, wq_hbm, wexp_hbm, comp_hbm, wl_hbm, part_hbm,
    out_ref, dx_ref, gwq_ref, gwexp_ref, gwout_ref, gwlat_ref, gains_ref,
    normed, wq, wexp, comp, wl, place,
    own, sib, half, full, res, fback,
    npart, nsib, nhalf, nfull,
    swq, swexp, swout, swlat, rwq, rwexp, rwout, rwlat, lowlat,
    cbuf, cgot, dlat, gm, gin, xh, oh, xl, ol,
    st_buf, st_s, st_r,
    p_s, p_r, fb_s, fb_r, n_s, n_r, w_s, w_r, c_s, c_r, dl_s, dl_r, gm_s, gm_r, gt_s, gt_r, wl_s, wl_r,
    oa_s, oa_r, ob_s, ob_r, xa_s, xa_r, xb_s, xb_r, l_in, l_own,
):
    t, right, left, far, twin = x_peers()
    e, peers = expert_peers()
    others = [(lax.rem(t + j, TENSOR), lax.rem(t + TENSOR - j, TENSOR)) for j in range(1, TENSOR)]
    greet([("tensor", to) for to, frm in others] + [("expert", to) for to, frm in peers])
    sends = []

    def send(src, dst, ssem, rsem, axis, to):
        c = remote(src, dst, ssem, rsem, axis, to)
        c.start()
        sends.append(c)

    def got(ref, ssem, rsem):
        remote(ref, ref, ssem, rsem, "tensor", twin).wait_recv()

    half_rope = ROPE // 2
    for i in (1, 3):
        wl[LATENT + i * half_rope : LATENT + (i + 1) * half_rope] = jnp.zeros((half_rope, COLS), BF16)
    wide = [
        (wq_hbm, wq),
        (wexp_hbm, wexp),
        (normed_hbm, normed),
        (comp_hbm, comp),
        (place_hbm, place),
        (wl_hbm.at[pl.ds(0, LATENT), cols(t, COLS)], wl.at[pl.ds(0, LATENT)]),
        (
            wl_hbm.at[pl.ds(LATENT, half_rope), cols(t, COLS)],
            wl.at[pl.ds(LATENT, half_rope)],
        ),
        (
            wl_hbm.at[pl.ds(LATENT + half_rope, half_rope), cols(t, COLS)],
            wl.at[pl.ds(LATENT + 2 * half_rope, half_rope)],
        ),
    ]
    early = [pltpu.make_async_copy(src, dst, l_in.at[i]) for i, (src, dst) in enumerate(wide)]
    for c in early:
        c.start()

    order = (far, right, left, t)
    chunks = []
    for k in range(LOCAL):

        def theirs(owner, k=k):
            return part_hbm.at[k, :, cols(owner, COLS)]

        def mine(j, k=k):
            return own[k, j].astype(F32)

        chunks.append(
            sum_stages(
                theirs, mine, ROWS, sib.at[k], half.at[k], full.at[k], p_s.at[k], p_r.at[k], send
            )
        )
    own_loads = {}
    for k in range(LOCAL):
        for j, owner in enumerate(order):
            c = pltpu.make_async_copy(part_hbm.at[k, :, cols(owner, COLS)], own.at[k, j], l_own.at[k, j])
            c.start()
            own_loads[k, j] = c
        chunks[k][0]()

    def forward_2(k):
        for j in range(4):
            own_loads[k, j].wait()
        chunks[k][1]()

    def forward_4(k):
        res[k] = chunks[k][3]().astype(BF16)
        fback[k, seat_rows(e)] = res[k, seat_rows(e)]
        for j, (to, frm) in enumerate(peers):
            send(
                res.at[k, seat_rows(to)], fback.at[k, seat_rows(e)], fb_s.at[k, j], fb_r.at[k, j], "expert", to
            )

    scale = HEAD ** (-0.5)
    cosine, sine = cos_ref[...], sin_ref[...]
    head = lane_head((GROUP, 2 * ROPE))
    dattn = dattn_ref[...]
    dmix = dot_nt(dattn, wout_ref[...]).astype(BF16)
    kr = kr_ref[...]
    qr = q_ref[:, 2 * NOPE :]
    turned = jnp.zeros((GROUP, 2 * ROPE), F32)
    rope_sum = jnp.zeros((GROUP, 2 * ROPE), F32)
    dq_parts = []
    dexp_parts = []
    for h in range(2):
        p = probs_ref[h]
        dm = dmix[:, h * VDIM : (h + 1) * VDIM]
        k = exp_ref[:, 256 * h : 256 * h + NOPE]
        v = exp_ref[:, 256 * h + NOPE : 256 * h + NOPE + VDIM]
        dv = dot_tn(p.astype(BF16), dm)
        dp = dot_nt(dm, v)
        ds = (p * (dp - jnp.sum(dp * p, axis=1, keepdims=True))).astype(BF16)
        dq_parts.append((dot_nn(ds, k) * scale).astype(BF16))
        turned = turned + jnp.where(head == h, dot_nn(ds, kr) * scale, 0.0)
        dk = dot_tn(ds, q_ref[:, h * NOPE : (h + 1) * NOPE]) * scale
        rope_sum = rope_sum + jnp.where(head == h, dot_tn(ds, qr) * scale, 0.0)
        dexp_parts += [dk.astype(BF16), dv.astype(BF16)]
    dexp = jnp.concatenate(dexp_parts, axis=1)
    dq_parts.append(turn(turned, cosine, -sine).astype(BF16))
    dq = dot_nt(jnp.concatenate(dq_parts, axis=1), regroup(BF16)).astype(BF16)

    early[1].wait()
    cpart = dot_nt(dexp, wexp[...])
    share = GROUP // TENSOR
    for i in range(TENSOR):
        r = slice(i * share, (i + 1) * share)
        cbuf[i, :, :LATENT] = cpart[r].astype(BF16)
        cbuf[i, :, LATENT:] = rope_sum[r].astype(BF16)
    for j, (to, frm) in enumerate(others):
        send(cbuf.at[to], cgot.at[t], c_s.at[j], c_r.at[j], "tensor", to)

    early[0].wait()
    for n in range(TENSOR):
        npart[n] = dot_nt(dq, wq[n * COLS : (n + 1) * COLS, :]).astype(BF16)
    n1, n2, n3, n4 = sum_stages(
        lambda owner: npart.at[owner],
        lambda j: npart[order[j]].astype(F32),
        GROUP, nsib, nhalf, nfull, n_s, n_r, send,
    )
    n1()
    forward_2(0)
    forward_2(1)

    def spread(i, source, landed):
        for j, (to, frm) in enumerate(peers):
            send(source(to), landed.at[e], w_s.at[i, j], w_r.at[i, j], "expert", to)

    def collect(i, landed, mine):
        total = mine
        for j, (to, frm) in enumerate(peers):
            got(landed.at[frm], w_s.at[i, j], w_r.at[i, j])
            total = total + landed[frm].astype(F32)
        return total

    mixed = mixed_ref[...]
    for n in range(4):
        s = slice(n * 512, (n + 1) * 512)
        swout[:, s] = dot_tn(mixed, dattn_ref[:, s]).astype(BF16)
    spread(0, lambda to: swout.at[:, cols(to, 128)], rwout)

    total = cbuf[t].astype(F32)
    for j, (to, frm) in enumerate(others):
        got(cgot.at[frm], c_s.at[j], c_r.at[j])
        total = total + cgot[frm].astype(F32)
    mine_rows = pl.ds(pl.multiple_of(t * share, share), share)
    dc = total[:, :LATENT]
    lat = lat_ref[mine_rows, :]
    linv = linv_ref[mine_rows, :]
    lu = dc * lgain_ref[...].astype(F32)
    dot = jnp.sum(lu * lat, axis=1, keepdims=True)
    dlat[t, :, :LATENT] = (linv * lu - lat * (linv * linv * linv * dot * (1.0 / LATENT))).astype(BF16)
    both = total[:, LATENT:]
    both = both + pltpu.roll(both, 2 * ROPE - ROPE // 2, 1)
    both = jnp.where(lane_head((share, 2 * ROPE)) == 0, both, 0.0)
    dlat[t, :, LATENT:] = turn(both, cos_ref[mine_rows, :], -sin_ref[mine_rows, :]).astype(BF16)
    for j, (to, frm) in enumerate(others):
        send(dlat.at[t], dlat.at[t], dl_s.at[j], dl_r.at[j], "tensor", to)
    lgain_row = jnp.sum(dc * lat * linv, axis=0, keepdims=True)

    n2()
    forward_2(2)
    chunks[0][2]()
    early[2].wait()
    for n in range(4):
        s = slice(n * 512, (n + 1) * 512)
        swq[:, s] = dot_tn(dq, normed[:, s]).astype(BF16)
    spread(1, lambda to: swq.at[:, cols(to, 128)], rwq)
    n3()
    forward_2(3)
    chunks[1][2]()

    def undeal_1(value, high, ss, rs):
        high[0] = dot_tn(seat_of_row(seat_ref[...]), value).astype(BF16)
        hop_start(high.at[0], high.at[1], PADCAP, ss, rs, send)

    def undeal_2(high, low, ss, rs, ss_next, rs_next):
        hop_wait(high.at[1], PADCAP, ss, rs)
        low[0] = dot_tn(row_of_seat(seat_row_ref[...]), high[1]).astype(BF16)
        hop_start(low.at[0], low.at[1], GROUPS, ss_next, rs_next, send)

    def undeal_3(low, ss, rs):
        hop_wait(low.at[1], GROUPS, ss, rs)
        return dot_tn(by_sixteen(), low[1]).astype(BF16)

    for j, (to, frm) in enumerate(others):
        got(dlat.at[frm], dl_s.at[j], dl_r.at[j])
    for i in (5, 6, 7):
        early[i].wait()
    dl = dlat[...].reshape(GROUP, WIDE_LAT)
    dn = dot_nn(dl, wl[...]) + n4()
    chunks[2][2]()
    forward_4(0)
    xd = x_ref[...].astype(F32)
    inv = inv_ref[...]
    u = dn * gain_ref[:, cols(t, COLS)].astype(F32)
    total = sum_rows_tensor(u * xd, st_buf, st_s, st_r)
    dx = (dmid_ref[...] + inv * u - xd * (inv * inv * inv * total * (1.0 / D))).astype(BF16)
    undeal_1(dx, xh, xa_s, xa_r)
    chunks[3][2]()
    gm[...] = jnp.zeros(gm.shape, F32)
    gm[0:1] = jnp.sum(dn * xd * inv, axis=0, keepdims=True)
    gm[1:2] = ffn_ref[...]
    gm[2:3] = lgain_row[:, :COLS]
    gm[3:4] = lgain_row[:, COLS:]
    for j, (to, frm) in enumerate(peers):
        send(gm, gin.at[e], gm_s.at[j], gm_r.at[j], "expert", to)

    pick_rows = lax.broadcasted_iota(jnp.int32, (WIDE_LAT, 128), 0)
    pick_cols = lax.broadcasted_iota(jnp.int32, (WIDE_LAT, 128), 1)
    pick_own = jnp.where((pick_rows == pick_cols + t * SLICE) & (pick_cols < SLICE), 1.0, 0.0).astype(BF16)
    dl_own = dot_nn(dl, pick_own).astype(BF16)
    for n in range(4):
        s = slice(n * 512, (n + 1) * 512)
        swlat[:, s] = dot_tn(dl_own, normed[:, s])[:SLICE].astype(BF16)
    spread(2, lambda to: swlat.at[:, cols(to, 128)], rwlat)
    early[3].wait()
    gwexp = dot_tn(comp[...], dexp)
    for i in range(GROUPS):
        swexp[i] = gwexp[32 * i : 32 * (i + 1)].astype(BF16)
    spread(3, lambda to: swexp.at[to], rwexp)

    forward_4(1)
    undeal_2(xh, xl, xa_s, xa_r, xb_s, xb_r)
    forward_4(2)
    forward_4(3)
    dx_ref[...] = undeal_3(xl, xb_s, xb_r)
    early[4].wait()
    routed = mid_ref[...] + shout_ref[...]
    for k in range(LOCAL):
        for j, (to, frm) in enumerate(peers):
            got(fback.at[k, seat_rows(frm)], fb_s.at[k, j], fb_r.at[k, j])
        gates = jnp.broadcast_to(gate_ref[k][:, None, :], (GROUPS, PADCAP, GROUP)).reshape(ROWS, GROUP)
        weight = place[k].astype(F32) * gates
        high = weight.astype(BF16)
        low = (weight - high.astype(F32)).astype(BF16)
        routed = routed + dot_tn(high, fback[k]) + dot_tn(low, fback[k])
    out = routed.astype(BF16)
    undeal_1(out, oh, oa_s, oa_r)

    gsum = gm[...]
    for j, (to, frm) in enumerate(peers):
        got(gin.at[frm], gm_s.at[j], gm_r.at[j])
        gsum = gsum + gin[frm]
    gains_ref[t] = gsum
    for j, (to, frm) in enumerate(others):
        send(gains_ref.at[t], gains_ref.at[t], gt_s.at[j], gt_r.at[j], "tensor", to)
    lat_sum = collect(2, rwlat, swlat[:, cols(e, 128)].astype(F32))
    lowlat[...] = lat_sum.astype(BF16)
    gwlat_ref[t] = lowlat[...]
    for j, (to, frm) in enumerate(others):
        send(lowlat, gwlat_ref.at[t], wl_s.at[j], wl_r.at[j], "tensor", to)
    undeal_2(oh, ol, oa_s, oa_r, ob_s, ob_r)
    gwout_ref[...] = collect(0, rwout, swout[:, cols(e, 128)].astype(F32))
    gwq_ref[...] = jnp.transpose(collect(1, rwq, swq[:, cols(e, 128)].astype(F32)))
    gwexp_ref[...] = collect(3, rwexp, swexp[e].astype(F32))
    out_ref[...] = undeal_3(ol, ob_s, ob_r)
    for j, (to, frm) in enumerate(others):
        got(gains_ref.at[frm], gt_s.at[j], gt_r.at[j])
        got(gwlat_ref.at[frm], wl_s.at[j], wl_r.at[j])
    for c in sends:
        c.wait_send()


def back_step(small, large, cid):
    vmem = pltpu.VMEM

    def out(*shape, dtype=BF16):
        return jax.ShapeDtypeStruct(shape, dtype)

    pair = lambda n: [DMA((n,)), DMA((n,))]
    grid_pair = lambda m, n: [DMA((m, n)), DMA((m, n))]
    return pl.pallas_call(
        back_kernel,
        out_shape=(
            out(GROUP, COLS),
            out(GROUP, COLS),
            out(D // GROUPS, 2 * HEAD, dtype=F32),
            out(LATENT // GROUPS, 512, dtype=F32),
            out(2 * VDIM, D // GROUPS, dtype=F32),
            out(TENSOR, SLICE, D // GROUPS),
            out(TENSOR, 8, COLS, dtype=F32),
        ),
        in_specs=[VM] * len(small) + [ANY] * len(large),
        out_specs=(VM,) * 7,
        scratch_shapes=[
            vmem((GROUP, D), BF16),
            vmem((D, 2 * HEAD), BF16),
            vmem((LATENT, 512), BF16),
            vmem((GROUP, LATENT), BF16),
            vmem((WIDE_LAT, COLS), BF16),
            vmem((LOCAL, ROWS, GROUP), BF16),
            vmem((LOCAL, 4, ROWS, COLS), BF16),
            vmem((LOCAL, 4, ROWS, COLS), BF16),
            vmem((LOCAL, 2, ROWS // 2, COLS), BF16),
            vmem((LOCAL, 2, ROWS, COLS), BF16),
            vmem((LOCAL, ROWS, COLS), BF16),
            vmem((LOCAL, ROWS, COLS), BF16),
            vmem((TENSOR, GROUP, COLS), BF16),
            vmem((4, GROUP, COLS), BF16),
            vmem((2, GROUP // 2, COLS), BF16),
            vmem((2, GROUP, COLS), BF16),
            vmem((2 * HEAD, D), BF16),
            vmem((GROUPS, LATENT // GROUPS, 512), BF16),
            vmem((2 * VDIM, D), BF16),
            vmem((SLICE, D), BF16),
            vmem((GROUPS, 2 * HEAD, D // GROUPS), BF16),
            vmem((GROUPS, LATENT // GROUPS, 512), BF16),
            vmem((GROUPS, 2 * VDIM, D // GROUPS), BF16),
            vmem((GROUPS, SLICE, D // GROUPS), BF16),
            vmem((SLICE, D // GROUPS), BF16),
            vmem((TENSOR, GROUP // TENSOR, WIDE_LAT), BF16),
            vmem((TENSOR, GROUP // TENSOR, WIDE_LAT), BF16),
            vmem((TENSOR, GROUP // TENSOR, WIDE_LAT), BF16),
            vmem((8, COLS), F32),
            vmem((GROUPS, 8, COLS), F32),
            vmem((2, ROWS, COLS), BF16),
            vmem((2, ROWS, COLS), BF16),
            vmem((2, GROUP, COLS), BF16),
            vmem((2, GROUP, COLS), BF16),
        ]
        + sum_rows_scratch()
        + grid_pair(LOCAL, 8)
        + grid_pair(LOCAL, 15)
        + pair(8)
        + grid_pair(4, 15)
        + pair(7)
        + pair(7)
        + pair(15)
        + pair(7)
        + pair(7)
        + pair(15)
        + pair(15)
        + pair(15)
        + pair(15)
        + [DMA((8,)), DMA((LOCAL, 4))],
        compiler_params=params(cid, 63),
        name="back_step",
    )(*small, *large)


def gather_stages(source, block, ss, rs, send):
    t, right, left, far, twin = x_peers()
    flip = twin - t

    def put(j, ref, to, src=None):
        send(ref if src is None else src, ref, ss.at[j], rs.at[j], "tensor", to)

    def arrived(j, ref):
        remote(ref, ref, ss.at[j], rs.at[j], "tensor", twin).wait_recv()

    def stage_1():
        put(0, block(t, None), right, source)
        put(1, block(t, None), left, source)
        put(4, block(t, None), twin, source)

    def stage_2():
        arrived(0, block(left, None))
        put(2, block(left, 0), right)
        put(5, block(left, None), twin)
        arrived(1, block(right, None))
        put(3, block(right, 1), left)
        put(6, block(right, None), twin)

    def stage_3():
        arrived(2, block(far, 0))
        put(7, block(far, 0), twin)
        arrived(3, block(far, 1))
        put(8, block(far, 1), twin)

    def stage_4():
        arrived(4, block(twin, None))
        arrived(5, block(left + flip, None))
        arrived(6, block(right + flip, None))
        arrived(7, block(far + flip, 0))
        arrived(8, block(far + flip, 1))

    return stage_1, stage_2, stage_3, stage_4


def column_blocks(ref, rows):
    def block(owner, part):
        r = pl.ds(0, rows) if part is None else pl.ds(part * (rows // 2), rows // 2)
        return ref.at[r, cols(owner, COLS)]

    return block


def iota(shape, dim):
    return lax.broadcasted_iota(jnp.int32, shape, dim)


def deal_in_kernel(lengths, order, group):
    n = lengths.shape[1]
    i, j = iota((n, n), 0), iota((n, n), 1)
    same, before = i == j, j < i

    def column(row):
        return jnp.sum(jnp.where(same, row, 0.0), axis=1, keepdims=True)

    def row(col):
        return jnp.sum(jnp.where(same, col, 0.0), axis=0, keepdims=True)

    def exclusive(values):
        return jnp.sum(jnp.where(before, values, 0.0), axis=1, keepdims=True)

    hit = column(order) == j.astype(F32)
    begins_col = exclusive(lengths)
    begins = row(begins_col)
    dealt_lengths = row(jnp.sum(jnp.where(hit, lengths, 0.0), axis=1, keepdims=True))
    dealt_col = exclusive(dealt_lengths)
    dealt = row(dealt_col)
    dealt_source_col = jnp.sum(jnp.where(hit, begins, 0.0), axis=1, keepdims=True)
    dealt_source = row(dealt_source_col)
    given = jnp.sum(jnp.where(hit, dealt_col, 0.0), axis=0, keepdims=True)
    given_col = column(given)

    def find(rows, lanes, starts, values):
        dim = 1 if lanes else 0
        shape = (GROUP, n) if lanes else (n, GROUP)
        place = jnp.sum(jnp.where(rows >= starts, 1.0, 0.0), axis=dim, keepdims=True) - 1.0
        on = iota(shape, dim).astype(F32) == place
        return place, jnp.sum(jnp.where(on, values, 0.0), axis=dim, keepdims=True)

    first = group * GROUP
    rows = (iota((GROUP, 1), 0) + first).astype(F32)
    rows_row = (iota((1, GROUP), 1) + first).astype(F32)
    which, start = find(rows, True, dealt, dealt)
    unused, shift = find(rows, True, dealt, dealt_source - dealt)
    which_row, shift_row = find(rows_row, False, dealt_col, dealt_source_col - dealt_col)
    source, source_row = rows + shift, rows_row + shift_row

    def rest(value):
        return value - GROUPS * jnp.floor(value * (1.0 / GROUPS))

    ahead = (rest(source) == rest(source_row)) & (source_row < source)
    rank = jnp.sum(jnp.where(ahead, 1.0, 0.0), axis=1, keepdims=True)
    seat = rest(source) * PADCAP + rank

    mine = (iota((GROUP, 1), 0) * GROUPS + group).astype(F32)
    mine_row = (iota((1, GROUP), 1) * GROUPS + group).astype(F32)
    unused, move = find(mine, True, begins, given - begins)
    unused, move_row = find(mine_row, False, begins_col, given_col - begins_col)
    to = jnp.floor((mine + move) * (1.0 / GROUP))
    to_row = jnp.floor((mine_row + move_row) * (1.0 / GROUP))
    ahead = (to == to_row) & (iota((GROUP, GROUP), 0) < iota((GROUP, GROUP), 1))
    rank = jnp.sum(jnp.where(ahead, 1.0, 0.0), axis=0, keepdims=True)
    seat_row = to_row * PADCAP + rank
    return rows - start, which, which_row, seat, seat_row


def front_kernel(
    tok_ref, cot_ref, len_ref, ord_ref, routes_ref, gates_ref, gain_ref, lgain_ref, fgain_ref,
    wq_hbm, wl_hbm, wexp_hbm, wout_hbm,
    xc_ref, dyc_ref, mid_ref, inv2_ref, ncols_ref, normed_ref, inv_ref, q_ref, exp_ref, kr_ref, comp_ref,
    lat_ref, linv_ref, probs_ref, mixed_ref, place_ref, gate_ref, seat_ref, seat_row_ref, cos_ref, sin_ref, dyfull,
    nfull_hbm, grads_hbm,
    hop_a, hop_b, hop_c, hop_d, xfull, wq, wl, wexp, wout, wrope, apart, sib, half, full, gout,
    st_buf, st_s, st_r,
    ha_s, ha_r, hb_s, hb_r, xg_s, xg_r, yg_s, yg_r, ng_s, ng_r, gg_s, gg_r, r_s, r_r, d_s, d_r, l_in, l_own, l_last,
):
    t, right, left, far, twin = x_peers()
    e, peers = expert_peers()
    greet(
        [("tensor", lax.rem(t + j, TENSOR)) for j in range(1, TENSOR)]
        + [("expert", to) for to, frm in peers]
    )
    sends = []

    def send(src, dst, ssem, rsem, axis, to):
        c = remote(src, dst, ssem, rsem, axis, to)
        c.start()
        sends.append(c)

    def got(ref, ssem, rsem):
        remote(ref, ref, ssem, rsem, "tensor", twin).wait_recv()

    def local(src, dst, sem):
        c = pltpu.make_async_copy(src, dst, sem)
        c.start()
        return c

    sixteen = by_sixteen()
    hop_a[:, :COLS] = dot_nn(sixteen, tok_ref[...]).astype(BF16)
    hop_a[:, COLS:] = dot_nn(sixteen, cot_ref[...]).astype(BF16)
    hop_start(hop_a, hop_b, GROUPS, ha_s, ha_r, send)
    early = [
        local(src, dst, l_in.at[i])
        for i, (src, dst) in enumerate([(wl_hbm, wl), (wq_hbm, wq), (wexp_hbm, wexp), (wout_hbm, wout)])
    ]

    offset, which, which_row, seat, seat_row = deal_in_kernel(
        len_ref[...].astype(F32), ord_ref[...].astype(F32), e
    )
    seat_ref[...] = seat
    seat_row_ref[...] = seat_row

    outward = row_of_seat(seat_row)
    hop_wait(hop_b, GROUPS, ha_s, ha_r)
    hop_c[...] = dot_nn(outward, hop_b[...]).astype(BF16)
    hop_start(hop_c, hop_d, PADCAP, hb_s, hb_r, send)
    hr = ROPE // 2
    lane = iota((GROUP, 2 * ROPE), 1)
    power = (lane & (hr - 1)).astype(F32) * (1.0 / hr)
    angle = offset * jnp.exp(power * (-math.log(10000.0)))
    cosine = jnp.cos(angle)
    sine = jnp.sin(angle)
    sine = jnp.where(lane < ROPE, -sine, sine)
    cos_ref[...] = cosine
    sin_ref[...] = sine

    number = iota((EXPERTS, 1), 0)
    expert = (number & 15) * LOCAL + (number >> 4)
    member = jnp.zeros((EXPERTS, GROUP), F32)
    gate_of = jnp.zeros((EXPERTS, GROUP), F32)
    for k in range(TOP):
        hit = routes_ref[k : k + 1, :] == expert
        member = member + jnp.where(hit, 1.0, 0.0)
        gate_of = gate_of + jnp.where(hit, gates_ref[k : k + 1, :], 0.0)
    earlier = jnp.where(iota((GROUP, GROUP), 0) < iota((GROUP, GROUP), 1), 1.0, 0.0).astype(BF16)
    count = dot_nn(member.astype(BF16), earlier)
    slot = jnp.where((member > 0.5) & (count < CAP - 0.5), count, -1.0)
    seats = iota((GROUPS, PADCAP, GROUP), 1).astype(F32)
    slot_gates = []
    for k in range(LOCAL):
        s = slice(k * GROUPS, (k + 1) * GROUPS)
        gate_ref[k] = gate_of[s]
        wide = jnp.broadcast_to(slot[s][:, None, :], (GROUPS, PADCAP, GROUP))
        on = jnp.where(wide == seats, 1.0, 0.0)
        place_ref[k] = on.reshape(ROWS, GROUP).astype(BF16)
        weight = on * jnp.broadcast_to(gate_of[s][:, None, :], (GROUPS, PADCAP, GROUP))
        slot_gates.append(jnp.sum(weight.reshape(ROWS, GROUP), axis=1, keepdims=True))
    early[0].wait()
    for i in range(4):
        row = LATENT + (i // 2) * hr
        wrope[i * hr : (i + 1) * hr] = wl[row : row + hr]
    inward = seat_of_row(seat)
    hop_wait(hop_d, PADCAP, hb_s, hb_r)

    xc_ref[...] = dot_nn(inward, hop_d[:, :COLS]).astype(BF16)
    xfull[:, cols(t, COLS)] = xc_ref[...]
    xg1, xg2, xg3, xg4 = gather_stages(xc_ref, column_blocks(xfull, GROUP), xg_s, xg_r, send)
    xg1()
    dyc_ref[...] = dot_nn(inward, hop_d[:, COLS:]).astype(BF16)
    dyfull[:, cols(t, COLS)] = dyc_ref[...]
    yg1, yg2, yg3, yg4 = gather_stages(dyc_ref, column_blocks(dyfull, GROUP), yg_s, yg_r, send)
    yg1()
    blocks = (t, far)

    def slot_gradients(b):
        for k in range(LOCAL):
            gout[b, k] = (slot_gates[k] * dot_nn(place_ref[k], dyfull[:, cols(blocks[b], COLS)])).astype(BF16)

    own_grads = {}

    def send_gradients(p, b):
        two = pl.ds(2 * p, 2)
        landed = grads_hbm.at[two, seat_rows(e), cols(blocks[b], COLS)]
        own_grads[p, b] = local(gout.at[b, two, seat_rows(e)], landed, l_own.at[p, b])
        for j, (to, frm) in enumerate(peers):
            send(gout.at[b, two, seat_rows(to)], landed, d_s.at[p, b, j], d_r.at[p, b, j], "expert", to)

    slot_gradients(0)
    send_gradients(0, 0)
    send_gradients(1, 0)
    xg2()
    yg2()
    xg3()
    yg3()
    slot_gradients(1)
    send_gradients(0, 1)
    send_gradients(1, 1)
    xg4()

    xd = xfull[...].astype(F32)
    inv = lax.rsqrt(jnp.sum(xd * xd, axis=1, keepdims=True) * (1.0 / D) + EPS)
    inv_ref[...] = inv
    normed = (xd * inv * gain_ref[...].astype(F32)).astype(BF16)
    normed_ref[...] = normed
    lat = dot_nt(normed, wl[:LATENT])
    lat_ref[...] = lat
    linv = lax.rsqrt(jnp.sum(lat * lat, axis=1, keepdims=True) * (1.0 / LATENT) + EPS)
    linv_ref[...] = linv
    kr = turn(dot_nt(normed, wrope[...]), cosine, sine).astype(BF16)
    kr_ref[...] = kr
    early[1].wait()
    pre = lax.dot_general(
        dot_nn(normed, wq[...]),
        regroup(F32),
        (((1,), (0,)), ((), ())),
        precision=lax.Precision.HIGHEST,
        preferred_element_type=F32,
    )
    q_ref[:, : 2 * NOPE] = pre[:, : 2 * NOPE].astype(BF16)
    qr = turn(pre[:, 2 * NOPE :], cosine, sine)
    q_ref[:, 2 * NOPE :] = qr.astype(BF16)
    comp = (lat * linv * lgain_ref[...].astype(F32)).astype(BF16)
    comp_ref[...] = comp
    early[2].wait()
    expanded = dot_nn(comp, wexp[...]).astype(BF16)
    exp_ref[...] = expanded

    def pair_block(p):
        return lambda owner: grads_hbm.at[pl.ds(2 * p, 2), :, cols(owner, COLS)]

    spread = [near_stages(pair_block(p), gg_s.at[p], gg_r.at[p], send) for p in range(2)]

    def gradients_got(p, b):
        own_grads[p, b].wait()
        for j, (to, frm) in enumerate(peers):
            ref = grads_hbm.at[pl.ds(2 * p, 2), seat_rows(frm), cols(blocks[b], COLS)]
            got(ref, d_s.at[p, b, j], d_r.at[p, b, j])

    def gradients_own(p):
        gradients_got(p, 0)
        spread[p][0]()

    def gradients_far(p):
        gradients_got(p, 1)
        spread[p][1]()

    gradients_own(0)

    head = lane_head((GROUP, 2 * ROPE))
    allowed = (which == which_row) & (iota((GROUP, GROUP), 0) >= iota((GROUP, GROUP), 1))
    scale = HEAD ** (-0.5)
    for h in range(2):
        q = q_ref[:, h * NOPE : (h + 1) * NOPE]
        k = expanded[:, 256 * h : 256 * h + NOPE]
        v = expanded[:, 256 * h + NOPE : 256 * h + NOPE + VDIM]
        turned = jnp.where(head == h, qr, 0.0).astype(BF16)
        raw = (dot_nt(q, k) + dot_nt(turned, kr)) * scale
        scores = jnp.where(allowed, raw, -1e30)
        expo = jnp.exp(scores - jnp.max(scores, axis=1, keepdims=True))
        probs = expo / jnp.sum(expo, axis=1, keepdims=True)
        probs_ref[h] = probs
        mixed_ref[:, h * VDIM : (h + 1) * VDIM] = dot_nn(probs.astype(BF16), v).astype(BF16)
    mixed = mixed_ref[...]
    early[3].wait()
    for n in range(TENSOR):
        apart[n] = dot_nn(mixed, wout[:, n * COLS : (n + 1) * COLS]).astype(BF16)

    order = (far, right, left, t)
    r1, r2, r3, r4 = sum_stages(
        lambda owner: apart.at[owner],
        lambda j: apart[order[j]].astype(F32),
        GROUP, sib, half, full, r_s, r_r, send,
    )
    r1()
    gradients_own(1)
    r2()
    gradients_far(0)
    r3()
    spread[0][2]()
    mid = xc_ref[...].astype(F32) + r4()
    mid_ref[...] = mid
    inv2 = lax.rsqrt(sum_rows_tensor(mid * mid, st_buf, st_s, st_r) * (1.0 / D) + EPS)
    inv2_ref[...] = inv2
    ncols_ref[...] = (mid * inv2 * fgain_ref[:, cols(t, COLS)].astype(F32)).astype(BF16)
    own_n = local(ncols_ref, nfull_hbm.at[:, cols(t, COLS)], l_last)
    ng1, ng2, ng3, ng4 = gather_stages(ncols_ref, column_blocks(nfull_hbm, GROUP), ng_s, ng_r, send)
    ng1()
    gradients_far(1)
    ng2()
    spread[1][2]()
    ng3()
    yg4()
    ng4()
    spread[0][3]()
    spread[1][3]()
    own_n.wait()
    for c in sends:
        c.wait_send()


def front_step(small, large, cid):
    vmem = pltpu.VMEM

    def out(*shape, dtype=BF16):
        return jax.ShapeDtypeStruct(shape, dtype)

    def pair(*shape):
        return [DMA(shape), DMA(shape)]

    return pl.pallas_call(
        front_kernel,
        out_shape=(
            out(GROUP, COLS),
            out(GROUP, COLS),
            out(GROUP, COLS, dtype=F32),
            out(GROUP, 1, dtype=F32),
            out(GROUP, COLS),
            out(GROUP, D),
            out(GROUP, 1, dtype=F32),
            out(GROUP, 2 * HEAD),
            out(GROUP, 512),
            out(GROUP, 2 * ROPE),
            out(GROUP, LATENT),
            out(GROUP, LATENT, dtype=F32),
            out(GROUP, 1, dtype=F32),
            out(2, GROUP, GROUP, dtype=F32),
            out(GROUP, 2 * VDIM),
            out(LOCAL, ROWS, GROUP),
            out(LOCAL, GROUPS, GROUP, dtype=F32),
            out(GROUP, 1, dtype=F32),
            out(1, GROUP, dtype=F32),
            out(GROUP, 2 * ROPE, dtype=F32),
            out(GROUP, 2 * ROPE, dtype=F32),
            out(GROUP, D),
            out(GROUP, D),
            out(LOCAL, ROWS, D),
        ),
        in_specs=[VM] * len(small) + [ANY] * len(large),
        out_specs=(VM,) * 22 + (ANY,) * 2,
        scratch_shapes=[
            vmem((GROUP, 2 * COLS), BF16),
            vmem((GROUP, 2 * COLS), BF16),
            vmem((ROWS, 2 * COLS), BF16),
            vmem((ROWS, 2 * COLS), BF16),
            vmem((GROUP, D), BF16),
            vmem((D, 2 * HEAD), BF16),
            vmem((LATENT + ROPE, D), BF16),
            vmem((LATENT, 512), BF16),
            vmem((2 * VDIM, D), BF16),
            vmem((2 * ROPE, D), BF16),
            vmem((TENSOR, GROUP, COLS), BF16),
            vmem((4, GROUP, COLS), BF16),
            vmem((2, GROUP // 2, COLS), BF16),
            vmem((2, GROUP, COLS), BF16),
            vmem((2, LOCAL, ROWS, COLS), BF16),
        ]
        + sum_rows_scratch()
        + pair(15)
        + pair(15)
        + pair(9)
        + pair(9)
        + pair(9)
        + pair(2, 6)
        + pair(8)
        + pair(2, 2, 15)
        + [DMA((4,)), DMA((2, 2)), DMA],
        compiler_params=params(cid, 60),
        name="front_step",
    )(*small, *large)


def per_device(
    tokens,
    cotangent,
    attn_gain,
    w_query,
    w_latent,
    latent_gain,
    w_expand,
    w_out,
    ffn_gain,
    shared_gate,
    shared_up,
    shared_down,
    expert_gate,
    expert_up,
    expert_down,
    seq_lengths,
    seq_order,
    routes,
    gate_weights,
):
    group = lax.axis_index("expert")
    half = ROPE // 2
    wlat_t = w_latent.T
    attn_row = attn_gain.reshape(1, D)
    ffn_row = ffn_gain.reshape(1, D)
    lgain = latent_gain.reshape(1, LATENT)

    (
        x_cols, dy_cols, middle, inv_two, normed_two_cols, normed, inv_one, query, expanded, key_rope, compressed,
        latent, inv_lat, probs, mixed, place, gate_of, seat, seat_row, cosine, sine, dy_full, normed_two, grad_rows
    ) = front_step(
        (
            tokens,
            cotangent,
            seq_lengths.reshape(1, -1),
            seq_order.reshape(1, -1),
            routes.T,
            gate_weights.T,
            attn_row,
            lgain,
            ffn_row,
        ),
        (w_query, wlat_t, w_expand, w_out),
        1,
    )

    (
        part, grad_eg, grad_eu, grad_ed, shared_out, dmid, dgain_ffn, d_attn, unused, shared_weights
    ) = moe_step(
        place,
        normed_two_cols,
        normed_two,
        dy_full,
        shared_gate.T,
        shared_up.T,
        shared_down,
        jnp.swapaxes(expert_gate, 1, 2),
        jnp.swapaxes(expert_up, 1, 2),
        expert_down,
        grad_rows,
        middle,
        inv_two,
        ffn_row,
        dy_cols,
        3,
    )
    shared_weights = jnp.sum(shared_weights.astype(F32), axis=0)

    output, input_grad, grad_wq, grad_wexp, grad_wout, grad_wlat, gains = back_step(
        (
            d_attn,
            mixed,
            w_out,
            query,
            expanded,
            key_rope,
            probs,
            cosine,
            sine,
            latent,
            inv_lat,
            lgain,
            x_cols,
            inv_one,
            attn_row,
            dmid,
            dgain_ffn,
            middle,
            shared_out,
            gate_of,
            seat,
            seat_row,
        ),
        (place, normed, w_query, w_expand, compressed, wlat_t, part),
        4,
    )
    grad_wlat = grad_wlat.reshape(WIDE_LAT, D // GROUPS)
    grad_wlat = jnp.concatenate(
        [grad_wlat[: LATENT + half], grad_wlat[LATENT + ROPE : LATENT + ROPE + half]], axis=0
    ).T.astype(F32)
    gain_grads = jnp.swapaxes(gains[:, :2], 0, 1).reshape(2, D)
    lgain_grad = jnp.sum(gains[:, 2:4], axis=0).reshape(LATENT)
    own = lax.dynamic_slice_in_dim(gain_grads, group * (D // GROUPS), D // GROUPS, 1)
    own_l = lax.dynamic_slice_in_dim(lgain_grad, group * (LATENT // GROUPS), LATENT // GROUPS, 0)
    return (
        output,
        input_grad,
        own[0],
        grad_wq,
        grad_wlat,
        own_l,
        grad_wexp,
        grad_wout,
        own[1],
        shared_weights[0].T,
        shared_weights[1].T,
        shared_weights[2],
        jnp.swapaxes(grad_eg, 1, 2),
        jnp.swapaxes(grad_eu, 1, 2),
        grad_ed,
    )


def solution(mesh):
    return jax.shard_map(
        per_device,
        mesh=mesh,
        in_specs=(
            P("expert", "tensor"),
            P("expert", "tensor"),
            P(),
            P(None, "tensor"),
            P(),
            P(),
            P(None, "tensor"),
            P("tensor", None),
            P(),
            P(None, "tensor"),
            P(None, "tensor"),
            P("tensor", None),
            P("expert", None, "tensor"),
            P("expert", None, "tensor"),
            P("expert", "tensor", None),
            P(),
            P(),
            P("expert", None),
            P("expert", None),
        ),
        out_specs=(
            P("expert", "tensor"),
            P("expert", "tensor"),
            P("expert"),
            P("expert", "tensor"),
            P("expert", None),
            P("expert"),
            P("expert", "tensor"),
            P("tensor", "expert"),
            P("expert"),
            P("expert", "tensor"),
            P("expert", "tensor"),
            P("tensor", "expert"),
            P("expert", None, "tensor"),
            P("expert", None, "tensor"),
            P("expert", "tensor", None),
        ),
        check_vma=False,
    )
```

```python
import math

import jax
import jax.numpy as jnp
from jax import lax
from jax.experimental import pallas as pl
from jax.experimental.pallas import tpu as pltpu
from jax.sharding import PartitionSpec as P

NOPE = 128
ROPE = 64
HEAD = NOPE + ROPE
LATENT = 512
VDIM = 128
D = 2048
GROUP = 256
TOP = 6
EXPERTS = 64
GROUPS = 16
LOCAL = 4
CAP = 27
PADCAP = 32
TENSOR = 8
COLS = D // TENSOR
EPS = 1e-06

XN = 4
YN = 4
ZN = 4
CORES = 2

F32 = jnp.float32
BF16 = jnp.bfloat16
MESH = pl.DeviceIdType.MESH
ANY = pl.BlockSpec(memory_space=pl.ANY)
VM = pl.BlockSpec(memory_space=pltpu.VMEM)
DMA = pltpu.SemaphoreType.DMA
MIB = 1024 * 1024


def remote(src, dst, ssem, rsem, axis, index):
    return pltpu.make_async_remote_copy(
        src_ref=src,
        dst_ref=dst,
        send_sem=ssem,
        recv_sem=rsem,
        device_id={axis: index},
        device_id_type=MESH,
    )


def greet(peers):
    barrier = pltpu.get_barrier_semaphore()
    for axis, index in peers:
        pl.semaphore_signal(barrier, inc=1, device_id={axis: index}, device_id_type=MESH)
    pl.semaphore_wait(barrier, len(peers))


def params(cid, vmem=48):
    return pltpu.CompilerParams(
        collective_id=cid, has_side_effects=True, vmem_limit_bytes=vmem * MIB
    )


def x_peers():
    t = lax.axis_index("tensor")
    x = t // CORES
    c = lax.rem(t, CORES)
    right = lax.rem(x + 1, XN) * CORES + c
    left = lax.rem(x + XN - 1, XN) * CORES + c
    far = lax.rem(x + 2, XN) * CORES + c
    twin = x * CORES + (1 - c)
    return t, right, left, far, twin


def greet_x():
    t, right, left, far, twin = x_peers()
    greet([("tensor", right), ("tensor", left), ("tensor", twin)])


def greet_tensor():
    t = lax.axis_index("tensor")
    greet([("tensor", lax.rem(t + j, TENSOR)) for j in range(1, TENSOR)])


def cols(index, width):
    return pl.ds(pl.multiple_of(index * width, width), width)


def gather_tensor(nch, src, out_ref, ssem, rsem):
    t, right, left, far, twin = x_peers()
    flip = twin - t
    rows, width = src.shape
    rc = rows // nch
    h = rc // 2

    def block(k, owner, part=None):
        if part is None:
            return out_ref.at[pl.ds(k * rc, rc), cols(owner, width)]
        return out_ref.at[pl.ds(k * rc + part * h, h), cols(owner, width)]

    sends = []

    def send(k, j, ref, dst, target):
        c = remote(ref, dst, ssem.at[k, j], rsem.at[k, j], "tensor", target)
        c.start()
        sends.append(c)

    def arrived(k, j, ref):
        remote(ref, ref, ssem.at[k, j], rsem.at[k, j], "tensor", twin).wait_recv()

    for k in range(nch):
        part = src.at[pl.ds(k * rc, rc), :]
        send(k, 0, part, block(k, t), right)
        send(k, 1, part, block(k, t), left)
        send(k, 4, part, block(k, t), twin)
    for k in range(nch):
        arrived(k, 0, block(k, left))
        send(k, 2, block(k, left, 0), block(k, left, 0), right)
        send(k, 5, block(k, left), block(k, left), twin)
        arrived(k, 1, block(k, right))
        send(k, 3, block(k, right, 1), block(k, right, 1), left)
        send(k, 6, block(k, right), block(k, right), twin)
    for k in range(nch):
        arrived(k, 2, block(k, far, 0))
        send(k, 7, block(k, far, 0), block(k, far, 0), twin)
        arrived(k, 3, block(k, far, 1))
        send(k, 8, block(k, far, 1), block(k, far, 1), twin)
    for k in range(nch):
        arrived(k, 4, block(k, twin))
        arrived(k, 5, block(k, left + flip))
        arrived(k, 6, block(k, right + flip))
        arrived(k, 7, block(k, far + flip, 0))
        arrived(k, 8, block(k, far + flip, 1))
    for s in sends:
        s.wait_send()


def gather_sems(nch):
    return [DMA((nch, 9)), DMA((nch, 9))]


def sum_rows_start(value, buf, ssem, rsem):
    t = lax.axis_index("tensor")
    rows = value.shape[0]
    mine = jnp.broadcast_to(jnp.sum(value, axis=1, keepdims=True), (rows, 128))
    buf[t] = jnp.transpose(mine)[:8]
    sends = []
    for j in range(1, TENSOR):
        to = lax.rem(t + j, TENSOR)
        c = remote(buf.at[t], buf.at[t], ssem.at[j], rsem.at[j], "tensor", to)
        c.start()
        sends.append(c)

    def finish():
        for j in range(1, TENSOR):
            ref = buf.at[lax.rem(t + TENSOR - j, TENSOR)]
            remote(ref, ref, ssem.at[j], rsem.at[j], "tensor", t).wait_recv()
        total = jnp.sum(buf[...], axis=0)
        for s in sends:
            s.wait_send()
        return jnp.transpose(total)[:, :1]

    return finish


def sum_rows_tensor(value, buf, ssem, rsem):
    return sum_rows_start(value, buf, ssem, rsem)()


def sum_rows_scratch():
    return [pltpu.VMEM((TENSOR, 8, GROUP), F32), DMA((TENSOR,)), DMA((TENSOR,))]


def dot_nn(a, b):
    return lax.dot_general(a, b, (((1,), (0,)), ((), ())), preferred_element_type=F32)


def dot_nt(a, b):
    return lax.dot_general(a, b, (((1,), (1,)), ((), ())), preferred_element_type=F32)


def dot_tn(a, b):
    return lax.dot_general(a, b, (((0,), (0,)), ((), ())), preferred_element_type=F32)


ROWS = GROUPS * PADCAP


def expert_peers():
    e = lax.axis_index("expert")
    z = e // YN
    y = lax.rem(e, YN)
    peers = []
    for dz in range(ZN):
        for dy in range(YN):
            if dz or dy:
                to = lax.rem(z + dz, ZN) * YN + lax.rem(y + dy, YN)
                frm = lax.rem(z + ZN - dz, ZN) * YN + lax.rem(y + YN - dy, YN)
                peers.append((to, frm))
    return e, peers


def seat_rows(index):
    return pl.ds(pl.multiple_of(index * PADCAP, PADCAP), PADCAP)


def moe_kernel(
    place_ref, rown_hbm, nfull_hbm, dy_hbm, sg_hbm, su_hbm, sd_hbm, wg_hbm, wu_hbm, wd_hbm, grads_hbm,
    mid_ref, inv_ref, gain_ref, dyc_ref,
    part_hbm, gg_hbm, gu_hbm, gd_hbm, shout_ref, dmid_ref, dgain_ref, dattn_hbm, wsend_hbm, wgot_hbm,
    sh_ref, dsg_ref, dsu_ref, nfull, dyf, rows, drows, sib, half, full, wbuf, gbuf, gout, pbuf, res, back, shsum, low,
    a_s, a_r, r_s, r_r, b_s, b_r, f_s, f_r, w_s, w_r, st_buf, st_s, st_r, l_in, l_w, l_g, l_out, l_own, l_sh, l_first,
):
    t, right, left, far, twin = x_peers()
    flip = twin - t
    e, peers = expert_peers()
    greet(
        [("tensor", lax.rem(t + j, TENSOR)) for j in range(1, TENSOR)]
        + [("expert", to) for to, frm in peers]
    )
    sends = []

    def send(src, dst, ssem, rsem, axis, to):
        c = remote(src, dst, ssem, rsem, axis, to)
        c.start()
        sends.append(c)

    def got(ref, ssem, rsem):
        remote(ref, ref, ssem, rsem, "tensor", twin).wait_recv()

    blocks = (t, far)
    own_copies = []
    for k in range(LOCAL):
        for b in range(2):
            c = pltpu.make_async_copy(
                rown_hbm.at[b, k], rows.at[k, :, cols(blocks[b], COLS)], l_first.at[k, b]
            )
            c.start()
            own_copies.append(c)
    wide = sd_hbm.shape[0]
    sgv, suv, sdv = (drows.at[i, pl.ds(0, wide)] for i in range(3))
    early = [
        pltpu.make_async_copy(src, dst, l_in.at[i])
        for i, (src, dst) in enumerate(
            [(nfull_hbm, nfull), (sg_hbm, sgv), (su_hbm, suv), (sd_hbm, sdv), (dy_hbm, dyf)]
        )
    ]
    for c in early:
        c.start()

    def load(k):
        s = k % 2
        copies = [
            pltpu.make_async_copy(ref.at[k], wbuf.at[s, i], l_w.at[s, i])
            for i, ref in enumerate((wg_hbm, wu_hbm, wd_hbm))
        ]
        for c in copies:
            c.start()
        return copies

    loads = {0: load(0), 1: load(1)}

    grad_loads = [pltpu.make_async_copy(grads_hbm.at[k], gbuf.at[k], l_g.at[k]) for k in range(LOCAL)]
    for c in grad_loads:
        c.start()

    h = ROWS // 2

    def row_block(k):
        return lambda owner: rows.at[k, :, cols(owner, COLS)]

    near = [near_stages(row_block(k), a_s.at[k], a_r.at[k], send) for k in range(LOCAL)]

    def gather_1(k):
        for b in range(2):
            own_copies[2 * k + b].wait()
            near[k][b]()

    def gather_2(k):
        near[k][2]()

    def gather_4(k):
        near[k][3]()

    back_copies = {}

    order = (far, right, left, t)

    def slot(k):
        return k

    def rsend(k, j, src, dst, to):
        send(src, dst, r_s.at[k, j], r_r.at[k, j], "tensor", to)

    def rgot(k, j, ref):
        got(ref, r_s.at[k, j], r_r.at[k, j])

    def mine(k, j):
        return drows[slot(k), :, cols(order[j], COLS)].astype(F32)

    twin_sends = {}

    def sum_1(k):
        first = len(sends)
        for j, owner in enumerate(order):
            rsend(k, j, drows.at[slot(k), :, cols(owner + flip, COLS)], sib.at[k, j], twin)
        twin_sends[k] = sends[first:]
        del sends[first:]

    def sum_2(k):
        rgot(k, 0, sib.at[k, 0])
        sib[k, 0] = (mine(k, 0) + sib[k, 0].astype(F32)).astype(BF16)
        rsend(k, 4, sib.at[k, 0, pl.ds(0, h)], half.at[k, 0], right)
        rsend(k, 5, sib.at[k, 0, pl.ds(h, h)], half.at[k, 1], left)

    def sum_3(k):
        for j, to in ((1, right), (2, left)):
            rgot(k, j, sib.at[k, j])
            rgot(k, 3 + j, half.at[k, j - 1])
            both = mine(k, j) + sib[k, j].astype(F32)
            extra = half[k, j - 1].astype(F32)
            if j == 1:
                sib[k, j, :h] = (both[:h] + extra).astype(BF16)
                sib[k, j, h:] = both[h:].astype(BF16)
            else:
                sib[k, j, :h] = both[:h].astype(BF16)
                sib[k, j, h:] = (both[h:] + extra).astype(BF16)
            rsend(k, 5 + j, sib.at[k, j], full.at[k, j - 1], to)

    def sum_4(k):
        rgot(k, 3, sib.at[k, 3])
        rgot(k, 6, full.at[k, 0])
        rgot(k, 7, full.at[k, 1])
        value = mine(k, 3) + sib[k, 3].astype(F32) + full[k, 0].astype(F32) + full[k, 1].astype(F32)
        for c in twin_sends[k]:
            c.wait_send()
        if k == LOCAL:
            shsum[...] = value
            return
        res[k] = value.astype(BF16)
        c = pltpu.make_async_copy(res.at[k, seat_rows(e)], back.at[k, seat_rows(e)], l_own.at[k])
        c.start()
        back_copies[k] = c
        for j, (to, frm) in enumerate(peers):
            send(res.at[k, seat_rows(to)], back.at[k, seat_rows(e)], b_s.at[k, j], b_r.at[k, j], "expert", to)

    def shared_forward():
        for c in early[:4]:
            c.wait()
        n = nfull[...]
        g = dot_nt(n, sgv[...])
        u = dot_nt(n, suv[...])
        sig = jax.nn.sigmoid(g)
        silu = g * sig
        sh_ref[...] = (silu * u).astype(BF16)
        return g, u, sig, silu

    def shared_backward(g, u, sig, silu):
        early[4].wait()
        dh = dot_nt(dyf[...], sdv[...])
        dsg_ref[...] = (dh * u * (sig * (1.0 + g * (1.0 - sig)))).astype(BF16)
        dsu_ref[...] = (dh * silu).astype(BF16)

    tiles = [pl.ds(i * 512, 512) for i in range(D // 512)]

    def shared_rows():
        hid = sh_ref[...]
        dsg, dsu = dsg_ref[...], dsu_ref[...]
        for n in tiles:
            drows[LOCAL, :GROUP, n] = dot_nn(hid, sdv[:, n]).astype(BF16)
            drows[LOCAL, GROUP:, n] = (dot_nn(dsg, sgv[:, n]) + dot_nn(dsu, suv[:, n])).astype(BF16)

    stages = (drows.at[1], drows.at[2], pbuf)
    staged = []

    def shared_weights():
        pairs = ((dsg_ref, nfull), (dsu_ref, nfull), (sh_ref, dyf))
        for i, (lhs, rhs) in enumerate(pairs):
            for n in tiles:
                stages[i][:wide, n] = dot_tn(lhs[...], rhs[:, n]).astype(BF16)
            c = pltpu.make_async_copy(stages[i].at[pl.ds(0, wide)], wsend_hbm.at[i], l_sh.at[i])
            c.start()
            staged.append(c)

    def shared_send(i):
        for j, (to, frm) in enumerate(peers):
            send(wsend_hbm.at[i, :, cols(to, 128)], wgot_hbm.at[e, i], w_s.at[i, j], w_r.at[i, j], "expert", to)
        c = pltpu.make_async_copy(wsend_hbm.at[i, :, cols(e, 128)], wgot_hbm.at[e, i], l_sh.at[i])
        c.start()
        staged[i] = c

    out_copies = {}

    def compute_1(k):
        s = k % 2
        for c in loads[k] + [grad_loads[k]]:
            c.wait()
        r = rows[k]
        gate = dot_nt(r, wbuf[s, 0])
        up = dot_nt(r, wbuf[s, 1])
        dh = dot_nt(gbuf[k], wbuf[s, 2])
        sig = jax.nn.sigmoid(gate)
        silu = gate * sig
        hidden = (silu * up).astype(BF16)
        dg = (dh * up * (sig * (1.0 + gate * (1.0 - sig)))).astype(BF16)
        du = (dh * silu).astype(BF16)
        for n in tiles:
            drows[slot(k), :, n] = (
                dot_nn(dg, wbuf[s, 0, :, n]) + dot_nn(du, wbuf[s, 1, :, n])
            ).astype(BF16)
        return hidden, dg, du

    def compute_2(k, hidden, dg, du):
        s = k % 2
        if k:
            for c in out_copies[k - 1]:
                c.wait()
        for n in tiles:
            pbuf[:, n] = dot_nn(hidden, wbuf[s, 2, :, n]).astype(BF16)
            gout[0, :, n] = dot_tn(dg, rows[k, :, n]).astype(BF16)
            gout[1, :, n] = dot_tn(du, rows[k, :, n]).astype(BF16)
            gout[2, :, n] = dot_tn(hidden, gbuf[k, :, n]).astype(BF16)
        out_copies[k] = [
            pltpu.make_async_copy(src, dst.at[k], l_out.at[i])
            for i, (src, dst) in enumerate(
                [(pbuf, part_hbm), (gout.at[0], gg_hbm), (gout.at[1], gu_hbm), (gout.at[2], gd_hbm)]
            )
        ]
        for c in out_copies[k]:
            c.start()
        if k + 2 < LOCAL:
            loads[k + 2] = load(k + 2)

    for k in range(LOCAL):
        gather_1(k)
    state = shared_forward()
    shared_backward(*state)
    gather_2(0)
    shared_rows()
    sum_1(4)
    gather_2(1)
    gather_4(0)
    c0 = compute_1(0)
    sum_1(0)
    gather_2(2)
    shared_weights()
    gather_4(1)
    for i in range(3):
        staged[i].wait()
    c1 = compute_1(1)
    sum_1(1)
    shared_send(0)
    shared_send(1)
    gather_2(3)
    sum_2(0)
    compute_2(0, *c0)
    gather_4(2)
    c2 = compute_1(2)
    sum_1(2)
    sum_3(0)
    sum_2(1)
    compute_2(1, *c1)
    gather_4(3)
    c3 = compute_1(3)
    sum_1(3)
    sum_4(0)
    sum_3(1)
    sum_2(2)
    sum_2(3)
    compute_2(2, *c2)
    sum_2(4)
    sum_4(1)
    sum_3(2)
    sum_3(3)
    compute_2(3, *c3)
    sum_3(4)
    sum_4(2)
    sum_4(3)
    shared_send(2)
    sum_4(4)
    shout_ref[...] = shsum[:GROUP]

    dn = shsum[GROUP:]

    def combine(k):
        back_copies[k].wait()
        for j, (to, frm) in enumerate(peers):
            got(back.at[k, seat_rows(frm)], b_s.at[k, j], b_r.at[k, j])
        return dot_tn(place_ref[k], back[k])

    for k in range(LOCAL):
        dn = dn + combine(k)

    mid = mid_ref[...]
    inv = inv_ref[...]
    u = dn * gain_ref[:, cols(t, COLS)].astype(F32)
    total = sum_rows_tensor(u * mid, st_buf, st_s, st_r)
    dmid = dyc_ref[...].astype(F32) + inv * u - mid * (inv * inv * inv * total * (1.0 / D))
    dmid_ref[...] = dmid
    low[...] = dmid.astype(BF16)
    own = pltpu.make_async_copy(low, dattn_hbm.at[:, cols(t, COLS)], l_own.at[0])
    own.start()
    dgain_ref[...] = jnp.sum(dn * mid * inv, axis=0, keepdims=True)
    gather_tensor(1, low, dattn_hbm, f_s, f_r)
    own.wait()
    for c in out_copies[LOCAL - 1]:
        c.wait()
    for i in range(3):
        staged[i].wait()
        for j, (to, frm) in enumerate(peers):
            got(wgot_hbm.at[frm, i], w_s.at[i, j], w_r.at[i, j])
    for c in sends:
        c.wait_send()


def moe_step(place, rown, nfull, dy, sg, su, sd, wg, wu, wd, grads, mid, inv, gain, dyc, cid):
    hid = wd.shape[1]
    wide = sd.shape[0]
    wshape = jax.ShapeDtypeStruct((LOCAL, hid, D), BF16)
    vmem = pltpu.VMEM
    return pl.pallas_call(
        moe_kernel,
        out_shape=(
            jax.ShapeDtypeStruct((LOCAL, ROWS, D), BF16),
            wshape,
            wshape,
            wshape,
            jax.ShapeDtypeStruct((GROUP, COLS), F32),
            jax.ShapeDtypeStruct((GROUP, COLS), F32),
            jax.ShapeDtypeStruct((1, COLS), F32),
            jax.ShapeDtypeStruct((GROUP, D), BF16),
            jax.ShapeDtypeStruct((3, wide, D), BF16),
            jax.ShapeDtypeStruct((GROUPS, 3, wide, D // GROUPS), BF16),
        ),
        in_specs=[VM] + [ANY] * 10 + [VM] * 4,
        out_specs=(ANY, ANY, ANY, ANY, VM, VM, VM, ANY, ANY, ANY),
        scratch_shapes=[
            vmem((GROUP, wide), BF16),
            vmem((GROUP, wide), BF16),
            vmem((GROUP, wide), BF16),
            vmem((GROUP, D), BF16),
            vmem((GROUP, D), BF16),
            vmem((LOCAL, ROWS, D), BF16),
            vmem((LOCAL + 1, ROWS, D), BF16),
            vmem((LOCAL + 1, 4, ROWS, COLS), BF16),
            vmem((LOCAL + 1, 2, ROWS // 2, COLS), BF16),
            vmem((LOCAL + 1, 2, ROWS, COLS), BF16),
            vmem((2, 3, hid, D), BF16),
            vmem((LOCAL, ROWS, D), BF16),
            vmem((3, hid, D), BF16),
            vmem((ROWS, D), BF16),
            vmem((LOCAL, ROWS, COLS), BF16),
            vmem((LOCAL, ROWS, COLS), BF16),
            vmem((2 * GROUP, COLS), F32),
            vmem((GROUP, COLS), BF16),
            DMA((LOCAL, 6)),
            DMA((LOCAL, 6)),
            DMA((LOCAL + 1, 8)),
            DMA((LOCAL + 1, 8)),
            DMA((LOCAL, 15)),
            DMA((LOCAL, 15)),
            DMA((1, 9)),
            DMA((1, 9)),
            DMA((3, 15)),
            DMA((3, 15)),
            vmem((TENSOR, 8, GROUP), F32),
            DMA((TENSOR,)),
            DMA((TENSOR,)),
            DMA((5,)),
            DMA((2, 3)),
            DMA((LOCAL,)),
            DMA((4,)),
            DMA((LOCAL,)),
            DMA((3,)),
            DMA((LOCAL, 2)),
        ],
        compiler_params=params(cid, 63),
        cost_estimate=pl.CostEstimate(
            flops=40 * 10**9, bytes_accessed=100 * MIB, transcendentals=0
        ),
        name="moe_step",
    )(place, rown, nfull, dy, sg, su, sd, wg, wu, wd, grads, mid, inv, gain, dyc)


def swap_halves(value):
    return pltpu.roll(value, 64, 1)


def turn(value, cosine, sine):
    return value * cosine + swap_halves(value) * sine


def lane_head(shape):
    lane = lax.broadcasted_iota(jnp.int32, shape, 1)
    return (lane >> 5) & 1


def regroup(dtype):
    n = 2 * HEAD
    given = lax.broadcasted_iota(jnp.int32, (n, n), 0)
    made = lax.broadcasted_iota(jnp.int32, (n, n), 1)
    r = made - 2 * NOPE
    turned = ((r >> 5) & 1) * HEAD + NOPE + (r >> 6) * (ROPE // 2) + (r & 31)
    source = jnp.where(made < NOPE, made, jnp.where(made < 2 * NOPE, made + ROPE, turned))
    return jnp.where(given == source, 1.0, 0.0).astype(dtype)


def band(index, rows):
    return pl.ds(pl.multiple_of(index * rows, rows), rows)


def hop_start(src, dst, rows, ss, rs, send):
    e, peers = expert_peers()
    dst[band(e, rows)] = src[band(e, rows)]
    for j, (to, frm) in enumerate(peers):
        send(src.at[band(to, rows)], dst.at[band(e, rows)], ss.at[j], rs.at[j], "expert", to)


def hop_wait(dst, rows, ss, rs):
    e, peers = expert_peers()
    for j, (to, frm) in enumerate(peers):
        ref = dst.at[band(frm, rows)]
        remote(ref, ref, ss.at[j], rs.at[j], "expert", to).wait_recv()


def one_hot(test):
    return jnp.where(test, 1.0, 0.0).astype(BF16)


def by_sixteen():
    made, given = iota((GROUP, GROUP), 0), iota((GROUP, GROUP), 1)
    return one_hot(given == (made & 15) * GROUPS + (made >> 4))


def seat_of_row(index):
    return one_hot(iota((GROUP, ROWS), 1).astype(F32) == index)


def row_of_seat(index):
    return one_hot(iota((ROWS, GROUP), 0).astype(F32) == index)


def near_stages(block, ss, rs, send):
    t, right, left, far, twin = x_peers()
    flip = twin - t

    def put(j, owner, to):
        send(block(owner), block(owner), ss.at[j], rs.at[j], "tensor", to)

    def arrived(j, owner):
        ref = block(owner)
        remote(ref, ref, ss.at[j], rs.at[j], "tensor", twin).wait_recv()

    def stage_1():
        put(0, t, right)
        put(1, t, left)
        put(2, t, twin)

    def stage_far():
        put(3, far, twin)

    def stage_2():
        arrived(0, left)
        put(4, left, twin)
        arrived(1, right)
        put(5, right, twin)

    def stage_3():
        arrived(2, twin)
        arrived(3, far + flip)
        arrived(4, left + flip)
        arrived(5, right + flip)

    return stage_1, stage_far, stage_2, stage_3


def sum_stages(theirs, mine, rows, sib, half, full, ss, rs, send):
    t, right, left, far, twin = x_peers()
    flip = twin - t
    order = (far, right, left, t)
    h = rows // 2

    def put(j, src, dst, to):
        send(src, dst, ss.at[j], rs.at[j], "tensor", to)

    def arrived(j, ref):
        remote(ref, ref, ss.at[j], rs.at[j], "tensor", twin).wait_recv()

    def stage_1():
        for j, owner in enumerate(order):
            put(j, theirs(owner + flip), sib.at[j], twin)

    def stage_2():
        arrived(0, sib.at[0])
        sib[0] = (mine(0) + sib[0].astype(F32)).astype(sib.dtype)
        put(4, sib.at[0, pl.ds(0, h)], half.at[0], right)
        put(5, sib.at[0, pl.ds(h, h)], half.at[1], left)

    def stage_3():
        for j, to in ((1, right), (2, left)):
            arrived(j, sib.at[j])
            arrived(3 + j, half.at[j - 1])
            both = mine(j) + sib[j].astype(F32)
            extra = half[j - 1].astype(F32)
            if j == 1:
                sib[j, :h] = (both[:h] + extra).astype(sib.dtype)
                sib[j, h:] = both[h:].astype(sib.dtype)
            else:
                sib[j, :h] = both[:h].astype(sib.dtype)
                sib[j, h:] = (both[h:] + extra).astype(sib.dtype)
            put(5 + j, sib.at[j], full.at[j - 1], to)

    def stage_4():
        arrived(3, sib.at[3])
        arrived(6, full.at[0])
        arrived(7, full.at[1])
        return mine(3) + sib[3].astype(F32) + full[0].astype(F32) + full[1].astype(F32)

    return stage_1, stage_2, stage_3, stage_4


SLICE = 80
WIDE_LAT = LATENT + 2 * ROPE


def back_kernel(
    dattn_ref, mixed_ref, wout_ref, q_ref, exp_ref, kr_ref, probs_ref, cos_ref, sin_ref, lat_ref, linv_ref,
    lgain_ref, x_ref, inv_ref, gain_ref, dmid_ref, ffn_ref, mid_ref, shout_ref, gate_ref, seat_ref, seat_row_ref,
    place_hbm, normed_hbm, wq_hbm, wexp_hbm, comp_hbm, wl_hbm, part_hbm,
    out_ref, dx_ref, gwq_ref, gwexp_ref, gwout_ref, gwlat_ref, gains_ref,
    normed, wq, wexp, comp, wl, place,
    own, sib, half, full, res, fback,
    npart, nsib, nhalf, nfull,
    swq, swexp, swout, swlat, rwq, rwexp, rwout, rwlat, lowlat,
    cbuf, cgot, dlat, gm, gin, xh, oh, xl, ol,
    st_buf, st_s, st_r,
    p_s, p_r, fb_s, fb_r, n_s, n_r, w_s, w_r, c_s, c_r, dl_s, dl_r, gm_s, gm_r, gt_s, gt_r, wl_s, wl_r,
    oa_s, oa_r, ob_s, ob_r, xa_s, xa_r, xb_s, xb_r, l_in, l_own,
):
    t, right, left, far, twin = x_peers()
    e, peers = expert_peers()
    others = [(lax.rem(t + j, TENSOR), lax.rem(t + TENSOR - j, TENSOR)) for j in range(1, TENSOR)]
    greet([("tensor", to) for to, frm in others] + [("expert", to) for to, frm in peers])
    sends = []

    def send(src, dst, ssem, rsem, axis, to):
        c = remote(src, dst, ssem, rsem, axis, to)
        c.start()
        sends.append(c)

    def got(ref, ssem, rsem):
        remote(ref, ref, ssem, rsem, "tensor", twin).wait_recv()

    half_rope = ROPE // 2
    for i in (1, 3):
        wl[LATENT + i * half_rope : LATENT + (i + 1) * half_rope] = jnp.zeros((half_rope, COLS), BF16)
    wide = [
        (wq_hbm, wq),
        (wexp_hbm, wexp),
        (normed_hbm, normed),
        (comp_hbm, comp),
        (place_hbm, place),
        (wl_hbm.at[pl.ds(0, LATENT), cols(t, COLS)], wl.at[pl.ds(0, LATENT)]),
        (
            wl_hbm.at[pl.ds(LATENT, half_rope), cols(t, COLS)],
            wl.at[pl.ds(LATENT, half_rope)],
        ),
        (
            wl_hbm.at[pl.ds(LATENT + half_rope, half_rope), cols(t, COLS)],
            wl.at[pl.ds(LATENT + 2 * half_rope, half_rope)],
        ),
    ]
    early = [pltpu.make_async_copy(src, dst, l_in.at[i]) for i, (src, dst) in enumerate(wide)]
    for c in early:
        c.start()

    order = (far, right, left, t)
    chunks = []
    for k in range(LOCAL):

        def theirs(owner, k=k):
            return part_hbm.at[k, :, cols(owner, COLS)]

        def mine(j, k=k):
            return own[k, j].astype(F32)

        chunks.append(
            sum_stages(
                theirs, mine, ROWS, sib.at[k], half.at[k], full.at[k], p_s.at[k], p_r.at[k], send
            )
        )
    own_loads = {}
    for k in range(LOCAL):
        for j, owner in enumerate(order):
            c = pltpu.make_async_copy(part_hbm.at[k, :, cols(owner, COLS)], own.at[k, j], l_own.at[k, j])
            c.start()
            own_loads[k, j] = c
        chunks[k][0]()

    def forward_2(k):
        for j in range(4):
            own_loads[k, j].wait()
        chunks[k][1]()

    def forward_4(k):
        res[k] = chunks[k][3]().astype(BF16)
        fback[k, seat_rows(e)] = res[k, seat_rows(e)]
        for j, (to, frm) in enumerate(peers):
            send(
                res.at[k, seat_rows(to)], fback.at[k, seat_rows(e)], fb_s.at[k, j], fb_r.at[k, j], "expert", to
            )

    def spread(i, source, landed):
        for j, (to, frm) in enumerate(peers):
            send(source(to), landed.at[e], w_s.at[i, j], w_r.at[i, j], "expert", to)

    def collect(i, landed, mine):
        total = mine
        for j, (to, frm) in enumerate(peers):
            got(landed.at[frm], w_s.at[i, j], w_r.at[i, j])
            total = total + landed[frm].astype(F32)
        return total

    mixed = mixed_ref[...]
    for n in range(4):
        s = slice(n * 512, (n + 1) * 512)
        swout[:, s] = dot_tn(mixed, dattn_ref[:, s]).astype(BF16)
    spread(0, lambda to: swout.at[:, cols(to, 128)], rwout)

    scale = HEAD ** (-0.5)
    cosine, sine = cos_ref[...], sin_ref[...]
    head = lane_head((GROUP, 2 * ROPE))
    dattn = dattn_ref[...]
    dmix = dot_nt(dattn, wout_ref[...]).astype(BF16)
    kr = kr_ref[...]
    qr = q_ref[:, 2 * NOPE :]
    turned = jnp.zeros((GROUP, 2 * ROPE), F32)
    rope_sum = jnp.zeros((GROUP, 2 * ROPE), F32)
    dq_parts = []
    dexp_parts = []
    for h in range(2):
        p = probs_ref[h]
        dm = dmix[:, h * VDIM : (h + 1) * VDIM]
        k = exp_ref[:, 256 * h : 256 * h + NOPE]
        v = exp_ref[:, 256 * h + NOPE : 256 * h + NOPE + VDIM]
        dv = dot_tn(p.astype(BF16), dm)
        dp = dot_nt(dm, v)
        ds = (p * (dp - jnp.sum(dp * p, axis=1, keepdims=True))).astype(BF16)
        dq_parts.append((dot_nn(ds, k) * scale).astype(BF16))
        turned = turned + jnp.where(head == h, dot_nn(ds, kr) * scale, 0.0)
        dk = dot_tn(ds, q_ref[:, h * NOPE : (h + 1) * NOPE]) * scale
        rope_sum = rope_sum + jnp.where(head == h, dot_tn(ds, qr) * scale, 0.0)
        dexp_parts += [dk.astype(BF16), dv.astype(BF16)]
    dexp = jnp.concatenate(dexp_parts, axis=1)
    dq_parts.append(turn(turned, cosine, -sine).astype(BF16))
    dq = dot_nt(jnp.concatenate(dq_parts, axis=1), regroup(BF16)).astype(BF16)

    early[1].wait()
    cpart = dot_nt(dexp, wexp[...])
    share = GROUP // TENSOR
    for i in range(TENSOR):
        r = slice(i * share, (i + 1) * share)
        cbuf[i, :, :LATENT] = cpart[r].astype(BF16)
        cbuf[i, :, LATENT:] = rope_sum[r].astype(BF16)
    for j, (to, frm) in enumerate(others):
        send(cbuf.at[to], cgot.at[t], c_s.at[j], c_r.at[j], "tensor", to)

    early[0].wait()
    for n in range(TENSOR):
        npart[n] = dot_nt(dq, wq[n * COLS : (n + 1) * COLS, :]).astype(BF16)
    n1, n2, n3, n4 = sum_stages(
        lambda owner: npart.at[owner],
        lambda j: npart[order[j]].astype(F32),
        GROUP, nsib, nhalf, nfull, n_s, n_r, send,
    )
    n1()
    forward_2(0)
    forward_2(1)

    early[2].wait()
    for n in range(4):
        s = slice(n * 512, (n + 1) * 512)
        swq[:, s] = dot_tn(dq, normed[:, s]).astype(BF16)
    def spread_query(i):
        part = pl.ds(i * HEAD, HEAD)
        for j, (to, frm) in enumerate(peers):
            send(
                swq.at[part, cols(to, 128)], rwq.at[e, part], w_s.at[1 + 3 * i, j], w_r.at[1 + 3 * i, j],
                "expert", to,
            )

    early[3].wait()
    gwexp = dot_tn(comp[...], dexp)
    for i in range(GROUPS):
        swexp[i] = gwexp[32 * i : 32 * (i + 1)].astype(BF16)
    spread(3, lambda to: swexp.at[to], rwexp)
    spread_query(0)

    total = cbuf[t].astype(F32)
    for j, (to, frm) in enumerate(others):
        got(cgot.at[frm], c_s.at[j], c_r.at[j])
        total = total + cgot[frm].astype(F32)
    mine_rows = pl.ds(pl.multiple_of(t * share, share), share)
    dc = total[:, :LATENT]
    lat = lat_ref[mine_rows, :]
    linv = linv_ref[mine_rows, :]
    lu = dc * lgain_ref[...].astype(F32)
    dot = jnp.sum(lu * lat, axis=1, keepdims=True)
    dlat[t, :, :LATENT] = (linv * lu - lat * (linv * linv * linv * dot * (1.0 / LATENT))).astype(BF16)
    both = total[:, LATENT:]
    both = both + pltpu.roll(both, 2 * ROPE - ROPE // 2, 1)
    both = jnp.where(lane_head((share, 2 * ROPE)) == 0, both, 0.0)
    dlat[t, :, LATENT:] = turn(both, cos_ref[mine_rows, :], -sin_ref[mine_rows, :]).astype(BF16)
    for j, (to, frm) in enumerate(others):
        send(dlat.at[t], dlat.at[t], dl_s.at[j], dl_r.at[j], "tensor", to)
    lgain_row = jnp.sum(dc * lat * linv, axis=0, keepdims=True)

    n2()
    forward_2(2)
    forward_2(3)
    n3()
    chunks[0][2]()

    def undeal_1(value, high, ss, rs):
        high[0] = dot_tn(seat_of_row(seat_ref[...]), value).astype(BF16)
        hop_start(high.at[0], high.at[1], PADCAP, ss, rs, send)

    def undeal_2(high, low, ss, rs, ss_next, rs_next):
        hop_wait(high.at[1], PADCAP, ss, rs)
        low[0] = dot_tn(row_of_seat(seat_row_ref[...]), high[1]).astype(BF16)
        hop_start(low.at[0], low.at[1], GROUPS, ss_next, rs_next, send)

    def undeal_3(low, ss, rs):
        hop_wait(low.at[1], GROUPS, ss, rs)
        return dot_tn(by_sixteen(), low[1]).astype(BF16)

    for j, (to, frm) in enumerate(others):
        got(dlat.at[frm], dl_s.at[j], dl_r.at[j])
    for i in (5, 6, 7):
        early[i].wait()
    dl = dlat[...].reshape(GROUP, WIDE_LAT)
    latent_cols = dot_nn(dl, wl[...])
    dn = latent_cols + n4()
    xd = x_ref[...].astype(F32)
    inv = inv_ref[...]
    u = dn * gain_ref[:, cols(t, COLS)].astype(F32)
    total = sum_rows_tensor(u * xd, st_buf, st_s, st_r)
    chunks[1][2]()
    dx = (dmid_ref[...] + inv * u - xd * (inv * inv * inv * total * (1.0 / D))).astype(BF16)
    undeal_1(dx, xh, xa_s, xa_r)
    chunks[2][2]()
    forward_4(0)
    spread_query(1)
    chunks[3][2]()
    gm[...] = jnp.zeros(gm.shape, F32)
    gm[0:1] = jnp.sum(dn * xd * inv, axis=0, keepdims=True)
    gm[1:2] = ffn_ref[...]
    gm[2:3] = lgain_row[:, :COLS]
    gm[3:4] = lgain_row[:, COLS:]
    for j, (to, frm) in enumerate(peers):
        send(gm, gin.at[e], gm_s.at[j], gm_r.at[j], "expert", to)

    pick_rows = lax.broadcasted_iota(jnp.int32, (WIDE_LAT, 128), 0)
    pick_cols = lax.broadcasted_iota(jnp.int32, (WIDE_LAT, 128), 1)
    pick_own = jnp.where((pick_rows == pick_cols + t * SLICE) & (pick_cols < SLICE), 1.0, 0.0).astype(BF16)
    dl_own = dot_nn(dl, pick_own).astype(BF16)
    for n in range(4):
        s = slice(n * 512, (n + 1) * 512)
        swlat[:, s] = dot_tn(dl_own, normed[:, s])[:SLICE].astype(BF16)
    spread(2, lambda to: swlat.at[:, cols(to, 128)], rwlat)

    forward_4(1)
    undeal_2(xh, xl, xa_s, xa_r, xb_s, xb_r)
    forward_4(2)
    forward_4(3)
    early[4].wait()
    routed = mid_ref[...] + shout_ref[...]
    for k in range(LOCAL):
        for j, (to, frm) in enumerate(peers):
            got(fback.at[k, seat_rows(frm)], fb_s.at[k, j], fb_r.at[k, j])
        gates = jnp.broadcast_to(gate_ref[k][:, None, :], (GROUPS, PADCAP, GROUP)).reshape(ROWS, GROUP)
        weight = place[k].astype(F32) * gates
        high = weight.astype(BF16)
        low = (weight - high.astype(F32)).astype(BF16)
        routed = routed + dot_tn(high, fback[k]) + dot_tn(low, fback[k])
    out = routed.astype(BF16)
    undeal_1(out, oh, oa_s, oa_r)
    dx_ref[...] = undeal_3(xl, xb_s, xb_r)

    gsum = gm[...]
    for j, (to, frm) in enumerate(peers):
        got(gin.at[frm], gm_s.at[j], gm_r.at[j])
        gsum = gsum + gin[frm]
    gains_ref[t] = gsum
    for j, (to, frm) in enumerate(others):
        send(gains_ref.at[t], gains_ref.at[t], gt_s.at[j], gt_r.at[j], "tensor", to)
    lat_sum = collect(2, rwlat, swlat[:, cols(e, 128)].astype(F32))
    lowlat[...] = lat_sum.astype(BF16)
    gwlat_ref[t] = lowlat[...]
    for j, (to, frm) in enumerate(others):
        send(lowlat, gwlat_ref.at[t], wl_s.at[j], wl_r.at[j], "tensor", to)
    undeal_2(oh, ol, oa_s, oa_r, ob_s, ob_r)
    gwout_ref[...] = collect(0, rwout, swout[:, cols(e, 128)].astype(F32))
    total = swq[:, cols(e, 128)].astype(F32)
    for j, (to, frm) in enumerate(peers):
        for i in range(2):
            got(rwq.at[frm, pl.ds(i * HEAD, HEAD)], w_s.at[1 + 3 * i, j], w_r.at[1 + 3 * i, j])
        total = total + rwq[frm].astype(F32)
    gwq_ref[...] = jnp.transpose(total)
    gwexp_ref[...] = collect(3, rwexp, swexp[e].astype(F32))
    out_ref[...] = undeal_3(ol, ob_s, ob_r)
    for j, (to, frm) in enumerate(others):
        got(gains_ref.at[frm], gt_s.at[j], gt_r.at[j])
        got(gwlat_ref.at[frm], wl_s.at[j], wl_r.at[j])
    for c in sends:
        c.wait_send()


def back_step(small, large, cid):
    vmem = pltpu.VMEM

    def out(*shape, dtype=BF16):
        return jax.ShapeDtypeStruct(shape, dtype)

    pair = lambda n: [DMA((n,)), DMA((n,))]
    grid_pair = lambda m, n: [DMA((m, n)), DMA((m, n))]
    return pl.pallas_call(
        back_kernel,
        out_shape=(
            out(GROUP, COLS),
            out(GROUP, COLS),
            out(D // GROUPS, 2 * HEAD, dtype=F32),
            out(LATENT // GROUPS, 512, dtype=F32),
            out(2 * VDIM, D // GROUPS, dtype=F32),
            out(TENSOR, SLICE, D // GROUPS),
            out(TENSOR, 8, COLS, dtype=F32),
        ),
        in_specs=[VM] * len(small) + [ANY] * len(large),
        out_specs=(VM,) * 7,
        scratch_shapes=[
            vmem((GROUP, D), BF16),
            vmem((D, 2 * HEAD), BF16),
            vmem((LATENT, 512), BF16),
            vmem((GROUP, LATENT), BF16),
            vmem((WIDE_LAT, COLS), BF16),
            vmem((LOCAL, ROWS, GROUP), BF16),
            vmem((LOCAL, 4, ROWS, COLS), BF16),
            vmem((LOCAL, 4, ROWS, COLS), BF16),
            vmem((LOCAL, 2, ROWS // 2, COLS), BF16),
            vmem((LOCAL, 2, ROWS, COLS), BF16),
            vmem((LOCAL, ROWS, COLS), BF16),
            vmem((LOCAL, ROWS, COLS), BF16),
            vmem((TENSOR, GROUP, COLS), BF16),
            vmem((4, GROUP, COLS), BF16),
            vmem((2, GROUP // 2, COLS), BF16),
            vmem((2, GROUP, COLS), BF16),
            vmem((2 * HEAD, D), BF16),
            vmem((GROUPS, LATENT // GROUPS, 512), BF16),
            vmem((2 * VDIM, D), BF16),
            vmem((SLICE, D), BF16),
            vmem((GROUPS, 2 * HEAD, D // GROUPS), BF16),
            vmem((GROUPS, LATENT // GROUPS, 512), BF16),
            vmem((GROUPS, 2 * VDIM, D // GROUPS), BF16),
            vmem((GROUPS, SLICE, D // GROUPS), BF16),
            vmem((SLICE, D // GROUPS), BF16),
            vmem((TENSOR, GROUP // TENSOR, WIDE_LAT), BF16),
            vmem((TENSOR, GROUP // TENSOR, WIDE_LAT), BF16),
            vmem((TENSOR, GROUP // TENSOR, WIDE_LAT), BF16),
            vmem((8, COLS), F32),
            vmem((GROUPS, 8, COLS), F32),
            vmem((2, ROWS, COLS), BF16),
            vmem((2, ROWS, COLS), BF16),
            vmem((2, GROUP, COLS), BF16),
            vmem((2, GROUP, COLS), BF16),
        ]
        + sum_rows_scratch()
        + grid_pair(LOCAL, 8)
        + grid_pair(LOCAL, 15)
        + pair(8)
        + grid_pair(5, 15)
        + pair(7)
        + pair(7)
        + pair(15)
        + pair(7)
        + pair(7)
        + pair(15)
        + pair(15)
        + pair(15)
        + pair(15)
        + [DMA((8,)), DMA((LOCAL, 4))],
        compiler_params=params(cid, 63),
        name="back_step",
    )(*small, *large)


def gather_stages(source, block, ss, rs, send):
    t, right, left, far, twin = x_peers()
    flip = twin - t

    def put(j, ref, to, src=None):
        send(ref if src is None else src, ref, ss.at[j], rs.at[j], "tensor", to)

    def arrived(j, ref):
        remote(ref, ref, ss.at[j], rs.at[j], "tensor", twin).wait_recv()

    def stage_1():
        put(0, block(t, None), right, source)
        put(1, block(t, None), left, source)
        put(4, block(t, None), twin, source)

    def stage_2():
        arrived(0, block(left, None))
        put(2, block(left, 0), right)
        put(5, block(left, None), twin)
        arrived(1, block(right, None))
        put(3, block(right, 1), left)
        put(6, block(right, None), twin)

    def stage_3():
        arrived(2, block(far, 0))
        put(7, block(far, 0), twin)
        arrived(3, block(far, 1))
        put(8, block(far, 1), twin)

    def stage_4():
        arrived(4, block(twin, None))
        arrived(5, block(left + flip, None))
        arrived(6, block(right + flip, None))
        arrived(7, block(far + flip, 0))
        arrived(8, block(far + flip, 1))

    return stage_1, stage_2, stage_3, stage_4


def column_blocks(ref, rows):
    def block(owner, part):
        r = pl.ds(0, rows) if part is None else pl.ds(part * (rows // 2), rows // 2)
        return ref.at[r, cols(owner, COLS)]

    return block


def iota(shape, dim):
    return lax.broadcasted_iota(jnp.int32, shape, dim)


def deal_in_kernel(lengths, order, group):
    n = lengths.shape[1]
    i, j = iota((n, n), 0), iota((n, n), 1)
    same, before = i == j, j < i

    def column(row):
        return jnp.sum(jnp.where(same, row, 0.0), axis=1, keepdims=True)

    def row(col):
        return jnp.sum(jnp.where(same, col, 0.0), axis=0, keepdims=True)

    def exclusive(values):
        return jnp.sum(jnp.where(before, values, 0.0), axis=1, keepdims=True)

    hit = column(order) == j.astype(F32)
    begins_col = exclusive(lengths)
    begins = row(begins_col)
    dealt_lengths = row(jnp.sum(jnp.where(hit, lengths, 0.0), axis=1, keepdims=True))
    dealt_col = exclusive(dealt_lengths)
    dealt = row(dealt_col)
    dealt_source_col = jnp.sum(jnp.where(hit, begins, 0.0), axis=1, keepdims=True)
    dealt_source = row(dealt_source_col)
    given = jnp.sum(jnp.where(hit, dealt_col, 0.0), axis=0, keepdims=True)
    given_col = column(given)

    def find(rows, lanes, starts, values):
        dim = 1 if lanes else 0
        shape = (GROUP, n) if lanes else (n, GROUP)
        place = jnp.sum(jnp.where(rows >= starts, 1.0, 0.0), axis=dim, keepdims=True) - 1.0
        on = iota(shape, dim).astype(F32) == place
        return place, jnp.sum(jnp.where(on, values, 0.0), axis=dim, keepdims=True)

    first = group * GROUP
    rows = (iota((GROUP, 1), 0) + first).astype(F32)
    rows_row = (iota((1, GROUP), 1) + first).astype(F32)
    which, start = find(rows, True, dealt, dealt)
    unused, shift = find(rows, True, dealt, dealt_source - dealt)
    which_row, shift_row = find(rows_row, False, dealt_col, dealt_source_col - dealt_col)
    source, source_row = rows + shift, rows_row + shift_row

    def rest(value):
        return value - GROUPS * jnp.floor(value * (1.0 / GROUPS))

    ahead = (rest(source) == rest(source_row)) & (source_row < source)
    rank = jnp.sum(jnp.where(ahead, 1.0, 0.0), axis=1, keepdims=True)
    seat = rest(source) * PADCAP + rank

    mine = (iota((GROUP, 1), 0) * GROUPS + group).astype(F32)
    mine_row = (iota((1, GROUP), 1) * GROUPS + group).astype(F32)
    unused, move = find(mine, True, begins, given - begins)
    unused, move_row = find(mine_row, False, begins_col, given_col - begins_col)
    to = jnp.floor((mine + move) * (1.0 / GROUP))
    to_row = jnp.floor((mine_row + move_row) * (1.0 / GROUP))
    ahead = (to == to_row) & (iota((GROUP, GROUP), 0) < iota((GROUP, GROUP), 1))
    rank = jnp.sum(jnp.where(ahead, 1.0, 0.0), axis=0, keepdims=True)
    seat_row = to_row * PADCAP + rank
    return rows - start, which, which_row, seat, seat_row


def front_kernel(
    tok_ref, cot_ref, len_ref, ord_ref, routes_ref, gates_ref, gain_ref, lgain_ref, fgain_ref,
    wq_hbm, wl_hbm, wexp_hbm, wout_hbm,
    xc_ref, dyc_ref, mid_ref, inv2_ref, ncols_ref, normed_ref, inv_ref, q_ref, exp_ref, kr_ref, comp_ref,
    lat_ref, linv_ref, probs_ref, mixed_ref, place_ref, gate_ref, seat_ref, seat_row_ref, cos_ref, sin_ref, dyfull, nfull,
    rown_hbm, grads_hbm,
    hop_a, hop_b, hop_c, hop_d, xfull, wq, wl, wexp, wout, wrope, apart, sib, half, full, gout, dbuf,
    st_buf, st_s, st_r,
    ha_s, ha_r, hb_s, hb_r, xg_s, xg_r, yg_s, yg_r, ng_s, ng_r, gg_s, gg_r, r_s, r_r, d_s, d_r, e_s, e_r, l_in, l_own, l_last,
):
    t, right, left, far, twin = x_peers()
    e, peers = expert_peers()
    greet(
        [("tensor", lax.rem(t + j, TENSOR)) for j in range(1, TENSOR)]
        + [("expert", to) for to, frm in peers]
    )
    sends = []

    def send(src, dst, ssem, rsem, axis, to):
        c = remote(src, dst, ssem, rsem, axis, to)
        c.start()
        sends.append(c)

    def got(ref, ssem, rsem):
        remote(ref, ref, ssem, rsem, "tensor", twin).wait_recv()

    def local(src, dst, sem):
        c = pltpu.make_async_copy(src, dst, sem)
        c.start()
        return c

    sixteen = by_sixteen()
    hop_a[:, :COLS] = dot_nn(sixteen, tok_ref[...]).astype(BF16)
    hop_a[:, COLS:] = dot_nn(sixteen, cot_ref[...]).astype(BF16)
    hop_start(hop_a, hop_b, GROUPS, ha_s, ha_r, send)
    early = [
        local(src, dst, l_in.at[i])
        for i, (src, dst) in enumerate([(wl_hbm, wl), (wq_hbm, wq), (wexp_hbm, wexp), (wout_hbm, wout)])
    ]

    offset, which, which_row, seat, seat_row = deal_in_kernel(
        len_ref[...].astype(F32), ord_ref[...].astype(F32), e
    )
    seat_ref[...] = seat
    seat_row_ref[...] = seat_row

    outward = row_of_seat(seat_row)
    hop_wait(hop_b, GROUPS, ha_s, ha_r)
    hop_c[...] = dot_nn(outward, hop_b[...]).astype(BF16)
    hop_start(hop_c, hop_d, PADCAP, hb_s, hb_r, send)
    hr = ROPE // 2
    lane = iota((GROUP, 2 * ROPE), 1)
    power = (lane & (hr - 1)).astype(F32) * (1.0 / hr)
    angle = offset * jnp.exp(power * (-math.log(10000.0)))
    cosine = jnp.cos(angle)
    sine = jnp.sin(angle)
    sine = jnp.where(lane < ROPE, -sine, sine)
    cos_ref[...] = cosine
    sin_ref[...] = sine

    number = iota((EXPERTS, 1), 0)
    expert = (number & 15) * LOCAL + (number >> 4)
    member = jnp.zeros((EXPERTS, GROUP), F32)
    gate_of = jnp.zeros((EXPERTS, GROUP), F32)
    for k in range(TOP):
        hit = routes_ref[k : k + 1, :] == expert
        member = member + jnp.where(hit, 1.0, 0.0)
        gate_of = gate_of + jnp.where(hit, gates_ref[k : k + 1, :], 0.0)
    earlier = jnp.where(iota((GROUP, GROUP), 0) < iota((GROUP, GROUP), 1), 1.0, 0.0).astype(BF16)
    count = dot_nn(member.astype(BF16), earlier)
    slot = jnp.where((member > 0.5) & (count < CAP - 0.5), count, -1.0)
    seats = iota((GROUPS, PADCAP, GROUP), 1).astype(F32)
    slot_gates = []
    for k in range(LOCAL):
        s = slice(k * GROUPS, (k + 1) * GROUPS)
        gate_ref[k] = gate_of[s]
        wide = jnp.broadcast_to(slot[s][:, None, :], (GROUPS, PADCAP, GROUP))
        on = jnp.where(wide == seats, 1.0, 0.0)
        place_ref[k] = on.reshape(ROWS, GROUP).astype(BF16)
        weight = on * jnp.broadcast_to(gate_of[s][:, None, :], (GROUPS, PADCAP, GROUP))
        slot_gates.append(jnp.sum(weight.reshape(ROWS, GROUP), axis=1, keepdims=True))
    early[0].wait()
    for i in range(4):
        row = LATENT + (i // 2) * hr
        wrope[i * hr : (i + 1) * hr] = wl[row : row + hr]
    inward = seat_of_row(seat)
    hop_wait(hop_d, PADCAP, hb_s, hb_r)

    xc_ref[...] = dot_nn(inward, hop_d[:, :COLS]).astype(BF16)
    xfull[:, cols(t, COLS)] = xc_ref[...]
    xg1, xg2, xg3, xg4 = gather_stages(xc_ref, column_blocks(xfull, GROUP), xg_s, xg_r, send)
    xg1()
    dyc_ref[...] = dot_nn(inward, hop_d[:, COLS:]).astype(BF16)
    dyfull[:, cols(t, COLS)] = dyc_ref[...]
    yg1, yg2, yg3, yg4 = gather_stages(dyc_ref, column_blocks(dyfull, GROUP), yg_s, yg_r, send)
    yg1()
    blocks = (t, far)

    def slot_gradients(b):
        for k in range(LOCAL):
            gout[b, k] = (slot_gates[k] * dot_nn(place_ref[k], dyfull[:, cols(blocks[b], COLS)])).astype(BF16)

    own_grads = {}

    def send_gradients(p, b):
        two = pl.ds(2 * p, 2)
        landed = grads_hbm.at[two, seat_rows(e), cols(blocks[b], COLS)]
        own_grads[p, b] = local(gout.at[b, two, seat_rows(e)], landed, l_own.at[p, b])
        for j, (to, frm) in enumerate(peers):
            send(gout.at[b, two, seat_rows(to)], landed, d_s.at[p, b, j], d_r.at[p, b, j], "expert", to)

    slot_gradients(0)
    send_gradients(0, 0)
    send_gradients(1, 0)
    xg2()
    yg2()
    xg3()
    yg3()
    slot_gradients(1)
    send_gradients(0, 1)
    send_gradients(1, 1)
    xg4()

    xd = xfull[...].astype(F32)
    inv = lax.rsqrt(jnp.sum(xd * xd, axis=1, keepdims=True) * (1.0 / D) + EPS)
    inv_ref[...] = inv
    normed = (xd * inv * gain_ref[...].astype(F32)).astype(BF16)
    normed_ref[...] = normed
    lat = dot_nt(normed, wl[:LATENT])
    lat_ref[...] = lat
    linv = lax.rsqrt(jnp.sum(lat * lat, axis=1, keepdims=True) * (1.0 / LATENT) + EPS)
    linv_ref[...] = linv
    kr = turn(dot_nt(normed, wrope[...]), cosine, sine).astype(BF16)
    kr_ref[...] = kr
    early[1].wait()
    pre = lax.dot_general(
        dot_nn(normed, wq[...]),
        regroup(F32),
        (((1,), (0,)), ((), ())),
        precision=lax.Precision.HIGHEST,
        preferred_element_type=F32,
    )
    q_ref[:, : 2 * NOPE] = pre[:, : 2 * NOPE].astype(BF16)
    qr = turn(pre[:, 2 * NOPE :], cosine, sine)
    q_ref[:, 2 * NOPE :] = qr.astype(BF16)
    comp = (lat * linv * lgain_ref[...].astype(F32)).astype(BF16)
    comp_ref[...] = comp
    early[2].wait()
    expanded = dot_nn(comp, wexp[...]).astype(BF16)
    exp_ref[...] = expanded

    def grad_block(k):
        return lambda owner: grads_hbm.at[k, :, cols(owner, COLS)]

    spread = [near_stages(grad_block(k), gg_s.at[k], gg_r.at[k], send) for k in range(LOCAL)]
    seen = set()

    def gradients(k, b):
        p = k // 2
        if (p, b) not in seen:
            seen.add((p, b))
            own_grads[p, b].wait()
            for j, (to, frm) in enumerate(peers):
                ref = grads_hbm.at[pl.ds(2 * p, 2), seat_rows(frm), cols(blocks[b], COLS)]
                got(ref, d_s.at[p, b, j], d_r.at[p, b, j])
        spread[k][b]()

    head = lane_head((GROUP, 2 * ROPE))
    allowed = (which == which_row) & (iota((GROUP, GROUP), 0) >= iota((GROUP, GROUP), 1))
    scale = HEAD ** (-0.5)
    for h in range(2):
        q = q_ref[:, h * NOPE : (h + 1) * NOPE]
        k = expanded[:, 256 * h : 256 * h + NOPE]
        v = expanded[:, 256 * h + NOPE : 256 * h + NOPE + VDIM]
        turned = jnp.where(head == h, qr, 0.0).astype(BF16)
        raw = (dot_nt(q, k) + dot_nt(turned, kr)) * scale
        scores = jnp.where(allowed, raw, -1e30)
        expo = jnp.exp(scores - jnp.max(scores, axis=1, keepdims=True))
        probs = expo / jnp.sum(expo, axis=1, keepdims=True)
        probs_ref[h] = probs
        mixed_ref[:, h * VDIM : (h + 1) * VDIM] = dot_nn(probs.astype(BF16), v).astype(BF16)
    mixed = mixed_ref[...]
    early[3].wait()
    for n in range(TENSOR):
        apart[n] = dot_nn(mixed, wout[:, n * COLS : (n + 1) * COLS]).astype(BF16)

    order = (far, right, left, t)
    r1, r2, r3, r4 = sum_stages(
        lambda owner: apart.at[owner],
        lambda j: apart[order[j]].astype(F32),
        GROUP, sib, half, full, r_s, r_r, send,
    )
    r1()
    gradients(0, 0)
    r2()
    r3()
    gradients(1, 0)
    mid = xc_ref[...].astype(F32) + r4()
    mid_ref[...] = mid
    finish = sum_rows_start(mid * mid, st_buf, st_s, st_r)
    spread[0][2]()
    inv2 = lax.rsqrt(finish() * (1.0 / D) + EPS)
    inv2_ref[...] = inv2
    ncols_ref[...] = (mid * inv2 * fgain_ref[:, cols(t, COLS)].astype(F32)).astype(BF16)
    nfull[:, cols(t, COLS)] = ncols_ref[...]
    ng1, ng2, ng3, ng4 = gather_stages(ncols_ref, column_blocks(nfull, GROUP), ng_s, ng_r, send)
    ng1()
    own_rows = {}

    def dispatch(b):
        for p in range(2):
            for k in (2 * p, 2 * p + 1):
                dbuf[b, k] = dot_nn(place_ref[k], nfull[:, cols(blocks[b], COLS)]).astype(BF16)
            two = pl.ds(2 * p, 2)
            landed = rown_hbm.at[b, two, seat_rows(e)]
            own_rows[p, b] = local(dbuf.at[b, two, seat_rows(e)], landed, l_last.at[p, b])
            for j, (to, frm) in enumerate(peers):
                send(dbuf.at[b, two, seat_rows(to)], landed, e_s.at[p, b, j], e_r.at[p, b, j], "expert", to)

    dispatch(0)
    gradients(2, 0)
    gradients(0, 1)
    gradients(1, 1)
    spread[1][2]()
    ng2()
    gradients(3, 0)
    gradients(2, 1)
    gradients(3, 1)
    ng3()
    dispatch(1)
    spread[2][2]()
    yg4()
    ng4()
    spread[3][2]()
    for k in range(LOCAL):
        spread[k][3]()
    for p in range(2):
        for b in range(2):
            own_rows[p, b].wait()
            for j, (to, frm) in enumerate(peers):
                got(rown_hbm.at[b, pl.ds(2 * p, 2), seat_rows(frm)], e_s.at[p, b, j], e_r.at[p, b, j])
    for c in sends:
        c.wait_send()


def front_step(small, large, cid):
    vmem = pltpu.VMEM

    def out(*shape, dtype=BF16):
        return jax.ShapeDtypeStruct(shape, dtype)

    def pair(*shape):
        return [DMA(shape), DMA(shape)]

    return pl.pallas_call(
        front_kernel,
        out_shape=(
            out(GROUP, COLS),
            out(GROUP, COLS),
            out(GROUP, COLS, dtype=F32),
            out(GROUP, 1, dtype=F32),
            out(GROUP, COLS),
            out(GROUP, D),
            out(GROUP, 1, dtype=F32),
            out(GROUP, 2 * HEAD),
            out(GROUP, 512),
            out(GROUP, 2 * ROPE),
            out(GROUP, LATENT),
            out(GROUP, LATENT, dtype=F32),
            out(GROUP, 1, dtype=F32),
            out(2, GROUP, GROUP, dtype=F32),
            out(GROUP, 2 * VDIM),
            out(LOCAL, ROWS, GROUP),
            out(LOCAL, GROUPS, GROUP, dtype=F32),
            out(GROUP, 1, dtype=F32),
            out(1, GROUP, dtype=F32),
            out(GROUP, 2 * ROPE, dtype=F32),
            out(GROUP, 2 * ROPE, dtype=F32),
            out(GROUP, D),
            out(GROUP, D),
            out(2, LOCAL, ROWS, COLS),
            out(LOCAL, ROWS, D),
        ),
        in_specs=[VM] * len(small) + [ANY] * len(large),
        out_specs=(VM,) * 23 + (ANY,) * 2,
        scratch_shapes=[
            vmem((GROUP, 2 * COLS), BF16),
            vmem((GROUP, 2 * COLS), BF16),
            vmem((ROWS, 2 * COLS), BF16),
            vmem((ROWS, 2 * COLS), BF16),
            vmem((GROUP, D), BF16),
            vmem((D, 2 * HEAD), BF16),
            vmem((LATENT + ROPE, D), BF16),
            vmem((LATENT, 512), BF16),
            vmem((2 * VDIM, D), BF16),
            vmem((2 * ROPE, D), BF16),
            vmem((TENSOR, GROUP, COLS), BF16),
            vmem((4, GROUP, COLS), BF16),
            vmem((2, GROUP // 2, COLS), BF16),
            vmem((2, GROUP, COLS), BF16),
            vmem((2, LOCAL, ROWS, COLS), BF16),
            vmem((2, LOCAL, ROWS, COLS), BF16),
        ]
        + sum_rows_scratch()
        + pair(15)
        + pair(15)
        + pair(9)
        + pair(9)
        + pair(9)
        + pair(LOCAL, 6)
        + pair(8)
        + pair(2, 2, 15)
        + pair(2, 2, 15)
        + [DMA((4,)), DMA((2, 2)), DMA((2, 2))],
        compiler_params=params(cid, 60),
        name="front_step",
    )(*small, *large)


def per_device(
    tokens,
    cotangent,
    attn_gain,
    w_query,
    w_latent,
    latent_gain,
    w_expand,
    w_out,
    ffn_gain,
    shared_gate,
    shared_up,
    shared_down,
    expert_gate,
    expert_up,
    expert_down,
    seq_lengths,
    seq_order,
    routes,
    gate_weights,
):
    group = lax.axis_index("expert")
    half = ROPE // 2
    wlat_t = w_latent.T
    attn_row = attn_gain.reshape(1, D)
    ffn_row = ffn_gain.reshape(1, D)
    lgain = latent_gain.reshape(1, LATENT)

    (
        x_cols, dy_cols, middle, inv_two, normed_two_cols, normed, inv_one, query, expanded, key_rope, compressed,
        latent, inv_lat, probs, mixed, place, gate_of, seat, seat_row, cosine, sine, dy_full, normed_two, own_slots, grad_rows
    ) = front_step(
        (
            tokens,
            cotangent,
            seq_lengths.reshape(1, -1),
            seq_order.reshape(1, -1),
            routes.T,
            gate_weights.T,
            attn_row,
            lgain,
            ffn_row,
        ),
        (w_query, wlat_t, w_expand, w_out),
        1,
    )

    (
        part, grad_eg, grad_eu, grad_ed, shared_out, dmid, dgain_ffn, d_attn, unused, shared_weights
    ) = moe_step(
        place,
        own_slots,
        normed_two,
        dy_full,
        shared_gate.T,
        shared_up.T,
        shared_down,
        jnp.swapaxes(expert_gate, 1, 2),
        jnp.swapaxes(expert_up, 1, 2),
        expert_down,
        grad_rows,
        middle,
        inv_two,
        ffn_row,
        dy_cols,
        3,
    )
    shared_weights = jnp.sum(shared_weights.astype(F32), axis=0)

    output, input_grad, grad_wq, grad_wexp, grad_wout, grad_wlat, gains = back_step(
        (
            d_attn,
            mixed,
            w_out,
            query,
            expanded,
            key_rope,
            probs,
            cosine,
            sine,
            latent,
            inv_lat,
            lgain,
            x_cols,
            inv_one,
            attn_row,
            dmid,
            dgain_ffn,
            middle,
            shared_out,
            gate_of,
            seat,
            seat_row,
        ),
        (place, normed, w_query, w_expand, compressed, wlat_t, part),
        4,
    )
    grad_wlat = grad_wlat.reshape(WIDE_LAT, D // GROUPS)
    grad_wlat = jnp.concatenate(
        [grad_wlat[: LATENT + half], grad_wlat[LATENT + ROPE : LATENT + ROPE + half]], axis=0
    ).T.astype(F32)
    gain_grads = jnp.swapaxes(gains[:, :2], 0, 1).reshape(2, D)
    lgain_grad = jnp.sum(gains[:, 2:4], axis=0).reshape(LATENT)
    own = lax.dynamic_slice_in_dim(gain_grads, group * (D // GROUPS), D // GROUPS, 1)
    own_l = lax.dynamic_slice_in_dim(lgain_grad, group * (LATENT // GROUPS), LATENT // GROUPS, 0)
    return (
        output,
        input_grad,
        own[0],
        grad_wq,
        grad_wlat,
        own_l,
        grad_wexp,
        grad_wout,
        own[1],
        shared_weights[0].T,
        shared_weights[1].T,
        shared_weights[2],
        jnp.swapaxes(grad_eg, 1, 2).astype(F32),
        jnp.swapaxes(grad_eu, 1, 2).astype(F32),
        grad_ed.astype(F32),
    )


def solution(mesh):
    return jax.shard_map(
        per_device,
        mesh=mesh,
        in_specs=(
            P("expert", "tensor"),
            P("expert", "tensor"),
            P(),
            P(None, "tensor"),
            P(),
            P(),
            P(None, "tensor"),
            P("tensor", None),
            P(),
            P(None, "tensor"),
            P(None, "tensor"),
            P("tensor", None),
            P("expert", None, "tensor"),
            P("expert", None, "tensor"),
            P("expert", "tensor", None),
            P(),
            P(),
            P("expert", None),
            P("expert", None),
        ),
        out_specs=(
            P("expert", "tensor"),
            P("expert", "tensor"),
            P("expert"),
            P("expert", "tensor"),
            P("expert", None),
            P("expert"),
            P("expert", "tensor"),
            P("tensor", "expert"),
            P("expert"),
            P("expert", "tensor"),
            P("expert", "tensor"),
            P("tensor", "expert"),
            P("expert", None, "tensor"),
            P("expert", None, "tensor"),
            P("expert", "tensor", None),
        ),
        check_vma=False,
    )
```

```python
import math

import jax
import jax.numpy as jnp
from jax import lax
from jax.experimental import pallas as pl
from jax.experimental.pallas import tpu as pltpu
from jax.sharding import PartitionSpec as P

NOPE = 128
ROPE = 64
HEAD = NOPE + ROPE
LATENT = 512
VDIM = 128
D = 2048
GROUP = 256
TOP = 6
EXPERTS = 64
GROUPS = 16
LOCAL = 4
CAP = 27
PADCAP = 32
TENSOR = 8
COLS = D // TENSOR
EPS = 1e-06

XN = 4
YN = 4
ZN = 4
CORES = 2

F32 = jnp.float32
BF16 = jnp.bfloat16
MESH = pl.DeviceIdType.MESH
ANY = pl.BlockSpec(memory_space=pl.ANY)
VM = pl.BlockSpec(memory_space=pltpu.VMEM)
DMA = pltpu.SemaphoreType.DMA
MIB = 1024 * 1024


def remote(src, dst, ssem, rsem, axis, index):
    return pltpu.make_async_remote_copy(
        src_ref=src,
        dst_ref=dst,
        send_sem=ssem,
        recv_sem=rsem,
        device_id={axis: index},
        device_id_type=MESH,
    )


def greet(peers):
    barrier = pltpu.get_barrier_semaphore()
    for axis, index in peers:
        pl.semaphore_signal(barrier, inc=1, device_id={axis: index}, device_id_type=MESH)
    pl.semaphore_wait(barrier, len(peers))


def params(cid, vmem=48):
    return pltpu.CompilerParams(
        collective_id=cid, has_side_effects=True, vmem_limit_bytes=vmem * MIB
    )


def x_peers():
    t = lax.axis_index("tensor")
    x = t // CORES
    c = lax.rem(t, CORES)
    right = lax.rem(x + 1, XN) * CORES + c
    left = lax.rem(x + XN - 1, XN) * CORES + c
    far = lax.rem(x + 2, XN) * CORES + c
    twin = x * CORES + (1 - c)
    return t, right, left, far, twin


def greet_x():
    t, right, left, far, twin = x_peers()
    greet([("tensor", right), ("tensor", left), ("tensor", twin)])


def greet_tensor():
    t = lax.axis_index("tensor")
    greet([("tensor", lax.rem(t + j, TENSOR)) for j in range(1, TENSOR)])


def cols(index, width):
    return pl.ds(pl.multiple_of(index * width, width), width)


def gather_tensor(nch, src, out_ref, ssem, rsem):
    t, right, left, far, twin = x_peers()
    flip = twin - t
    rows, width = src.shape
    rc = rows // nch
    h = rc // 2

    def block(k, owner, part=None):
        if part is None:
            return out_ref.at[pl.ds(k * rc, rc), cols(owner, width)]
        return out_ref.at[pl.ds(k * rc + part * h, h), cols(owner, width)]

    sends = []

    def send(k, j, ref, dst, target):
        c = remote(ref, dst, ssem.at[k, j], rsem.at[k, j], "tensor", target)
        c.start()
        sends.append(c)

    def arrived(k, j, ref):
        remote(ref, ref, ssem.at[k, j], rsem.at[k, j], "tensor", twin).wait_recv()

    for k in range(nch):
        part = src.at[pl.ds(k * rc, rc), :]
        send(k, 0, part, block(k, t), right)
        send(k, 1, part, block(k, t), left)
        send(k, 4, part, block(k, t), twin)
    for k in range(nch):
        arrived(k, 0, block(k, left))
        send(k, 2, block(k, left, 0), block(k, left, 0), right)
        send(k, 5, block(k, left), block(k, left), twin)
        arrived(k, 1, block(k, right))
        send(k, 3, block(k, right, 1), block(k, right, 1), left)
        send(k, 6, block(k, right), block(k, right), twin)
    for k in range(nch):
        arrived(k, 2, block(k, far, 0))
        send(k, 7, block(k, far, 0), block(k, far, 0), twin)
        arrived(k, 3, block(k, far, 1))
        send(k, 8, block(k, far, 1), block(k, far, 1), twin)
    for k in range(nch):
        arrived(k, 4, block(k, twin))
        arrived(k, 5, block(k, left + flip))
        arrived(k, 6, block(k, right + flip))
        arrived(k, 7, block(k, far + flip, 0))
        arrived(k, 8, block(k, far + flip, 1))
    for s in sends:
        s.wait_send()


def gather_sems(nch):
    return [DMA((nch, 9)), DMA((nch, 9))]


def sum_rows_start(value, buf, ssem, rsem):
    t = lax.axis_index("tensor")
    rows = value.shape[0]
    mine = jnp.broadcast_to(jnp.sum(value, axis=1, keepdims=True), (rows, 128))
    buf[t] = jnp.transpose(mine)[:8]
    sends = []
    for j in range(1, TENSOR):
        to = lax.rem(t + j, TENSOR)
        c = remote(buf.at[t], buf.at[t], ssem.at[j], rsem.at[j], "tensor", to)
        c.start()
        sends.append(c)

    def finish():
        for j in range(1, TENSOR):
            ref = buf.at[lax.rem(t + TENSOR - j, TENSOR)]
            remote(ref, ref, ssem.at[j], rsem.at[j], "tensor", t).wait_recv()
        total = jnp.sum(buf[...], axis=0)
        for s in sends:
            s.wait_send()
        return jnp.transpose(total)[:, :1]

    return finish


def sum_rows_tensor(value, buf, ssem, rsem):
    return sum_rows_start(value, buf, ssem, rsem)()


def sum_rows_scratch():
    return [pltpu.VMEM((TENSOR, 8, GROUP), F32), DMA((TENSOR,)), DMA((TENSOR,))]


def dot_nn(a, b):
    return lax.dot_general(a, b, (((1,), (0,)), ((), ())), preferred_element_type=F32)


def dot_nt(a, b):
    return lax.dot_general(a, b, (((1,), (1,)), ((), ())), preferred_element_type=F32)


def dot_tn(a, b):
    return lax.dot_general(a, b, (((0,), (0,)), ((), ())), preferred_element_type=F32)


ROWS = GROUPS * PADCAP


def expert_peers():
    e = lax.axis_index("expert")
    z = e // YN
    y = lax.rem(e, YN)
    peers = []
    for dz in range(ZN):
        for dy in range(YN):
            if dz or dy:
                to = lax.rem(z + dz, ZN) * YN + lax.rem(y + dy, YN)
                frm = lax.rem(z + ZN - dz, ZN) * YN + lax.rem(y + YN - dy, YN)
                peers.append((to, frm))
    return e, peers


def seat_rows(index):
    return pl.ds(pl.multiple_of(index * PADCAP, PADCAP), PADCAP)


def moe_kernel(
    place_ref, rown_hbm, nfull_hbm, dy_hbm, sg_hbm, su_hbm, sd_hbm, wg_hbm, wu_hbm, wd_hbm, grads_hbm,
    mid_ref, inv_ref, gain_ref, dyc_ref,
    part_hbm, gg_hbm, gu_hbm, gd_hbm, shout_ref, dmid_ref, dgain_ref, dattn_hbm, wsend_hbm, wsum_ref,
    sh_ref, dsg_ref, dsu_ref, nfull, dyf, rows, drows, sib, half, full, wbuf, gbuf, gout, pbuf, res, back, shsum, low,
    a_s, a_r, r_s, r_r, b_s, b_r, f_s, f_r, st_buf, st_s, st_r, l_in, l_w, l_g, l_out, l_own, l_sh, l_first,
    wown, w_a, w_p, w_b, w_s, w_r, l_wn,
):
    t, right, left, far, twin = x_peers()
    flip = twin - t
    e, peers = expert_peers()
    greet(
        [("tensor", lax.rem(t + j, TENSOR)) for j in range(1, TENSOR)]
        + [("expert", to) for to, frm in peers]
    )
    sends = []

    def send(src, dst, ssem, rsem, axis, to):
        c = remote(src, dst, ssem, rsem, axis, to)
        c.start()
        sends.append(c)

    def got(ref, ssem, rsem):
        remote(ref, ref, ssem, rsem, "tensor", twin).wait_recv()

    blocks = (t, far)
    own_copies = []
    for k in range(LOCAL):
        for b in range(2):
            c = pltpu.make_async_copy(
                rown_hbm.at[b, k], rows.at[k, :, cols(blocks[b], COLS)], l_first.at[k, b]
            )
            c.start()
            own_copies.append(c)
    wide = sd_hbm.shape[0]
    sgv, suv, sdv = (drows.at[i, pl.ds(0, wide)] for i in range(3))
    early = [
        pltpu.make_async_copy(src, dst, l_in.at[i])
        for i, (src, dst) in enumerate(
            [(nfull_hbm, nfull), (sg_hbm, sgv), (su_hbm, suv), (sd_hbm, sdv), (dy_hbm, dyf)]
        )
    ]
    for c in early:
        c.start()

    def load(k):
        s = k % 2
        copies = [
            pltpu.make_async_copy(ref.at[k], wbuf.at[s, i], l_w.at[s, i])
            for i, ref in enumerate((wg_hbm, wu_hbm, wd_hbm))
        ]
        for c in copies:
            c.start()
        return copies

    loads = {0: load(0)}

    grad_loads = [pltpu.make_async_copy(grads_hbm.at[k], gbuf.at[k], l_g.at[k]) for k in range(LOCAL)]
    grad_loads[0].start()

    h = ROWS // 2

    def row_block(k):
        return lambda owner: rows.at[k, :, cols(owner, COLS)]

    near = [near_stages(row_block(k), a_s.at[k], a_r.at[k], send) for k in range(LOCAL)]

    def gather_1(k):
        for b in range(2):
            own_copies[2 * k + b].wait()
            near[k][b]()

    def gather_2(k):
        near[k][2]()

    def gather_4(k):
        near[k][3]()

    back_copies = {}

    order = (far, right, left, t)

    def slot(k):
        return k

    def rsend(k, j, src, dst, to):
        send(src, dst, r_s.at[k, j], r_r.at[k, j], "tensor", to)

    def rgot(k, j, ref):
        got(ref, r_s.at[k, j], r_r.at[k, j])

    def mine(k, j):
        return drows[slot(k), :, cols(order[j], COLS)].astype(F32)

    twin_sends = {}

    def sum_1(k):
        first = len(sends)
        for j, owner in enumerate(order):
            rsend(k, j, drows.at[slot(k), :, cols(owner + flip, COLS)], sib.at[k, j], twin)
        twin_sends[k] = sends[first:]
        del sends[first:]

    def sum_2(k):
        rgot(k, 0, sib.at[k, 0])
        sib[k, 0] = (mine(k, 0) + sib[k, 0].astype(F32)).astype(BF16)
        rsend(k, 4, sib.at[k, 0, pl.ds(0, h)], half.at[k, 0], right)
        rsend(k, 5, sib.at[k, 0, pl.ds(h, h)], half.at[k, 1], left)

    def sum_3(k):
        for j, to in ((1, right), (2, left)):
            rgot(k, j, sib.at[k, j])
            rgot(k, 3 + j, half.at[k, j - 1])
            both = mine(k, j) + sib[k, j].astype(F32)
            extra = half[k, j - 1].astype(F32)
            if j == 1:
                sib[k, j, :h] = (both[:h] + extra).astype(BF16)
                sib[k, j, h:] = both[h:].astype(BF16)
            else:
                sib[k, j, :h] = both[:h].astype(BF16)
                sib[k, j, h:] = (both[h:] + extra).astype(BF16)
            rsend(k, 5 + j, sib.at[k, j], full.at[k, j - 1], to)

    def sum_4(k):
        rgot(k, 3, sib.at[k, 3])
        rgot(k, 6, full.at[k, 0])
        rgot(k, 7, full.at[k, 1])
        value = mine(k, 3) + sib[k, 3].astype(F32) + full[k, 0].astype(F32) + full[k, 1].astype(F32)
        for c in twin_sends[k]:
            c.wait_send()
        if k == LOCAL:
            shsum[...] = value
            return
        res[k] = value.astype(BF16)
        c = pltpu.make_async_copy(res.at[k, seat_rows(e)], back.at[k, seat_rows(e)], l_own.at[k])
        c.start()
        back_copies[k] = c
        for j, (to, frm) in enumerate(peers):
            send(res.at[k, seat_rows(to)], back.at[k, seat_rows(e)], b_s.at[k, j], b_r.at[k, j], "expert", to)

    def shared_forward():
        for c in early[:4]:
            c.wait()
        n = nfull[...]
        g = dot_nt(n, sgv[...])
        u = dot_nt(n, suv[...])
        sig = jax.nn.sigmoid(g)
        silu = g * sig
        sh_ref[...] = (silu * u).astype(BF16)
        return g, u, sig, silu

    def shared_backward(g, u, sig, silu):
        early[4].wait()
        dh = dot_nt(dyf[...], sdv[...])
        dsg_ref[...] = (dh * u * (sig * (1.0 + g * (1.0 - sig)))).astype(BF16)
        dsu_ref[...] = (dh * silu).astype(BF16)

    tiles = [pl.ds(i * 512, 512) for i in range(D // 512)]

    def shared_rows():
        hid = sh_ref[...]
        dsg, dsu = dsg_ref[...], dsu_ref[...]
        for n in tiles:
            drows[LOCAL, :GROUP, n] = dot_nn(hid, sdv[:, n]).astype(BF16)
            drows[LOCAL, GROUP:, n] = (dot_nn(dsg, sgv[:, n]) + dot_nn(dsu, suv[:, n])).astype(BF16)

    stages = (drows.at[1], drows.at[2], pbuf)
    staged = []

    def shared_weights():
        pairs = ((dsg_ref, nfull), (dsu_ref, nfull), (sh_ref, dyf))
        for i, (lhs, rhs) in enumerate(pairs):
            for n in tiles:
                stages[i][:wide, n] = dot_tn(lhs[...], rhs[:, n]).astype(BF16)
            c = pltpu.make_async_copy(stages[i].at[pl.ds(0, wide)], wsend_hbm.at[i], l_sh.at[i])
            c.start()
            staged.append(c)
            for p in range(2):
                for j in range(4):
                    d = j * YN + lax.rem(e, YN) if p == 0 else (e // YN) * YN + j
                    c = pltpu.make_async_copy(
                        stages[i].at[pl.ds(p * wide // 2, wide // 2), cols(d, 128)],
                        wown.at[2 * i + p, j],
                        l_wn.at[2 * i + p, j],
                    )
                    c.start()
                    staged.append(c)

    def piece_ref(i, p):
        return lambda dz, dy: wsend_hbm.at[i, pl.ds(p * wide // 2, wide // 2), cols(dz * YN + dy, 128)]

    def piece_own(i, p):
        return lambda dz, dy: wown[2 * i + p, dz if p == 0 else dy].astype(F32)

    shared_sums = [
        two_phase(
            piece_ref(n // 2, n % 2), piece_own(n // 2, n % 2),
            w_a.at[n], w_p.at[n], w_b.at[n], w_s.at[n], w_r.at[n], "yz"[n % 2], send,
        )
        for n in range(6)
    ]

    out_copies = {}

    def compute_1(k):
        s = k % 2
        for c in loads[k] + [grad_loads[k]]:
            c.wait()
        r = rows[k]
        gate = dot_nt(r, wbuf[s, 0])
        up = dot_nt(r, wbuf[s, 1])
        dh = dot_nt(gbuf[k], wbuf[s, 2])
        sig = jax.nn.sigmoid(gate)
        silu = gate * sig
        hidden = (silu * up).astype(BF16)
        dg = (dh * up * (sig * (1.0 + gate * (1.0 - sig)))).astype(BF16)
        du = (dh * silu).astype(BF16)
        for n in tiles:
            drows[slot(k), :, n] = (
                dot_nn(dg, wbuf[s, 0, :, n]) + dot_nn(du, wbuf[s, 1, :, n])
            ).astype(BF16)
        return hidden, dg, du

    def compute_2(k, hidden, dg, du):
        s = k % 2
        if k:
            for c in out_copies[k - 1]:
                c.wait()
        for n in tiles:
            pbuf[:, n] = dot_nn(hidden, wbuf[s, 2, :, n]).astype(BF16)
            gout[0, :, n] = dot_tn(dg, rows[k, :, n]).astype(BF16)
            gout[1, :, n] = dot_tn(du, rows[k, :, n]).astype(BF16)
            gout[2, :, n] = dot_tn(hidden, gbuf[k, :, n]).astype(BF16)
        out_copies[k] = [
            pltpu.make_async_copy(src, dst.at[k], l_out.at[i])
            for i, (src, dst) in enumerate(
                [(pbuf, part_hbm), (gout.at[0], gg_hbm), (gout.at[1], gu_hbm), (gout.at[2], gd_hbm)]
            )
        ]
        for c in out_copies[k]:
            c.start()
        if k + 2 < LOCAL:
            loads[k + 2] = load(k + 2)

    for k in range(LOCAL):
        gather_1(k)
    loads[1] = load(1)
    grad_loads[1].start()
    state = shared_forward()
    shared_backward(*state)
    gather_2(0)
    shared_rows()
    sum_1(4)
    gather_2(1)
    gather_4(0)
    c0 = compute_1(0)
    sum_1(0)
    grad_loads[2].start()
    grad_loads[3].start()
    gather_2(2)
    shared_weights()
    gather_4(1)
    for c in staged:
        c.wait()
    c1 = compute_1(1)
    sum_1(1)
    for piece in shared_sums:
        piece[0]()
    gather_2(3)
    sum_2(0)
    compute_2(0, *c0)
    gather_4(2)
    c2 = compute_1(2)
    sum_1(2)
    sum_3(0)
    sum_2(1)
    compute_2(1, *c1)
    gather_4(3)
    c3 = compute_1(3)
    sum_1(3)
    sum_4(0)
    sum_3(1)
    sum_2(2)
    sum_2(3)
    compute_2(2, *c2)
    sum_2(4)
    sum_4(1)
    sum_3(2)
    sum_3(3)
    compute_2(3, *c3)
    for piece in shared_sums:
        piece[1]()
    sum_3(4)
    sum_4(2)
    sum_4(3)
    sum_4(4)
    shout_ref[...] = shsum[:GROUP]

    dn = shsum[GROUP:]

    def combine(k):
        back_copies[k].wait()
        for j, (to, frm) in enumerate(peers):
            got(back.at[k, seat_rows(frm)], b_s.at[k, j], b_r.at[k, j])
        return dot_tn(place_ref[k], back[k])

    for k in range(LOCAL):
        dn = dn + combine(k)

    mid = mid_ref[...]
    inv = inv_ref[...]
    u = dn * gain_ref[:, cols(t, COLS)].astype(F32)
    total = sum_rows_tensor(u * mid, st_buf, st_s, st_r)
    dmid = dyc_ref[...].astype(F32) + inv * u - mid * (inv * inv * inv * total * (1.0 / D))
    dmid_ref[...] = dmid
    low[...] = dmid.astype(BF16)
    own = pltpu.make_async_copy(low, dattn_hbm.at[:, cols(t, COLS)], l_own.at[0])
    own.start()
    dgain_ref[...] = jnp.sum(dn * mid * inv, axis=0, keepdims=True)
    gather_tensor(1, low, dattn_hbm, f_s, f_r)
    own.wait()
    for c in out_copies[LOCAL - 1]:
        c.wait()
    for n in range(6):
        wsum_ref[n // 2, pl.ds((n % 2) * wide // 2, wide // 2)] = shared_sums[n][2]()
    for c in sends:
        c.wait_send()


def moe_step(place, rown, nfull, dy, sg, su, sd, wg, wu, wd, grads, mid, inv, gain, dyc, cid):
    hid = wd.shape[1]
    wide = sd.shape[0]
    wshape = jax.ShapeDtypeStruct((LOCAL, hid, D), BF16)
    vmem = pltpu.VMEM
    return pl.pallas_call(
        moe_kernel,
        out_shape=(
            jax.ShapeDtypeStruct((LOCAL, ROWS, D), BF16),
            wshape,
            wshape,
            wshape,
            jax.ShapeDtypeStruct((GROUP, COLS), F32),
            jax.ShapeDtypeStruct((GROUP, COLS), F32),
            jax.ShapeDtypeStruct((1, COLS), F32),
            jax.ShapeDtypeStruct((GROUP, D), BF16),
            jax.ShapeDtypeStruct((3, wide, D), BF16),
            jax.ShapeDtypeStruct((3, wide, D // GROUPS), F32),
        ),
        in_specs=[VM] + [ANY] * 10 + [VM] * 4,
        out_specs=(ANY, ANY, ANY, ANY, VM, VM, VM, ANY, ANY, VM),
        scratch_shapes=[
            vmem((GROUP, wide), BF16),
            vmem((GROUP, wide), BF16),
            vmem((GROUP, wide), BF16),
            vmem((GROUP, D), BF16),
            vmem((GROUP, D), BF16),
            vmem((LOCAL, ROWS, D), BF16),
            vmem((LOCAL + 1, ROWS, D), BF16),
            vmem((LOCAL + 1, 4, ROWS, COLS), BF16),
            vmem((LOCAL + 1, 2, ROWS // 2, COLS), BF16),
            vmem((LOCAL + 1, 2, ROWS, COLS), BF16),
            vmem((2, 3, hid, D), BF16),
            vmem((LOCAL, ROWS, D), BF16),
            vmem((3, hid, D), BF16),
            vmem((ROWS, D), BF16),
            vmem((LOCAL, ROWS, COLS), BF16),
            vmem((LOCAL, ROWS, COLS), BF16),
            vmem((2 * GROUP, COLS), F32),
            vmem((GROUP, COLS), BF16),
            DMA((LOCAL, 6)),
            DMA((LOCAL, 6)),
            DMA((LOCAL + 1, 8)),
            DMA((LOCAL + 1, 8)),
            DMA((LOCAL, 15)),
            DMA((LOCAL, 15)),
            DMA((1, 9)),
            DMA((1, 9)),
            vmem((TENSOR, 8, GROUP), F32),
            DMA((TENSOR,)),
            DMA((TENSOR,)),
            DMA((5,)),
            DMA((2, 3)),
            DMA((LOCAL,)),
            DMA((4,)),
            DMA((LOCAL,)),
            DMA((3,)),
            DMA((LOCAL, 2)),
            vmem((6, 4, wide // 2, D // GROUPS), BF16),
        ]
        + two_phase_scratch(6, wide // 2, D // GROUPS)
        + [DMA((6, 4))],
        compiler_params=params(cid, 63),
        cost_estimate=pl.CostEstimate(
            flops=40 * 10**9, bytes_accessed=100 * MIB, transcendentals=0
        ),
        name="moe_step",
    )(place, rown, nfull, dy, sg, su, sd, wg, wu, wd, grads, mid, inv, gain, dyc)


def swap_halves(value):
    return pltpu.roll(value, 64, 1)


def turn(value, cosine, sine):
    return value * cosine + swap_halves(value) * sine


def lane_head(shape):
    lane = lax.broadcasted_iota(jnp.int32, shape, 1)
    return (lane >> 5) & 1


def regroup(dtype):
    n = 2 * HEAD
    given = lax.broadcasted_iota(jnp.int32, (n, n), 0)
    made = lax.broadcasted_iota(jnp.int32, (n, n), 1)
    r = made - 2 * NOPE
    turned = ((r >> 5) & 1) * HEAD + NOPE + (r >> 6) * (ROPE // 2) + (r & 31)
    source = jnp.where(made < NOPE, made, jnp.where(made < 2 * NOPE, made + ROPE, turned))
    return jnp.where(given == source, 1.0, 0.0).astype(dtype)


def band(index, rows):
    return pl.ds(pl.multiple_of(index * rows, rows), rows)


def hop_start(src, dst, rows, ss, rs, send):
    e, peers = expert_peers()
    dst[band(e, rows)] = src[band(e, rows)]
    for j, (to, frm) in enumerate(peers):
        send(src.at[band(to, rows)], dst.at[band(e, rows)], ss.at[j], rs.at[j], "expert", to)


def hop_wait(dst, rows, ss, rs):
    e, peers = expert_peers()
    for j, (to, frm) in enumerate(peers):
        ref = dst.at[band(frm, rows)]
        remote(ref, ref, ss.at[j], rs.at[j], "expert", to).wait_recv()


def one_hot(test):
    return jnp.where(test, 1.0, 0.0).astype(BF16)


def by_sixteen():
    made, given = iota((GROUP, GROUP), 0), iota((GROUP, GROUP), 1)
    return one_hot(given == (made & 15) * GROUPS + (made >> 4))


def seat_of_row(index):
    return one_hot(iota((GROUP, ROWS), 1).astype(F32) == index)


def row_of_seat(index):
    return one_hot(iota((ROWS, GROUP), 0).astype(F32) == index)


def near_stages(block, ss, rs, send):
    t, right, left, far, twin = x_peers()
    flip = twin - t

    def put(j, owner, to):
        send(block(owner), block(owner), ss.at[j], rs.at[j], "tensor", to)

    def arrived(j, owner):
        ref = block(owner)
        remote(ref, ref, ss.at[j], rs.at[j], "tensor", twin).wait_recv()

    def stage_1():
        put(0, t, right)
        put(1, t, left)
        put(2, t, twin)

    def stage_far():
        put(3, far, twin)

    def stage_2():
        arrived(0, left)
        put(4, left, twin)
        arrived(1, right)
        put(5, right, twin)

    def stage_3():
        arrived(2, twin)
        arrived(3, far + flip)
        arrived(4, left + flip)
        arrived(5, right + flip)

    return stage_1, stage_far, stage_2, stage_3


def sum_stages(theirs, mine, rows, sib, half, full, ss, rs, send):
    t, right, left, far, twin = x_peers()
    flip = twin - t
    order = (far, right, left, t)
    h = rows // 2

    def put(j, src, dst, to):
        send(src, dst, ss.at[j], rs.at[j], "tensor", to)

    def arrived(j, ref):
        remote(ref, ref, ss.at[j], rs.at[j], "tensor", twin).wait_recv()

    def stage_1():
        for j, owner in enumerate(order):
            put(j, theirs(owner + flip), sib.at[j], twin)

    def stage_2():
        arrived(0, sib.at[0])
        sib[0] = (mine(0) + sib[0].astype(F32)).astype(sib.dtype)
        put(4, sib.at[0, pl.ds(0, h)], half.at[0], right)
        put(5, sib.at[0, pl.ds(h, h)], half.at[1], left)

    def stage_3():
        for j, to in ((1, right), (2, left)):
            arrived(j, sib.at[j])
            arrived(3 + j, half.at[j - 1])
            both = mine(j) + sib[j].astype(F32)
            extra = half[j - 1].astype(F32)
            if j == 1:
                sib[j, :h] = (both[:h] + extra).astype(sib.dtype)
                sib[j, h:] = both[h:].astype(sib.dtype)
            else:
                sib[j, :h] = both[:h].astype(sib.dtype)
                sib[j, h:] = (both[h:] + extra).astype(sib.dtype)
            put(5 + j, sib.at[j], full.at[j - 1], to)

    def stage_4():
        arrived(3, sib.at[3])
        arrived(6, full.at[0])
        arrived(7, full.at[1])
        return mine(3) + sib[3].astype(F32) + full[0].astype(F32) + full[1].astype(F32)

    return stage_1, stage_2, stage_3, stage_4


def two_phase(src, own, land_a, part, land_b, ss, rs, first, send):
    e = lax.axis_index("expert")
    z, y = e // YN, lax.rem(e, YN)
    one, two = (y, z) if first == "y" else (z, y)

    def at(i, j):
        return (j, i) if first == "y" else (i, j)

    def device(i, j):
        dz, dy = at(i, j)
        return dz * YN + dy

    def plus(v, d):
        return lax.rem(v + d, 4)

    def arrived(j, ref):
        remote(ref, ref, ss.at[j], rs.at[j], "expert", e).wait_recv()

    def stage_1():
        for d in (1, 3, 2):
            i = plus(one, d)
            for j in range(4):
                n = 4 * (d - 1) + j
                send(src(*at(i, j)), land_a.at[d - 1, j], ss.at[n], rs.at[n], "expert", device(i, two))

    def stage_2():
        for d in range(3):
            for j in range(4):
                arrived(4 * d + j, land_a.at[d, j])
        for j in range(4):
            total = own(*at(one, j))
            for d in range(3):
                total = total + land_a[d, j].astype(F32)
            part[j] = total.astype(BF16)
        for d in (1, 3, 2):
            j = plus(two, d)
            send(part.at[j], land_b.at[d - 1], ss.at[11 + d], rs.at[11 + d], "expert", device(one, j))

    def stage_3():
        total = part[two].astype(F32)
        for d in range(3):
            arrived(12 + d, land_b.at[d])
            total = total + land_b[d].astype(F32)
        return total

    return stage_1, stage_2, stage_3


def two_phase_scratch(pieces, rows, width):
    return [
        pltpu.VMEM((pieces, 3, 4, rows, width), BF16),
        pltpu.VMEM((pieces, 4, rows, width), BF16),
        pltpu.VMEM((pieces, 3, rows, width), BF16),
        DMA((pieces, 15)),
        DMA((pieces, 15)),
    ]


SLICE = 80
WIDE_LAT = LATENT + 2 * ROPE


def back_kernel(
    dattn_ref, mixed_ref, wout_ref, q_ref, exp_ref, kr_ref, probs_ref, cos_ref, sin_ref, lat_ref, linv_ref,
    lgain_ref, x_ref, inv_ref, gain_ref, dmid_ref, ffn_ref, mid_ref, shout_ref, gate_ref, seat_ref, seat_row_ref,
    place_hbm, normed_hbm, wq_hbm, wexp_hbm, comp_hbm, wl_hbm, part_hbm,
    out_ref, dx_ref, gwq_ref, gwexp_ref, gwout_ref, gwlat_ref, gains_ref,
    normed, wq, wexp, comp, wl, place,
    own, sib, half, full, res, fback,
    npart, nsib, nhalf, nfull,
    swq, swexp, swout, swlat, rwlat, lowlat, *rest
):
    q_red, e_red, o_red, rest = rest[:5], rest[5:10], rest[10:15], rest[15:]
    (
        cbuf, cgot, dlat, gm, gin, xh, oh, xl, ol,
        st_buf, st_s, st_r,
        p_s, p_r, fb_s, fb_r, n_s, n_r, w_s, w_r, c_s, c_r, dl_s, dl_r, gm_s, gm_r, gt_s, gt_r, wl_s, wl_r,
        oa_s, oa_r, ob_s, ob_r, xa_s, xa_r, xb_s, xb_r, l_in, l_own,
    ) = rest
    t, right, left, far, twin = x_peers()
    e, peers = expert_peers()
    others = [(lax.rem(t + j, TENSOR), lax.rem(t + TENSOR - j, TENSOR)) for j in range(1, TENSOR)]
    greet([("tensor", to) for to, frm in others] + [("expert", to) for to, frm in peers])
    sends = []

    def send(src, dst, ssem, rsem, axis, to):
        c = remote(src, dst, ssem, rsem, axis, to)
        c.start()
        sends.append(c)

    def got(ref, ssem, rsem):
        remote(ref, ref, ssem, rsem, "tensor", twin).wait_recv()

    half_rope = ROPE // 2
    for i in (1, 3):
        wl[LATENT + i * half_rope : LATENT + (i + 1) * half_rope] = jnp.zeros((half_rope, COLS), BF16)
    wide = [
        (wq_hbm, wq),
        (wexp_hbm, wexp),
        (normed_hbm, normed),
        (comp_hbm, comp),
        (place_hbm, place),
        (wl_hbm.at[pl.ds(0, LATENT), cols(t, COLS)], wl.at[pl.ds(0, LATENT)]),
        (
            wl_hbm.at[pl.ds(LATENT, half_rope), cols(t, COLS)],
            wl.at[pl.ds(LATENT, half_rope)],
        ),
        (
            wl_hbm.at[pl.ds(LATENT + half_rope, half_rope), cols(t, COLS)],
            wl.at[pl.ds(LATENT + 2 * half_rope, half_rope)],
        ),
    ]
    early = [pltpu.make_async_copy(src, dst, l_in.at[i]) for i, (src, dst) in enumerate(wide)]
    for c in early:
        c.start()

    order = (far, right, left, t)
    chunks = []
    for k in range(LOCAL):

        def theirs(owner, k=k):
            return part_hbm.at[k, :, cols(owner, COLS)]

        def mine(j, k=k):
            return own[k, j].astype(F32)

        chunks.append(
            sum_stages(
                theirs, mine, ROWS, sib.at[k], half.at[k], full.at[k], p_s.at[k], p_r.at[k], send
            )
        )
    own_loads = {}
    for k in range(LOCAL):
        for j, owner in enumerate(order):
            c = pltpu.make_async_copy(part_hbm.at[k, :, cols(owner, COLS)], own.at[k, j], l_own.at[k, j])
            c.start()
            own_loads[k, j] = c
        chunks[k][0]()

    def forward_2(k):
        for j in range(4):
            own_loads[k, j].wait()
        chunks[k][1]()

    def forward_4(k):
        res[k] = chunks[k][3]().astype(BF16)
        fback[k, seat_rows(e)] = res[k, seat_rows(e)]
        for j, (to, frm) in enumerate(peers):
            send(
                res.at[k, seat_rows(to)], fback.at[k, seat_rows(e)], fb_s.at[k, j], fb_r.at[k, j], "expert", to
            )

    def reduce_pieces(scratch, ref_of, value_of):
        land_a, part, land_b, ss, rs = scratch
        return [
            two_phase(
                lambda dz, dy, i=i: ref_of(i, dz * YN + dy),
                lambda dz, dy, i=i: value_of(i, dz * YN + dy).astype(F32),
                land_a.at[i], part.at[i], land_b.at[i], ss.at[i], rs.at[i], "yz"[i], send,
            )
            for i in range(2)
        ]

    def run(pieces, stage):
        return [piece[stage]() for piece in pieces]

    def rows_of(i, n):
        return pl.ds(i * n, n)

    query_sum = reduce_pieces(
        q_red,
        lambda i, d: swq.at[rows_of(i, HEAD), cols(d, 128)],
        lambda i, d: swq[rows_of(i, HEAD), cols(d, 128)],
    )
    expand_sum = reduce_pieces(
        e_red, lambda i, d: swexp.at[d, :, rows_of(i, 256)], lambda i, d: swexp[d, :, rows_of(i, 256)]
    )
    out_sum = reduce_pieces(
        o_red,
        lambda i, d: swout.at[rows_of(i, VDIM), cols(d, 128)],
        lambda i, d: swout[rows_of(i, VDIM), cols(d, 128)],
    )

    mixed = mixed_ref[...]
    for n in range(4):
        s = slice(n * 512, (n + 1) * 512)
        swout[:, s] = dot_tn(mixed, dattn_ref[:, s]).astype(BF16)
    run(out_sum, 0)

    scale = HEAD ** (-0.5)
    cosine, sine = cos_ref[...], sin_ref[...]
    head = lane_head((GROUP, 2 * ROPE))
    dattn = dattn_ref[...]
    dmix = dot_nt(dattn, wout_ref[...]).astype(BF16)
    kr = kr_ref[...]
    qr = q_ref[:, 2 * NOPE :]
    turned = jnp.zeros((GROUP, 2 * ROPE), F32)
    rope_sum = jnp.zeros((GROUP, 2 * ROPE), F32)
    dq_parts = []
    dexp_parts = []
    for h in range(2):
        p = probs_ref[h]
        dm = dmix[:, h * VDIM : (h + 1) * VDIM]
        k = exp_ref[:, 256 * h : 256 * h + NOPE]
        v = exp_ref[:, 256 * h + NOPE : 256 * h + NOPE + VDIM]
        dv = dot_tn(p.astype(BF16), dm)
        dp = dot_nt(dm, v)
        ds = (p * (dp - jnp.sum(dp * p, axis=1, keepdims=True))).astype(BF16)
        dq_parts.append((dot_nn(ds, k) * scale).astype(BF16))
        turned = turned + jnp.where(head == h, dot_nn(ds, kr) * scale, 0.0)
        dk = dot_tn(ds, q_ref[:, h * NOPE : (h + 1) * NOPE]) * scale
        rope_sum = rope_sum + jnp.where(head == h, dot_tn(ds, qr) * scale, 0.0)
        dexp_parts += [dk.astype(BF16), dv.astype(BF16)]
    dexp = jnp.concatenate(dexp_parts, axis=1)
    dq_parts.append(turn(turned, cosine, -sine).astype(BF16))
    dq = dot_nt(jnp.concatenate(dq_parts, axis=1), regroup(BF16)).astype(BF16)

    early[1].wait()
    cpart = dot_nt(dexp, wexp[...])
    share = GROUP // TENSOR
    for i in range(TENSOR):
        r = slice(i * share, (i + 1) * share)
        cbuf[i, :, :LATENT] = cpart[r].astype(BF16)
        cbuf[i, :, LATENT:] = rope_sum[r].astype(BF16)
    for j, (to, frm) in enumerate(others):
        send(cbuf.at[to], cgot.at[t], c_s.at[j], c_r.at[j], "tensor", to)

    early[0].wait()
    for n in range(TENSOR):
        npart[n] = dot_nt(dq, wq[n * COLS : (n + 1) * COLS, :]).astype(BF16)
    n1, n2, n3, n4 = sum_stages(
        lambda owner: npart.at[owner],
        lambda j: npart[order[j]].astype(F32),
        GROUP, nsib, nhalf, nfull, n_s, n_r, send,
    )
    n1()
    forward_2(0)
    forward_2(1)

    early[2].wait()
    for n in range(4):
        s = slice(n * 512, (n + 1) * 512)
        swq[:, s] = dot_tn(dq, normed[:, s]).astype(BF16)
    early[3].wait()
    gwexp = dot_tn(comp[...], dexp)
    for i in range(GROUPS):
        swexp[i] = gwexp[32 * i : 32 * (i + 1)].astype(BF16)
    run(expand_sum, 0)
    run(query_sum, 0)

    total = cbuf[t].astype(F32)
    for j, (to, frm) in enumerate(others):
        got(cgot.at[frm], c_s.at[j], c_r.at[j])
        total = total + cgot[frm].astype(F32)
    mine_rows = pl.ds(pl.multiple_of(t * share, share), share)
    dc = total[:, :LATENT]
    lat = lat_ref[mine_rows, :]
    linv = linv_ref[mine_rows, :]
    lu = dc * lgain_ref[...].astype(F32)
    dot = jnp.sum(lu * lat, axis=1, keepdims=True)
    dlat[t, :, :LATENT] = (linv * lu - lat * (linv * linv * linv * dot * (1.0 / LATENT))).astype(BF16)
    both = total[:, LATENT:]
    both = both + pltpu.roll(both, 2 * ROPE - ROPE // 2, 1)
    both = jnp.where(lane_head((share, 2 * ROPE)) == 0, both, 0.0)
    dlat[t, :, LATENT:] = turn(both, cos_ref[mine_rows, :], -sin_ref[mine_rows, :]).astype(BF16)
    for j, (to, frm) in enumerate(others):
        send(dlat.at[t], dlat.at[t], dl_s.at[j], dl_r.at[j], "tensor", to)
    lgain_row = jnp.sum(dc * lat * linv, axis=0, keepdims=True)

    n2()
    forward_2(2)
    forward_2(3)
    n3()
    chunks[0][2]()

    def undeal_1(value, high, ss, rs):
        high[0] = dot_tn(seat_of_row(seat_ref[...]), value).astype(BF16)
        hop_start(high.at[0], high.at[1], PADCAP, ss, rs, send)

    def undeal_2(high, low, ss, rs, ss_next, rs_next):
        hop_wait(high.at[1], PADCAP, ss, rs)
        low[0] = dot_tn(row_of_seat(seat_row_ref[...]), high[1]).astype(BF16)
        hop_start(low.at[0], low.at[1], GROUPS, ss_next, rs_next, send)

    def undeal_3(low, ss, rs):
        hop_wait(low.at[1], GROUPS, ss, rs)
        return dot_tn(by_sixteen(), low[1]).astype(BF16)

    for j, (to, frm) in enumerate(others):
        got(dlat.at[frm], dl_s.at[j], dl_r.at[j])
    for i in (5, 6, 7):
        early[i].wait()
    dl = dlat[...].reshape(GROUP, WIDE_LAT)
    latent_cols = dot_nn(dl, wl[...])
    dn = latent_cols + n4()
    xd = x_ref[...].astype(F32)
    inv = inv_ref[...]
    u = dn * gain_ref[:, cols(t, COLS)].astype(F32)
    finish = sum_rows_start(u * xd, st_buf, st_s, st_r)
    run(out_sum, 1)
    run(expand_sum, 1)
    run(query_sum, 1)
    total = finish()
    chunks[1][2]()
    dx = (dmid_ref[...] + inv * u - xd * (inv * inv * inv * total * (1.0 / D))).astype(BF16)
    undeal_1(dx, xh, xa_s, xa_r)
    chunks[2][2]()
    forward_4(0)
    chunks[3][2]()
    gm[...] = jnp.zeros(gm.shape, F32)
    gm[0:1] = jnp.sum(dn * xd * inv, axis=0, keepdims=True)
    gm[1:2] = ffn_ref[...]
    gm[2:3] = lgain_row[:, :COLS]
    gm[3:4] = lgain_row[:, COLS:]
    for j, (to, frm) in enumerate(peers):
        send(gm, gin.at[e], gm_s.at[j], gm_r.at[j], "expert", to)

    pick_rows = lax.broadcasted_iota(jnp.int32, (WIDE_LAT, 128), 0)
    pick_cols = lax.broadcasted_iota(jnp.int32, (WIDE_LAT, 128), 1)
    pick_own = jnp.where((pick_rows == pick_cols + t * SLICE) & (pick_cols < SLICE), 1.0, 0.0).astype(BF16)
    dl_own = dot_nn(dl, pick_own).astype(BF16)
    for n in range(4):
        s = slice(n * 512, (n + 1) * 512)
        swlat[:, s] = dot_tn(dl_own, normed[:, s])[:SLICE].astype(BF16)
    for j, (to, frm) in enumerate(peers):
        send(swlat.at[:, cols(to, 128)], rwlat.at[e], w_s.at[j], w_r.at[j], "expert", to)

    forward_4(1)
    undeal_2(xh, xl, xa_s, xa_r, xb_s, xb_r)
    forward_4(2)
    forward_4(3)
    early[4].wait()
    routed = mid_ref[...] + shout_ref[...]
    for k in range(LOCAL):
        for j, (to, frm) in enumerate(peers):
            got(fback.at[k, seat_rows(frm)], fb_s.at[k, j], fb_r.at[k, j])
        gates = jnp.broadcast_to(gate_ref[k][:, None, :], (GROUPS, PADCAP, GROUP)).reshape(ROWS, GROUP)
        weight = place[k].astype(F32) * gates
        high = weight.astype(BF16)
        low = (weight - high.astype(F32)).astype(BF16)
        routed = routed + dot_tn(high, fback[k]) + dot_tn(low, fback[k])
    out = routed.astype(BF16)
    undeal_1(out, oh, oa_s, oa_r)
    dx_ref[...] = undeal_3(xl, xb_s, xb_r)

    gsum = gm[...]
    for j, (to, frm) in enumerate(peers):
        got(gin.at[frm], gm_s.at[j], gm_r.at[j])
        gsum = gsum + gin[frm]
    gains_ref[t] = gsum
    for j, (to, frm) in enumerate(others):
        send(gains_ref.at[t], gains_ref.at[t], gt_s.at[j], gt_r.at[j], "tensor", to)
    lat_sum = swlat[:, cols(e, 128)].astype(F32)
    for j, (to, frm) in enumerate(peers):
        got(rwlat.at[frm], w_s.at[j], w_r.at[j])
        lat_sum = lat_sum + rwlat[frm].astype(F32)
    lowlat[...] = lat_sum.astype(BF16)
    gwlat_ref[t] = lowlat[...]
    for j, (to, frm) in enumerate(others):
        send(lowlat, gwlat_ref.at[t], wl_s.at[j], wl_r.at[j], "tensor", to)
    undeal_2(oh, ol, oa_s, oa_r, ob_s, ob_r)
    gwout_ref[...] = jnp.concatenate(run(out_sum, 2), axis=0)
    gwq_ref[...] = jnp.transpose(jnp.concatenate(run(query_sum, 2), axis=0))
    gwexp_ref[...] = jnp.concatenate(run(expand_sum, 2), axis=1)
    out_ref[...] = undeal_3(ol, ob_s, ob_r)
    for j, (to, frm) in enumerate(others):
        got(gains_ref.at[frm], gt_s.at[j], gt_r.at[j])
        got(gwlat_ref.at[frm], wl_s.at[j], wl_r.at[j])
    for c in sends:
        c.wait_send()


def back_step(small, large, cid):
    vmem = pltpu.VMEM

    def out(*shape, dtype=BF16):
        return jax.ShapeDtypeStruct(shape, dtype)

    pair = lambda n: [DMA((n,)), DMA((n,))]
    grid_pair = lambda m, n: [DMA((m, n)), DMA((m, n))]
    return pl.pallas_call(
        back_kernel,
        out_shape=(
            out(GROUP, COLS),
            out(GROUP, COLS),
            out(D // GROUPS, 2 * HEAD, dtype=F32),
            out(LATENT // GROUPS, 512, dtype=F32),
            out(2 * VDIM, D // GROUPS, dtype=F32),
            out(TENSOR, SLICE, D // GROUPS),
            out(TENSOR, 8, COLS, dtype=F32),
        ),
        in_specs=[VM] * len(small) + [ANY] * len(large),
        out_specs=(VM,) * 7,
        scratch_shapes=[
            vmem((GROUP, D), BF16),
            vmem((D, 2 * HEAD), BF16),
            vmem((LATENT, 512), BF16),
            vmem((GROUP, LATENT), BF16),
            vmem((WIDE_LAT, COLS), BF16),
            vmem((LOCAL, ROWS, GROUP), BF16),
            vmem((LOCAL, 4, ROWS, COLS), BF16),
            vmem((LOCAL, 4, ROWS, COLS), BF16),
            vmem((LOCAL, 2, ROWS // 2, COLS), BF16),
            vmem((LOCAL, 2, ROWS, COLS), BF16),
            vmem((LOCAL, ROWS, COLS), BF16),
            vmem((LOCAL, ROWS, COLS), BF16),
            vmem((TENSOR, GROUP, COLS), BF16),
            vmem((4, GROUP, COLS), BF16),
            vmem((2, GROUP // 2, COLS), BF16),
            vmem((2, GROUP, COLS), BF16),
            vmem((2 * HEAD, D), BF16),
            vmem((GROUPS, LATENT // GROUPS, 512), BF16),
            vmem((2 * VDIM, D), BF16),
            vmem((SLICE, D), BF16),
            vmem((GROUPS, SLICE, D // GROUPS), BF16),
            vmem((SLICE, D // GROUPS), BF16),
        ]
        + two_phase_scratch(2, HEAD, D // GROUPS)
        + two_phase_scratch(2, LATENT // GROUPS, 256)
        + two_phase_scratch(2, VDIM, D // GROUPS)
        + [
            vmem((TENSOR, GROUP // TENSOR, WIDE_LAT), BF16),
            vmem((TENSOR, GROUP // TENSOR, WIDE_LAT), BF16),
            vmem((TENSOR, GROUP // TENSOR, WIDE_LAT), BF16),
            vmem((8, COLS), F32),
            vmem((GROUPS, 8, COLS), F32),
            vmem((2, ROWS, COLS), BF16),
            vmem((2, ROWS, COLS), BF16),
            vmem((2, GROUP, COLS), BF16),
            vmem((2, GROUP, COLS), BF16),
        ]
        + sum_rows_scratch()
        + grid_pair(LOCAL, 8)
        + grid_pair(LOCAL, 15)
        + pair(8)
        + pair(15)
        + pair(7)
        + pair(7)
        + pair(15)
        + pair(7)
        + pair(7)
        + pair(15)
        + pair(15)
        + pair(15)
        + pair(15)
        + [DMA((8,)), DMA((LOCAL, 4))],
        compiler_params=params(cid, 63),
        name="back_step",
    )(*small, *large)


def gather_stages(source, block, ss, rs, send):
    t, right, left, far, twin = x_peers()
    flip = twin - t

    def put(j, ref, to, src=None):
        send(ref if src is None else src, ref, ss.at[j], rs.at[j], "tensor", to)

    def arrived(j, ref):
        remote(ref, ref, ss.at[j], rs.at[j], "tensor", twin).wait_recv()

    def stage_1():
        put(0, block(t, None), right, source)
        put(1, block(t, None), left, source)
        put(4, block(t, None), twin, source)

    def stage_2():
        arrived(0, block(left, None))
        put(2, block(left, 0), right)
        put(5, block(left, None), twin)
        arrived(1, block(right, None))
        put(3, block(right, 1), left)
        put(6, block(right, None), twin)

    def stage_3():
        arrived(2, block(far, 0))
        put(7, block(far, 0), twin)
        arrived(3, block(far, 1))
        put(8, block(far, 1), twin)

    def stage_4():
        arrived(4, block(twin, None))
        arrived(5, block(left + flip, None))
        arrived(6, block(right + flip, None))
        arrived(7, block(far + flip, 0))
        arrived(8, block(far + flip, 1))

    return stage_1, stage_2, stage_3, stage_4


def column_blocks(ref, rows):
    def block(owner, part):
        r = pl.ds(0, rows) if part is None else pl.ds(part * (rows // 2), rows // 2)
        return ref.at[r, cols(owner, COLS)]

    return block


def iota(shape, dim):
    return lax.broadcasted_iota(jnp.int32, shape, dim)


def deal_in_kernel(lengths, order, group):
    n = lengths.shape[1]
    i, j = iota((n, n), 0), iota((n, n), 1)
    same, before = i == j, j < i

    def column(row):
        return jnp.sum(jnp.where(same, row, 0.0), axis=1, keepdims=True)

    def row(col):
        return jnp.sum(jnp.where(same, col, 0.0), axis=0, keepdims=True)

    def exclusive(values):
        return jnp.sum(jnp.where(before, values, 0.0), axis=1, keepdims=True)

    hit = column(order) == j.astype(F32)
    begins_col = exclusive(lengths)
    begins = row(begins_col)
    dealt_lengths = row(jnp.sum(jnp.where(hit, lengths, 0.0), axis=1, keepdims=True))
    dealt_col = exclusive(dealt_lengths)
    dealt = row(dealt_col)
    dealt_source_col = jnp.sum(jnp.where(hit, begins, 0.0), axis=1, keepdims=True)
    dealt_source = row(dealt_source_col)
    given = jnp.sum(jnp.where(hit, dealt_col, 0.0), axis=0, keepdims=True)
    given_col = column(given)

    def find(rows, lanes, starts, values):
        dim = 1 if lanes else 0
        shape = (GROUP, n) if lanes else (n, GROUP)
        place = jnp.sum(jnp.where(rows >= starts, 1.0, 0.0), axis=dim, keepdims=True) - 1.0
        on = iota(shape, dim).astype(F32) == place
        return place, jnp.sum(jnp.where(on, values, 0.0), axis=dim, keepdims=True)

    first = group * GROUP
    rows = (iota((GROUP, 1), 0) + first).astype(F32)
    rows_row = (iota((1, GROUP), 1) + first).astype(F32)
    which, start = find(rows, True, dealt, dealt)
    unused, shift = find(rows, True, dealt, dealt_source - dealt)
    which_row, shift_row = find(rows_row, False, dealt_col, dealt_source_col - dealt_col)
    source, source_row = rows + shift, rows_row + shift_row

    def rest(value):
        return value - GROUPS * jnp.floor(value * (1.0 / GROUPS))

    ahead = (rest(source) == rest(source_row)) & (source_row < source)
    rank = jnp.sum(jnp.where(ahead, 1.0, 0.0), axis=1, keepdims=True)
    seat = rest(source) * PADCAP + rank

    mine = (iota((GROUP, 1), 0) * GROUPS + group).astype(F32)
    mine_row = (iota((1, GROUP), 1) * GROUPS + group).astype(F32)
    unused, move = find(mine, True, begins, given - begins)
    unused, move_row = find(mine_row, False, begins_col, given_col - begins_col)
    to = jnp.floor((mine + move) * (1.0 / GROUP))
    to_row = jnp.floor((mine_row + move_row) * (1.0 / GROUP))
    ahead = (to == to_row) & (iota((GROUP, GROUP), 0) < iota((GROUP, GROUP), 1))
    rank = jnp.sum(jnp.where(ahead, 1.0, 0.0), axis=0, keepdims=True)
    seat_row = to_row * PADCAP + rank
    return rows - start, which, which_row, seat, seat_row


def front_kernel(
    tok_ref, cot_ref, len_ref, ord_ref, routes_ref, gates_ref, gain_ref, lgain_ref, fgain_ref,
    wq_hbm, wl_hbm, wexp_hbm, wout_hbm,
    xc_ref, dyc_ref, mid_ref, inv2_ref, ncols_ref, normed_ref, inv_ref, q_ref, exp_ref, kr_ref, comp_ref,
    lat_ref, linv_ref, probs_ref, mixed_ref, place_ref, gate_ref, seat_ref, seat_row_ref, cos_ref, sin_ref, dyfull, nfull,
    rown_hbm, grads_hbm,
    hop_a, hop_b, hop_c, hop_d, xfull, wq, wl, wexp, wout, wrope, apart, sib, half, full, gout, dbuf,
    st_buf, st_s, st_r,
    ha_s, ha_r, hb_s, hb_r, xg_s, xg_r, yg_s, yg_r, ng_s, ng_r, gg_s, gg_r, r_s, r_r, d_s, d_r, e_s, e_r, l_in, l_own, l_last,
):
    t, right, left, far, twin = x_peers()
    e, peers = expert_peers()
    greet(
        [("tensor", lax.rem(t + j, TENSOR)) for j in range(1, TENSOR)]
        + [("expert", to) for to, frm in peers]
    )
    sends = []

    def send(src, dst, ssem, rsem, axis, to):
        c = remote(src, dst, ssem, rsem, axis, to)
        c.start()
        sends.append(c)

    def got(ref, ssem, rsem):
        remote(ref, ref, ssem, rsem, "tensor", twin).wait_recv()

    def local(src, dst, sem):
        c = pltpu.make_async_copy(src, dst, sem)
        c.start()
        return c

    sixteen = by_sixteen()
    hop_a[:, :COLS] = dot_nn(sixteen, tok_ref[...]).astype(BF16)
    hop_a[:, COLS:] = dot_nn(sixteen, cot_ref[...]).astype(BF16)
    hop_start(hop_a, hop_b, GROUPS, ha_s, ha_r, send)
    early = [
        local(src, dst, l_in.at[i])
        for i, (src, dst) in enumerate([(wl_hbm, wl), (wq_hbm, wq), (wexp_hbm, wexp), (wout_hbm, wout)])
    ]

    offset, which, which_row, seat, seat_row = deal_in_kernel(
        len_ref[...].astype(F32), ord_ref[...].astype(F32), e
    )
    seat_ref[...] = seat
    seat_row_ref[...] = seat_row

    outward = row_of_seat(seat_row)
    hop_wait(hop_b, GROUPS, ha_s, ha_r)
    hop_c[...] = dot_nn(outward, hop_b[...]).astype(BF16)
    hop_start(hop_c, hop_d, PADCAP, hb_s, hb_r, send)
    hr = ROPE // 2
    lane = iota((GROUP, 2 * ROPE), 1)
    power = (lane & (hr - 1)).astype(F32) * (1.0 / hr)
    angle = offset * jnp.exp(power * (-math.log(10000.0)))
    cosine = jnp.cos(angle)
    sine = jnp.sin(angle)
    sine = jnp.where(lane < ROPE, -sine, sine)
    cos_ref[...] = cosine
    sin_ref[...] = sine

    number = iota((EXPERTS, 1), 0)
    expert = (number & 15) * LOCAL + (number >> 4)
    member = jnp.zeros((EXPERTS, GROUP), F32)
    gate_of = jnp.zeros((EXPERTS, GROUP), F32)
    for k in range(TOP):
        hit = routes_ref[k : k + 1, :] == expert
        member = member + jnp.where(hit, 1.0, 0.0)
        gate_of = gate_of + jnp.where(hit, gates_ref[k : k + 1, :], 0.0)
    earlier = jnp.where(iota((GROUP, GROUP), 0) < iota((GROUP, GROUP), 1), 1.0, 0.0).astype(BF16)
    count = dot_nn(member.astype(BF16), earlier)
    slot = jnp.where((member > 0.5) & (count < CAP - 0.5), count, -1.0)
    seats = iota((GROUPS, PADCAP, GROUP), 1).astype(F32)
    slot_gates = []
    for k in range(LOCAL):
        s = slice(k * GROUPS, (k + 1) * GROUPS)
        gate_ref[k] = gate_of[s]
        wide = jnp.broadcast_to(slot[s][:, None, :], (GROUPS, PADCAP, GROUP))
        on = jnp.where(wide == seats, 1.0, 0.0)
        place_ref[k] = on.reshape(ROWS, GROUP).astype(BF16)
        weight = on * jnp.broadcast_to(gate_of[s][:, None, :], (GROUPS, PADCAP, GROUP))
        slot_gates.append(jnp.sum(weight.reshape(ROWS, GROUP), axis=1, keepdims=True))
    early[0].wait()
    for i in range(4):
        row = LATENT + (i // 2) * hr
        wrope[i * hr : (i + 1) * hr] = wl[row : row + hr]
    inward = seat_of_row(seat)
    hop_wait(hop_d, PADCAP, hb_s, hb_r)

    xc_ref[...] = dot_nn(inward, hop_d[:, :COLS]).astype(BF16)
    xfull[:, cols(t, COLS)] = xc_ref[...]
    xg1, xg2, xg3, xg4 = gather_stages(xc_ref, column_blocks(xfull, GROUP), xg_s, xg_r, send)
    xg1()
    dyc_ref[...] = dot_nn(inward, hop_d[:, COLS:]).astype(BF16)
    dyfull[:, cols(t, COLS)] = dyc_ref[...]
    yg1, yg2, yg3, yg4 = gather_stages(dyc_ref, column_blocks(dyfull, GROUP), yg_s, yg_r, send)
    yg1()
    blocks = (t, far)

    def slot_gradients(b):
        for k in range(LOCAL):
            gout[b, k] = (slot_gates[k] * dot_nn(place_ref[k], dyfull[:, cols(blocks[b], COLS)])).astype(BF16)

    own_grads = {}

    def send_gradients(p, b):
        two = pl.ds(2 * p, 2)
        landed = grads_hbm.at[two, seat_rows(e), cols(blocks[b], COLS)]
        own_grads[p, b] = local(gout.at[b, two, seat_rows(e)], landed, l_own.at[p, b])
        for j, (to, frm) in enumerate(peers):
            send(gout.at[b, two, seat_rows(to)], landed, d_s.at[p, b, j], d_r.at[p, b, j], "expert", to)

    slot_gradients(0)
    send_gradients(0, 0)
    send_gradients(1, 0)
    xg2()
    yg2()
    xg3()
    yg3()
    slot_gradients(1)
    send_gradients(0, 1)
    send_gradients(1, 1)
    xg4()

    xd = xfull[...].astype(F32)
    inv = lax.rsqrt(jnp.sum(xd * xd, axis=1, keepdims=True) * (1.0 / D) + EPS)
    inv_ref[...] = inv
    normed = (xd * inv * gain_ref[...].astype(F32)).astype(BF16)
    normed_ref[...] = normed
    lat = dot_nt(normed, wl[:LATENT])
    lat_ref[...] = lat
    linv = lax.rsqrt(jnp.sum(lat * lat, axis=1, keepdims=True) * (1.0 / LATENT) + EPS)
    linv_ref[...] = linv
    kr = turn(dot_nt(normed, wrope[...]), cosine, sine).astype(BF16)
    kr_ref[...] = kr
    early[1].wait()
    pre = lax.dot_general(
        dot_nn(normed, wq[...]),
        regroup(F32),
        (((1,), (0,)), ((), ())),
        precision=lax.Precision.HIGHEST,
        preferred_element_type=F32,
    )
    q_ref[:, : 2 * NOPE] = pre[:, : 2 * NOPE].astype(BF16)
    qr = turn(pre[:, 2 * NOPE :], cosine, sine)
    q_ref[:, 2 * NOPE :] = qr.astype(BF16)
    comp = (lat * linv * lgain_ref[...].astype(F32)).astype(BF16)
    comp_ref[...] = comp
    early[2].wait()
    expanded = dot_nn(comp, wexp[...]).astype(BF16)
    exp_ref[...] = expanded

    def grad_block(k):
        return lambda owner: grads_hbm.at[k, :, cols(owner, COLS)]

    spread = [near_stages(grad_block(k), gg_s.at[k], gg_r.at[k], send) for k in range(LOCAL)]
    seen = set()

    def gradients(k, b):
        p = k // 2
        if (p, b) not in seen:
            seen.add((p, b))
            own_grads[p, b].wait()
            for j, (to, frm) in enumerate(peers):
                ref = grads_hbm.at[pl.ds(2 * p, 2), seat_rows(frm), cols(blocks[b], COLS)]
                got(ref, d_s.at[p, b, j], d_r.at[p, b, j])
        spread[k][b]()

    head = lane_head((GROUP, 2 * ROPE))
    allowed = (which == which_row) & (iota((GROUP, GROUP), 0) >= iota((GROUP, GROUP), 1))
    scale = HEAD ** (-0.5)
    for h in range(2):
        q = q_ref[:, h * NOPE : (h + 1) * NOPE]
        k = expanded[:, 256 * h : 256 * h + NOPE]
        v = expanded[:, 256 * h + NOPE : 256 * h + NOPE + VDIM]
        turned = jnp.where(head == h, qr, 0.0).astype(BF16)
        raw = (dot_nt(q, k) + dot_nt(turned, kr)) * scale
        scores = jnp.where(allowed, raw, -1e30)
        expo = jnp.exp(scores - jnp.max(scores, axis=1, keepdims=True))
        probs = expo / jnp.sum(expo, axis=1, keepdims=True)
        probs_ref[h] = probs
        mixed_ref[:, h * VDIM : (h + 1) * VDIM] = dot_nn(probs.astype(BF16), v).astype(BF16)
    mixed = mixed_ref[...]
    early[3].wait()
    for n in range(TENSOR):
        apart[n] = dot_nn(mixed, wout[:, n * COLS : (n + 1) * COLS]).astype(BF16)

    order = (far, right, left, t)
    r1, r2, r3, r4 = sum_stages(
        lambda owner: apart.at[owner],
        lambda j: apart[order[j]].astype(F32),
        GROUP, sib, half, full, r_s, r_r, send,
    )
    r1()
    gradients(0, 0)
    r2()
    r3()
    gradients(1, 0)
    mid = xc_ref[...].astype(F32) + r4()
    mid_ref[...] = mid
    finish = sum_rows_start(mid * mid, st_buf, st_s, st_r)
    spread[0][2]()
    inv2 = lax.rsqrt(finish() * (1.0 / D) + EPS)
    inv2_ref[...] = inv2
    ncols_ref[...] = (mid * inv2 * fgain_ref[:, cols(t, COLS)].astype(F32)).astype(BF16)
    nfull[:, cols(t, COLS)] = ncols_ref[...]
    ng1, ng2, ng3, ng4 = gather_stages(ncols_ref, column_blocks(nfull, GROUP), ng_s, ng_r, send)
    ng1()
    own_rows = {}

    def dispatch(b):
        for p in range(2):
            for k in (2 * p, 2 * p + 1):
                dbuf[b, k] = dot_nn(place_ref[k], nfull[:, cols(blocks[b], COLS)]).astype(BF16)
            two = pl.ds(2 * p, 2)
            landed = rown_hbm.at[b, two, seat_rows(e)]
            own_rows[p, b] = local(dbuf.at[b, two, seat_rows(e)], landed, l_last.at[p, b])
            for j, (to, frm) in enumerate(peers):
                send(dbuf.at[b, two, seat_rows(to)], landed, e_s.at[p, b, j], e_r.at[p, b, j], "expert", to)

    dispatch(0)
    gradients(2, 0)
    gradients(0, 1)
    gradients(1, 1)
    spread[1][2]()
    ng2()
    gradients(3, 0)
    gradients(2, 1)
    gradients(3, 1)
    ng3()
    dispatch(1)
    spread[2][2]()
    yg4()
    ng4()
    spread[3][2]()
    for k in range(LOCAL):
        spread[k][3]()
    for p in range(2):
        for b in range(2):
            own_rows[p, b].wait()
            for j, (to, frm) in enumerate(peers):
                got(rown_hbm.at[b, pl.ds(2 * p, 2), seat_rows(frm)], e_s.at[p, b, j], e_r.at[p, b, j])
    for c in sends:
        c.wait_send()


def front_step(small, large, cid):
    vmem = pltpu.VMEM

    def out(*shape, dtype=BF16):
        return jax.ShapeDtypeStruct(shape, dtype)

    def pair(*shape):
        return [DMA(shape), DMA(shape)]

    return pl.pallas_call(
        front_kernel,
        out_shape=(
            out(GROUP, COLS),
            out(GROUP, COLS),
            out(GROUP, COLS, dtype=F32),
            out(GROUP, 1, dtype=F32),
            out(GROUP, COLS),
            out(GROUP, D),
            out(GROUP, 1, dtype=F32),
            out(GROUP, 2 * HEAD),
            out(GROUP, 512),
            out(GROUP, 2 * ROPE),
            out(GROUP, LATENT),
            out(GROUP, LATENT, dtype=F32),
            out(GROUP, 1, dtype=F32),
            out(2, GROUP, GROUP, dtype=F32),
            out(GROUP, 2 * VDIM),
            out(LOCAL, ROWS, GROUP),
            out(LOCAL, GROUPS, GROUP, dtype=F32),
            out(GROUP, 1, dtype=F32),
            out(1, GROUP, dtype=F32),
            out(GROUP, 2 * ROPE, dtype=F32),
            out(GROUP, 2 * ROPE, dtype=F32),
            out(GROUP, D),
            out(GROUP, D),
            out(2, LOCAL, ROWS, COLS),
            out(LOCAL, ROWS, D),
        ),
        in_specs=[VM] * len(small) + [ANY] * len(large),
        out_specs=(VM,) * 23 + (ANY,) * 2,
        scratch_shapes=[
            vmem((GROUP, 2 * COLS), BF16),
            vmem((GROUP, 2 * COLS), BF16),
            vmem((ROWS, 2 * COLS), BF16),
            vmem((ROWS, 2 * COLS), BF16),
            vmem((GROUP, D), BF16),
            vmem((D, 2 * HEAD), BF16),
            vmem((LATENT + ROPE, D), BF16),
            vmem((LATENT, 512), BF16),
            vmem((2 * VDIM, D), BF16),
            vmem((2 * ROPE, D), BF16),
            vmem((TENSOR, GROUP, COLS), BF16),
            vmem((4, GROUP, COLS), BF16),
            vmem((2, GROUP // 2, COLS), BF16),
            vmem((2, GROUP, COLS), BF16),
            vmem((2, LOCAL, ROWS, COLS), BF16),
            vmem((2, LOCAL, ROWS, COLS), BF16),
        ]
        + sum_rows_scratch()
        + pair(15)
        + pair(15)
        + pair(9)
        + pair(9)
        + pair(9)
        + pair(LOCAL, 6)
        + pair(8)
        + pair(2, 2, 15)
        + pair(2, 2, 15)
        + [DMA((4,)), DMA((2, 2)), DMA((2, 2))],
        compiler_params=params(cid, 60),
        name="front_step",
    )(*small, *large)


def finish_kernel(
    gg_ref, gu_ref, gd_ref, wsum_ref, out_in, dx_in, gwq_in, gwexp_in, gwout_in, gwlat_in, gains_in,
    ogg_ref, ogu_ref, ogd_ref, sg_ref, su_ref, sd_ref, out_ref, dx_ref, gwq_ref, gwexp_ref, gwout_ref, gwlat_ref,
    attn_ref, ffn_ref, lgain_ref,
):
    ogg_ref[...] = gg_ref[...].astype(F32)
    ogu_ref[...] = gu_ref[...].astype(F32)
    ogd_ref[...] = gd_ref[...].astype(F32)

    @pl.when((pl.program_id(0) == 0) & (pl.program_id(1) == 0))
    def small():
        e = lax.axis_index("expert")
        sg_ref[...] = wsum_ref[0]
        su_ref[...] = wsum_ref[1]
        sd_ref[...] = wsum_ref[2]
        out_ref[...] = out_in[...]
        dx_ref[...] = dx_in[...]
        gwq_ref[...] = gwq_in[...]
        gwexp_ref[...] = gwexp_in[...]
        gwout_ref[...] = gwout_in[...]
        lat = gwlat_in[...].astype(F32).reshape(WIDE_LAT, D // GROUPS)
        half = ROPE // 2
        gwlat_ref[: LATENT + half] = lat[: LATENT + half]
        gwlat_ref[LATENT + half :] = lat[LATENT + ROPE : LATENT + ROPE + half]
        own = gains_in[e // 2]
        side = lax.rem(e, 2) == 0
        attn_ref[...] = jnp.where(side, own[0:1, :128], own[0:1, 128:])
        ffn_ref[...] = jnp.where(side, own[1:2, :128], own[1:2, 128:])
        rows = jnp.sum(gains_in[...], axis=0)[2:4]
        row = jnp.where(e < 8, rows[0:1], rows[1:2])
        wanted = iota((COLS, 128), 1) + lax.rem(e, 8) * (LATENT // GROUPS)
        pick_own = jnp.where(iota((COLS, 128), 0) == wanted, 1.0, 0.0)
        lgain_ref[...] = lax.dot_general(
            row, pick_own, (((1,), (0,)), ((), ())),
            precision=lax.Precision.HIGHEST, preferred_element_type=F32,
        )


def finish_step(grads, rest):
    def out(*shape, dtype=F32):
        return jax.ShapeDtypeStruct(shape, dtype)

    hid = grads[0].shape[1]
    wide = rest[0].shape[1]
    block = pl.BlockSpec((1, hid, D // 2), lambda i, j: (i, 0, j))

    def whole(shape):
        return pl.BlockSpec(shape, lambda i, j: (0,) * len(shape))

    outs = (
        out(wide, 128), out(wide, 128), out(wide, 128), out(GROUP, COLS, dtype=BF16), out(GROUP, COLS, dtype=BF16),
        out(128, 2 * HEAD), out(LATENT // GROUPS, 512), out(2 * VDIM, 128), out(LATENT + ROPE, 128),
        out(1, 128), out(1, 128), out(1, 128),
    )
    return pl.pallas_call(
        finish_kernel,
        grid=(LOCAL, 2),
        out_shape=(out(LOCAL, hid, D),) * 3 + outs,
        in_specs=[block] * 3 + [whole(a.shape) for a in rest],
        out_specs=(block,) * 3 + tuple(whole(o.shape) for o in outs),
        compiler_params=pltpu.CompilerParams(vmem_limit_bytes=40 * MIB),
        name="finish_step",
    )(*grads, *rest)


def per_device(
    tokens,
    cotangent,
    attn_gain,
    w_query,
    w_latent,
    latent_gain,
    w_expand,
    w_out,
    ffn_gain,
    shared_gate,
    shared_up,
    shared_down,
    expert_gate,
    expert_up,
    expert_down,
    seq_lengths,
    seq_order,
    routes,
    gate_weights,
):
    wlat_t = w_latent.T
    attn_row = attn_gain.reshape(1, D)
    ffn_row = ffn_gain.reshape(1, D)
    lgain = latent_gain.reshape(1, LATENT)

    (
        x_cols, dy_cols, middle, inv_two, normed_two_cols, normed, inv_one, query, expanded, key_rope, compressed,
        latent, inv_lat, probs, mixed, place, gate_of, seat, seat_row, cosine, sine, dy_full, normed_two, own_slots, grad_rows
    ) = front_step(
        (
            tokens,
            cotangent,
            seq_lengths.reshape(1, -1),
            seq_order.reshape(1, -1),
            routes.T,
            gate_weights.T,
            attn_row,
            lgain,
            ffn_row,
        ),
        (w_query, wlat_t, w_expand, w_out),
        1,
    )

    (
        part, grad_eg, grad_eu, grad_ed, shared_out, dmid, dgain_ffn, d_attn, unused, shared_weights
    ) = moe_step(
        place,
        own_slots,
        normed_two,
        dy_full,
        shared_gate.T,
        shared_up.T,
        shared_down,
        jnp.swapaxes(expert_gate, 1, 2),
        jnp.swapaxes(expert_up, 1, 2),
        expert_down,
        grad_rows,
        middle,
        inv_two,
        ffn_row,
        dy_cols,
        3,
    )
    output, input_grad, grad_wq, grad_wexp, grad_wout, grad_wlat, gains = back_step(
        (
            d_attn,
            mixed,
            w_out,
            query,
            expanded,
            key_rope,
            probs,
            cosine,
            sine,
            latent,
            inv_lat,
            lgain,
            x_cols,
            inv_one,
            attn_row,
            dmid,
            dgain_ffn,
            middle,
            shared_out,
            gate_of,
            seat,
            seat_row,
        ),
        (place, normed, w_query, w_expand, compressed, wlat_t, part),
        4,
    )
    (
        grad_eg, grad_eu, grad_ed, sg, su, sd, output, input_grad, grad_wq, grad_wexp, grad_wout, grad_wlat,
        attn_out, ffn_out, lgain_out
    ) = finish_step(
        (grad_eg, grad_eu, grad_ed),
        (shared_weights, output, input_grad, grad_wq, grad_wexp, grad_wout, grad_wlat, gains),
    )
    return (
        output,
        input_grad,
        attn_out[0],
        grad_wq,
        grad_wlat.T,
        lgain_out[0, : LATENT // GROUPS],
        grad_wexp,
        grad_wout,
        ffn_out[0],
        sg.T,
        su.T,
        sd,
        jnp.swapaxes(grad_eg, 1, 2),
        jnp.swapaxes(grad_eu, 1, 2),
        grad_ed,
    )


def solution(mesh):
    return jax.shard_map(
        per_device,
        mesh=mesh,
        in_specs=(
            P("expert", "tensor"),
            P("expert", "tensor"),
            P(),
            P(None, "tensor"),
            P(),
            P(),
            P(None, "tensor"),
            P("tensor", None),
            P(),
            P(None, "tensor"),
            P(None, "tensor"),
            P("tensor", None),
            P("expert", None, "tensor"),
            P("expert", None, "tensor"),
            P("expert", "tensor", None),
            P(),
            P(),
            P("expert", None),
            P("expert", None),
        ),
        out_specs=(
            P("expert", "tensor"),
            P("expert", "tensor"),
            P("expert"),
            P("expert", "tensor"),
            P("expert", None),
            P("expert"),
            P("expert", "tensor"),
            P("tensor", "expert"),
            P("expert"),
            P("expert", "tensor"),
            P("expert", "tensor"),
            P("tensor", "expert"),
            P("expert", None, "tensor"),
            P("expert", None, "tensor"),
            P("expert", "tensor", None),
        ),
        check_vma=False,
    )
```

```python
import math

import jax
import jax.numpy as jnp
from jax import lax
from jax.experimental import pallas as pl
from jax.experimental.pallas import tpu as pltpu
from jax.sharding import PartitionSpec as P

NOPE = 128
ROPE = 64
HEAD = NOPE + ROPE
LATENT = 512
VDIM = 128
D = 2048
GROUP = 256
TOP = 6
EXPERTS = 64
GROUPS = 16
LOCAL = 4
CAP = 27
PADCAP = 32
TENSOR = 8
COLS = D // TENSOR
EPS = 1e-06

XN = 4
YN = 4
ZN = 4
CORES = 2

F32 = jnp.float32
BF16 = jnp.bfloat16
MESH = pl.DeviceIdType.MESH
ANY = pl.BlockSpec(memory_space=pl.ANY)
VM = pl.BlockSpec(memory_space=pltpu.VMEM)
DMA = pltpu.SemaphoreType.DMA
MIB = 1024 * 1024


def remote(src, dst, ssem, rsem, axis, index):
    return pltpu.make_async_remote_copy(
        src_ref=src,
        dst_ref=dst,
        send_sem=ssem,
        recv_sem=rsem,
        device_id={axis: index},
        device_id_type=MESH,
    )


def greet(peers):
    barrier = pltpu.get_barrier_semaphore()
    for axis, index in peers:
        pl.semaphore_signal(barrier, inc=1, device_id={axis: index}, device_id_type=MESH)
    pl.semaphore_wait(barrier, len(peers))


def params(cid, vmem=48):
    return pltpu.CompilerParams(
        collective_id=cid, has_side_effects=True, vmem_limit_bytes=vmem * MIB
    )


def x_peers():
    t = lax.axis_index("tensor")
    x = t // CORES
    c = lax.rem(t, CORES)
    right = lax.rem(x + 1, XN) * CORES + c
    left = lax.rem(x + XN - 1, XN) * CORES + c
    far = lax.rem(x + 2, XN) * CORES + c
    twin = x * CORES + (1 - c)
    return t, right, left, far, twin


def greet_x():
    t, right, left, far, twin = x_peers()
    greet([("tensor", right), ("tensor", left), ("tensor", twin)])


def greet_tensor():
    t = lax.axis_index("tensor")
    greet([("tensor", lax.rem(t + j, TENSOR)) for j in range(1, TENSOR)])


def cols(index, width):
    return pl.ds(pl.multiple_of(index * width, width), width)


def gather_tensor(nch, src, out_ref, ssem, rsem):
    t, right, left, far, twin = x_peers()
    flip = twin - t
    rows, width = src.shape
    rc = rows // nch
    h = rc // 2

    def block(k, owner, part=None):
        if part is None:
            return out_ref.at[pl.ds(k * rc, rc), cols(owner, width)]
        return out_ref.at[pl.ds(k * rc + part * h, h), cols(owner, width)]

    sends = []

    def send(k, j, ref, dst, target):
        c = remote(ref, dst, ssem.at[k, j], rsem.at[k, j], "tensor", target)
        c.start()
        sends.append(c)

    def arrived(k, j, ref):
        remote(ref, ref, ssem.at[k, j], rsem.at[k, j], "tensor", twin).wait_recv()

    for k in range(nch):
        part = src.at[pl.ds(k * rc, rc), :]
        send(k, 0, part, block(k, t), right)
        send(k, 1, part, block(k, t), left)
        send(k, 4, part, block(k, t), twin)
    for k in range(nch):
        arrived(k, 0, block(k, left))
        send(k, 2, block(k, left, 0), block(k, left, 0), right)
        send(k, 5, block(k, left), block(k, left), twin)
        arrived(k, 1, block(k, right))
        send(k, 3, block(k, right, 1), block(k, right, 1), left)
        send(k, 6, block(k, right), block(k, right), twin)
    for k in range(nch):
        arrived(k, 2, block(k, far, 0))
        send(k, 7, block(k, far, 0), block(k, far, 0), twin)
        arrived(k, 3, block(k, far, 1))
        send(k, 8, block(k, far, 1), block(k, far, 1), twin)
    for k in range(nch):
        arrived(k, 4, block(k, twin))
        arrived(k, 5, block(k, left + flip))
        arrived(k, 6, block(k, right + flip))
        arrived(k, 7, block(k, far + flip, 0))
        arrived(k, 8, block(k, far + flip, 1))
    for s in sends:
        s.wait_send()


def gather_sems(nch):
    return [DMA((nch, 9)), DMA((nch, 9))]


def sum_rows_start(value, buf, ssem, rsem):
    t = lax.axis_index("tensor")
    rows = value.shape[0]
    mine = jnp.broadcast_to(jnp.sum(value, axis=1, keepdims=True), (rows, 128))
    buf[t] = jnp.transpose(mine)[:8]
    sends = []
    for j in range(1, TENSOR):
        to = lax.rem(t + j, TENSOR)
        c = remote(buf.at[t], buf.at[t], ssem.at[j], rsem.at[j], "tensor", to)
        c.start()
        sends.append(c)

    def finish():
        for j in range(1, TENSOR):
            ref = buf.at[lax.rem(t + TENSOR - j, TENSOR)]
            remote(ref, ref, ssem.at[j], rsem.at[j], "tensor", t).wait_recv()
        total = jnp.sum(buf[...], axis=0)
        for s in sends:
            s.wait_send()
        return jnp.transpose(total)[:, :1]

    return finish


def sum_rows_tensor(value, buf, ssem, rsem):
    return sum_rows_start(value, buf, ssem, rsem)()


def sum_rows_scratch():
    return [pltpu.VMEM((TENSOR, 8, GROUP), F32), DMA((TENSOR,)), DMA((TENSOR,))]


def dot_nn(a, b):
    return lax.dot_general(a, b, (((1,), (0,)), ((), ())), preferred_element_type=F32)


def dot_nt(a, b):
    return lax.dot_general(a, b, (((1,), (1,)), ((), ())), preferred_element_type=F32)


def dot_tn(a, b):
    return lax.dot_general(a, b, (((0,), (0,)), ((), ())), preferred_element_type=F32)


ROWS = GROUPS * PADCAP
OTHERS = ROWS - PADCAP


def expert_peers():
    e = lax.axis_index("expert")
    z = e // YN
    y = lax.rem(e, YN)
    peers = []
    for dz in range(ZN):
        for dy in range(YN):
            if dz or dy:
                to = lax.rem(z + dz, ZN) * YN + lax.rem(y + dy, YN)
                frm = lax.rem(z + ZN - dz, ZN) * YN + lax.rem(y + YN - dy, YN)
                peers.append((to, frm))
    return e, peers


def seat_rows(index):
    return pl.ds(pl.multiple_of(index * PADCAP, PADCAP), PADCAP)


def moe_kernel(
    place_ref, rown_hbm, nfull_hbm, dy_hbm, sg_hbm, su_hbm, sd_hbm, wg_hbm, wu_hbm, wd_hbm, grads_hbm,
    mid_ref, inv_ref, gain_ref, dyc_ref,
    part_hbm, gg_hbm, gu_hbm, gd_hbm, shout_ref, dmid_ref, dgain_ref, dattn_hbm, wsend_hbm, wsum_ref,
    sh_ref, dsg_ref, dsu_ref, nfull, dyf, rows, drows, sib, half, full, wbuf, gbuf, gout, pbuf, res, back, shsum, low,
    a_s, a_r, r_s, r_r, b_s, b_r, f_s, f_r, st_buf, st_s, st_r, l_in, l_w, l_g, l_out, l_own, l_sh, l_first,
    wown, w_a, w_p, w_b, w_s, w_r, l_wn,
):
    t, right, left, far, twin = x_peers()
    flip = twin - t
    e, peers = expert_peers()
    greet(
        [("tensor", lax.rem(t + j, TENSOR)) for j in range(1, TENSOR)]
        + [("expert", to) for to, frm in peers]
    )
    sends = []

    def send(src, dst, ssem, rsem, axis, to):
        c = remote(src, dst, ssem, rsem, axis, to)
        c.start()
        sends.append(c)

    def send_many(targets, total, ssem, rsem, axis):
        for src, dst, to in targets:
            remote(src, dst, ssem, rsem, axis, to).start()
        sends.append(remote(total, total, ssem, rsem, axis, targets[0][2]))

    def got(ref, ssem, rsem):
        remote(ref, ref, ssem, rsem, "tensor", twin).wait_recv()

    blocks = (t, far)
    own_copies = []
    for k in range(LOCAL):
        for b in range(2):
            c = pltpu.make_async_copy(
                rown_hbm.at[b, k], rows.at[k, :, cols(blocks[b], COLS)], l_first.at[k, b]
            )
            c.start()
            own_copies.append(c)
    wide = sd_hbm.shape[0]
    sgv, suv, sdv = (drows.at[i, pl.ds(0, wide)] for i in range(3))
    early = [
        pltpu.make_async_copy(src, dst, l_in.at[i])
        for i, (src, dst) in enumerate(
            [(nfull_hbm, nfull), (sg_hbm, sgv), (su_hbm, suv), (sd_hbm, sdv), (dy_hbm, dyf)]
        )
    ]
    for c in early:
        c.start()

    def load(k):
        s = k % 2
        copies = [
            pltpu.make_async_copy(ref.at[k], wbuf.at[s, i], l_w.at[s, i])
            for i, ref in enumerate((wg_hbm, wu_hbm, wd_hbm))
        ]
        for c in copies:
            c.start()
        return copies

    loads = {0: load(0)}

    grad_loads = [pltpu.make_async_copy(grads_hbm.at[k], gbuf.at[k], l_g.at[k]) for k in range(LOCAL)]
    grad_loads[0].start()

    h = ROWS // 2

    def row_block(k):
        return lambda owner: rows.at[k, :, cols(owner, COLS)]

    near = [near_stages(row_block(k), a_s.at[k], a_r.at[k], send) for k in range(LOCAL)]

    def gather_1(k):
        for b in range(2):
            own_copies[2 * k + b].wait()
            near[k][b]()

    def gather_2(k):
        near[k][2]()

    def gather_4(k):
        near[k][3]()

    back_copies = {}

    order = (far, right, left, t)

    def slot(k):
        return k

    def rsend(k, j, src, dst, to):
        send(src, dst, r_s.at[k, j], r_r.at[k, j], "tensor", to)

    def rgot(k, j, ref):
        got(ref, r_s.at[k, j], r_r.at[k, j])

    def mine(k, j):
        return drows[slot(k), :, cols(order[j], COLS)].astype(F32)

    twin_sends = {}

    def sum_1(k):
        first = len(sends)
        for j, owner in enumerate(order):
            rsend(k, j, drows.at[slot(k), :, cols(owner + flip, COLS)], sib.at[k, j], twin)
        twin_sends[k] = sends[first:]
        del sends[first:]

    def sum_2(k):
        rgot(k, 0, sib.at[k, 0])
        sib[k, 0] = (mine(k, 0) + sib[k, 0].astype(F32)).astype(BF16)
        rsend(k, 4, sib.at[k, 0, pl.ds(0, h)], half.at[k, 0], right)
        rsend(k, 5, sib.at[k, 0, pl.ds(h, h)], half.at[k, 1], left)

    def sum_3(k):
        for j, to in ((1, right), (2, left)):
            rgot(k, j, sib.at[k, j])
            rgot(k, 3 + j, half.at[k, j - 1])
            both = mine(k, j) + sib[k, j].astype(F32)
            extra = half[k, j - 1].astype(F32)
            if j == 1:
                sib[k, j, :h] = (both[:h] + extra).astype(BF16)
                sib[k, j, h:] = both[h:].astype(BF16)
            else:
                sib[k, j, :h] = both[:h].astype(BF16)
                sib[k, j, h:] = (both[h:] + extra).astype(BF16)
            rsend(k, 5 + j, sib.at[k, j], full.at[k, j - 1], to)

    def sum_4(k):
        rgot(k, 3, sib.at[k, 3])
        rgot(k, 6, full.at[k, 0])
        rgot(k, 7, full.at[k, 1])
        value = mine(k, 3) + sib[k, 3].astype(F32) + full[k, 0].astype(F32) + full[k, 1].astype(F32)
        for c in twin_sends[k]:
            c.wait_send()
        if k == LOCAL:
            shsum[...] = value
            return
        res[k] = value.astype(BF16)
        c = pltpu.make_async_copy(res.at[k, seat_rows(e)], back.at[k, seat_rows(e)], l_own.at[k])
        c.start()
        back_copies[k] = c
        targets = [(res.at[k, seat_rows(to)], back.at[k, seat_rows(e)], to) for to, frm in peers]
        send_many(targets, back.at[k, pl.ds(0, OTHERS)], b_s.at[k], b_r.at[k], "expert")

    def shared_forward():
        for c in early[:4]:
            c.wait()
        n = nfull[...]
        g = dot_nt(n, sgv[...])
        u = dot_nt(n, suv[...])
        sig = jax.nn.sigmoid(g)
        silu = g * sig
        sh_ref[...] = (silu * u).astype(BF16)
        return g, u, sig, silu

    def shared_backward(g, u, sig, silu):
        early[4].wait()
        dh = dot_nt(dyf[...], sdv[...])
        dsg_ref[...] = (dh * u * (sig * (1.0 + g * (1.0 - sig)))).astype(BF16)
        dsu_ref[...] = (dh * silu).astype(BF16)

    tiles = [pl.ds(i * 512, 512) for i in range(D // 512)]

    def shared_rows():
        hid = sh_ref[...]
        dsg, dsu = dsg_ref[...], dsu_ref[...]
        for n in tiles:
            drows[LOCAL, :GROUP, n] = dot_nn(hid, sdv[:, n]).astype(BF16)
            drows[LOCAL, GROUP:, n] = (dot_nn(dsg, sgv[:, n]) + dot_nn(dsu, suv[:, n])).astype(BF16)

    stages = (drows.at[1], drows.at[2], pbuf)
    staged = []

    def shared_weights():
        pairs = ((dsg_ref, nfull), (dsu_ref, nfull), (sh_ref, dyf))
        for i, (lhs, rhs) in enumerate(pairs):
            for n in tiles:
                stages[i][:wide, n] = dot_tn(lhs[...], rhs[:, n]).astype(BF16)
            c = pltpu.make_async_copy(stages[i].at[pl.ds(0, wide)], wsend_hbm.at[i], l_sh.at[i])
            c.start()
            staged.append(c)
            for p in range(2):
                for j in range(4):
                    d = j * YN + lax.rem(e, YN) if p == 0 else (e // YN) * YN + j
                    c = pltpu.make_async_copy(
                        stages[i].at[pl.ds(p * wide // 2, wide // 2), cols(d, 128)],
                        wown.at[2 * i + p, j],
                        l_wn.at[2 * i + p, j],
                    )
                    c.start()
                    staged.append(c)

    def piece_ref(i, p):
        return lambda dz, dy: wsend_hbm.at[i, pl.ds(p * wide // 2, wide // 2), cols(dz * YN + dy, 128)]

    def piece_own(i, p):
        return lambda dz, dy: wown[2 * i + p, dz if p == 0 else dy].astype(F32)

    shared_sums = [
        two_phase(
            piece_ref(n // 2, n % 2), piece_own(n // 2, n % 2),
            w_a.at[n], w_p.at[n], w_b.at[n], w_s.at[n], w_r.at[n], "yz"[n % 2], send_many,
        )
        for n in range(6)
    ]

    out_copies = {}

    def compute_1(k):
        s = k % 2
        for c in loads[k] + [grad_loads[k]]:
            c.wait()
        r = rows[k]
        gate = dot_nt(r, wbuf[s, 0])
        up = dot_nt(r, wbuf[s, 1])
        dh = dot_nt(gbuf[k], wbuf[s, 2])
        sig = jax.nn.sigmoid(gate)
        silu = gate * sig
        hidden = (silu * up).astype(BF16)
        dg = (dh * up * (sig * (1.0 + gate * (1.0 - sig)))).astype(BF16)
        du = (dh * silu).astype(BF16)
        for n in tiles:
            drows[slot(k), :, n] = (
                dot_nn(dg, wbuf[s, 0, :, n]) + dot_nn(du, wbuf[s, 1, :, n])
            ).astype(BF16)
        return hidden, dg, du

    def compute_2(k, hidden, dg, du):
        s = k % 2
        if k:
            for c in out_copies[k - 1]:
                c.wait()
        for n in tiles:
            pbuf[:, n] = dot_nn(hidden, wbuf[s, 2, :, n]).astype(BF16)
            gout[0, :, n] = dot_tn(dg, rows[k, :, n]).astype(BF16)
            gout[1, :, n] = dot_tn(du, rows[k, :, n]).astype(BF16)
            gout[2, :, n] = dot_tn(hidden, gbuf[k, :, n]).astype(BF16)
        out_copies[k] = [
            pltpu.make_async_copy(src, dst.at[k], l_out.at[i])
            for i, (src, dst) in enumerate(
                [(pbuf, part_hbm), (gout.at[0], gg_hbm), (gout.at[1], gu_hbm), (gout.at[2], gd_hbm)]
            )
        ]
        for c in out_copies[k]:
            c.start()
        if k + 2 < LOCAL:
            loads[k + 2] = load(k + 2)

    for k in range(LOCAL):
        gather_1(k)
    loads[1] = load(1)
    grad_loads[1].start()
    state = shared_forward()
    shared_backward(*state)
    gather_2(0)
    shared_rows()
    sum_1(4)
    gather_2(1)
    gather_4(0)
    c0 = compute_1(0)
    sum_1(0)
    grad_loads[2].start()
    grad_loads[3].start()
    gather_2(2)
    shared_weights()
    gather_4(1)
    for c in staged:
        c.wait()
    c1 = compute_1(1)
    sum_1(1)
    for piece in shared_sums:
        piece[0]()
    gather_2(3)
    sum_2(0)
    compute_2(0, *c0)
    gather_4(2)
    c2 = compute_1(2)
    sum_1(2)
    sum_3(0)
    sum_2(1)
    compute_2(1, *c1)
    gather_4(3)
    c3 = compute_1(3)
    sum_1(3)
    sum_4(0)
    sum_3(1)
    sum_2(2)
    sum_2(3)
    compute_2(2, *c2)
    sum_2(4)
    sum_4(1)
    sum_3(2)
    sum_3(3)
    compute_2(3, *c3)
    for piece in shared_sums:
        piece[1]()
    sum_3(4)
    sum_4(2)
    sum_4(3)
    sum_4(4)
    shout_ref[...] = shsum[:GROUP]

    dn = shsum[GROUP:]

    def combine(k):
        back_copies[k].wait()
        got(back.at[k, pl.ds(0, OTHERS)], b_s.at[k], b_r.at[k])
        return dot_tn(place_ref[k], back[k])

    for k in range(LOCAL):
        dn = dn + combine(k)

    mid = mid_ref[...]
    inv = inv_ref[...]
    u = dn * own_gain(gain_ref, t)
    total = sum_rows_tensor(u * mid, st_buf, st_s, st_r)
    dmid = dyc_ref[...].astype(F32) + inv * u - mid * (inv * inv * inv * total * (1.0 / D))
    dmid_ref[...] = dmid
    low[...] = dmid.astype(BF16)
    own = pltpu.make_async_copy(low, dattn_hbm.at[:, cols(t, COLS)], l_own.at[0])
    own.start()
    dgain_ref[...] = jnp.sum(dn * mid * inv, axis=0, keepdims=True)
    gather_tensor(1, low, dattn_hbm, f_s, f_r)
    own.wait()
    for c in out_copies[LOCAL - 1]:
        c.wait()
    for n in range(6):
        wsum_ref[n // 2, pl.ds((n % 2) * wide // 2, wide // 2)] = shared_sums[n][2]()
    for c in sends:
        c.wait_send()


def moe_step(place, rown, nfull, dy, sg, su, sd, wg, wu, wd, grads, mid, inv, gain, dyc, cid):
    hid = wd.shape[1]
    wide = sd.shape[0]
    wshape = jax.ShapeDtypeStruct((LOCAL, hid, D), BF16)
    vmem = pltpu.VMEM
    return pl.pallas_call(
        moe_kernel,
        out_shape=(
            jax.ShapeDtypeStruct((LOCAL, ROWS, D), BF16),
            wshape,
            wshape,
            wshape,
            jax.ShapeDtypeStruct((GROUP, COLS), F32),
            jax.ShapeDtypeStruct((GROUP, COLS), F32),
            jax.ShapeDtypeStruct((1, COLS), F32),
            jax.ShapeDtypeStruct((GROUP, D), BF16),
            jax.ShapeDtypeStruct((3, wide, D), BF16),
            jax.ShapeDtypeStruct((3, wide, D // GROUPS), F32),
        ),
        in_specs=[VM] + [ANY] * 10 + [VM] * 4,
        out_specs=(ANY, ANY, ANY, ANY, VM, VM, VM, ANY, ANY, VM),
        scratch_shapes=[
            vmem((GROUP, wide), BF16),
            vmem((GROUP, wide), BF16),
            vmem((GROUP, wide), BF16),
            vmem((GROUP, D), BF16),
            vmem((GROUP, D), BF16),
            vmem((LOCAL, ROWS, D), BF16),
            vmem((LOCAL + 1, ROWS, D), BF16),
            vmem((LOCAL + 1, 4, ROWS, COLS), BF16),
            vmem((LOCAL + 1, 2, ROWS // 2, COLS), BF16),
            vmem((LOCAL + 1, 2, ROWS, COLS), BF16),
            vmem((2, 3, hid, D), BF16),
            vmem((LOCAL, ROWS, D), BF16),
            vmem((3, hid, D), BF16),
            vmem((ROWS, D), BF16),
            vmem((LOCAL, ROWS, COLS), BF16),
            vmem((LOCAL, ROWS, COLS), BF16),
            vmem((2 * GROUP, COLS), F32),
            vmem((GROUP, COLS), BF16),
            DMA((LOCAL, 6)),
            DMA((LOCAL, 6)),
            DMA((LOCAL + 1, 8)),
            DMA((LOCAL + 1, 8)),
            DMA((LOCAL,)),
            DMA((LOCAL,)),
            DMA((1, 9)),
            DMA((1, 9)),
            vmem((TENSOR, 8, GROUP), F32),
            DMA((TENSOR,)),
            DMA((TENSOR,)),
            DMA((5,)),
            DMA((2, 3)),
            DMA((LOCAL,)),
            DMA((4,)),
            DMA((LOCAL,)),
            DMA((3,)),
            DMA((LOCAL, 2)),
            vmem((6, 4, wide // 2, D // GROUPS), BF16),
        ]
        + two_phase_scratch(6, wide // 2, D // GROUPS)
        + [DMA((6, 4))],
        compiler_params=params(cid, 63),
        cost_estimate=pl.CostEstimate(
            flops=40 * 10**9, bytes_accessed=100 * MIB, transcendentals=0
        ),
        name="moe_step",
    )(place, rown, nfull, dy, sg, su, sd, wg, wu, wd, grads, mid, inv, gain, dyc)


def swap_halves(value):
    return pltpu.roll(value, 64, 1)


def turn(value, cosine, sine):
    return value * cosine + swap_halves(value) * sine


def lane_head(shape):
    lane = lax.broadcasted_iota(jnp.int32, shape, 1)
    return (lane >> 5) & 1


def regroup(dtype):
    n = 2 * HEAD
    given = lax.broadcasted_iota(jnp.int32, (n, n), 0)
    made = lax.broadcasted_iota(jnp.int32, (n, n), 1)
    r = made - 2 * NOPE
    turned = ((r >> 5) & 1) * HEAD + NOPE + (r >> 6) * (ROPE // 2) + (r & 31)
    source = jnp.where(made < NOPE, made, jnp.where(made < 2 * NOPE, made + ROPE, turned))
    return jnp.where(given == source, 1.0, 0.0).astype(dtype)


def band(index, rows):
    return pl.ds(pl.multiple_of(index * rows, rows), rows)


def hop_start(src, dst, rows, ss, rs, send_many):
    e, peers = expert_peers()
    dst[band(e, rows)] = src[band(e, rows)]
    targets = [(src.at[band(to, rows)], dst.at[band(e, rows)], to) for to, frm in peers]
    send_many(targets, dst.at[pl.ds(0, 15 * rows)], ss, rs, "expert")


def hop_wait(dst, rows, ss, rs):
    ref = dst.at[pl.ds(0, 15 * rows)]
    remote(ref, ref, ss, rs, "expert", lax.axis_index("expert")).wait_recv()


def one_hot(test):
    return jnp.where(test, 1.0, 0.0).astype(BF16)


def by_sixteen():
    made, given = iota((GROUP, GROUP), 0), iota((GROUP, GROUP), 1)
    return one_hot(given == (made & 15) * GROUPS + (made >> 4))


def seat_of_row(index):
    return one_hot(iota((GROUP, ROWS), 1).astype(F32) == index)


def row_of_seat(index):
    return one_hot(iota((ROWS, GROUP), 0).astype(F32) == index)


def near_stages(block, ss, rs, send):
    t, right, left, far, twin = x_peers()
    flip = twin - t

    def put(j, owner, to):
        send(block(owner), block(owner), ss.at[j], rs.at[j], "tensor", to)

    def arrived(j, owner):
        ref = block(owner)
        remote(ref, ref, ss.at[j], rs.at[j], "tensor", twin).wait_recv()

    def stage_1():
        put(0, t, right)
        put(1, t, left)
        put(2, t, twin)

    def stage_far():
        put(3, far, twin)

    def stage_2():
        arrived(0, left)
        put(4, left, twin)
        arrived(1, right)
        put(5, right, twin)

    def stage_3():
        arrived(2, twin)
        arrived(3, far + flip)
        arrived(4, left + flip)
        arrived(5, right + flip)

    return stage_1, stage_far, stage_2, stage_3


def sum_stages(theirs, mine, rows, sib, half, full, ss, rs, send):
    t, right, left, far, twin = x_peers()
    flip = twin - t
    order = (far, right, left, t)
    h = rows // 2

    def put(j, src, dst, to):
        send(src, dst, ss.at[j], rs.at[j], "tensor", to)

    def arrived(j, ref):
        remote(ref, ref, ss.at[j], rs.at[j], "tensor", twin).wait_recv()

    def stage_1():
        for j, owner in enumerate(order):
            put(j, theirs(owner + flip), sib.at[j], twin)

    def stage_2():
        arrived(0, sib.at[0])
        sib[0] = (mine(0) + sib[0].astype(F32)).astype(sib.dtype)
        put(4, sib.at[0, pl.ds(0, h)], half.at[0], right)
        put(5, sib.at[0, pl.ds(h, h)], half.at[1], left)

    def stage_3():
        for j, to in ((1, right), (2, left)):
            arrived(j, sib.at[j])
            arrived(3 + j, half.at[j - 1])
            both = mine(j) + sib[j].astype(F32)
            extra = half[j - 1].astype(F32)
            if j == 1:
                sib[j, :h] = (both[:h] + extra).astype(sib.dtype)
                sib[j, h:] = both[h:].astype(sib.dtype)
            else:
                sib[j, :h] = both[:h].astype(sib.dtype)
                sib[j, h:] = (both[h:] + extra).astype(sib.dtype)
            put(5 + j, sib.at[j], full.at[j - 1], to)

    def stage_4():
        arrived(3, sib.at[3])
        arrived(6, full.at[0])
        arrived(7, full.at[1])
        return mine(3) + sib[3].astype(F32) + full[0].astype(F32) + full[1].astype(F32)

    return stage_1, stage_2, stage_3, stage_4


def two_phase(src, own, land_a, part, land_b, ss, rs, first, send_many):
    e = lax.axis_index("expert")
    z, y = e // YN, lax.rem(e, YN)
    one, two = (y, z) if first == "y" else (z, y)

    def at(i, j):
        return (j, i) if first == "y" else (i, j)

    def device(i, j):
        dz, dy = at(i, j)
        return dz * YN + dy

    def plus(v, d):
        return lax.rem(v + d, 4)

    def arrived(n, ref):
        remote(ref, ref, ss.at[n], rs.at[n], "expert", e).wait_recv()

    def stage_1():
        targets = []
        for d in (1, 3, 2):
            i = plus(one, d)
            targets += [(src(*at(i, j)), land_a.at[d - 1, j], device(i, two)) for j in range(4)]
        send_many(targets, land_a, ss.at[0], rs.at[0], "expert")

    def stage_2():
        arrived(0, land_a)
        for j in range(4):
            total = own(*at(one, j))
            for d in range(3):
                total = total + land_a[d, j].astype(F32)
            part[j] = total.astype(BF16)
        targets = []
        for d in (1, 3, 2):
            j = plus(two, d)
            targets.append((part.at[j], land_b.at[d - 1], device(one, j)))
        send_many(targets, land_b, ss.at[1], rs.at[1], "expert")

    def stage_3():
        arrived(1, land_b)
        total = part[two].astype(F32)
        for d in range(3):
            total = total + land_b[d].astype(F32)
        return total

    return stage_1, stage_2, stage_3


def two_phase_scratch(pieces, rows, width):
    return [
        pltpu.VMEM((pieces, 3, 4, rows, width), BF16),
        pltpu.VMEM((pieces, 4, rows, width), BF16),
        pltpu.VMEM((pieces, 3, rows, width), BF16),
        DMA((pieces, 2)),
        DMA((pieces, 2)),
    ]


SLICE = 80
WIDE_LAT = LATENT + 2 * ROPE


def back_kernel(
    dattn_ref, mixed_ref, wout_ref, q_ref, exp_ref, kr_ref, probs_ref, cos_ref, sin_ref, lat_ref, linv_ref,
    lgain_ref, x_ref, inv_ref, gain_ref, dmid_ref, ffn_ref, mid_ref, shout_ref, gate_ref, seat_ref, seat_row_ref,
    place_hbm, normed_hbm, wq_hbm, wexp_hbm, comp_hbm, wl_hbm, part_hbm,
    out_ref, dx_ref, gwq_ref, gwexp_ref, gwout_ref, gwlat_ref, gains_ref,
    normed, wq, wexp, comp, wl, place,
    own, sib, half, full, res, fback,
    npart, nsib, nhalf, nfull,
    swq, swexp, swout, swlat, rwlat, lowlat, *rest
):
    q_red, e_red, o_red, rest = rest[:5], rest[5:10], rest[10:15], rest[15:]
    (
        cbuf, cgot, dlat, gm, gin, xh, oh, xl, ol,
        st_buf, st_s, st_r,
        p_s, p_r, fb_s, fb_r, n_s, n_r, w_s, w_r, c_s, c_r, dl_s, dl_r, gm_s, gm_r, gt_s, gt_r, wl_s, wl_r,
        oa_s, oa_r, ob_s, ob_r, xa_s, xa_r, xb_s, xb_r, l_in, l_own,
    ) = rest
    t, right, left, far, twin = x_peers()
    e, peers = expert_peers()
    others = [(lax.rem(t + j, TENSOR), lax.rem(t + TENSOR - j, TENSOR)) for j in range(1, TENSOR)]
    greet([("tensor", to) for to, frm in others] + [("expert", to) for to, frm in peers])
    sends = []

    def send(src, dst, ssem, rsem, axis, to):
        c = remote(src, dst, ssem, rsem, axis, to)
        c.start()
        sends.append(c)

    def send_many(targets, total, ssem, rsem, axis):
        for src, dst, to in targets:
            remote(src, dst, ssem, rsem, axis, to).start()
        sends.append(remote(total, total, ssem, rsem, axis, targets[0][2]))

    def got(ref, ssem, rsem):
        remote(ref, ref, ssem, rsem, "tensor", twin).wait_recv()

    half_rope = ROPE // 2
    for i in (1, 3):
        wl[LATENT + i * half_rope : LATENT + (i + 1) * half_rope] = jnp.zeros((half_rope, COLS), BF16)
    wide = [
        (wq_hbm, wq),
        (wexp_hbm, wexp),
        (normed_hbm, normed),
        (comp_hbm, comp),
        (place_hbm, place),
        (wl_hbm.at[pl.ds(0, LATENT), cols(t, COLS)], wl.at[pl.ds(0, LATENT)]),
        (
            wl_hbm.at[pl.ds(LATENT, half_rope), cols(t, COLS)],
            wl.at[pl.ds(LATENT, half_rope)],
        ),
        (
            wl_hbm.at[pl.ds(LATENT + half_rope, half_rope), cols(t, COLS)],
            wl.at[pl.ds(LATENT + 2 * half_rope, half_rope)],
        ),
    ]
    early = [pltpu.make_async_copy(src, dst, l_in.at[i]) for i, (src, dst) in enumerate(wide)]
    for c in early:
        c.start()

    order = (far, right, left, t)
    chunks = []
    for k in range(LOCAL):

        def theirs(owner, k=k):
            return part_hbm.at[k, :, cols(owner, COLS)]

        def mine(j, k=k):
            return own[k, j].astype(F32)

        chunks.append(
            sum_stages(
                theirs, mine, ROWS, sib.at[k], half.at[k], full.at[k], p_s.at[k], p_r.at[k], send
            )
        )
    own_loads = {}
    for k in range(LOCAL):
        for j, owner in enumerate(order):
            c = pltpu.make_async_copy(part_hbm.at[k, :, cols(owner, COLS)], own.at[k, j], l_own.at[k, j])
            c.start()
            own_loads[k, j] = c
        chunks[k][0]()

    def forward_2(k):
        for j in range(4):
            own_loads[k, j].wait()
        chunks[k][1]()

    def forward_4(k):
        res[k] = chunks[k][3]().astype(BF16)
        fback[k, seat_rows(e)] = res[k, seat_rows(e)]
        targets = [(res.at[k, seat_rows(to)], fback.at[k, seat_rows(e)], to) for to, frm in peers]
        send_many(targets, fback.at[k, pl.ds(0, OTHERS)], fb_s.at[k], fb_r.at[k], "expert")

    def reduce_pieces(scratch, ref_of, value_of):
        land_a, part, land_b, ss, rs = scratch
        return [
            two_phase(
                lambda dz, dy, i=i: ref_of(i, dz * YN + dy),
                lambda dz, dy, i=i: value_of(i, dz * YN + dy).astype(F32),
                land_a.at[i], part.at[i], land_b.at[i], ss.at[i], rs.at[i], "yz"[i], send_many,
            )
            for i in range(2)
        ]

    def run(pieces, stage):
        return [piece[stage]() for piece in pieces]

    def rows_of(i, n):
        return pl.ds(i * n, n)

    query_sum = reduce_pieces(
        q_red,
        lambda i, d: swq.at[rows_of(i, HEAD), cols(d, 128)],
        lambda i, d: swq[rows_of(i, HEAD), cols(d, 128)],
    )
    expand_sum = reduce_pieces(
        e_red, lambda i, d: swexp.at[d, :, rows_of(i, 256)], lambda i, d: swexp[d, :, rows_of(i, 256)]
    )
    out_sum = reduce_pieces(
        o_red,
        lambda i, d: swout.at[rows_of(i, VDIM), cols(d, 128)],
        lambda i, d: swout[rows_of(i, VDIM), cols(d, 128)],
    )

    mixed = mixed_ref[...]
    for n in range(4):
        s = slice(n * 512, (n + 1) * 512)
        swout[:, s] = dot_tn(mixed, dattn_ref[:, s]).astype(BF16)
    run(out_sum, 0)

    scale = HEAD ** (-0.5)
    cosine, sine = cos_ref[...], sin_ref[...]
    head = lane_head((GROUP, 2 * ROPE))
    dattn = dattn_ref[...]
    dmix = dot_nt(dattn, wout_ref[...]).astype(BF16)
    kr = kr_ref[...]
    qr = q_ref[:, 2 * NOPE :]
    turned = jnp.zeros((GROUP, 2 * ROPE), F32)
    rope_sum = jnp.zeros((GROUP, 2 * ROPE), F32)
    dq_parts = []
    dexp_parts = []
    for h in range(2):
        p = probs_ref[h]
        dm = dmix[:, h * VDIM : (h + 1) * VDIM]
        k = exp_ref[:, 256 * h : 256 * h + NOPE]
        v = exp_ref[:, 256 * h + NOPE : 256 * h + NOPE + VDIM]
        dv = dot_tn(p.astype(BF16), dm)
        dp = dot_nt(dm, v)
        ds = (p * (dp - jnp.sum(dp * p, axis=1, keepdims=True))).astype(BF16)
        dq_parts.append((dot_nn(ds, k) * scale).astype(BF16))
        turned = turned + jnp.where(head == h, dot_nn(ds, kr) * scale, 0.0)
        dk = dot_tn(ds, q_ref[:, h * NOPE : (h + 1) * NOPE]) * scale
        rope_sum = rope_sum + jnp.where(head == h, dot_tn(ds, qr) * scale, 0.0)
        dexp_parts += [dk.astype(BF16), dv.astype(BF16)]
    dexp = jnp.concatenate(dexp_parts, axis=1)
    dq_parts.append(turn(turned, cosine, -sine).astype(BF16))
    dq = dot_nt(jnp.concatenate(dq_parts, axis=1), regroup(BF16)).astype(BF16)

    early[1].wait()
    cpart = dot_nt(dexp, wexp[...])
    share = GROUP // TENSOR
    for i in range(TENSOR):
        r = slice(i * share, (i + 1) * share)
        cbuf[i, :, :LATENT] = cpart[r].astype(BF16)
        cbuf[i, :, LATENT:] = rope_sum[r].astype(BF16)
    for j, (to, frm) in enumerate(others):
        send(cbuf.at[to], cgot.at[t], c_s.at[j], c_r.at[j], "tensor", to)

    early[0].wait()
    for n in range(TENSOR):
        npart[n] = dot_nt(dq, wq[n * COLS : (n + 1) * COLS, :]).astype(BF16)
    n1, n2, n3, n4 = sum_stages(
        lambda owner: npart.at[owner],
        lambda j: npart[order[j]].astype(F32),
        GROUP, nsib, nhalf, nfull, n_s, n_r, send,
    )
    n1()
    forward_2(0)
    forward_2(1)

    early[2].wait()
    for n in range(4):
        s = slice(n * 512, (n + 1) * 512)
        swq[:, s] = dot_tn(dq, normed[:, s]).astype(BF16)
    early[3].wait()
    gwexp = dot_tn(comp[...], dexp)
    for i in range(GROUPS):
        swexp[i] = gwexp[32 * i : 32 * (i + 1)].astype(BF16)
    run(expand_sum, 0)
    run(query_sum, 0)

    total = cbuf[t].astype(F32)
    for j, (to, frm) in enumerate(others):
        got(cgot.at[frm], c_s.at[j], c_r.at[j])
        total = total + cgot[frm].astype(F32)
    mine_rows = pl.ds(pl.multiple_of(t * share, share), share)
    dc = total[:, :LATENT]
    lat = lat_ref[mine_rows, :]
    linv = linv_ref[mine_rows, :]
    lu = dc * gain_row(lgain_ref)
    dot = jnp.sum(lu * lat, axis=1, keepdims=True)
    dlat[t, :, :LATENT] = (linv * lu - lat * (linv * linv * linv * dot * (1.0 / LATENT))).astype(BF16)
    both = total[:, LATENT:]
    both = both + pltpu.roll(both, 2 * ROPE - ROPE // 2, 1)
    both = jnp.where(lane_head((share, 2 * ROPE)) == 0, both, 0.0)
    dlat[t, :, LATENT:] = turn(both, cos_ref[mine_rows, :], -sin_ref[mine_rows, :]).astype(BF16)
    for j, (to, frm) in enumerate(others):
        send(dlat.at[t], dlat.at[t], dl_s.at[j], dl_r.at[j], "tensor", to)
    lgain_row = jnp.sum(dc * lat * linv, axis=0, keepdims=True)

    n2()
    forward_2(2)
    forward_2(3)
    n3()
    chunks[0][2]()

    def undeal_1(value, high, ss, rs):
        high[0] = dot_tn(seat_of_row(seat_ref[...]), value).astype(BF16)
        hop_start(high.at[0], high.at[1], PADCAP, ss, rs, send_many)

    def undeal_2(high, low, ss, rs, ss_next, rs_next):
        hop_wait(high.at[1], PADCAP, ss, rs)
        low[0] = dot_tn(row_of_seat(seat_row_ref[...]), high[1]).astype(BF16)
        hop_start(low.at[0], low.at[1], GROUPS, ss_next, rs_next, send_many)

    def undeal_3(low, ss, rs):
        hop_wait(low.at[1], GROUPS, ss, rs)
        return dot_tn(by_sixteen(), low[1]).astype(BF16)

    for j, (to, frm) in enumerate(others):
        got(dlat.at[frm], dl_s.at[j], dl_r.at[j])
    for i in (5, 6, 7):
        early[i].wait()
    dl = dlat[...].reshape(GROUP, WIDE_LAT)
    latent_cols = dot_nn(dl, wl[...])
    dn = latent_cols + n4()
    xd = x_ref[...].astype(F32)
    inv = inv_ref[...]
    u = dn * own_gain(gain_ref, t)
    finish = sum_rows_start(u * xd, st_buf, st_s, st_r)
    run(out_sum, 1)
    run(expand_sum, 1)
    run(query_sum, 1)
    total = finish()
    chunks[1][2]()
    dx = (dmid_ref[...] + inv * u - xd * (inv * inv * inv * total * (1.0 / D))).astype(BF16)
    undeal_1(dx, xh, xa_s, xa_r)
    chunks[2][2]()
    forward_4(0)
    chunks[3][2]()
    gm[...] = jnp.zeros(gm.shape, F32)
    gm[0:1] = jnp.sum(dn * xd * inv, axis=0, keepdims=True)
    gm[1:2] = ffn_ref[...]
    gm[2:3] = lgain_row[:, :COLS]
    gm[3:4] = lgain_row[:, COLS:]
    gin[e] = gm[...]
    send_many([(gm, gin.at[e], to) for to, frm in peers], gin.at[pl.ds(0, GROUPS - 1)], gm_s, gm_r, "expert")

    pick_rows = lax.broadcasted_iota(jnp.int32, (WIDE_LAT, 128), 0)
    pick_cols = lax.broadcasted_iota(jnp.int32, (WIDE_LAT, 128), 1)
    pick_own = jnp.where((pick_rows == pick_cols + t * SLICE) & (pick_cols < SLICE), 1.0, 0.0).astype(BF16)
    dl_own = dot_nn(dl, pick_own).astype(BF16)
    for n in range(4):
        s = slice(n * 512, (n + 1) * 512)
        swlat[:, s] = dot_tn(dl_own, normed[:, s])[:SLICE].astype(BF16)
    rwlat[e] = swlat[:, cols(e, 128)]
    targets = [(swlat.at[:, cols(to, 128)], rwlat.at[e], to) for to, frm in peers]
    send_many(targets, rwlat.at[pl.ds(0, GROUPS - 1)], w_s, w_r, "expert")

    forward_4(1)
    undeal_2(xh, xl, xa_s, xa_r, xb_s, xb_r)
    forward_4(2)
    forward_4(3)
    early[4].wait()
    routed = mid_ref[...] + shout_ref[...]
    for k in range(LOCAL):
        got(fback.at[k, pl.ds(0, OTHERS)], fb_s.at[k], fb_r.at[k])
        gates = jnp.broadcast_to(gate_ref[k][:, None, :], (GROUPS, PADCAP, GROUP)).reshape(ROWS, GROUP)
        weight = place[k].astype(F32) * gates
        high = weight.astype(BF16)
        low = (weight - high.astype(F32)).astype(BF16)
        routed = routed + dot_tn(high, fback[k]) + dot_tn(low, fback[k])
    out = routed.astype(BF16)
    undeal_1(out, oh, oa_s, oa_r)
    dx_ref[...] = undeal_3(xl, xb_s, xb_r)

    got(gin.at[pl.ds(0, GROUPS - 1)], gm_s, gm_r)
    gains_ref[t] = jnp.sum(gin[...], axis=0)
    for j, (to, frm) in enumerate(others):
        send(gains_ref.at[t], gains_ref.at[t], gt_s.at[j], gt_r.at[j], "tensor", to)
    got(rwlat.at[pl.ds(0, GROUPS - 1)], w_s, w_r)
    lat_sum = rwlat[0].astype(F32)
    for i in range(1, GROUPS):
        lat_sum = lat_sum + rwlat[i].astype(F32)
    lowlat[...] = lat_sum.astype(BF16)
    gwlat_ref[t] = lowlat[...]
    for j, (to, frm) in enumerate(others):
        send(lowlat, gwlat_ref.at[t], wl_s.at[j], wl_r.at[j], "tensor", to)
    undeal_2(oh, ol, oa_s, oa_r, ob_s, ob_r)
    gwout_ref[...] = jnp.concatenate(run(out_sum, 2), axis=0)
    gwq_ref[...] = jnp.transpose(jnp.concatenate(run(query_sum, 2), axis=0))
    gwexp_ref[...] = jnp.concatenate(run(expand_sum, 2), axis=1)
    out_ref[...] = undeal_3(ol, ob_s, ob_r)
    for j, (to, frm) in enumerate(others):
        got(gains_ref.at[frm], gt_s.at[j], gt_r.at[j])
        got(gwlat_ref.at[frm], wl_s.at[j], wl_r.at[j])
    for c in sends:
        c.wait_send()


def back_step(small, large, cid):
    vmem = pltpu.VMEM

    def out(*shape, dtype=BF16):
        return jax.ShapeDtypeStruct(shape, dtype)

    pair = lambda n: [DMA((n,)), DMA((n,))]
    grid_pair = lambda m, n: [DMA((m, n)), DMA((m, n))]
    return pl.pallas_call(
        back_kernel,
        out_shape=(
            out(GROUP, COLS),
            out(GROUP, COLS),
            out(D // GROUPS, 2 * HEAD, dtype=F32),
            out(LATENT // GROUPS, 512, dtype=F32),
            out(2 * VDIM, D // GROUPS, dtype=F32),
            out(TENSOR, SLICE, D // GROUPS),
            out(TENSOR, 8, COLS, dtype=F32),
        ),
        in_specs=[VM] * len(small) + [ANY] * len(large),
        out_specs=(VM,) * 7,
        scratch_shapes=[
            vmem((GROUP, D), BF16),
            vmem((D, 2 * HEAD), BF16),
            vmem((LATENT, 512), BF16),
            vmem((GROUP, LATENT), BF16),
            vmem((WIDE_LAT, COLS), BF16),
            vmem((LOCAL, ROWS, GROUP), BF16),
            vmem((LOCAL, 4, ROWS, COLS), BF16),
            vmem((LOCAL, 4, ROWS, COLS), BF16),
            vmem((LOCAL, 2, ROWS // 2, COLS), BF16),
            vmem((LOCAL, 2, ROWS, COLS), BF16),
            vmem((LOCAL, ROWS, COLS), BF16),
            vmem((LOCAL, ROWS, COLS), BF16),
            vmem((TENSOR, GROUP, COLS), BF16),
            vmem((4, GROUP, COLS), BF16),
            vmem((2, GROUP // 2, COLS), BF16),
            vmem((2, GROUP, COLS), BF16),
            vmem((2 * HEAD, D), BF16),
            vmem((GROUPS, LATENT // GROUPS, 512), BF16),
            vmem((2 * VDIM, D), BF16),
            vmem((SLICE, D), BF16),
            vmem((GROUPS, SLICE, D // GROUPS), BF16),
            vmem((SLICE, D // GROUPS), BF16),
        ]
        + two_phase_scratch(2, HEAD, D // GROUPS)
        + two_phase_scratch(2, LATENT // GROUPS, 256)
        + two_phase_scratch(2, VDIM, D // GROUPS)
        + [
            vmem((TENSOR, GROUP // TENSOR, WIDE_LAT), BF16),
            vmem((TENSOR, GROUP // TENSOR, WIDE_LAT), BF16),
            vmem((TENSOR, GROUP // TENSOR, WIDE_LAT), BF16),
            vmem((8, COLS), F32),
            vmem((GROUPS, 8, COLS), F32),
            vmem((2, ROWS, COLS), BF16),
            vmem((2, ROWS, COLS), BF16),
            vmem((2, GROUP, COLS), BF16),
            vmem((2, GROUP, COLS), BF16),
        ]
        + sum_rows_scratch()
        + grid_pair(LOCAL, 8)
        + pair(LOCAL)
        + pair(8)
        + [DMA] * 2
        + pair(7)
        + pair(7)
        + [DMA] * 2
        + pair(7)
        + pair(7)
        + [DMA] * 8
        + [DMA((8,)), DMA((LOCAL, 4))],
        compiler_params=params(cid, 63),
        name="back_step",
    )(*small, *large)


def gather_stages(source, block, ss, rs, send):
    t, right, left, far, twin = x_peers()
    flip = twin - t

    def put(j, ref, to, src=None):
        send(ref if src is None else src, ref, ss.at[j], rs.at[j], "tensor", to)

    def arrived(j, ref):
        remote(ref, ref, ss.at[j], rs.at[j], "tensor", twin).wait_recv()

    def stage_1():
        put(0, block(t, None), right, source)
        put(1, block(t, None), left, source)
        put(4, block(t, None), twin, source)

    def stage_2():
        arrived(0, block(left, None))
        put(2, block(left, 0), right)
        put(5, block(left, None), twin)
        arrived(1, block(right, None))
        put(3, block(right, 1), left)
        put(6, block(right, None), twin)

    def stage_3():
        arrived(2, block(far, 0))
        put(7, block(far, 0), twin)
        arrived(3, block(far, 1))
        put(8, block(far, 1), twin)

    def stage_4():
        arrived(4, block(twin, None))
        arrived(5, block(left + flip, None))
        arrived(6, block(right + flip, None))
        arrived(7, block(far + flip, 0))
        arrived(8, block(far + flip, 1))

    return stage_1, stage_2, stage_3, stage_4


def column_blocks(ref, rows):
    def block(owner, part):
        r = pl.ds(0, rows) if part is None else pl.ds(part * (rows // 2), rows // 2)
        return ref.at[r, cols(owner, COLS)]

    return block


def gain_row(ref):
    return ref[...].astype(F32).reshape(1, ref.shape[0])


def own_gain(ref, t):
    whole = gain_row(ref)
    total = jnp.zeros((1, COLS), F32)
    for i in range(TENSOR):
        total = total + jnp.where(t == i, whole[:, i * COLS : (i + 1) * COLS], 0.0)
    return total


def iota(shape, dim):
    return lax.broadcasted_iota(jnp.int32, shape, dim)


def deal_in_kernel(lengths, order, group):
    n = lengths.shape[1]
    i, j = iota((n, n), 0), iota((n, n), 1)
    same, before = i == j, j < i

    def column(row):
        return jnp.sum(jnp.where(same, row, 0.0), axis=1, keepdims=True)

    def row(col):
        return jnp.sum(jnp.where(same, col, 0.0), axis=0, keepdims=True)

    def exclusive(values):
        return jnp.sum(jnp.where(before, values, 0.0), axis=1, keepdims=True)

    hit = column(order) == j.astype(F32)
    begins_col = exclusive(lengths)
    begins = row(begins_col)
    dealt_lengths = row(jnp.sum(jnp.where(hit, lengths, 0.0), axis=1, keepdims=True))
    dealt_col = exclusive(dealt_lengths)
    dealt = row(dealt_col)
    dealt_source_col = jnp.sum(jnp.where(hit, begins, 0.0), axis=1, keepdims=True)
    dealt_source = row(dealt_source_col)
    given = jnp.sum(jnp.where(hit, dealt_col, 0.0), axis=0, keepdims=True)
    given_col = column(given)

    def find(rows, lanes, starts, values):
        dim = 1 if lanes else 0
        shape = (GROUP, n) if lanes else (n, GROUP)
        place = jnp.sum(jnp.where(rows >= starts, 1.0, 0.0), axis=dim, keepdims=True) - 1.0
        on = iota(shape, dim).astype(F32) == place
        return place, jnp.sum(jnp.where(on, values, 0.0), axis=dim, keepdims=True)

    first = group * GROUP
    rows = (iota((GROUP, 1), 0) + first).astype(F32)
    rows_row = (iota((1, GROUP), 1) + first).astype(F32)
    which, start = find(rows, True, dealt, dealt)
    unused, shift = find(rows, True, dealt, dealt_source - dealt)
    which_row, shift_row = find(rows_row, False, dealt_col, dealt_source_col - dealt_col)
    source, source_row = rows + shift, rows_row + shift_row

    def rest(value):
        return value - GROUPS * jnp.floor(value * (1.0 / GROUPS))

    ahead = (rest(source) == rest(source_row)) & (source_row < source)
    rank = jnp.sum(jnp.where(ahead, 1.0, 0.0), axis=1, keepdims=True)
    seat = rest(source) * PADCAP + rank

    mine = (iota((GROUP, 1), 0) * GROUPS + group).astype(F32)
    mine_row = (iota((1, GROUP), 1) * GROUPS + group).astype(F32)
    unused, move = find(mine, True, begins, given - begins)
    unused, move_row = find(mine_row, False, begins_col, given_col - begins_col)
    to = jnp.floor((mine + move) * (1.0 / GROUP))
    to_row = jnp.floor((mine_row + move_row) * (1.0 / GROUP))
    ahead = (to == to_row) & (iota((GROUP, GROUP), 0) < iota((GROUP, GROUP), 1))
    rank = jnp.sum(jnp.where(ahead, 1.0, 0.0), axis=0, keepdims=True)
    seat_row = to_row * PADCAP + rank
    return rows - start, which, which_row, seat, seat_row


def front_kernel(
    tok_ref, cot_ref, len_ref, ord_ref, routes_ref, gates_ref, gain_ref, lgain_ref, fgain_ref,
    wq_hbm, wl_hbm, wexp_hbm, wout_hbm,
    xc_ref, dyc_ref, mid_ref, inv2_ref, ncols_ref, normed_ref, inv_ref, q_ref, exp_ref, kr_ref, comp_ref,
    lat_ref, linv_ref, probs_ref, mixed_ref, place_ref, gate_ref, seat_ref, seat_row_ref, cos_ref, sin_ref, dyfull, nfull,
    rown_hbm, grads_hbm,
    hop_a, hop_b, hop_c, hop_d, xfull, wq, wl, wexp, wout, wrope, apart, sib, half, full, gout, dbuf,
    st_buf, st_s, st_r,
    ha_s, ha_r, hb_s, hb_r, xg_s, xg_r, yg_s, yg_r, ng_s, ng_r, gg_s, gg_r, r_s, r_r, d_s, d_r, e_s, e_r, l_in, l_own, l_last,
):
    t, right, left, far, twin = x_peers()
    e, peers = expert_peers()
    greet(
        [("tensor", lax.rem(t + j, TENSOR)) for j in range(1, TENSOR)]
        + [("expert", to) for to, frm in peers]
    )
    sends = []

    def send(src, dst, ssem, rsem, axis, to):
        c = remote(src, dst, ssem, rsem, axis, to)
        c.start()
        sends.append(c)

    def send_many(targets, total, ssem, rsem, axis):
        for src, dst, to in targets:
            remote(src, dst, ssem, rsem, axis, to).start()
        sends.append(remote(total, total, ssem, rsem, axis, targets[0][2]))

    def got(ref, ssem, rsem):
        remote(ref, ref, ssem, rsem, "tensor", twin).wait_recv()

    def local(src, dst, sem):
        c = pltpu.make_async_copy(src, dst, sem)
        c.start()
        return c

    sixteen = by_sixteen()
    hop_a[:, :COLS] = dot_nn(sixteen, tok_ref[...]).astype(BF16)
    hop_a[:, COLS:] = dot_nn(sixteen, cot_ref[...]).astype(BF16)
    hop_start(hop_a, hop_b, GROUPS, ha_s, ha_r, send_many)
    early = [
        local(src, dst, l_in.at[i])
        for i, (src, dst) in enumerate([(wl_hbm, wl), (wq_hbm, wq), (wexp_hbm, wexp), (wout_hbm, wout)])
    ]

    offset, which, which_row, seat, seat_row = deal_in_kernel(
        len_ref[...].astype(F32), ord_ref[...].astype(F32), e
    )
    seat_ref[...] = seat
    seat_row_ref[...] = seat_row

    outward = row_of_seat(seat_row)
    hop_wait(hop_b, GROUPS, ha_s, ha_r)
    hop_c[...] = dot_nn(outward, hop_b[...]).astype(BF16)
    hop_start(hop_c, hop_d, PADCAP, hb_s, hb_r, send_many)
    hr = ROPE // 2
    lane = iota((GROUP, 2 * ROPE), 1)
    power = (lane & (hr - 1)).astype(F32) * (1.0 / hr)
    angle = offset * jnp.exp(power * (-math.log(10000.0)))
    cosine = jnp.cos(angle)
    sine = jnp.sin(angle)
    sine = jnp.where(lane < ROPE, -sine, sine)
    cos_ref[...] = cosine
    sin_ref[...] = sine

    number = iota((EXPERTS, 1), 0)
    expert = (number & 15) * LOCAL + (number >> 4)
    member = jnp.zeros((EXPERTS, GROUP), F32)
    gate_of = jnp.zeros((EXPERTS, GROUP), F32)
    for k in range(TOP):
        hit = routes_ref[k : k + 1, :] == expert
        member = member + jnp.where(hit, 1.0, 0.0)
        gate_of = gate_of + jnp.where(hit, gates_ref[k : k + 1, :], 0.0)
    earlier = jnp.where(iota((GROUP, GROUP), 0) < iota((GROUP, GROUP), 1), 1.0, 0.0).astype(BF16)
    count = dot_nn(member.astype(BF16), earlier)
    slot = jnp.where((member > 0.5) & (count < CAP - 0.5), count, -1.0)
    seats = iota((GROUPS, PADCAP, GROUP), 1).astype(F32)
    slot_gates = []
    for k in range(LOCAL):
        s = slice(k * GROUPS, (k + 1) * GROUPS)
        gate_ref[k] = gate_of[s]
        wide = jnp.broadcast_to(slot[s][:, None, :], (GROUPS, PADCAP, GROUP))
        on = jnp.where(wide == seats, 1.0, 0.0)
        place_ref[k] = on.reshape(ROWS, GROUP).astype(BF16)
        weight = on * jnp.broadcast_to(gate_of[s][:, None, :], (GROUPS, PADCAP, GROUP))
        slot_gates.append(jnp.sum(weight.reshape(ROWS, GROUP), axis=1, keepdims=True))
    early[0].wait()
    for i in range(4):
        row = LATENT + (i // 2) * hr
        wrope[i * hr : (i + 1) * hr] = wl[row : row + hr]
    inward = seat_of_row(seat)
    hop_wait(hop_d, PADCAP, hb_s, hb_r)

    xc_ref[...] = dot_nn(inward, hop_d[:, :COLS]).astype(BF16)
    xfull[:, cols(t, COLS)] = xc_ref[...]
    xg1, xg2, xg3, xg4 = gather_stages(xc_ref, column_blocks(xfull, GROUP), xg_s, xg_r, send)
    xg1()
    dyc_ref[...] = dot_nn(inward, hop_d[:, COLS:]).astype(BF16)
    dyfull[:, cols(t, COLS)] = dyc_ref[...]
    yg1, yg2, yg3, yg4 = gather_stages(dyc_ref, column_blocks(dyfull, GROUP), yg_s, yg_r, send)
    yg1()
    blocks = (t, far)

    def slot_gradients(b):
        for k in range(LOCAL):
            gout[b, k] = (slot_gates[k] * dot_nn(place_ref[k], dyfull[:, cols(blocks[b], COLS)])).astype(BF16)

    own_grads = {}

    def send_gradients(p, b):
        two = pl.ds(2 * p, 2)
        landed = grads_hbm.at[two, seat_rows(e), cols(blocks[b], COLS)]
        own_grads[p, b] = local(gout.at[b, two, seat_rows(e)], landed, l_own.at[p, b])
        targets = [(gout.at[b, two, seat_rows(to)], landed, to) for to, frm in peers]
        send_many(targets, gout.at[b, two, pl.ds(0, OTHERS)], d_s.at[p, b], d_r.at[p, b], "expert")

    slot_gradients(0)
    send_gradients(0, 0)
    send_gradients(1, 0)
    xg2()
    yg2()
    xg3()
    yg3()
    slot_gradients(1)
    send_gradients(0, 1)
    send_gradients(1, 1)
    xg4()

    xd = xfull[...].astype(F32)
    inv = lax.rsqrt(jnp.sum(xd * xd, axis=1, keepdims=True) * (1.0 / D) + EPS)
    inv_ref[...] = inv
    normed = (xd * inv * gain_row(gain_ref)).astype(BF16)
    normed_ref[...] = normed
    lat = dot_nt(normed, wl[:LATENT])
    lat_ref[...] = lat
    linv = lax.rsqrt(jnp.sum(lat * lat, axis=1, keepdims=True) * (1.0 / LATENT) + EPS)
    linv_ref[...] = linv
    kr = turn(dot_nt(normed, wrope[...]), cosine, sine).astype(BF16)
    kr_ref[...] = kr
    early[1].wait()
    pre = lax.dot_general(
        dot_nn(normed, wq[...]),
        regroup(F32),
        (((1,), (0,)), ((), ())),
        precision=lax.Precision.HIGHEST,
        preferred_element_type=F32,
    )
    q_ref[:, : 2 * NOPE] = pre[:, : 2 * NOPE].astype(BF16)
    qr = turn(pre[:, 2 * NOPE :], cosine, sine)
    q_ref[:, 2 * NOPE :] = qr.astype(BF16)
    comp = (lat * linv * gain_row(lgain_ref)).astype(BF16)
    comp_ref[...] = comp
    early[2].wait()
    expanded = dot_nn(comp, wexp[...]).astype(BF16)
    exp_ref[...] = expanded

    def grad_block(k):
        return lambda owner: grads_hbm.at[k, :, cols(owner, COLS)]

    spread = [near_stages(grad_block(k), gg_s.at[k], gg_r.at[k], send) for k in range(LOCAL)]
    seen = set()

    def gradients(k, b):
        p = k // 2
        if (p, b) not in seen:
            seen.add((p, b))
            own_grads[p, b].wait()
            got(gout.at[b, pl.ds(2 * p, 2), pl.ds(0, OTHERS)], d_s.at[p, b], d_r.at[p, b])
        spread[k][b]()

    head = lane_head((GROUP, 2 * ROPE))
    allowed = (which == which_row) & (iota((GROUP, GROUP), 0) >= iota((GROUP, GROUP), 1))
    scale = HEAD ** (-0.5)
    for h in range(2):
        q = q_ref[:, h * NOPE : (h + 1) * NOPE]
        k = expanded[:, 256 * h : 256 * h + NOPE]
        v = expanded[:, 256 * h + NOPE : 256 * h + NOPE + VDIM]
        turned = jnp.where(head == h, qr, 0.0).astype(BF16)
        raw = (dot_nt(q, k) + dot_nt(turned, kr)) * scale
        scores = jnp.where(allowed, raw, -1e30)
        expo = jnp.exp(scores - jnp.max(scores, axis=1, keepdims=True))
        probs = expo / jnp.sum(expo, axis=1, keepdims=True)
        probs_ref[h] = probs
        mixed_ref[:, h * VDIM : (h + 1) * VDIM] = dot_nn(probs.astype(BF16), v).astype(BF16)
    mixed = mixed_ref[...]
    early[3].wait()
    for n in range(TENSOR):
        apart[n] = dot_nn(mixed, wout[:, n * COLS : (n + 1) * COLS]).astype(BF16)

    order = (far, right, left, t)
    r1, r2, r3, r4 = sum_stages(
        lambda owner: apart.at[owner],
        lambda j: apart[order[j]].astype(F32),
        GROUP, sib, half, full, r_s, r_r, send,
    )
    r1()
    gradients(0, 0)
    r2()
    r3()
    gradients(1, 0)
    mid = xc_ref[...].astype(F32) + r4()
    mid_ref[...] = mid
    finish = sum_rows_start(mid * mid, st_buf, st_s, st_r)
    spread[0][2]()
    inv2 = lax.rsqrt(finish() * (1.0 / D) + EPS)
    inv2_ref[...] = inv2
    ncols_ref[...] = (mid * inv2 * own_gain(fgain_ref, t)).astype(BF16)
    nfull[:, cols(t, COLS)] = ncols_ref[...]
    ng1, ng2, ng3, ng4 = gather_stages(ncols_ref, column_blocks(nfull, GROUP), ng_s, ng_r, send)
    ng1()
    own_rows = {}

    def dispatch(b):
        for p in range(2):
            for k in (2 * p, 2 * p + 1):
                dbuf[b, k] = dot_nn(place_ref[k], nfull[:, cols(blocks[b], COLS)]).astype(BF16)
            two = pl.ds(2 * p, 2)
            landed = rown_hbm.at[b, two, seat_rows(e)]
            own_rows[p, b] = local(dbuf.at[b, two, seat_rows(e)], landed, l_last.at[p, b])
            targets = [(dbuf.at[b, two, seat_rows(to)], landed, to) for to, frm in peers]
            send_many(targets, dbuf.at[b, two, pl.ds(0, OTHERS)], e_s.at[p, b], e_r.at[p, b], "expert")

    dispatch(0)
    gradients(2, 0)
    gradients(0, 1)
    gradients(1, 1)
    spread[1][2]()
    ng2()
    gradients(3, 0)
    gradients(2, 1)
    gradients(3, 1)
    ng3()
    dispatch(1)
    spread[2][2]()
    yg4()
    ng4()
    spread[3][2]()
    for k in range(LOCAL):
        spread[k][3]()
    for p in range(2):
        for b in range(2):
            own_rows[p, b].wait()
            got(dbuf.at[b, pl.ds(2 * p, 2), pl.ds(0, OTHERS)], e_s.at[p, b], e_r.at[p, b])
    for c in sends:
        c.wait_send()


def front_step(small, large, cid):
    vmem = pltpu.VMEM

    def out(*shape, dtype=BF16):
        return jax.ShapeDtypeStruct(shape, dtype)

    def pair(*shape):
        return [DMA(shape), DMA(shape)]

    return pl.pallas_call(
        front_kernel,
        out_shape=(
            out(GROUP, COLS),
            out(GROUP, COLS),
            out(GROUP, COLS, dtype=F32),
            out(GROUP, 1, dtype=F32),
            out(GROUP, COLS),
            out(GROUP, D),
            out(GROUP, 1, dtype=F32),
            out(GROUP, 2 * HEAD),
            out(GROUP, 512),
            out(GROUP, 2 * ROPE),
            out(GROUP, LATENT),
            out(GROUP, LATENT, dtype=F32),
            out(GROUP, 1, dtype=F32),
            out(2, GROUP, GROUP, dtype=F32),
            out(GROUP, 2 * VDIM),
            out(LOCAL, ROWS, GROUP),
            out(LOCAL, GROUPS, GROUP, dtype=F32),
            out(GROUP, 1, dtype=F32),
            out(1, GROUP, dtype=F32),
            out(GROUP, 2 * ROPE, dtype=F32),
            out(GROUP, 2 * ROPE, dtype=F32),
            out(GROUP, D),
            out(GROUP, D),
            out(2, LOCAL, ROWS, COLS),
            out(LOCAL, ROWS, D),
        ),
        in_specs=[VM] * len(small) + [ANY] * len(large),
        out_specs=(VM,) * 23 + (ANY,) * 2,
        scratch_shapes=[
            vmem((GROUP, 2 * COLS), BF16),
            vmem((GROUP, 2 * COLS), BF16),
            vmem((ROWS, 2 * COLS), BF16),
            vmem((ROWS, 2 * COLS), BF16),
            vmem((GROUP, D), BF16),
            vmem((D, 2 * HEAD), BF16),
            vmem((LATENT + ROPE, D), BF16),
            vmem((LATENT, 512), BF16),
            vmem((2 * VDIM, D), BF16),
            vmem((2 * ROPE, D), BF16),
            vmem((TENSOR, GROUP, COLS), BF16),
            vmem((4, GROUP, COLS), BF16),
            vmem((2, GROUP // 2, COLS), BF16),
            vmem((2, GROUP, COLS), BF16),
            vmem((2, LOCAL, ROWS, COLS), BF16),
            vmem((2, LOCAL, ROWS, COLS), BF16),
        ]
        + sum_rows_scratch()
        + [DMA] * 4
        + pair(9)
        + pair(9)
        + pair(9)
        + pair(LOCAL, 6)
        + pair(8)
        + pair(2, 2)
        + pair(2, 2)
        + [DMA((4,)), DMA((2, 2)), DMA((2, 2))],
        compiler_params=params(cid, 60),
        name="front_step",
    )(*small, *large)


def finish_kernel(
    gg_ref, gu_ref, gd_ref, wsum_ref, out_in, dx_in, gwq_in, gwexp_in, gwout_in, gwlat_in, gains_in,
    ogg_ref, ogu_ref, ogd_ref, sg_ref, su_ref, sd_ref, out_ref, dx_ref, gwq_ref, gwexp_ref, gwout_ref, gwlat_ref,
    attn_ref, ffn_ref, lgain_ref,
):
    ogg_ref[...] = gg_ref[...].astype(F32)
    ogu_ref[...] = gu_ref[...].astype(F32)
    ogd_ref[...] = gd_ref[...].astype(F32)

    @pl.when((pl.program_id(0) == 0) & (pl.program_id(1) == 0))
    def small():
        e = lax.axis_index("expert")
        sg_ref[...] = wsum_ref[0]
        su_ref[...] = wsum_ref[1]
        sd_ref[...] = wsum_ref[2]
        out_ref[...] = out_in[...]
        dx_ref[...] = dx_in[...]
        gwq_ref[...] = gwq_in[...]
        gwexp_ref[...] = gwexp_in[...]
        gwout_ref[...] = gwout_in[...]
        lat = gwlat_in[...].astype(F32).reshape(WIDE_LAT, D // GROUPS)
        half = ROPE // 2
        gwlat_ref[: LATENT + half] = lat[: LATENT + half]
        gwlat_ref[LATENT + half :] = lat[LATENT + ROPE : LATENT + ROPE + half]
        own = gains_in[e // 2]
        side = lax.rem(e, 2) == 0
        attn_ref[...] = jnp.where(side, own[0:1, :128], own[0:1, 128:])
        ffn_ref[...] = jnp.where(side, own[1:2, :128], own[1:2, 128:])
        rows = jnp.sum(gains_in[...], axis=0)[2:4]
        row = jnp.where(e < 8, rows[0:1], rows[1:2])
        wanted = iota((COLS, 128), 1) + lax.rem(e, 8) * (LATENT // GROUPS)
        pick_own = jnp.where(iota((COLS, 128), 0) == wanted, 1.0, 0.0)
        lgain_ref[...] = lax.dot_general(
            row, pick_own, (((1,), (0,)), ((), ())),
            precision=lax.Precision.HIGHEST, preferred_element_type=F32,
        )


def finish_step(grads, rest):
    def out(*shape, dtype=F32):
        return jax.ShapeDtypeStruct(shape, dtype)

    hid = grads[0].shape[1]
    wide = rest[0].shape[1]
    block = pl.BlockSpec((1, hid, D // 2), lambda i, j: (i, 0, j))

    def whole(shape):
        return pl.BlockSpec(shape, lambda i, j: (0,) * len(shape))

    outs = (
        out(wide, 128), out(wide, 128), out(wide, 128), out(GROUP, COLS, dtype=BF16), out(GROUP, COLS, dtype=BF16),
        out(128, 2 * HEAD), out(LATENT // GROUPS, 512), out(2 * VDIM, 128), out(LATENT + ROPE, 128),
        out(1, 128), out(1, 128), out(1, 128),
    )
    return pl.pallas_call(
        finish_kernel,
        grid=(LOCAL, 2),
        out_shape=(out(LOCAL, hid, D),) * 3 + outs,
        in_specs=[block] * 3 + [whole(a.shape) for a in rest],
        out_specs=(block,) * 3 + tuple(whole(o.shape) for o in outs),
        compiler_params=pltpu.CompilerParams(vmem_limit_bytes=63 * MIB),
        name="finish_step",
    )(*grads, *rest)


def per_device(
    tokens,
    cotangent,
    attn_gain,
    w_query,
    w_latent,
    latent_gain,
    w_expand,
    w_out,
    ffn_gain,
    shared_gate,
    shared_up,
    shared_down,
    expert_gate,
    expert_up,
    expert_down,
    seq_lengths,
    seq_order,
    routes,
    gate_weights,
):
    wlat_t = w_latent.T
    attn_row, ffn_row, lgain = attn_gain, ffn_gain, latent_gain

    (
        x_cols, dy_cols, middle, inv_two, normed_two_cols, normed, inv_one, query, expanded, key_rope, compressed,
        latent, inv_lat, probs, mixed, place, gate_of, seat, seat_row, cosine, sine, dy_full, normed_two, own_slots, grad_rows
    ) = front_step(
        (
            tokens,
            cotangent,
            seq_lengths.reshape(1, -1),
            seq_order.reshape(1, -1),
            routes.T,
            gate_weights.T,
            attn_row,
            lgain,
            ffn_row,
        ),
        (w_query, wlat_t, w_expand, w_out),
        1,
    )

    (
        part, grad_eg, grad_eu, grad_ed, shared_out, dmid, dgain_ffn, d_attn, unused, shared_weights
    ) = moe_step(
        place,
        own_slots,
        normed_two,
        dy_full,
        shared_gate.T,
        shared_up.T,
        shared_down,
        jnp.swapaxes(expert_gate, 1, 2),
        jnp.swapaxes(expert_up, 1, 2),
        expert_down,
        grad_rows,
        middle,
        inv_two,
        ffn_row,
        dy_cols,
        3,
    )
    output, input_grad, grad_wq, grad_wexp, grad_wout, grad_wlat, gains = back_step(
        (
            d_attn,
            mixed,
            w_out,
            query,
            expanded,
            key_rope,
            probs,
            cosine,
            sine,
            latent,
            inv_lat,
            lgain,
            x_cols,
            inv_one,
            attn_row,
            dmid,
            dgain_ffn,
            middle,
            shared_out,
            gate_of,
            seat,
            seat_row,
        ),
        (place, normed, w_query, w_expand, compressed, wlat_t, part),
        4,
    )
    (
        grad_eg, grad_eu, grad_ed, sg, su, sd, output, input_grad, grad_wq, grad_wexp, grad_wout, grad_wlat,
        attn_out, ffn_out, lgain_out
    ) = finish_step(
        (grad_eg, grad_eu, grad_ed),
        (shared_weights, output, input_grad, grad_wq, grad_wexp, grad_wout, grad_wlat, gains),
    )
    return (
        output,
        input_grad,
        attn_out[0],
        grad_wq,
        grad_wlat.T,
        lgain_out[0, : LATENT // GROUPS],
        grad_wexp,
        grad_wout,
        ffn_out[0],
        sg.T,
        su.T,
        sd,
        jnp.swapaxes(grad_eg, 1, 2),
        jnp.swapaxes(grad_eu, 1, 2),
        grad_ed,
    )


def solution(mesh):
    return jax.shard_map(
        per_device,
        mesh=mesh,
        in_specs=(
            P("expert", "tensor"),
            P("expert", "tensor"),
            P(),
            P(None, "tensor"),
            P(),
            P(),
            P(None, "tensor"),
            P("tensor", None),
            P(),
            P(None, "tensor"),
            P(None, "tensor"),
            P("tensor", None),
            P("expert", None, "tensor"),
            P("expert", None, "tensor"),
            P("expert", "tensor", None),
            P(),
            P(),
            P("expert", None),
            P("expert", None),
        ),
        out_specs=(
            P("expert", "tensor"),
            P("expert", "tensor"),
            P("expert"),
            P("expert", "tensor"),
            P("expert", None),
            P("expert"),
            P("expert", "tensor"),
            P("tensor", "expert"),
            P("expert"),
            P("expert", "tensor"),
            P("expert", "tensor"),
            P("tensor", "expert"),
            P("expert", None, "tensor"),
            P("expert", None, "tensor"),
            P("expert", "tensor", None),
        ),
        check_vma=False,
    )
```

```python
import math

import jax
import jax.numpy as jnp
from jax import lax
from jax.experimental import pallas as pl
from jax.experimental.pallas import tpu as pltpu
from jax.sharding import PartitionSpec as P

NOPE = 128
ROPE = 64
HEAD = NOPE + ROPE
LATENT = 512
VDIM = 128
D = 2048
GROUP = 256
TOP = 6
EXPERTS = 64
GROUPS = 16
LOCAL = 4
CAP = 27
PADCAP = 32
TENSOR = 8
COLS = D // TENSOR
EPS = 1e-06

XN = 4
YN = 4
ZN = 4
CORES = 2

F32 = jnp.float32
BF16 = jnp.bfloat16
MESH = pl.DeviceIdType.MESH
ANY = pl.BlockSpec(memory_space=pl.ANY)
VM = pl.BlockSpec(memory_space=pltpu.VMEM)
DMA = pltpu.SemaphoreType.DMA
MIB = 1024 * 1024


def remote(src, dst, ssem, rsem, axis, index):
    return pltpu.make_async_remote_copy(
        src_ref=src,
        dst_ref=dst,
        send_sem=ssem,
        recv_sem=rsem,
        device_id={axis: index},
        device_id_type=MESH,
    )


def greet(peers):
    barrier = pltpu.get_barrier_semaphore()
    for axis, index in peers:
        pl.semaphore_signal(barrier, inc=1, device_id={axis: index}, device_id_type=MESH)
    pl.semaphore_wait(barrier, len(peers))


def params(cid, vmem=48.0):
    return pltpu.CompilerParams(
        collective_id=cid, has_side_effects=True, vmem_limit_bytes=int(vmem * MIB)
    )


def x_peers():
    t = lax.axis_index("tensor")
    x = t // CORES
    c = lax.rem(t, CORES)
    right = lax.rem(x + 1, XN) * CORES + c
    left = lax.rem(x + XN - 1, XN) * CORES + c
    far = lax.rem(x + 2, XN) * CORES + c
    twin = x * CORES + (1 - c)
    return t, right, left, far, twin


def greet_x():
    t, right, left, far, twin = x_peers()
    greet([("tensor", right), ("tensor", left), ("tensor", twin)])


def greet_tensor():
    t = lax.axis_index("tensor")
    greet([("tensor", lax.rem(t + j, TENSOR)) for j in range(1, TENSOR)])


def cols(index, width):
    return pl.ds(pl.multiple_of(index * width, width), width)


def sum_rows_start(value, buf, ssem, rsem):
    t = lax.axis_index("tensor")
    rows = value.shape[0]
    mine = jnp.broadcast_to(jnp.sum(value, axis=1, keepdims=True), (rows, 128))
    buf[t] = jnp.transpose(mine)[:8]
    sends = []
    for j in range(1, TENSOR):
        to = lax.rem(t + j, TENSOR)
        c = remote(buf.at[t], buf.at[t], ssem.at[j], rsem.at[j], "tensor", to)
        c.start()
        sends.append(c)

    def finish():
        for j in range(1, TENSOR):
            ref = buf.at[lax.rem(t + TENSOR - j, TENSOR)]
            remote(ref, ref, ssem.at[j], rsem.at[j], "tensor", t).wait_recv()
        total = jnp.sum(buf[...], axis=0)
        for s in sends:
            s.wait_send()
        return jnp.transpose(total)[:, :1]

    return finish


def sum_rows_tensor(value, buf, ssem, rsem):
    return sum_rows_start(value, buf, ssem, rsem)()


def sum_rows_scratch():
    return [pltpu.VMEM((TENSOR, 8, GROUP), F32), DMA((TENSOR,)), DMA((TENSOR,))]


def dot_nn(a, b):
    return lax.dot_general(a, b, (((1,), (0,)), ((), ())), preferred_element_type=F32)


def dot_nt(a, b):
    return lax.dot_general(a, b, (((1,), (1,)), ((), ())), preferred_element_type=F32)


def dot_tn(a, b):
    return lax.dot_general(a, b, (((0,), (0,)), ((), ())), preferred_element_type=F32)


ROWS = GROUPS * PADCAP
OTHERS = ROWS - PADCAP
EARLY = 2


def expert_peers():
    e = lax.axis_index("expert")
    z = e // YN
    y = lax.rem(e, YN)
    peers = []
    for dz in range(ZN):
        for dy in range(YN):
            if dz or dy:
                to = lax.rem(z + dz, ZN) * YN + lax.rem(y + dy, YN)
                frm = lax.rem(z + ZN - dz, ZN) * YN + lax.rem(y + YN - dy, YN)
                peers.append((to, frm))
    return e, peers


def seat_rows(index):
    return pl.ds(pl.multiple_of(index * PADCAP, PADCAP), PADCAP)


def moe_kernel(
    place_ref, rown_hbm, nfull_hbm, dy_hbm, sg_hbm, su_hbm, sd_hbm, wg_hbm, wu_hbm, wd_hbm, grads_hbm,
    mid_ref, inv_ref, gain_ref, dyc_ref,
    part_hbm, gg_hbm, gu_hbm, gd_hbm, shout_ref, dmid_ref, dgain_ref, dattn_hbm, wsend_hbm, p_res, wsum_ref,
    sh_ref, dsg_ref, dsu_ref, nfull, dyf, rows, drows, sib, half, full, wbuf, gbuf, gout, pbuf, res, back, shsum, low,
    a_s, a_r, r_s, r_r, b_s, b_r, f_s, f_r, st_buf, st_s, st_r, l_in, l_w, l_g, l_out, l_own, l_sh, l_first,
    wown, w_a, w_p, w_b, w_s, w_r, l_wn,
    p_own, p_sib, p_half, p_full, p_s, p_r, l_p,
):
    t, right, left, far, twin = x_peers()
    flip = twin - t
    e, peers = expert_peers()
    greet(
        [("tensor", lax.rem(t + j, TENSOR)) for j in range(1, TENSOR)]
        + [("expert", to) for to, frm in peers]
    )
    sends = []

    def send(src, dst, ssem, rsem, axis, to):
        c = remote(src, dst, ssem, rsem, axis, to)
        c.start()
        sends.append(c)

    def send_many(targets, total, ssem, rsem, axis):
        for src, dst, to in targets:
            remote(src, dst, ssem, rsem, axis, to).start()
        sends.append(remote(total, total, ssem, rsem, axis, targets[0][2]))

    def got(ref, ssem, rsem):
        remote(ref, ref, ssem, rsem, "tensor", twin).wait_recv()

    blocks = (t, far)
    own_copies = []
    for k in range(LOCAL):
        for b in range(2):
            c = pltpu.make_async_copy(
                rown_hbm.at[b, k], rows.at[k, :, cols(blocks[b], COLS)], l_first.at[k, b]
            )
            c.start()
            own_copies.append(c)
    wide = sd_hbm.shape[0]
    sgv, suv, sdv = (drows.at[i, pl.ds(0, wide)] for i in range(3))
    early = [
        pltpu.make_async_copy(src, dst, l_in.at[i])
        for i, (src, dst) in enumerate(
            [(nfull_hbm, nfull), (sg_hbm, sgv), (su_hbm, suv), (sd_hbm, sdv), (dy_hbm, dyf)]
        )
    ]
    for c in early:
        c.start()

    def load(k):
        s = k % 2
        copies = [
            pltpu.make_async_copy(ref.at[k], wbuf.at[s, i], l_w.at[s, i])
            for i, ref in enumerate((wg_hbm, wu_hbm, wd_hbm))
        ]
        for c in copies:
            c.start()
        return copies

    loads = {0: load(0)}

    grad_loads = [pltpu.make_async_copy(grads_hbm.at[k], gbuf.at[k % 3], l_g.at[k]) for k in range(LOCAL)]
    grad_loads[0].start()

    h = ROWS // 2

    def row_block(k):
        return lambda owner: rows.at[k, :, cols(owner, COLS)]

    near = [near_stages(row_block(k), a_s.at[k], a_r.at[k], send) for k in range(LOCAL)]

    def gather_1(k):
        for b in range(2):
            own_copies[2 * k + b].wait()
            near[k][b]()

    def gather_2(k):
        near[k][2]()

    def gather_4(k):
        near[k][3]()

    back_copies = {}

    order = (far, right, left, t)

    def slot(k):
        return k

    def rsend(k, j, src, dst, to):
        send(src, dst, r_s.at[k, j], r_r.at[k, j], "tensor", to)

    def rgot(k, j, ref):
        got(ref, r_s.at[k, j], r_r.at[k, j])

    def mine(k, j):
        return drows[slot(k), :, cols(order[j], COLS)].astype(F32)

    twin_sends = {}

    def sum_1(k):
        first = len(sends)
        for j, owner in enumerate(order):
            rsend(k, j, drows.at[slot(k), :, cols(owner + flip, COLS)], sib.at[k, j], twin)
        twin_sends[k] = sends[first:]
        del sends[first:]

    def sum_2(k):
        rgot(k, 0, sib.at[k, 0])
        sib[k, 0] = (mine(k, 0) + sib[k, 0].astype(F32)).astype(BF16)
        rsend(k, 4, sib.at[k, 0, pl.ds(0, h)], half.at[k, 0], right)
        rsend(k, 5, sib.at[k, 0, pl.ds(h, h)], half.at[k, 1], left)

    def sum_3(k):
        for j, to in ((1, right), (2, left)):
            rgot(k, j, sib.at[k, j])
            rgot(k, 3 + j, half.at[k, j - 1])
            both = mine(k, j) + sib[k, j].astype(F32)
            extra = half[k, j - 1].astype(F32)
            if j == 1:
                sib[k, j, :h] = (both[:h] + extra).astype(BF16)
                sib[k, j, h:] = both[h:].astype(BF16)
            else:
                sib[k, j, :h] = both[:h].astype(BF16)
                sib[k, j, h:] = (both[h:] + extra).astype(BF16)
            rsend(k, 5 + j, sib.at[k, j], full.at[k, j - 1], to)

    def sum_4(k):
        rgot(k, 3, sib.at[k, 3])
        rgot(k, 6, full.at[k, 0])
        rgot(k, 7, full.at[k, 1])
        value = mine(k, 3) + sib[k, 3].astype(F32) + full[k, 0].astype(F32) + full[k, 1].astype(F32)
        for c in twin_sends[k]:
            c.wait_send()
        if k == LOCAL:
            shsum[...] = value
            return
        res[k] = value.astype(BF16)
        c = pltpu.make_async_copy(res.at[k, seat_rows(e)], back.at[k, seat_rows(e)], l_own.at[k])
        c.start()
        back_copies[k] = c
        targets = [(res.at[k, seat_rows(to)], back.at[k, seat_rows(e)], to) for to, frm in peers]
        send_many(targets, back.at[k, pl.ds(0, OTHERS)], b_s.at[k], b_r.at[k], "expert")

    def shared_forward():
        for c in early[:4]:
            c.wait()
        n = nfull[...]
        g = dot_nt(n, sgv[...])
        u = dot_nt(n, suv[...])
        sig = jax.nn.sigmoid(g)
        silu = g * sig
        sh_ref[...] = (silu * u).astype(BF16)
        return g, u, sig, silu

    def shared_backward(g, u, sig, silu):
        early[4].wait()
        dh = dot_nt(dyf[...], sdv[...])
        dsg_ref[...] = (dh * u * (sig * (1.0 + g * (1.0 - sig)))).astype(BF16)
        dsu_ref[...] = (dh * silu).astype(BF16)

    tiles = [pl.ds(i * 512, 512) for i in range(D // 512)]

    def shared_rows():
        hid = sh_ref[...]
        dsg, dsu = dsg_ref[...], dsu_ref[...]
        for n in tiles:
            drows[LOCAL, :GROUP, n] = dot_nn(hid, sdv[:, n]).astype(BF16)
            drows[LOCAL, GROUP:, n] = (dot_nn(dsg, sgv[:, n]) + dot_nn(dsu, suv[:, n])).astype(BF16)

    stages = (drows.at[1], drows.at[2], pbuf)
    staged = []

    def shared_weights():
        pairs = ((dsg_ref, nfull), (dsu_ref, nfull), (sh_ref, dyf))
        for i, (lhs, rhs) in enumerate(pairs):
            for n in tiles:
                stages[i][:wide, n] = dot_tn(lhs[...], rhs[:, n]).astype(BF16)
            c = pltpu.make_async_copy(stages[i].at[pl.ds(0, wide)], wsend_hbm.at[i], l_sh.at[i])
            c.start()
            staged.append(c)
            for p in range(2):
                for j in range(4):
                    d = j * YN + lax.rem(e, YN) if p == 0 else (e // YN) * YN + j
                    c = pltpu.make_async_copy(
                        stages[i].at[pl.ds(p * wide // 2, wide // 2), cols(d, 128)],
                        wown.at[2 * i + p, j],
                        l_wn.at[2 * i + p, j],
                    )
                    c.start()
                    staged.append(c)

    def piece_ref(i, p):
        return lambda dz, dy: wsend_hbm.at[i, pl.ds(p * wide // 2, wide // 2), cols(dz * YN + dy, 128)]

    def piece_own(i, p):
        return lambda dz, dy: wown[2 * i + p, dz if p == 0 else dy].astype(F32)

    shared_sums = [
        two_phase(
            piece_ref(n // 2, n % 2), piece_own(n // 2, n % 2),
            w_a.at[n], w_p.at[n], w_b.at[n], w_s.at[n], w_r.at[n], "yz"[n % 2], send_many,
        )
        for n in range(6)
    ]

    out_copies = {}

    def compute_1(k):
        s = k % 2
        for c in loads[k] + [grad_loads[k]]:
            c.wait()
        r = rows[k]
        gate = dot_nt(r, wbuf[s, 0])
        up = dot_nt(r, wbuf[s, 1])
        dh = dot_nt(gbuf[k % 3], wbuf[s, 2])
        sig = jax.nn.sigmoid(gate)
        silu = gate * sig
        hidden = (silu * up).astype(BF16)
        dg = (dh * up * (sig * (1.0 + gate * (1.0 - sig)))).astype(BF16)
        du = (dh * silu).astype(BF16)
        for n in tiles:
            drows[slot(k), :, n] = (
                dot_nn(dg, wbuf[s, 0, :, n]) + dot_nn(du, wbuf[s, 1, :, n])
            ).astype(BF16)
        return hidden, dg, du

    def compute_2(k, hidden, dg, du):
        s = k % 2
        if k:
            for c in out_copies[k - 1]:
                c.wait()
        for n in tiles:
            pbuf[:, n] = dot_nn(hidden, wbuf[s, 2, :, n]).astype(BF16)
            gout[0, :, n] = dot_tn(dg, rows[k, :, n]).astype(BF16)
            gout[1, :, n] = dot_tn(du, rows[k, :, n]).astype(BF16)
            gout[2, :, n] = dot_tn(hidden, gbuf[k % 3, :, n]).astype(BF16)
        out_copies[k] = [
            pltpu.make_async_copy(src, dst.at[k], l_out.at[i])
            for i, (src, dst) in enumerate(
                [(pbuf, part_hbm), (gout.at[0], gg_hbm), (gout.at[1], gu_hbm), (gout.at[2], gd_hbm)]
            )
        ]
        for c in out_copies[k]:
            c.start()
        if k + 2 < LOCAL:
            loads[k + 2] = load(k + 2)
        if k + 3 < LOCAL:
            grad_loads[k + 3].start()

    forward = [
        sum_stages(
            lambda owner, k=k: part_hbm.at[k, :, cols(owner, COLS)],
            lambda j, k=k: p_own[k, j].astype(F32),
            ROWS, p_sib.at[k], p_half.at[k], p_full.at[k], p_s.at[k], p_r.at[k], send,
        )
        for k in range(EARLY)
    ]
    forward_loads = {}

    def forward_1(k):
        forward_loads[k] = [
            pltpu.make_async_copy(part_hbm.at[k, :, cols(owner, COLS)], p_own.at[k, j], l_p.at[k, j])
            for j, owner in enumerate(order)
        ]
        for c in forward_loads[k]:
            c.start()
        forward[k][0]()

    def forward_2(k):
        for c in forward_loads[k]:
            c.wait()
        forward[k][1]()

    def forward_3(k):
        forward[k][2]()

    def forward_4(k):
        p_res[k] = forward[k][3]().astype(BF16)

    for k in range(LOCAL):
        gather_1(k)
    loads[1] = load(1)
    grad_loads[1].start()
    state = shared_forward()
    shared_backward(*state)
    gather_2(0)
    shared_rows()
    sum_1(4)
    gather_2(1)
    gather_4(0)
    c0 = compute_1(0)
    sum_1(0)
    grad_loads[2].start()
    gather_2(2)
    shared_weights()
    gather_4(1)
    for c in staged:
        c.wait()
    c1 = compute_1(1)
    sum_1(1)
    for piece in shared_sums:
        piece[0]()
    gather_2(3)
    sum_2(0)
    compute_2(0, *c0)
    gather_4(2)
    c2 = compute_1(2)
    sum_1(2)
    sum_3(0)
    sum_2(1)
    compute_2(1, *c1)
    gather_4(3)
    c3 = compute_1(3)
    sum_1(3)
    sum_4(0)
    sum_3(1)
    sum_2(2)
    sum_2(3)
    compute_2(2, *c2)
    forward_1(0)
    forward_1(1)
    sum_2(4)
    sum_4(1)
    sum_3(2)
    sum_3(3)
    compute_2(3, *c3)
    for piece in shared_sums:
        piece[1]()
    sum_3(4)
    sum_4(2)
    forward_2(0)
    forward_2(1)
    sum_4(3)
    sum_4(4)
    shout_ref[...] = shsum[:GROUP]

    dn = shsum[GROUP:]

    def combine(k):
        back_copies[k].wait()
        got(back.at[k, pl.ds(0, OTHERS)], b_s.at[k], b_r.at[k])
        return dot_tn(place_ref[k], back[k])

    for k in range(LOCAL):
        dn = dn + combine(k)

    mid = mid_ref[...]
    inv = inv_ref[...]
    u = dn * own_gain(gain_ref, t)
    finish = sum_rows_start(u * mid, st_buf, st_s, st_r)
    forward_3(0)
    total = finish()
    dmid = dyc_ref[...].astype(F32) + inv * u - mid * (inv * inv * inv * total * (1.0 / D))
    dmid_ref[...] = dmid
    low[...] = dmid.astype(BF16)
    own = pltpu.make_async_copy(low, dattn_hbm.at[:, cols(t, COLS)], l_own.at[0])
    own.start()
    dgain_ref[...] = jnp.sum(dn * mid * inv, axis=0, keepdims=True)
    f1, f2, f3, f4 = gather_stages(low, column_blocks(dattn_hbm, GROUP), f_s.at[0], f_r.at[0], send)
    f1()
    f2()
    forward_3(1)
    f3()
    forward_4(0)
    f4()
    forward_4(1)
    own.wait()
    for c in out_copies[LOCAL - 1]:
        c.wait()
    for n in range(6):
        wsum_ref[n // 2, pl.ds((n % 2) * wide // 2, wide // 2)] = shared_sums[n][2]()
    for c in sends:
        c.wait_send()


def moe_step(place, rown, nfull, dy, sg, su, sd, wg, wu, wd, grads, mid, inv, gain, dyc, cid):
    hid = wd.shape[1]
    wide = sd.shape[0]
    wshape = jax.ShapeDtypeStruct((LOCAL, hid, D), BF16)
    vmem = pltpu.VMEM
    return pl.pallas_call(
        moe_kernel,
        out_shape=(
            jax.ShapeDtypeStruct((LOCAL, ROWS, D), BF16),
            wshape,
            wshape,
            wshape,
            jax.ShapeDtypeStruct((GROUP, COLS), F32),
            jax.ShapeDtypeStruct((GROUP, COLS), F32),
            jax.ShapeDtypeStruct((1, COLS), F32),
            jax.ShapeDtypeStruct((GROUP, D), BF16),
            jax.ShapeDtypeStruct((3, wide, D), BF16),
            jax.ShapeDtypeStruct((EARLY, ROWS, COLS), BF16),
            jax.ShapeDtypeStruct((3, wide, D // GROUPS), F32),
        ),
        in_specs=[VM] + [ANY] * 10 + [VM] * 4,
        out_specs=(ANY, ANY, ANY, ANY, VM, VM, VM, ANY, ANY, VM, VM),
        scratch_shapes=[
            vmem((GROUP, wide), BF16),
            vmem((GROUP, wide), BF16),
            vmem((GROUP, wide), BF16),
            vmem((GROUP, D), BF16),
            vmem((GROUP, D), BF16),
            vmem((LOCAL, ROWS, D), BF16),
            vmem((LOCAL + 1, ROWS, D), BF16),
            vmem((LOCAL + 1, 4, ROWS, COLS), BF16),
            vmem((LOCAL + 1, 2, ROWS // 2, COLS), BF16),
            vmem((LOCAL + 1, 2, ROWS, COLS), BF16),
            vmem((2, 3, hid, D), BF16),
            vmem((3, ROWS, D), BF16),
            vmem((3, hid, D), BF16),
            vmem((ROWS, D), BF16),
            vmem((LOCAL, ROWS, COLS), BF16),
            vmem((LOCAL, ROWS, COLS), BF16),
            vmem((2 * GROUP, COLS), F32),
            vmem((GROUP, COLS), BF16),
            DMA((LOCAL, 6)),
            DMA((LOCAL, 6)),
            DMA((LOCAL + 1, 8)),
            DMA((LOCAL + 1, 8)),
            DMA((LOCAL,)),
            DMA((LOCAL,)),
            DMA((1, 9)),
            DMA((1, 9)),
            vmem((TENSOR, 8, GROUP), F32),
            DMA((TENSOR,)),
            DMA((TENSOR,)),
            DMA((5,)),
            DMA((2, 3)),
            DMA((LOCAL,)),
            DMA((4,)),
            DMA((LOCAL,)),
            DMA((3,)),
            DMA((LOCAL, 2)),
            vmem((6, 4, wide // 2, D // GROUPS), BF16),
        ]
        + two_phase_scratch(6, wide // 2, D // GROUPS)
        + [
            DMA((6, 4)),
            vmem((EARLY, 4, ROWS, COLS), BF16),
            vmem((EARLY, 4, ROWS, COLS), BF16),
            vmem((EARLY, 2, ROWS // 2, COLS), BF16),
            vmem((EARLY, 2, ROWS, COLS), BF16),
            DMA((EARLY, 8)),
            DMA((EARLY, 8)),
            DMA((EARLY, 4)),
        ],
        compiler_params=params(cid, 63.5),
        cost_estimate=pl.CostEstimate(
            flops=40 * 10**9, bytes_accessed=100 * MIB, transcendentals=0
        ),
        name="moe_step",
    )(place, rown, nfull, dy, sg, su, sd, wg, wu, wd, grads, mid, inv, gain, dyc)


def swap_halves(value):
    return pltpu.roll(value, 64, 1)


def turn(value, cosine, sine):
    return value * cosine + swap_halves(value) * sine


def lane_head(shape):
    lane = lax.broadcasted_iota(jnp.int32, shape, 1)
    return (lane >> 5) & 1


def regroup(dtype):
    n = 2 * HEAD
    given = lax.broadcasted_iota(jnp.int32, (n, n), 0)
    made = lax.broadcasted_iota(jnp.int32, (n, n), 1)
    r = made - 2 * NOPE
    turned = ((r >> 5) & 1) * HEAD + NOPE + (r >> 6) * (ROPE // 2) + (r & 31)
    source = jnp.where(made < NOPE, made, jnp.where(made < 2 * NOPE, made + ROPE, turned))
    return jnp.where(given == source, 1.0, 0.0).astype(dtype)


def band(index, rows):
    return pl.ds(pl.multiple_of(index * rows, rows), rows)


def hop_start(src, dst, rows, ss, rs, send_many):
    e, peers = expert_peers()
    dst[band(e, rows)] = src[band(e, rows)]
    targets = [(src.at[band(to, rows)], dst.at[band(e, rows)], to) for to, frm in peers]
    send_many(targets, dst.at[pl.ds(0, 15 * rows)], ss, rs, "expert")


def hop_wait(dst, rows, ss, rs):
    ref = dst.at[pl.ds(0, 15 * rows)]
    remote(ref, ref, ss, rs, "expert", lax.axis_index("expert")).wait_recv()


def one_hot(test):
    return jnp.where(test, 1.0, 0.0).astype(BF16)


def by_sixteen():
    made, given = iota((GROUP, GROUP), 0), iota((GROUP, GROUP), 1)
    return one_hot(given == (made & 15) * GROUPS + (made >> 4))


def seat_of_row(index):
    return one_hot(iota((GROUP, ROWS), 1).astype(F32) == index)


def row_of_seat(index):
    return one_hot(iota((ROWS, GROUP), 0).astype(F32) == index)


def near_stages(block, ss, rs, send):
    t, right, left, far, twin = x_peers()
    flip = twin - t

    def put(j, owner, to):
        send(block(owner), block(owner), ss.at[j], rs.at[j], "tensor", to)

    def arrived(j, owner):
        ref = block(owner)
        remote(ref, ref, ss.at[j], rs.at[j], "tensor", twin).wait_recv()

    def stage_1():
        put(0, t, right)
        put(1, t, left)
        put(2, t, twin)

    def stage_far():
        put(3, far, twin)

    def stage_2():
        arrived(0, left)
        put(4, left, twin)
        arrived(1, right)
        put(5, right, twin)

    def stage_3():
        arrived(2, twin)
        arrived(3, far + flip)
        arrived(4, left + flip)
        arrived(5, right + flip)

    return stage_1, stage_far, stage_2, stage_3


def sum_stages(theirs, mine, rows, sib, half, full, ss, rs, send):
    t, right, left, far, twin = x_peers()
    flip = twin - t
    order = (far, right, left, t)
    h = rows // 2

    def put(j, src, dst, to):
        send(src, dst, ss.at[j], rs.at[j], "tensor", to)

    def arrived(j, ref):
        remote(ref, ref, ss.at[j], rs.at[j], "tensor", twin).wait_recv()

    def stage_1():
        for j, owner in enumerate(order):
            put(j, theirs(owner + flip), sib.at[j], twin)

    def stage_2():
        arrived(0, sib.at[0])
        sib[0] = (mine(0) + sib[0].astype(F32)).astype(sib.dtype)
        put(4, sib.at[0, pl.ds(0, h)], half.at[0], right)
        put(5, sib.at[0, pl.ds(h, h)], half.at[1], left)

    def stage_3():
        for j, to in ((1, right), (2, left)):
            arrived(j, sib.at[j])
            arrived(3 + j, half.at[j - 1])
            both = mine(j) + sib[j].astype(F32)
            extra = half[j - 1].astype(F32)
            if j == 1:
                sib[j, :h] = (both[:h] + extra).astype(sib.dtype)
                sib[j, h:] = both[h:].astype(sib.dtype)
            else:
                sib[j, :h] = both[:h].astype(sib.dtype)
                sib[j, h:] = (both[h:] + extra).astype(sib.dtype)
            put(5 + j, sib.at[j], full.at[j - 1], to)

    def stage_4():
        arrived(3, sib.at[3])
        arrived(6, full.at[0])
        arrived(7, full.at[1])
        return mine(3) + sib[3].astype(F32) + full[0].astype(F32) + full[1].astype(F32)

    return stage_1, stage_2, stage_3, stage_4


def two_phase(src, own, land_a, part, land_b, ss, rs, first, send_many):
    e = lax.axis_index("expert")
    z, y = e // YN, lax.rem(e, YN)
    one, two = (y, z) if first == "y" else (z, y)

    def at(i, j):
        return (j, i) if first == "y" else (i, j)

    def device(i, j):
        dz, dy = at(i, j)
        return dz * YN + dy

    def plus(v, d):
        return lax.rem(v + d, 4)

    def arrived(n, ref):
        remote(ref, ref, ss.at[n], rs.at[n], "expert", e).wait_recv()

    def stage_1():
        targets = []
        for d in (1, 3, 2):
            i = plus(one, d)
            targets += [(src(*at(i, j)), land_a.at[d - 1, j], device(i, two)) for j in range(4)]
        send_many(targets, land_a, ss.at[0], rs.at[0], "expert")

    def stage_2():
        arrived(0, land_a)
        for j in range(4):
            total = own(*at(one, j))
            for d in range(3):
                total = total + land_a[d, j].astype(F32)
            part[j] = total.astype(BF16)
        targets = []
        for d in (1, 3, 2):
            j = plus(two, d)
            targets.append((part.at[j], land_b.at[d - 1], device(one, j)))
        send_many(targets, land_b, ss.at[1], rs.at[1], "expert")

    def stage_3():
        arrived(1, land_b)
        total = part[two].astype(F32)
        for d in range(3):
            total = total + land_b[d].astype(F32)
        return total

    return stage_1, stage_2, stage_3


def two_phase_scratch(pieces, rows, width):
    return [
        pltpu.VMEM((pieces, 3, 4, rows, width), BF16),
        pltpu.VMEM((pieces, 4, rows, width), BF16),
        pltpu.VMEM((pieces, 3, rows, width), BF16),
        DMA((pieces, 2)),
        DMA((pieces, 2)),
    ]


SLICE = 80
WIDE_LAT = LATENT + 2 * ROPE


def back_kernel(
    dattn_ref, mixed_ref, wout_ref, q_ref, exp_ref, kr_ref, probs_ref, cos_ref, sin_ref, lat_ref, linv_ref,
    lgain_ref, x_ref, inv_ref, gain_ref, dmid_ref, ffn_ref, mid_ref, shout_ref, fearly_ref, gate_ref, seat_ref, seat_row_ref,
    place_hbm, normed_hbm, wq_hbm, wexp_hbm, comp_hbm, wl_hbm, part_hbm,
    out_ref, dx_ref, gwq_ref, gwexp_ref, gwout_ref, gwlat_ref, gains_ref,
    normed, wq, wexp, comp, wl, place,
    own, sib, half, full, res, fback,
    npart, nsib, nhalf, nfull,
    swq, swexp, swout, swlat, rwlat, lowlat, *rest
):
    q_red, e_red, o_red, rest = rest[:5], rest[5:10], rest[10:15], rest[15:]
    (
        cbuf, cgot, dlat, gm, gin, xh, oh, xl, ol,
        st_buf, st_s, st_r,
        p_s, p_r, fb_s, fb_r, n_s, n_r, w_s, w_r, c_s, c_r, dl_s, dl_r, gm_s, gm_r, gt_s, gt_r, wl_s, wl_r,
        oa_s, oa_r, ob_s, ob_r, xa_s, xa_r, xb_s, xb_r, l_in, l_own,
    ) = rest
    t, right, left, far, twin = x_peers()
    e, peers = expert_peers()
    others = [(lax.rem(t + j, TENSOR), lax.rem(t + TENSOR - j, TENSOR)) for j in range(1, TENSOR)]
    greet([("tensor", to) for to, frm in others] + [("expert", to) for to, frm in peers])
    sends = []

    def send(src, dst, ssem, rsem, axis, to):
        c = remote(src, dst, ssem, rsem, axis, to)
        c.start()
        sends.append(c)

    def send_many(targets, total, ssem, rsem, axis):
        for src, dst, to in targets:
            remote(src, dst, ssem, rsem, axis, to).start()
        sends.append(remote(total, total, ssem, rsem, axis, targets[0][2]))

    def got(ref, ssem, rsem):
        remote(ref, ref, ssem, rsem, "tensor", twin).wait_recv()

    half_rope = ROPE // 2
    for i in (1, 3):
        wl[LATENT + i * half_rope : LATENT + (i + 1) * half_rope] = jnp.zeros((half_rope, COLS), BF16)
    wide = [
        (wq_hbm, wq),
        (wexp_hbm, wexp),
        (normed_hbm, normed),
        (comp_hbm, comp),
        (place_hbm, place),
        (wl_hbm.at[pl.ds(0, LATENT), cols(t, COLS)], wl.at[pl.ds(0, LATENT)]),
        (
            wl_hbm.at[pl.ds(LATENT, half_rope), cols(t, COLS)],
            wl.at[pl.ds(LATENT, half_rope)],
        ),
        (
            wl_hbm.at[pl.ds(LATENT + half_rope, half_rope), cols(t, COLS)],
            wl.at[pl.ds(LATENT + 2 * half_rope, half_rope)],
        ),
    ]
    early = [pltpu.make_async_copy(src, dst, l_in.at[i]) for i, (src, dst) in enumerate(wide)]
    for c in early:
        c.start()

    order = (far, right, left, t)
    chunks = []
    late = LOCAL - EARLY
    for k in range(late):

        def theirs(owner, k=k):
            return part_hbm.at[EARLY + k, :, cols(owner, COLS)]

        def mine(j, k=k):
            return own[k, j].astype(F32)

        chunks.append(
            sum_stages(
                theirs, mine, ROWS, sib.at[k], half.at[k], full.at[k], p_s.at[k], p_r.at[k], send
            )
        )
    own_loads = {}
    for k in range(late):
        for j, owner in enumerate(order):
            c = pltpu.make_async_copy(
                part_hbm.at[EARLY + k, :, cols(owner, COLS)], own.at[k, j], l_own.at[k, j]
            )
            c.start()
            own_loads[k, j] = c
        chunks[k][0]()

    def return_rows(k, rows):
        fback[k, seat_rows(e)] = rows[seat_rows(e)]
        targets = [(rows.at[seat_rows(to)], fback.at[k, seat_rows(e)], to) for to, frm in peers]
        send_many(targets, fback.at[k, pl.ds(0, OTHERS)], fb_s.at[k], fb_r.at[k], "expert")

    for k in range(EARLY):
        return_rows(k, fearly_ref.at[k])

    def forward_2(k):
        for j in range(4):
            own_loads[k, j].wait()
        chunks[k][1]()

    def forward_4(k):
        res[k] = chunks[k][3]().astype(BF16)
        return_rows(EARLY + k, res.at[k])

    def reduce_pieces(scratch, ref_of, value_of):
        land_a, part, land_b, ss, rs = scratch
        return [
            two_phase(
                lambda dz, dy, i=i: ref_of(i, dz * YN + dy),
                lambda dz, dy, i=i: value_of(i, dz * YN + dy).astype(F32),
                land_a.at[i], part.at[i], land_b.at[i], ss.at[i], rs.at[i], "yz"[i], send_many,
            )
            for i in range(2)
        ]

    def run(pieces, stage):
        return [piece[stage]() for piece in pieces]

    def rows_of(i, n):
        return pl.ds(i * n, n)

    query_sum = reduce_pieces(
        q_red,
        lambda i, d: swq.at[rows_of(i, HEAD), cols(d, 128)],
        lambda i, d: swq[rows_of(i, HEAD), cols(d, 128)],
    )
    expand_sum = reduce_pieces(
        e_red, lambda i, d: swexp.at[d, :, rows_of(i, 256)], lambda i, d: swexp[d, :, rows_of(i, 256)]
    )
    out_sum = reduce_pieces(
        o_red,
        lambda i, d: swout.at[rows_of(i, VDIM), cols(d, 128)],
        lambda i, d: swout[rows_of(i, VDIM), cols(d, 128)],
    )

    mixed = mixed_ref[...]
    for n in range(4):
        s = slice(n * 512, (n + 1) * 512)
        swout[:, s] = dot_tn(mixed, dattn_ref[:, s]).astype(BF16)
    run(out_sum, 0)

    scale = HEAD ** (-0.5)
    cosine, sine = cos_ref[...], sin_ref[...]
    head = lane_head((GROUP, 2 * ROPE))
    dattn = dattn_ref[...]
    dmix = dot_nt(dattn, wout_ref[...]).astype(BF16)
    kr = kr_ref[...]
    qr = q_ref[:, 2 * NOPE :]
    turned = jnp.zeros((GROUP, 2 * ROPE), F32)
    rope_sum = jnp.zeros((GROUP, 2 * ROPE), F32)
    dq_parts = []
    dexp_parts = []
    for h in range(2):
        p = probs_ref[h]
        dm = dmix[:, h * VDIM : (h + 1) * VDIM]
        k = exp_ref[:, 256 * h : 256 * h + NOPE]
        v = exp_ref[:, 256 * h + NOPE : 256 * h + NOPE + VDIM]
        dv = dot_tn(p.astype(BF16), dm)
        dp = dot_nt(dm, v)
        ds = (p * (dp - jnp.sum(dp * p, axis=1, keepdims=True))).astype(BF16)
        dq_parts.append((dot_nn(ds, k) * scale).astype(BF16))
        turned = turned + jnp.where(head == h, dot_nn(ds, kr) * scale, 0.0)
        dk = dot_tn(ds, q_ref[:, h * NOPE : (h + 1) * NOPE]) * scale
        rope_sum = rope_sum + jnp.where(head == h, dot_tn(ds, qr) * scale, 0.0)
        dexp_parts += [dk.astype(BF16), dv.astype(BF16)]
    dexp = jnp.concatenate(dexp_parts, axis=1)
    dq_parts.append(turn(turned, cosine, -sine).astype(BF16))
    dq = dot_nt(jnp.concatenate(dq_parts, axis=1), regroup(BF16)).astype(BF16)

    early[1].wait()
    cpart = dot_nt(dexp, wexp[...])
    share = GROUP // TENSOR
    for i in range(TENSOR):
        r = slice(i * share, (i + 1) * share)
        cbuf[i, :, :LATENT] = cpart[r].astype(BF16)
        cbuf[i, :, LATENT:] = rope_sum[r].astype(BF16)
    for j, (to, frm) in enumerate(others):
        send(cbuf.at[to], cgot.at[t], c_s.at[j], c_r.at[j], "tensor", to)

    early[0].wait()
    for n in range(TENSOR):
        npart[n] = dot_nt(dq, wq[n * COLS : (n + 1) * COLS, :]).astype(BF16)
    n1, n2, n3, n4 = sum_stages(
        lambda owner: npart.at[owner],
        lambda j: npart[order[j]].astype(F32),
        GROUP, nsib, nhalf, nfull, n_s, n_r, send,
    )
    n1()
    forward_2(0)

    early[2].wait()
    for n in range(4):
        s = slice(n * 512, (n + 1) * 512)
        swq[:, s] = dot_tn(dq, normed[:, s]).astype(BF16)
    early[3].wait()
    gwexp = dot_tn(comp[...], dexp)
    for i in range(GROUPS):
        swexp[i] = gwexp[32 * i : 32 * (i + 1)].astype(BF16)
    run(expand_sum, 0)
    run(query_sum, 0)

    total = cbuf[t].astype(F32)
    for j, (to, frm) in enumerate(others):
        got(cgot.at[frm], c_s.at[j], c_r.at[j])
        total = total + cgot[frm].astype(F32)
    mine_rows = pl.ds(pl.multiple_of(t * share, share), share)
    dc = total[:, :LATENT]
    lat = lat_ref[mine_rows, :]
    linv = linv_ref[mine_rows, :]
    lu = dc * gain_row(lgain_ref)
    dot = jnp.sum(lu * lat, axis=1, keepdims=True)
    dlat[t, :, :LATENT] = (linv * lu - lat * (linv * linv * linv * dot * (1.0 / LATENT))).astype(BF16)
    both = total[:, LATENT:]
    both = both + pltpu.roll(both, 2 * ROPE - ROPE // 2, 1)
    both = jnp.where(lane_head((share, 2 * ROPE)) == 0, both, 0.0)
    dlat[t, :, LATENT:] = turn(both, cos_ref[mine_rows, :], -sin_ref[mine_rows, :]).astype(BF16)
    for j, (to, frm) in enumerate(others):
        send(dlat.at[t], dlat.at[t], dl_s.at[j], dl_r.at[j], "tensor", to)
    lgain_row = jnp.sum(dc * lat * linv, axis=0, keepdims=True)

    n2()
    forward_2(1)
    n3()
    chunks[0][2]()

    def undeal_1(value, high, ss, rs):
        high[0] = dot_tn(seat_of_row(seat_ref[...]), value).astype(BF16)
        hop_start(high.at[0], high.at[1], PADCAP, ss, rs, send_many)

    def undeal_2(high, low, ss, rs, ss_next, rs_next):
        hop_wait(high.at[1], PADCAP, ss, rs)
        low[0] = dot_tn(row_of_seat(seat_row_ref[...]), high[1]).astype(BF16)
        hop_start(low.at[0], low.at[1], GROUPS, ss_next, rs_next, send_many)

    def undeal_3(low, ss, rs):
        hop_wait(low.at[1], GROUPS, ss, rs)
        return dot_tn(by_sixteen(), low[1]).astype(BF16)

    for j, (to, frm) in enumerate(others):
        got(dlat.at[frm], dl_s.at[j], dl_r.at[j])
    for i in (5, 6, 7):
        early[i].wait()
    dl = dlat[...].reshape(GROUP, WIDE_LAT)
    latent_cols = dot_nn(dl, wl[...])
    dn = latent_cols + n4()
    xd = x_ref[...].astype(F32)
    inv = inv_ref[...]
    u = dn * own_gain(gain_ref, t)
    finish = sum_rows_start(u * xd, st_buf, st_s, st_r)
    run(out_sum, 1)
    run(expand_sum, 1)
    run(query_sum, 1)
    total = finish()
    chunks[1][2]()
    dx = (dmid_ref[...] + inv * u - xd * (inv * inv * inv * total * (1.0 / D))).astype(BF16)
    undeal_1(dx, xh, xa_s, xa_r)
    forward_4(0)
    early[4].wait()

    def combine(k, rows):
        gates = jnp.broadcast_to(gate_ref[k][:, None, :], (GROUPS, PADCAP, GROUP)).reshape(ROWS, GROUP)
        weight = place[k].astype(F32) * gates
        high = weight.astype(BF16)
        low = (weight - high.astype(F32)).astype(BF16)
        return dot_tn(high, rows) + dot_tn(low, rows)

    routed = mid_ref[...] + shout_ref[...]
    for k in range(EARLY):
        got(fback.at[k, pl.ds(0, OTHERS)], fb_s.at[k], fb_r.at[k])
        routed = routed + combine(k, fback[k])
    gm[...] = jnp.zeros(gm.shape, F32)
    gm[0:1] = jnp.sum(dn * xd * inv, axis=0, keepdims=True)
    gm[1:2] = ffn_ref[...]
    gm[2:3] = lgain_row[:, :COLS]
    gm[3:4] = lgain_row[:, COLS:]
    gin[e] = gm[...]
    send_many([(gm, gin.at[e], to) for to, frm in peers], gin.at[pl.ds(0, GROUPS - 1)], gm_s, gm_r, "expert")

    pick_rows = lax.broadcasted_iota(jnp.int32, (WIDE_LAT, 128), 0)
    pick_cols = lax.broadcasted_iota(jnp.int32, (WIDE_LAT, 128), 1)
    pick_own = jnp.where((pick_rows == pick_cols + t * SLICE) & (pick_cols < SLICE), 1.0, 0.0).astype(BF16)
    dl_own = dot_nn(dl, pick_own).astype(BF16)
    for n in range(4):
        s = slice(n * 512, (n + 1) * 512)
        swlat[:, s] = dot_tn(dl_own, normed[:, s])[:SLICE].astype(BF16)
    rwlat[e] = swlat[:, cols(e, 128)]
    targets = [(swlat.at[:, cols(to, 128)], rwlat.at[e], to) for to, frm in peers]
    send_many(targets, rwlat.at[pl.ds(0, GROUPS - 1)], w_s, w_r, "expert")

    forward_4(1)
    undeal_2(xh, xl, xa_s, xa_r, xb_s, xb_r)
    for k in range(late):
        got(fback.at[EARLY + k, pl.ds(0, OTHERS)], fb_s.at[EARLY + k], fb_r.at[EARLY + k])
        routed = routed + combine(EARLY + k, fback[EARLY + k])
    out = routed.astype(BF16)
    undeal_1(out, oh, oa_s, oa_r)
    dx_ref[...] = undeal_3(xl, xb_s, xb_r)

    got(gin.at[pl.ds(0, GROUPS - 1)], gm_s, gm_r)
    gains_ref[t] = jnp.sum(gin[...], axis=0)
    for j, (to, frm) in enumerate(others):
        send(gains_ref.at[t], gains_ref.at[t], gt_s.at[j], gt_r.at[j], "tensor", to)
    got(rwlat.at[pl.ds(0, GROUPS - 1)], w_s, w_r)
    lat_sum = rwlat[0].astype(F32)
    for i in range(1, GROUPS):
        lat_sum = lat_sum + rwlat[i].astype(F32)
    lowlat[...] = lat_sum.astype(BF16)
    gwlat_ref[t] = lowlat[...]
    for j, (to, frm) in enumerate(others):
        send(lowlat, gwlat_ref.at[t], wl_s.at[j], wl_r.at[j], "tensor", to)
    undeal_2(oh, ol, oa_s, oa_r, ob_s, ob_r)
    gwout_ref[...] = jnp.concatenate(run(out_sum, 2), axis=0)
    gwq_ref[...] = jnp.transpose(jnp.concatenate(run(query_sum, 2), axis=0))
    gwexp_ref[...] = jnp.concatenate(run(expand_sum, 2), axis=1)
    out_ref[...] = undeal_3(ol, ob_s, ob_r)
    for j, (to, frm) in enumerate(others):
        got(gains_ref.at[frm], gt_s.at[j], gt_r.at[j])
        got(gwlat_ref.at[frm], wl_s.at[j], wl_r.at[j])
    for c in sends:
        c.wait_send()


def back_step(small, large, cid):
    vmem = pltpu.VMEM

    def out(*shape, dtype=BF16):
        return jax.ShapeDtypeStruct(shape, dtype)

    late = LOCAL - EARLY
    pair = lambda n: [DMA((n,)), DMA((n,))]
    grid_pair = lambda m, n: [DMA((m, n)), DMA((m, n))]
    return pl.pallas_call(
        back_kernel,
        out_shape=(
            out(GROUP, COLS),
            out(GROUP, COLS),
            out(D // GROUPS, 2 * HEAD, dtype=F32),
            out(LATENT // GROUPS, 512, dtype=F32),
            out(2 * VDIM, D // GROUPS, dtype=F32),
            out(TENSOR, SLICE, D // GROUPS),
            out(TENSOR, 8, COLS, dtype=F32),
        ),
        in_specs=[VM] * len(small) + [ANY] * len(large),
        out_specs=(VM,) * 7,
        scratch_shapes=[
            vmem((GROUP, D), BF16),
            vmem((D, 2 * HEAD), BF16),
            vmem((LATENT, 512), BF16),
            vmem((GROUP, LATENT), BF16),
            vmem((WIDE_LAT, COLS), BF16),
            vmem((LOCAL, ROWS, GROUP), BF16),
            vmem((late, 4, ROWS, COLS), BF16),
            vmem((late, 4, ROWS, COLS), BF16),
            vmem((late, 2, ROWS // 2, COLS), BF16),
            vmem((late, 2, ROWS, COLS), BF16),
            vmem((late, ROWS, COLS), BF16),
            vmem((LOCAL, ROWS, COLS), BF16),
            vmem((TENSOR, GROUP, COLS), BF16),
            vmem((4, GROUP, COLS), BF16),
            vmem((2, GROUP // 2, COLS), BF16),
            vmem((2, GROUP, COLS), BF16),
            vmem((2 * HEAD, D), BF16),
            vmem((GROUPS, LATENT // GROUPS, 512), BF16),
            vmem((2 * VDIM, D), BF16),
            vmem((SLICE, D), BF16),
            vmem((GROUPS, SLICE, D // GROUPS), BF16),
            vmem((SLICE, D // GROUPS), BF16),
        ]
        + two_phase_scratch(2, HEAD, D // GROUPS)
        + two_phase_scratch(2, LATENT // GROUPS, 256)
        + two_phase_scratch(2, VDIM, D // GROUPS)
        + [
            vmem((TENSOR, GROUP // TENSOR, WIDE_LAT), BF16),
            vmem((TENSOR, GROUP // TENSOR, WIDE_LAT), BF16),
            vmem((TENSOR, GROUP // TENSOR, WIDE_LAT), BF16),
            vmem((8, COLS), F32),
            vmem((GROUPS, 8, COLS), F32),
            vmem((2, ROWS, COLS), BF16),
            vmem((2, ROWS, COLS), BF16),
            vmem((2, GROUP, COLS), BF16),
            vmem((2, GROUP, COLS), BF16),
        ]
        + sum_rows_scratch()
        + grid_pair(late, 8)
        + pair(LOCAL)
        + pair(8)
        + [DMA] * 2
        + pair(7)
        + pair(7)
        + [DMA] * 2
        + pair(7)
        + pair(7)
        + [DMA] * 8
        + [DMA((8,)), DMA((late, 4))],
        compiler_params=params(cid, 63),
        name="back_step",
    )(*small, *large)


def gather_stages(source, block, ss, rs, send):
    t, right, left, far, twin = x_peers()
    flip = twin - t

    def put(j, ref, to, src=None):
        send(ref if src is None else src, ref, ss.at[j], rs.at[j], "tensor", to)

    def arrived(j, ref):
        remote(ref, ref, ss.at[j], rs.at[j], "tensor", twin).wait_recv()

    def stage_1():
        put(0, block(t, None), right, source)
        put(1, block(t, None), left, source)
        put(4, block(t, None), twin, source)

    def stage_2():
        arrived(0, block(left, None))
        put(2, block(left, 0), right)
        put(5, block(left, None), twin)
        arrived(1, block(right, None))
        put(3, block(right, 1), left)
        put(6, block(right, None), twin)

    def stage_3():
        arrived(2, block(far, 0))
        put(7, block(far, 0), twin)
        arrived(3, block(far, 1))
        put(8, block(far, 1), twin)

    def stage_4():
        arrived(4, block(twin, None))
        arrived(5, block(left + flip, None))
        arrived(6, block(right + flip, None))
        arrived(7, block(far + flip, 0))
        arrived(8, block(far + flip, 1))

    return stage_1, stage_2, stage_3, stage_4


def column_blocks(ref, rows):
    def block(owner, part):
        r = pl.ds(0, rows) if part is None else pl.ds(part * (rows // 2), rows // 2)
        return ref.at[r, cols(owner, COLS)]

    return block


def gain_row(ref):
    return ref[...].astype(F32).reshape(1, ref.shape[0])


def own_gain(ref, t):
    whole = gain_row(ref)
    total = jnp.zeros((1, COLS), F32)
    for i in range(TENSOR):
        total = total + jnp.where(t == i, whole[:, i * COLS : (i + 1) * COLS], 0.0)
    return total


def iota(shape, dim):
    return lax.broadcasted_iota(jnp.int32, shape, dim)


def deal_in_kernel(lengths, order, group):
    n = lengths.shape[1]
    i, j = iota((n, n), 0), iota((n, n), 1)
    same, before = i == j, j < i

    def column(row):
        return jnp.sum(jnp.where(same, row, 0.0), axis=1, keepdims=True)

    def row(col):
        return jnp.sum(jnp.where(same, col, 0.0), axis=0, keepdims=True)

    def exclusive(values):
        return jnp.sum(jnp.where(before, values, 0.0), axis=1, keepdims=True)

    hit = column(order) == j.astype(F32)
    begins_col = exclusive(lengths)
    begins = row(begins_col)
    dealt_lengths = row(jnp.sum(jnp.where(hit, lengths, 0.0), axis=1, keepdims=True))
    dealt_col = exclusive(dealt_lengths)
    dealt = row(dealt_col)
    dealt_source_col = jnp.sum(jnp.where(hit, begins, 0.0), axis=1, keepdims=True)
    dealt_source = row(dealt_source_col)
    given = jnp.sum(jnp.where(hit, dealt_col, 0.0), axis=0, keepdims=True)
    given_col = column(given)

    def find(rows, lanes, starts, values):
        dim = 1 if lanes else 0
        shape = (GROUP, n) if lanes else (n, GROUP)
        place = jnp.sum(jnp.where(rows >= starts, 1.0, 0.0), axis=dim, keepdims=True) - 1.0
        on = iota(shape, dim).astype(F32) == place
        return place, jnp.sum(jnp.where(on, values, 0.0), axis=dim, keepdims=True)

    first = group * GROUP
    rows = (iota((GROUP, 1), 0) + first).astype(F32)
    rows_row = (iota((1, GROUP), 1) + first).astype(F32)
    which, start = find(rows, True, dealt, dealt)
    unused, shift = find(rows, True, dealt, dealt_source - dealt)
    which_row, shift_row = find(rows_row, False, dealt_col, dealt_source_col - dealt_col)
    source, source_row = rows + shift, rows_row + shift_row

    def rest(value):
        return value - GROUPS * jnp.floor(value * (1.0 / GROUPS))

    ahead = (rest(source) == rest(source_row)) & (source_row < source)
    rank = jnp.sum(jnp.where(ahead, 1.0, 0.0), axis=1, keepdims=True)
    seat = rest(source) * PADCAP + rank

    mine = (iota((GROUP, 1), 0) * GROUPS + group).astype(F32)
    mine_row = (iota((1, GROUP), 1) * GROUPS + group).astype(F32)
    unused, move = find(mine, True, begins, given - begins)
    unused, move_row = find(mine_row, False, begins_col, given_col - begins_col)
    to = jnp.floor((mine + move) * (1.0 / GROUP))
    to_row = jnp.floor((mine_row + move_row) * (1.0 / GROUP))
    ahead = (to == to_row) & (iota((GROUP, GROUP), 0) < iota((GROUP, GROUP), 1))
    rank = jnp.sum(jnp.where(ahead, 1.0, 0.0), axis=0, keepdims=True)
    seat_row = to_row * PADCAP + rank
    return rows - start, which, which_row, seat, seat_row


def front_kernel(
    tok_ref, cot_ref, len_ref, ord_ref, routes_ref, gates_ref, gain_ref, lgain_ref, fgain_ref,
    wq_hbm, wl_hbm, wexp_hbm, wout_hbm,
    xc_ref, dyc_ref, mid_ref, inv2_ref, ncols_ref, normed_ref, inv_ref, q_ref, exp_ref, kr_ref, comp_ref,
    lat_ref, linv_ref, probs_ref, mixed_ref, place_ref, gate_ref, seat_ref, seat_row_ref, cos_ref, sin_ref, dyfull, nfull,
    rown_hbm, grads_hbm,
    hop_a, hop_b, hop_c, hop_d, xfull, wq, wl, wexp, wout, wrope, apart, sib, half, full, gout, dbuf,
    st_buf, st_s, st_r,
    ha_s, ha_r, hb_s, hb_r, xg_s, xg_r, yg_s, yg_r, ng_s, ng_r, gg_s, gg_r, r_s, r_r, d_s, d_r, e_s, e_r, l_in, l_own, l_last,
):
    t, right, left, far, twin = x_peers()
    e, peers = expert_peers()
    greet(
        [("tensor", lax.rem(t + j, TENSOR)) for j in range(1, TENSOR)]
        + [("expert", to) for to, frm in peers]
    )
    sends = []

    def send(src, dst, ssem, rsem, axis, to):
        c = remote(src, dst, ssem, rsem, axis, to)
        c.start()
        sends.append(c)

    def send_many(targets, total, ssem, rsem, axis):
        for src, dst, to in targets:
            remote(src, dst, ssem, rsem, axis, to).start()
        sends.append(remote(total, total, ssem, rsem, axis, targets[0][2]))

    def got(ref, ssem, rsem):
        remote(ref, ref, ssem, rsem, "tensor", twin).wait_recv()

    def local(src, dst, sem):
        c = pltpu.make_async_copy(src, dst, sem)
        c.start()
        return c

    sixteen = by_sixteen()
    hop_a[:, :COLS] = dot_nn(sixteen, tok_ref[...]).astype(BF16)
    hop_a[:, COLS:] = dot_nn(sixteen, cot_ref[...]).astype(BF16)
    hop_start(hop_a, hop_b, GROUPS, ha_s, ha_r, send_many)
    early = [
        local(src, dst, l_in.at[i])
        for i, (src, dst) in enumerate([(wl_hbm, wl), (wq_hbm, wq), (wexp_hbm, wexp), (wout_hbm, wout)])
    ]

    offset, which, which_row, seat, seat_row = deal_in_kernel(
        len_ref[...].astype(F32), ord_ref[...].astype(F32), e
    )
    seat_ref[...] = seat
    seat_row_ref[...] = seat_row

    outward = row_of_seat(seat_row)
    hop_wait(hop_b, GROUPS, ha_s, ha_r)
    hop_c[...] = dot_nn(outward, hop_b[...]).astype(BF16)
    hop_start(hop_c, hop_d, PADCAP, hb_s, hb_r, send_many)
    hr = ROPE // 2
    lane = iota((GROUP, 2 * ROPE), 1)
    power = (lane & (hr - 1)).astype(F32) * (1.0 / hr)
    angle = offset * jnp.exp(power * (-math.log(10000.0)))
    cosine = jnp.cos(angle)
    sine = jnp.sin(angle)
    sine = jnp.where(lane < ROPE, -sine, sine)
    cos_ref[...] = cosine
    sin_ref[...] = sine

    number = iota((EXPERTS, 1), 0)
    expert = (number & 15) * LOCAL + (number >> 4)
    member = jnp.zeros((EXPERTS, GROUP), F32)
    gate_of = jnp.zeros((EXPERTS, GROUP), F32)
    for k in range(TOP):
        hit = routes_ref[k : k + 1, :] == expert
        member = member + jnp.where(hit, 1.0, 0.0)
        gate_of = gate_of + jnp.where(hit, gates_ref[k : k + 1, :], 0.0)
    earlier = jnp.where(iota((GROUP, GROUP), 0) < iota((GROUP, GROUP), 1), 1.0, 0.0).astype(BF16)
    count = dot_nn(member.astype(BF16), earlier)
    slot = jnp.where((member > 0.5) & (count < CAP - 0.5), count, -1.0)
    seats = iota((GROUPS, PADCAP, GROUP), 1).astype(F32)
    slot_gates = []
    for k in range(LOCAL):
        s = slice(k * GROUPS, (k + 1) * GROUPS)
        gate_ref[k] = gate_of[s]
        wide = jnp.broadcast_to(slot[s][:, None, :], (GROUPS, PADCAP, GROUP))
        on = jnp.where(wide == seats, 1.0, 0.0)
        place_ref[k] = on.reshape(ROWS, GROUP).astype(BF16)
        weight = on * jnp.broadcast_to(gate_of[s][:, None, :], (GROUPS, PADCAP, GROUP))
        slot_gates.append(jnp.sum(weight.reshape(ROWS, GROUP), axis=1, keepdims=True))
    early[0].wait()
    for i in range(4):
        row = LATENT + (i // 2) * hr
        wrope[i * hr : (i + 1) * hr] = wl[row : row + hr]
    inward = seat_of_row(seat)
    hop_wait(hop_d, PADCAP, hb_s, hb_r)

    xc_ref[...] = dot_nn(inward, hop_d[:, :COLS]).astype(BF16)
    xfull[:, cols(t, COLS)] = xc_ref[...]
    xg1, xg2, xg3, xg4 = gather_stages(xc_ref, column_blocks(xfull, GROUP), xg_s, xg_r, send)
    xg1()
    dyc_ref[...] = dot_nn(inward, hop_d[:, COLS:]).astype(BF16)
    dyfull[:, cols(t, COLS)] = dyc_ref[...]
    yg1, yg2, yg3, yg4 = gather_stages(dyc_ref, column_blocks(dyfull, GROUP), yg_s, yg_r, send)
    yg1()
    blocks = (t, far)

    def slot_gradients(b):
        for k in range(LOCAL):
            gout[b, k] = (slot_gates[k] * dot_nn(place_ref[k], dyfull[:, cols(blocks[b], COLS)])).astype(BF16)

    own_grads = {}

    def send_gradients(p, b):
        two = pl.ds(2 * p, 2)
        landed = grads_hbm.at[two, seat_rows(e), cols(blocks[b], COLS)]
        own_grads[p, b] = local(gout.at[b, two, seat_rows(e)], landed, l_own.at[p, b])
        targets = [(gout.at[b, two, seat_rows(to)], landed, to) for to, frm in peers]
        send_many(targets, gout.at[b, two, pl.ds(0, OTHERS)], d_s.at[p, b], d_r.at[p, b], "expert")

    slot_gradients(0)
    send_gradients(0, 0)
    send_gradients(1, 0)
    xg2()
    yg2()
    xg3()
    yg3()
    slot_gradients(1)
    send_gradients(0, 1)
    send_gradients(1, 1)
    xg4()

    xd = xfull[...].astype(F32)
    inv = lax.rsqrt(jnp.sum(xd * xd, axis=1, keepdims=True) * (1.0 / D) + EPS)
    inv_ref[...] = inv
    normed = (xd * inv * gain_row(gain_ref)).astype(BF16)
    normed_ref[...] = normed
    lat = dot_nt(normed, wl[:LATENT])
    lat_ref[...] = lat
    linv = lax.rsqrt(jnp.sum(lat * lat, axis=1, keepdims=True) * (1.0 / LATENT) + EPS)
    linv_ref[...] = linv
    kr = turn(dot_nt(normed, wrope[...]), cosine, sine).astype(BF16)
    kr_ref[...] = kr
    early[1].wait()
    pre = lax.dot_general(
        dot_nn(normed, wq[...]),
        regroup(F32),
        (((1,), (0,)), ((), ())),
        precision=lax.Precision.HIGHEST,
        preferred_element_type=F32,
    )
    q_ref[:, : 2 * NOPE] = pre[:, : 2 * NOPE].astype(BF16)
    qr = turn(pre[:, 2 * NOPE :], cosine, sine)
    q_ref[:, 2 * NOPE :] = qr.astype(BF16)
    comp = (lat * linv * gain_row(lgain_ref)).astype(BF16)
    comp_ref[...] = comp
    early[2].wait()
    expanded = dot_nn(comp, wexp[...]).astype(BF16)
    exp_ref[...] = expanded

    def grad_block(k):
        return lambda owner: grads_hbm.at[k, :, cols(owner, COLS)]

    spread = [near_stages(grad_block(k), gg_s.at[k], gg_r.at[k], send) for k in range(LOCAL)]
    seen = set()

    def gradients(k, b):
        p = k // 2
        if (p, b) not in seen:
            seen.add((p, b))
            own_grads[p, b].wait()
            got(gout.at[b, pl.ds(2 * p, 2), pl.ds(0, OTHERS)], d_s.at[p, b], d_r.at[p, b])
        spread[k][b]()

    head = lane_head((GROUP, 2 * ROPE))
    allowed = (which == which_row) & (iota((GROUP, GROUP), 0) >= iota((GROUP, GROUP), 1))
    scale = HEAD ** (-0.5)
    for h in range(2):
        q = q_ref[:, h * NOPE : (h + 1) * NOPE]
        k = expanded[:, 256 * h : 256 * h + NOPE]
        v = expanded[:, 256 * h + NOPE : 256 * h + NOPE + VDIM]
        turned = jnp.where(head == h, qr, 0.0).astype(BF16)
        raw = (dot_nt(q, k) + dot_nt(turned, kr)) * scale
        scores = jnp.where(allowed, raw, -1e30)
        expo = jnp.exp(scores - jnp.max(scores, axis=1, keepdims=True))
        probs = expo / jnp.sum(expo, axis=1, keepdims=True)
        probs_ref[h] = probs
        mixed_ref[:, h * VDIM : (h + 1) * VDIM] = dot_nn(probs.astype(BF16), v).astype(BF16)
    mixed = mixed_ref[...]
    early[3].wait()
    for n in range(TENSOR):
        apart[n] = dot_nn(mixed, wout[:, n * COLS : (n + 1) * COLS]).astype(BF16)

    order = (far, right, left, t)
    r1, r2, r3, r4 = sum_stages(
        lambda owner: apart.at[owner],
        lambda j: apart[order[j]].astype(F32),
        GROUP, sib, half, full, r_s, r_r, send,
    )
    r1()
    gradients(0, 0)
    r2()
    r3()
    gradients(1, 0)
    mid = xc_ref[...].astype(F32) + r4()
    mid_ref[...] = mid
    finish = sum_rows_start(mid * mid, st_buf, st_s, st_r)
    spread[0][2]()
    inv2 = lax.rsqrt(finish() * (1.0 / D) + EPS)
    inv2_ref[...] = inv2
    ncols_ref[...] = (mid * inv2 * own_gain(fgain_ref, t)).astype(BF16)
    nfull[:, cols(t, COLS)] = ncols_ref[...]
    ng1, ng2, ng3, ng4 = gather_stages(ncols_ref, column_blocks(nfull, GROUP), ng_s, ng_r, send)
    ng1()
    own_rows = {}

    def dispatch(b):
        for p in range(2):
            for k in (2 * p, 2 * p + 1):
                dbuf[b, k] = dot_nn(place_ref[k], nfull[:, cols(blocks[b], COLS)]).astype(BF16)
            two = pl.ds(2 * p, 2)
            landed = rown_hbm.at[b, two, seat_rows(e)]
            own_rows[p, b] = local(dbuf.at[b, two, seat_rows(e)], landed, l_last.at[p, b])
            targets = [(dbuf.at[b, two, seat_rows(to)], landed, to) for to, frm in peers]
            send_many(targets, dbuf.at[b, two, pl.ds(0, OTHERS)], e_s.at[p, b], e_r.at[p, b], "expert")

    dispatch(0)
    gradients(2, 0)
    gradients(0, 1)
    gradients(1, 1)
    spread[1][2]()
    ng2()
    gradients(3, 0)
    gradients(2, 1)
    gradients(3, 1)
    ng3()
    dispatch(1)
    spread[2][2]()
    yg4()
    ng4()
    spread[3][2]()
    for k in range(LOCAL):
        spread[k][3]()
    for p in range(2):
        for b in range(2):
            own_rows[p, b].wait()
            got(dbuf.at[b, pl.ds(2 * p, 2), pl.ds(0, OTHERS)], e_s.at[p, b], e_r.at[p, b])
    for c in sends:
        c.wait_send()


def front_step(small, large, cid):
    vmem = pltpu.VMEM

    def out(*shape, dtype=BF16):
        return jax.ShapeDtypeStruct(shape, dtype)

    def pair(*shape):
        return [DMA(shape), DMA(shape)]

    return pl.pallas_call(
        front_kernel,
        out_shape=(
            out(GROUP, COLS),
            out(GROUP, COLS),
            out(GROUP, COLS, dtype=F32),
            out(GROUP, 1, dtype=F32),
            out(GROUP, COLS),
            out(GROUP, D),
            out(GROUP, 1, dtype=F32),
            out(GROUP, 2 * HEAD),
            out(GROUP, 512),
            out(GROUP, 2 * ROPE),
            out(GROUP, LATENT),
            out(GROUP, LATENT, dtype=F32),
            out(GROUP, 1, dtype=F32),
            out(2, GROUP, GROUP, dtype=F32),
            out(GROUP, 2 * VDIM),
            out(LOCAL, ROWS, GROUP),
            out(LOCAL, GROUPS, GROUP, dtype=F32),
            out(GROUP, 1, dtype=F32),
            out(1, GROUP, dtype=F32),
            out(GROUP, 2 * ROPE, dtype=F32),
            out(GROUP, 2 * ROPE, dtype=F32),
            out(GROUP, D),
            out(GROUP, D),
            out(2, LOCAL, ROWS, COLS),
            out(LOCAL, ROWS, D),
        ),
        in_specs=[VM] * len(small) + [ANY] * len(large),
        out_specs=(VM,) * 23 + (ANY,) * 2,
        scratch_shapes=[
            vmem((GROUP, 2 * COLS), BF16),
            vmem((GROUP, 2 * COLS), BF16),
            vmem((ROWS, 2 * COLS), BF16),
            vmem((ROWS, 2 * COLS), BF16),
            vmem((GROUP, D), BF16),
            vmem((D, 2 * HEAD), BF16),
            vmem((LATENT + ROPE, D), BF16),
            vmem((LATENT, 512), BF16),
            vmem((2 * VDIM, D), BF16),
            vmem((2 * ROPE, D), BF16),
            vmem((TENSOR, GROUP, COLS), BF16),
            vmem((4, GROUP, COLS), BF16),
            vmem((2, GROUP // 2, COLS), BF16),
            vmem((2, GROUP, COLS), BF16),
            vmem((2, LOCAL, ROWS, COLS), BF16),
            vmem((2, LOCAL, ROWS, COLS), BF16),
        ]
        + sum_rows_scratch()
        + [DMA] * 4
        + pair(9)
        + pair(9)
        + pair(9)
        + pair(LOCAL, 6)
        + pair(8)
        + pair(2, 2)
        + pair(2, 2)
        + [DMA((4,)), DMA((2, 2)), DMA((2, 2))],
        compiler_params=params(cid, 60),
        name="front_step",
    )(*small, *large)


def finish_kernel(
    gg_ref, gu_ref, gd_ref, wsum_ref, out_in, dx_in, gwq_in, gwexp_in, gwout_in, gwlat_in, gains_in,
    ogg_ref, ogu_ref, ogd_ref, sg_ref, su_ref, sd_ref, out_ref, dx_ref, gwq_ref, gwexp_ref, gwout_ref, gwlat_ref,
    attn_ref, ffn_ref, lgain_ref,
):
    ogg_ref[...] = gg_ref[...].astype(F32)
    ogu_ref[...] = gu_ref[...].astype(F32)
    ogd_ref[...] = gd_ref[...].astype(F32)

    @pl.when((pl.program_id(0) == 0) & (pl.program_id(1) == 0))
    def small():
        e = lax.axis_index("expert")
        sg_ref[...] = wsum_ref[0]
        su_ref[...] = wsum_ref[1]
        sd_ref[...] = wsum_ref[2]
        out_ref[...] = out_in[...]
        dx_ref[...] = dx_in[...]
        gwq_ref[...] = gwq_in[...]
        gwexp_ref[...] = gwexp_in[...]
        gwout_ref[...] = gwout_in[...]
        lat = gwlat_in[...].astype(F32).reshape(WIDE_LAT, D // GROUPS)
        half = ROPE // 2
        gwlat_ref[: LATENT + half] = lat[: LATENT + half]
        gwlat_ref[LATENT + half :] = lat[LATENT + ROPE : LATENT + ROPE + half]
        own = gains_in[e // 2]
        side = lax.rem(e, 2) == 0
        attn_ref[...] = jnp.where(side, own[0:1, :128], own[0:1, 128:])
        ffn_ref[...] = jnp.where(side, own[1:2, :128], own[1:2, 128:])
        rows = jnp.sum(gains_in[...], axis=0)[2:4]
        row = jnp.where(e < 8, rows[0:1], rows[1:2])
        wanted = iota((COLS, 128), 1) + lax.rem(e, 8) * (LATENT // GROUPS)
        pick_own = jnp.where(iota((COLS, 128), 0) == wanted, 1.0, 0.0)
        lgain_ref[...] = lax.dot_general(
            row, pick_own, (((1,), (0,)), ((), ())),
            precision=lax.Precision.HIGHEST, preferred_element_type=F32,
        )


def finish_step(grads, rest):
    def out(*shape, dtype=F32):
        return jax.ShapeDtypeStruct(shape, dtype)

    hid = grads[0].shape[1]
    wide = rest[0].shape[1]
    block = pl.BlockSpec((1, hid, D // 2), lambda i, j: (i, 0, j))

    def whole(shape):
        return pl.BlockSpec(shape, lambda i, j: (0,) * len(shape))

    outs = (
        out(wide, 128), out(wide, 128), out(wide, 128), out(GROUP, COLS, dtype=BF16), out(GROUP, COLS, dtype=BF16),
        out(128, 2 * HEAD), out(LATENT // GROUPS, 512), out(2 * VDIM, 128), out(LATENT + ROPE, 128),
        out(1, 128), out(1, 128), out(1, 128),
    )
    return pl.pallas_call(
        finish_kernel,
        grid=(LOCAL, 2),
        out_shape=(out(LOCAL, hid, D),) * 3 + outs,
        in_specs=[block] * 3 + [whole(a.shape) for a in rest],
        out_specs=(block,) * 3 + tuple(whole(o.shape) for o in outs),
        compiler_params=pltpu.CompilerParams(vmem_limit_bytes=63 * MIB),
        name="finish_step",
    )(*grads, *rest)


def per_device(
    tokens,
    cotangent,
    attn_gain,
    w_query,
    w_latent,
    latent_gain,
    w_expand,
    w_out,
    ffn_gain,
    shared_gate,
    shared_up,
    shared_down,
    expert_gate,
    expert_up,
    expert_down,
    seq_lengths,
    seq_order,
    routes,
    gate_weights,
):
    wlat_t = w_latent.T
    attn_row, ffn_row, lgain = attn_gain, ffn_gain, latent_gain

    (
        x_cols, dy_cols, middle, inv_two, normed_two_cols, normed, inv_one, query, expanded, key_rope, compressed,
        latent, inv_lat, probs, mixed, place, gate_of, seat, seat_row, cosine, sine, dy_full, normed_two, own_slots, grad_rows
    ) = front_step(
        (
            tokens,
            cotangent,
            seq_lengths.reshape(1, -1),
            seq_order.reshape(1, -1),
            routes.T,
            gate_weights.T,
            attn_row,
            lgain,
            ffn_row,
        ),
        (w_query, wlat_t, w_expand, w_out),
        1,
    )

    (
        part, grad_eg, grad_eu, grad_ed, shared_out, dmid, dgain_ffn, d_attn, unused, early_back, shared_weights
    ) = moe_step(
        place,
        own_slots,
        normed_two,
        dy_full,
        shared_gate.T,
        shared_up.T,
        shared_down,
        jnp.swapaxes(expert_gate, 1, 2),
        jnp.swapaxes(expert_up, 1, 2),
        expert_down,
        grad_rows,
        middle,
        inv_two,
        ffn_row,
        dy_cols,
        3,
    )
    output, input_grad, grad_wq, grad_wexp, grad_wout, grad_wlat, gains = back_step(
        (
            d_attn,
            mixed,
            w_out,
            query,
            expanded,
            key_rope,
            probs,
            cosine,
            sine,
            latent,
            inv_lat,
            lgain,
            x_cols,
            inv_one,
            attn_row,
            dmid,
            dgain_ffn,
            middle,
            shared_out,
            early_back,
            gate_of,
            seat,
            seat_row,
        ),
        (place, normed, w_query, w_expand, compressed, wlat_t, part),
        4,
    )
    (
        grad_eg, grad_eu, grad_ed, sg, su, sd, output, input_grad, grad_wq, grad_wexp, grad_wout, grad_wlat,
        attn_out, ffn_out, lgain_out
    ) = finish_step(
        (grad_eg, grad_eu, grad_ed),
        (shared_weights, output, input_grad, grad_wq, grad_wexp, grad_wout, grad_wlat, gains),
    )
    return (
        output,
        input_grad,
        attn_out[0],
        grad_wq,
        grad_wlat.T,
        lgain_out[0, : LATENT // GROUPS],
        grad_wexp,
        grad_wout,
        ffn_out[0],
        sg.T,
        su.T,
        sd,
        jnp.swapaxes(grad_eg, 1, 2),
        jnp.swapaxes(grad_eu, 1, 2),
        grad_ed,
    )


def solution(mesh):
    return jax.shard_map(
        per_device,
        mesh=mesh,
        in_specs=(
            P("expert", "tensor"),
            P("expert", "tensor"),
            P(),
            P(None, "tensor"),
            P(),
            P(),
            P(None, "tensor"),
            P("tensor", None),
            P(),
            P(None, "tensor"),
            P(None, "tensor"),
            P("tensor", None),
            P("expert", None, "tensor"),
            P("expert", None, "tensor"),
            P("expert", "tensor", None),
            P(),
            P(),
            P("expert", None),
            P("expert", None),
        ),
        out_specs=(
            P("expert", "tensor"),
            P("expert", "tensor"),
            P("expert"),
            P("expert", "tensor"),
            P("expert", None),
            P("expert"),
            P("expert", "tensor"),
            P("tensor", "expert"),
            P("expert"),
            P("expert", "tensor"),
            P("expert", "tensor"),
            P("tensor", "expert"),
            P("expert", None, "tensor"),
            P("expert", None, "tensor"),
            P("expert", "tensor", None),
        ),
        check_vma=False,
    )
```

```python
import math

import jax
import jax.numpy as jnp
from jax import lax
from jax.experimental import pallas as pl
from jax.experimental.pallas import tpu as pltpu
from jax.sharding import PartitionSpec as P

NOPE = 128
ROPE = 64
HEAD = NOPE + ROPE
LATENT = 512
VDIM = 128
D = 2048
GROUP = 256
TOP = 6
EXPERTS = 64
GROUPS = 16
LOCAL = 4
CAP = 27
PADCAP = 32
TENSOR = 8
COLS = D // TENSOR
EPS = 1e-06

XN = 4
YN = 4
ZN = 4
CORES = 2

F32 = jnp.float32
BF16 = jnp.bfloat16
MESH = pl.DeviceIdType.MESH
ANY = pl.BlockSpec(memory_space=pl.ANY)
VM = pl.BlockSpec(memory_space=pltpu.VMEM)
DMA = pltpu.SemaphoreType.DMA
MIB = 1024 * 1024


def remote(src, dst, ssem, rsem, axis, index):
    return pltpu.make_async_remote_copy(
        src_ref=src,
        dst_ref=dst,
        send_sem=ssem,
        recv_sem=rsem,
        device_id={axis: index},
        device_id_type=MESH,
    )


def greet(peers):
    barrier = pltpu.get_barrier_semaphore()
    for axis, index in peers:
        pl.semaphore_signal(barrier, inc=1, device_id={axis: index}, device_id_type=MESH)
    pl.semaphore_wait(barrier, len(peers))


def params(cid, vmem=48.0):
    return pltpu.CompilerParams(
        collective_id=cid, has_side_effects=True, vmem_limit_bytes=int(vmem * MIB)
    )


def x_peers():
    t = lax.axis_index("tensor")
    x = t // CORES
    c = lax.rem(t, CORES)
    right = lax.rem(x + 1, XN) * CORES + c
    left = lax.rem(x + XN - 1, XN) * CORES + c
    far = lax.rem(x + 2, XN) * CORES + c
    twin = x * CORES + (1 - c)
    return t, right, left, far, twin


def greet_x():
    t, right, left, far, twin = x_peers()
    greet([("tensor", right), ("tensor", left), ("tensor", twin)])


def greet_tensor():
    t = lax.axis_index("tensor")
    greet([("tensor", lax.rem(t + j, TENSOR)) for j in range(1, TENSOR)])


def cols(index, width):
    return pl.ds(pl.multiple_of(index * width, width), width)


def sum_rows_start(value, buf, ssem, rsem):
    t = lax.axis_index("tensor")
    rows = value.shape[0]
    mine = jnp.broadcast_to(jnp.sum(value, axis=1, keepdims=True), (rows, 128))
    buf[t] = jnp.transpose(mine)[:8]
    sends = []
    for j in range(1, TENSOR):
        to = lax.rem(t + j, TENSOR)
        c = remote(buf.at[t], buf.at[t], ssem.at[j], rsem.at[j], "tensor", to)
        c.start()
        sends.append(c)

    def finish():
        for j in range(1, TENSOR):
            ref = buf.at[lax.rem(t + TENSOR - j, TENSOR)]
            remote(ref, ref, ssem.at[j], rsem.at[j], "tensor", t).wait_recv()
        total = jnp.sum(buf[...], axis=0)
        for s in sends:
            s.wait_send()
        return jnp.transpose(total)[:, :1]

    return finish


def sum_rows_tensor(value, buf, ssem, rsem):
    return sum_rows_start(value, buf, ssem, rsem)()


def sum_rows_scratch():
    return [pltpu.VMEM((TENSOR, 8, GROUP), F32), DMA((TENSOR,)), DMA((TENSOR,))]


def dot_nn(a, b):
    return lax.dot_general(a, b, (((1,), (0,)), ((), ())), preferred_element_type=F32)


def dot_nt(a, b):
    return lax.dot_general(a, b, (((1,), (1,)), ((), ())), preferred_element_type=F32)


def dot_tn(a, b):
    return lax.dot_general(a, b, (((0,), (0,)), ((), ())), preferred_element_type=F32)


ROWS = GROUPS * PADCAP
OTHERS = ROWS - PADCAP
EARLY = 2


def expert_peers():
    e = lax.axis_index("expert")
    z = e // YN
    y = lax.rem(e, YN)
    peers = []
    for dz in range(ZN):
        for dy in range(YN):
            if dz or dy:
                to = lax.rem(z + dz, ZN) * YN + lax.rem(y + dy, YN)
                frm = lax.rem(z + ZN - dz, ZN) * YN + lax.rem(y + YN - dy, YN)
                peers.append((to, frm))
    return e, peers


def seat_rows(index):
    return pl.ds(pl.multiple_of(index * PADCAP, PADCAP), PADCAP)


def moe_kernel(
    place_ref, rown_hbm, nfull_hbm, dy_hbm, sg_hbm, su_hbm, sd_hbm, wg_hbm, wu_hbm, wd_hbm, grads_hbm,
    mid_ref, inv_ref, gain_ref, dyc_ref,
    part_hbm, gg_hbm, gu_hbm, gd_hbm, shout_ref, dmid_ref, dgain_ref, dattn_hbm, wsend_hbm, p_res, wsum_ref,
    sh_ref, dsg_ref, dsu_ref, nfull, dyf, rows, drows, sib, half, full, wbuf, gbuf, gout, pbuf, res, back, shsum, low,
    a_s, a_r, r_s, r_r, b_s, b_r, f_s, f_r, st_buf, st_s, st_r, l_in, l_w, l_g, l_out, l_own, l_sh, l_first,
    wown, w_a, w_p, w_b, w_s, w_r, l_wn,
    p_own, p_sib, p_half, p_full, p_s, p_r, l_p,
):
    t, right, left, far, twin = x_peers()
    flip = twin - t
    e, peers = expert_peers()
    greet(
        [("tensor", lax.rem(t + j, TENSOR)) for j in range(1, TENSOR)]
        + [("expert", to) for to, frm in peers]
    )
    sends = []

    def send(src, dst, ssem, rsem, axis, to):
        c = remote(src, dst, ssem, rsem, axis, to)
        c.start()
        sends.append(c)

    def send_many(targets, total, ssem, rsem, axis):
        for src, dst, to in targets:
            remote(src, dst, ssem, rsem, axis, to).start()
        sends.append(remote(total, total, ssem, rsem, axis, targets[0][2]))

    def got(ref, ssem, rsem):
        remote(ref, ref, ssem, rsem, "tensor", twin).wait_recv()

    blocks = (t, far)
    own_copies = []
    for k in range(LOCAL):
        for b in range(2):
            c = pltpu.make_async_copy(
                rown_hbm.at[b, k], rows.at[k, :, cols(blocks[b], COLS)], l_first.at[k, b]
            )
            c.start()
            own_copies.append(c)
    wide = sd_hbm.shape[0]
    sgv, suv, sdv = (drows.at[i, pl.ds(0, wide)] for i in range(3))
    early = [
        pltpu.make_async_copy(src, dst, l_in.at[i])
        for i, (src, dst) in enumerate(
            [(nfull_hbm, nfull), (sg_hbm, sgv), (su_hbm, suv), (sd_hbm, sdv), (dy_hbm, dyf)]
        )
    ]
    for c in early:
        c.start()

    def load(k):
        s = k % 2
        copies = [
            pltpu.make_async_copy(ref.at[k], wbuf.at[s, i], l_w.at[s, i])
            for i, ref in enumerate((wg_hbm, wu_hbm, wd_hbm))
        ]
        for c in copies:
            c.start()
        return copies

    loads = {0: load(0)}

    grad_loads = [pltpu.make_async_copy(grads_hbm.at[k], gbuf.at[k % 3], l_g.at[k]) for k in range(LOCAL)]
    grad_loads[0].start()

    h = ROWS // 2

    def row_block(k):
        return lambda owner: rows.at[k, :, cols(owner, COLS)]

    near = [near_stages(row_block(k), a_s.at[k], a_r.at[k], send) for k in range(LOCAL)]

    def gather_1(k):
        for b in range(2):
            own_copies[2 * k + b].wait()
            near[k][b]()

    def gather_2(k):
        near[k][2]()

    def gather_4(k):
        near[k][3]()

    back_copies = {}

    order = (far, right, left, t)

    def slot(k):
        return k

    def rsend(k, j, src, dst, to):
        send(src, dst, r_s.at[k, j], r_r.at[k, j], "tensor", to)

    def rgot(k, j, ref):
        got(ref, r_s.at[k, j], r_r.at[k, j])

    def mine(k, j):
        return drows[slot(k), :, cols(order[j], COLS)].astype(F32)

    twin_sends = {}

    def sum_1(k):
        first = len(sends)
        for j, owner in enumerate(order):
            rsend(k, j, drows.at[slot(k), :, cols(owner + flip, COLS)], sib.at[k, j], twin)
        twin_sends[k] = sends[first:]
        del sends[first:]

    def sum_2(k):
        rgot(k, 0, sib.at[k, 0])
        sib[k, 0] = (mine(k, 0) + sib[k, 0].astype(F32)).astype(BF16)
        rsend(k, 4, sib.at[k, 0, pl.ds(0, h)], half.at[k, 0], right)
        rsend(k, 5, sib.at[k, 0, pl.ds(h, h)], half.at[k, 1], left)

    def sum_3(k):
        for j, to in ((1, right), (2, left)):
            rgot(k, j, sib.at[k, j])
            rgot(k, 3 + j, half.at[k, j - 1])
            both = mine(k, j) + sib[k, j].astype(F32)
            extra = half[k, j - 1].astype(F32)
            if j == 1:
                sib[k, j, :h] = (both[:h] + extra).astype(BF16)
                sib[k, j, h:] = both[h:].astype(BF16)
            else:
                sib[k, j, :h] = both[:h].astype(BF16)
                sib[k, j, h:] = (both[h:] + extra).astype(BF16)
            rsend(k, 5 + j, sib.at[k, j], full.at[k, j - 1], to)

    def sum_4(k):
        rgot(k, 3, sib.at[k, 3])
        rgot(k, 6, full.at[k, 0])
        rgot(k, 7, full.at[k, 1])
        value = mine(k, 3) + sib[k, 3].astype(F32) + full[k, 0].astype(F32) + full[k, 1].astype(F32)
        for c in twin_sends[k]:
            c.wait_send()
        if k == LOCAL:
            shsum[...] = value
            return
        res[k] = value.astype(BF16)
        c = pltpu.make_async_copy(res.at[k, seat_rows(e)], back.at[k, seat_rows(e)], l_own.at[k])
        c.start()
        back_copies[k] = c
        targets = [(res.at[k, seat_rows(to)], back.at[k, seat_rows(e)], to) for to, frm in peers]
        send_many(targets, back.at[k, pl.ds(0, OTHERS)], b_s.at[k], b_r.at[k], "expert")

    def shared_forward():
        for c in early[:4]:
            c.wait()
        n = nfull[...]
        g = dot_nt(n, sgv[...])
        u = dot_nt(n, suv[...])
        sig = jax.nn.sigmoid(g)
        silu = g * sig
        sh_ref[...] = (silu * u).astype(BF16)
        return g, u, sig, silu

    def shared_backward(g, u, sig, silu):
        early[4].wait()
        dh = dot_nt(dyf[...], sdv[...])
        dsg_ref[...] = (dh * u * (sig * (1.0 + g * (1.0 - sig)))).astype(BF16)
        dsu_ref[...] = (dh * silu).astype(BF16)

    tiles = [pl.ds(i * 512, 512) for i in range(D // 512)]

    def shared_rows():
        hid = sh_ref[...]
        dsg, dsu = dsg_ref[...], dsu_ref[...]
        for n in tiles:
            drows[LOCAL, :GROUP, n] = dot_nn(hid, sdv[:, n]).astype(BF16)
            drows[LOCAL, GROUP:, n] = (dot_nn(dsg, sgv[:, n]) + dot_nn(dsu, suv[:, n])).astype(BF16)

    stages = (drows.at[1], drows.at[2], pbuf)
    staged = []

    def shared_weights():
        pairs = ((dsg_ref, nfull), (dsu_ref, nfull), (sh_ref, dyf))
        for i, (lhs, rhs) in enumerate(pairs):
            for n in tiles:
                stages[i][:wide, n] = dot_tn(lhs[...], rhs[:, n]).astype(BF16)
            c = pltpu.make_async_copy(stages[i].at[pl.ds(0, wide)], wsend_hbm.at[i], l_sh.at[i])
            c.start()
            staged.append(c)
            for p in range(2):
                for j in range(4):
                    d = j * YN + lax.rem(e, YN) if p == 0 else (e // YN) * YN + j
                    c = pltpu.make_async_copy(
                        stages[i].at[pl.ds(p * wide // 2, wide // 2), cols(d, 128)],
                        wown.at[2 * i + p, j],
                        l_wn.at[2 * i + p, j],
                    )
                    c.start()
                    staged.append(c)

    def piece_ref(i, p):
        return lambda dz, dy: wsend_hbm.at[i, pl.ds(p * wide // 2, wide // 2), cols(dz * YN + dy, 128)]

    def piece_own(i, p):
        return lambda dz, dy: wown[2 * i + p, dz if p == 0 else dy].astype(F32)

    shared_sums = [
        two_phase(
            piece_ref(n // 2, n % 2), piece_own(n // 2, n % 2),
            w_a.at[n], w_p.at[n], w_b.at[n], w_s.at[n], w_r.at[n], "yz"[n % 2], send_many,
        )
        for n in range(6)
    ]

    out_copies = {}

    def compute_1(k):
        s = k % 2
        for c in loads[k] + [grad_loads[k]]:
            c.wait()
        r = rows[k]
        gate = dot_nt(r, wbuf[s, 0])
        up = dot_nt(r, wbuf[s, 1])
        dh = dot_nt(gbuf[k % 3], wbuf[s, 2])
        sig = jax.nn.sigmoid(gate)
        silu = gate * sig
        hidden = (silu * up).astype(BF16)
        dg = (dh * up * (sig * (1.0 + gate * (1.0 - sig)))).astype(BF16)
        du = (dh * silu).astype(BF16)
        for n in tiles:
            drows[slot(k), :, n] = (
                dot_nn(dg, wbuf[s, 0, :, n]) + dot_nn(du, wbuf[s, 1, :, n])
            ).astype(BF16)
        return hidden, dg, du

    def compute_2(k, hidden, dg, du):
        s = k % 2
        if k:
            for c in out_copies[k - 1]:
                c.wait()
        for n in tiles:
            pbuf[:, n] = dot_nn(hidden, wbuf[s, 2, :, n]).astype(BF16)
            gout[0, :, n] = dot_tn(dg, rows[k, :, n]).astype(BF16)
            gout[1, :, n] = dot_tn(du, rows[k, :, n]).astype(BF16)
            gout[2, :, n] = dot_tn(hidden, gbuf[k % 3, :, n]).astype(BF16)
        out_copies[k] = [
            pltpu.make_async_copy(src, dst.at[k], l_out.at[i])
            for i, (src, dst) in enumerate(
                [(pbuf, part_hbm), (gout.at[0], gg_hbm), (gout.at[1], gu_hbm), (gout.at[2], gd_hbm)]
            )
        ]
        for c in out_copies[k]:
            c.start()
        if k + 2 < LOCAL:
            loads[k + 2] = load(k + 2)
        if k + 3 < LOCAL:
            grad_loads[k + 3].start()

    forward = [
        sum_stages(
            lambda owner, k=k: part_hbm.at[k, :, cols(owner, COLS)],
            lambda j, k=k: p_own[k, j].astype(F32),
            ROWS, p_sib.at[k], p_half.at[k], p_full.at[k], p_s.at[k], p_r.at[k], send,
        )
        for k in range(EARLY)
    ]
    forward_loads = {}

    def forward_1(k):
        forward_loads[k] = [
            pltpu.make_async_copy(part_hbm.at[k, :, cols(owner, COLS)], p_own.at[k, j], l_p.at[k, j])
            for j, owner in enumerate(order)
        ]
        for c in forward_loads[k]:
            c.start()
        forward[k][0]()

    def forward_2(k):
        for c in forward_loads[k]:
            c.wait()
        forward[k][1]()

    def forward_3(k):
        forward[k][2]()

    def forward_4(k):
        p_res[k] = forward[k][3]().astype(BF16)

    for k in range(LOCAL):
        gather_1(k)
    loads[1] = load(1)
    grad_loads[1].start()
    state = shared_forward()
    shared_backward(*state)
    gather_2(0)
    shared_rows()
    sum_1(4)
    gather_2(1)
    gather_4(0)
    c0 = compute_1(0)
    sum_1(0)
    grad_loads[2].start()
    gather_2(2)
    shared_weights()
    gather_4(1)
    for c in staged:
        c.wait()
    c1 = compute_1(1)
    sum_1(1)
    for piece in shared_sums:
        piece[0]()
    gather_2(3)
    sum_2(0)
    compute_2(0, *c0)
    gather_4(2)
    c2 = compute_1(2)
    sum_1(2)
    sum_3(0)
    sum_2(1)
    compute_2(1, *c1)
    gather_4(3)
    c3 = compute_1(3)
    sum_1(3)
    sum_4(0)
    sum_3(1)
    sum_2(2)
    sum_2(3)
    compute_2(2, *c2)
    forward_1(0)
    forward_1(1)
    sum_2(4)
    sum_4(1)
    sum_3(2)
    sum_3(3)
    compute_2(3, *c3)
    for piece in shared_sums:
        piece[1]()
    sum_3(4)
    sum_4(2)
    forward_2(0)
    forward_2(1)
    sum_4(3)
    sum_4(4)
    shout_ref[...] = shsum[:GROUP]

    dn = shsum[GROUP:]

    def combine(k):
        back_copies[k].wait()
        got(back.at[k, pl.ds(0, OTHERS)], b_s.at[k], b_r.at[k])
        return dot_tn(place_ref[k], back[k])

    for k in range(LOCAL):
        dn = dn + combine(k)

    mid = mid_ref[...]
    inv = inv_ref[...]
    u = dn * own_gain(gain_ref, t)
    finish = sum_rows_start(u * mid, st_buf, st_s, st_r)
    forward_3(0)
    total = finish()
    dmid = dyc_ref[...].astype(F32) + inv * u - mid * (inv * inv * inv * total * (1.0 / D))
    dmid_ref[...] = dmid
    low[...] = dmid.astype(BF16)
    own = pltpu.make_async_copy(low, dattn_hbm.at[:, cols(t, COLS)], l_own.at[0])
    own.start()
    dgain_ref[...] = jnp.sum(dn * mid * inv, axis=0, keepdims=True)
    f1, f2, f3, f4 = gather_stages(low, column_blocks(dattn_hbm, GROUP), f_s.at[0], f_r.at[0], send)
    f1()
    f2()
    forward_3(1)
    f3()
    forward_4(0)
    f4()
    forward_4(1)
    own.wait()
    for c in out_copies[LOCAL - 1]:
        c.wait()
    for n in range(6):
        wsum_ref[n // 2, pl.ds((n % 2) * wide // 2, wide // 2)] = shared_sums[n][2]()
    for c in sends:
        c.wait_send()


def moe_step(place, rown, nfull, dy, sg, su, sd, wg, wu, wd, grads, mid, inv, gain, dyc, cid):
    hid = wd.shape[1]
    wide = sd.shape[0]
    wshape = jax.ShapeDtypeStruct((LOCAL, hid, D), BF16)
    vmem = pltpu.VMEM
    return pl.pallas_call(
        moe_kernel,
        out_shape=(
            jax.ShapeDtypeStruct((LOCAL, ROWS, D), BF16),
            wshape,
            wshape,
            wshape,
            jax.ShapeDtypeStruct((GROUP, COLS), F32),
            jax.ShapeDtypeStruct((GROUP, COLS), F32),
            jax.ShapeDtypeStruct((1, COLS), F32),
            jax.ShapeDtypeStruct((GROUP, D), BF16),
            jax.ShapeDtypeStruct((3, wide, D), BF16),
            jax.ShapeDtypeStruct((EARLY, ROWS, COLS), BF16),
            jax.ShapeDtypeStruct((3, wide, D // GROUPS), F32),
        ),
        in_specs=[VM] + [ANY] * 10 + [VM] * 4,
        out_specs=(ANY, ANY, ANY, ANY, VM, VM, VM, ANY, ANY, VM, VM),
        scratch_shapes=[
            vmem((GROUP, wide), BF16),
            vmem((GROUP, wide), BF16),
            vmem((GROUP, wide), BF16),
            vmem((GROUP, D), BF16),
            vmem((GROUP, D), BF16),
            vmem((LOCAL, ROWS, D), BF16),
            vmem((LOCAL + 1, ROWS, D), BF16),
            vmem((LOCAL + 1, 4, ROWS, COLS), BF16),
            vmem((LOCAL + 1, 2, ROWS // 2, COLS), BF16),
            vmem((LOCAL + 1, 2, ROWS, COLS), BF16),
            vmem((2, 3, hid, D), BF16),
            vmem((3, ROWS, D), BF16),
            vmem((3, hid, D), BF16),
            vmem((ROWS, D), BF16),
            vmem((LOCAL, ROWS, COLS), BF16),
            vmem((LOCAL, ROWS, COLS), BF16),
            vmem((2 * GROUP, COLS), F32),
            vmem((GROUP, COLS), BF16),
            DMA((LOCAL, 6)),
            DMA((LOCAL, 6)),
            DMA((LOCAL + 1, 8)),
            DMA((LOCAL + 1, 8)),
            DMA((LOCAL,)),
            DMA((LOCAL,)),
            DMA((1, 9)),
            DMA((1, 9)),
            vmem((TENSOR, 8, GROUP), F32),
            DMA((TENSOR,)),
            DMA((TENSOR,)),
            DMA((5,)),
            DMA((2, 3)),
            DMA((LOCAL,)),
            DMA((4,)),
            DMA((LOCAL,)),
            DMA((3,)),
            DMA((LOCAL, 2)),
            vmem((6, 4, wide // 2, D // GROUPS), BF16),
        ]
        + two_phase_scratch(6, wide // 2, D // GROUPS)
        + [
            DMA((6, 4)),
            vmem((EARLY, 4, ROWS, COLS), BF16),
            vmem((EARLY, 4, ROWS, COLS), BF16),
            vmem((EARLY, 2, ROWS // 2, COLS), BF16),
            vmem((EARLY, 2, ROWS, COLS), BF16),
            DMA((EARLY, 8)),
            DMA((EARLY, 8)),
            DMA((EARLY, 4)),
        ],
        compiler_params=params(cid, 63.5),
        cost_estimate=pl.CostEstimate(
            flops=40 * 10**9, bytes_accessed=100 * MIB, transcendentals=0
        ),
        name="moe_step",
    )(place, rown, nfull, dy, sg, su, sd, wg, wu, wd, grads, mid, inv, gain, dyc)


def swap_halves(value):
    return pltpu.roll(value, 64, 1)


def turn(value, cosine, sine):
    return value * cosine + swap_halves(value) * sine


def lane_head(shape):
    lane = lax.broadcasted_iota(jnp.int32, shape, 1)
    return (lane >> 5) & 1


def regroup(dtype):
    n = 2 * HEAD
    given = lax.broadcasted_iota(jnp.int32, (n, n), 0)
    made = lax.broadcasted_iota(jnp.int32, (n, n), 1)
    r = made - 2 * NOPE
    turned = ((r >> 5) & 1) * HEAD + NOPE + (r >> 6) * (ROPE // 2) + (r & 31)
    source = jnp.where(made < NOPE, made, jnp.where(made < 2 * NOPE, made + ROPE, turned))
    return jnp.where(given == source, 1.0, 0.0).astype(dtype)


def band(index, rows):
    return pl.ds(pl.multiple_of(index * rows, rows), rows)


def hop_start(src, dst, rows, ss, rs, send_many):
    e, peers = expert_peers()
    dst[band(e, rows)] = src[band(e, rows)]
    targets = [(src.at[band(to, rows)], dst.at[band(e, rows)], to) for to, frm in peers]
    send_many(targets, dst.at[pl.ds(0, 15 * rows)], ss, rs, "expert")


def hop_wait(dst, rows, ss, rs):
    ref = dst.at[pl.ds(0, 15 * rows)]
    remote(ref, ref, ss, rs, "expert", lax.axis_index("expert")).wait_recv()


def one_hot(test):
    return jnp.where(test, 1.0, 0.0).astype(BF16)


def by_sixteen():
    made, given = iota((GROUP, GROUP), 0), iota((GROUP, GROUP), 1)
    return one_hot(given == (made & 15) * GROUPS + (made >> 4))


def seat_of_row(index):
    return one_hot(iota((GROUP, ROWS), 1).astype(F32) == index)


def row_of_seat(index):
    return one_hot(iota((ROWS, GROUP), 0).astype(F32) == index)


def near_stages(block, ss, rs, send):
    t, right, left, far, twin = x_peers()
    flip = twin - t

    def put(j, owner, to):
        send(block(owner), block(owner), ss.at[j], rs.at[j], "tensor", to)

    def arrived(j, owner):
        ref = block(owner)
        remote(ref, ref, ss.at[j], rs.at[j], "tensor", twin).wait_recv()

    def stage_1():
        put(0, t, right)
        put(1, t, left)
        put(2, t, twin)

    def stage_far():
        put(3, far, twin)

    def stage_2():
        arrived(0, left)
        put(4, left, twin)
        arrived(1, right)
        put(5, right, twin)

    def stage_3():
        arrived(2, twin)
        arrived(3, far + flip)
        arrived(4, left + flip)
        arrived(5, right + flip)

    return stage_1, stage_far, stage_2, stage_3


def sum_stages(theirs, mine, rows, sib, half, full, ss, rs, send):
    t, right, left, far, twin = x_peers()
    flip = twin - t
    order = (far, right, left, t)
    h = rows // 2

    def put(j, src, dst, to):
        send(src, dst, ss.at[j], rs.at[j], "tensor", to)

    def arrived(j, ref):
        remote(ref, ref, ss.at[j], rs.at[j], "tensor", twin).wait_recv()

    def stage_1():
        for j, owner in enumerate(order):
            put(j, theirs(owner + flip), sib.at[j], twin)

    def stage_2():
        arrived(0, sib.at[0])
        sib[0] = (mine(0) + sib[0].astype(F32)).astype(sib.dtype)
        put(4, sib.at[0, pl.ds(0, h)], half.at[0], right)
        put(5, sib.at[0, pl.ds(h, h)], half.at[1], left)

    def stage_3():
        for j, to in ((1, right), (2, left)):
            arrived(j, sib.at[j])
            arrived(3 + j, half.at[j - 1])
            both = mine(j) + sib[j].astype(F32)
            extra = half[j - 1].astype(F32)
            if j == 1:
                sib[j, :h] = (both[:h] + extra).astype(sib.dtype)
                sib[j, h:] = both[h:].astype(sib.dtype)
            else:
                sib[j, :h] = both[:h].astype(sib.dtype)
                sib[j, h:] = (both[h:] + extra).astype(sib.dtype)
            put(5 + j, sib.at[j], full.at[j - 1], to)

    def stage_4():
        arrived(3, sib.at[3])
        arrived(6, full.at[0])
        arrived(7, full.at[1])
        return mine(3) + sib[3].astype(F32) + full[0].astype(F32) + full[1].astype(F32)

    return stage_1, stage_2, stage_3, stage_4


def two_phase(src, own, land_a, part, land_b, ss, rs, first, send_many):
    e = lax.axis_index("expert")
    z, y = e // YN, lax.rem(e, YN)
    one, two = (y, z) if first == "y" else (z, y)

    def at(i, j):
        return (j, i) if first == "y" else (i, j)

    def device(i, j):
        dz, dy = at(i, j)
        return dz * YN + dy

    def plus(v, d):
        return lax.rem(v + d, 4)

    def arrived(n, ref):
        remote(ref, ref, ss.at[n], rs.at[n], "expert", e).wait_recv()

    def stage_1():
        targets = []
        for d in (1, 3, 2):
            i = plus(one, d)
            targets += [(src(*at(i, j)), land_a.at[d - 1, j], device(i, two)) for j in range(4)]
        send_many(targets, land_a, ss.at[0], rs.at[0], "expert")

    def stage_2():
        arrived(0, land_a)
        for j in range(4):
            total = own(*at(one, j))
            for d in range(3):
                total = total + land_a[d, j].astype(F32)
            part[j] = total.astype(BF16)
        targets = []
        for d in (1, 3, 2):
            j = plus(two, d)
            targets.append((part.at[j], land_b.at[d - 1], device(one, j)))
        send_many(targets, land_b, ss.at[1], rs.at[1], "expert")

    def stage_3():
        arrived(1, land_b)
        total = part[two].astype(F32)
        for d in range(3):
            total = total + land_b[d].astype(F32)
        return total

    return stage_1, stage_2, stage_3


def two_phase_scratch(pieces, rows, width):
    return [
        pltpu.VMEM((pieces, 3, 4, rows, width), BF16),
        pltpu.VMEM((pieces, 4, rows, width), BF16),
        pltpu.VMEM((pieces, 3, rows, width), BF16),
        DMA((pieces, 2)),
        DMA((pieces, 2)),
    ]


SLICE = 80
WIDE_LAT = LATENT + 2 * ROPE


def back_kernel(
    dattn_ref, mixed_ref, wout_ref, q_ref, exp_ref, kr_ref, probs_ref, cos_ref, sin_ref, lat_ref, linv_ref,
    lgain_ref, x_ref, inv_ref, gain_ref, dmid_ref, ffn_ref, mid_ref, shout_ref, fearly_ref, gate_ref, seat_ref, seat_row_ref,
    place_hbm, normed_hbm, wq_hbm, wexp_hbm, comp_hbm, wl_hbm, part_hbm,
    out_ref, dx_ref, gwq_ref, gwexp_ref, gwout_ref, gwlat_ref, gains_ref,
    normed, wq, wexp, comp, wl, place,
    own, sib, half, full, res, fback,
    npart, nsib, nhalf, nfull,
    swq, swexp, swout, swlat, rwlat, lowlat, *rest
):
    q_red, e_red, o_red, rest = rest[:5], rest[5:10], rest[10:15], rest[15:]
    (
        cbuf, cgot, dlat, gm, gin, xh, oh, xl, ol,
        st_buf, st_s, st_r,
        p_s, p_r, fb_s, fb_r, n_s, n_r, w_s, w_r, c_s, c_r, dl_s, dl_r, gm_s, gm_r, gt_s, gt_r, wl_s, wl_r,
        oa_s, oa_r, ob_s, ob_r, xa_s, xa_r, xb_s, xb_r, l_in, l_own,
    ) = rest
    t, right, left, far, twin = x_peers()
    e, peers = expert_peers()
    others = [(lax.rem(t + j, TENSOR), lax.rem(t + TENSOR - j, TENSOR)) for j in range(1, TENSOR)]
    greet([("tensor", to) for to, frm in others] + [("expert", to) for to, frm in peers])
    sends = []

    def send(src, dst, ssem, rsem, axis, to):
        c = remote(src, dst, ssem, rsem, axis, to)
        c.start()
        sends.append(c)

    def send_many(targets, total, ssem, rsem, axis):
        for src, dst, to in targets:
            remote(src, dst, ssem, rsem, axis, to).start()
        sends.append(remote(total, total, ssem, rsem, axis, targets[0][2]))

    def got(ref, ssem, rsem):
        remote(ref, ref, ssem, rsem, "tensor", twin).wait_recv()

    half_rope = ROPE // 2
    for i in (1, 3):
        wl[LATENT + i * half_rope : LATENT + (i + 1) * half_rope] = jnp.zeros((half_rope, COLS), BF16)
    wide = [
        (wq_hbm, wq),
        (wexp_hbm, wexp),
        (normed_hbm, normed),
        (comp_hbm, comp),
        (place_hbm, place),
        (wl_hbm.at[pl.ds(0, LATENT), cols(t, COLS)], wl.at[pl.ds(0, LATENT)]),
        (
            wl_hbm.at[pl.ds(LATENT, half_rope), cols(t, COLS)],
            wl.at[pl.ds(LATENT, half_rope)],
        ),
        (
            wl_hbm.at[pl.ds(LATENT + half_rope, half_rope), cols(t, COLS)],
            wl.at[pl.ds(LATENT + 2 * half_rope, half_rope)],
        ),
    ]
    early = [pltpu.make_async_copy(src, dst, l_in.at[i]) for i, (src, dst) in enumerate(wide)]
    for c in early:
        c.start()

    order = (far, right, left, t)
    chunks = []
    late = LOCAL - EARLY
    for k in range(late):

        def theirs(owner, k=k):
            return part_hbm.at[EARLY + k, :, cols(owner, COLS)]

        def mine(j, k=k):
            return own[k, j].astype(F32)

        chunks.append(
            sum_stages(
                theirs, mine, ROWS, sib.at[k], half.at[k], full.at[k], p_s.at[k], p_r.at[k], send
            )
        )
    own_loads = {}
    for k in range(late):
        for j, owner in enumerate(order):
            c = pltpu.make_async_copy(
                part_hbm.at[EARLY + k, :, cols(owner, COLS)], own.at[k, j], l_own.at[k, j]
            )
            c.start()
            own_loads[k, j] = c
        chunks[k][0]()

    def return_rows(k, rows):
        fback[k, seat_rows(e)] = rows[seat_rows(e)]
        targets = [(rows.at[seat_rows(to)], fback.at[k, seat_rows(e)], to) for to, frm in peers]
        send_many(targets, fback.at[k, pl.ds(0, OTHERS)], fb_s.at[k], fb_r.at[k], "expert")

    for k in range(EARLY):
        return_rows(k, fearly_ref.at[k])

    def forward_2(k):
        for j in range(4):
            own_loads[k, j].wait()
        chunks[k][1]()

    def forward_4(k):
        res[k] = chunks[k][3]().astype(BF16)
        return_rows(EARLY + k, res.at[k])

    def reduce_pieces(scratch, ref_of, value_of):
        land_a, part, land_b, ss, rs = scratch
        return [
            two_phase(
                lambda dz, dy, i=i: ref_of(i, dz * YN + dy),
                lambda dz, dy, i=i: value_of(i, dz * YN + dy).astype(F32),
                land_a.at[i], part.at[i], land_b.at[i], ss.at[i], rs.at[i], "yz"[i], send_many,
            )
            for i in range(2)
        ]

    def run(pieces, stage):
        return [piece[stage]() for piece in pieces]

    def rows_of(i, n):
        return pl.ds(i * n, n)

    query_sum = reduce_pieces(
        q_red,
        lambda i, d: swq.at[rows_of(i, HEAD), cols(d, 128)],
        lambda i, d: swq[rows_of(i, HEAD), cols(d, 128)],
    )
    expand_sum = reduce_pieces(
        e_red, lambda i, d: swexp.at[d, :, rows_of(i, 256)], lambda i, d: swexp[d, :, rows_of(i, 256)]
    )
    out_sum = reduce_pieces(
        o_red,
        lambda i, d: swout.at[rows_of(i, VDIM), cols(d, 128)],
        lambda i, d: swout[rows_of(i, VDIM), cols(d, 128)],
    )

    mixed = mixed_ref[...]
    for n in range(4):
        s = slice(n * 512, (n + 1) * 512)
        swout[:, s] = dot_tn(mixed, dattn_ref[:, s]).astype(BF16)
    run(out_sum, 0)

    scale = HEAD ** (-0.5)
    cosine, sine = cos_ref[...], sin_ref[...]
    head = lane_head((GROUP, 2 * ROPE))
    dattn = dattn_ref[...]
    dmix = dot_nt(dattn, wout_ref[...]).astype(BF16)
    kr = kr_ref[...]
    qr = q_ref[:, 2 * NOPE :]
    turned = jnp.zeros((GROUP, 2 * ROPE), F32)
    rope_sum = jnp.zeros((GROUP, 2 * ROPE), F32)
    dq_parts = []
    dexp_parts = []
    for h in range(2):
        p = probs_ref[h]
        dm = dmix[:, h * VDIM : (h + 1) * VDIM]
        k = exp_ref[:, 256 * h : 256 * h + NOPE]
        v = exp_ref[:, 256 * h + NOPE : 256 * h + NOPE + VDIM]
        dv = dot_tn(p.astype(BF16), dm)
        dp = dot_nt(dm, v)
        ds = (p * (dp - jnp.sum(dp * p, axis=1, keepdims=True))).astype(BF16)
        dq_parts.append((dot_nn(ds, k) * scale).astype(BF16))
        turned = turned + jnp.where(head == h, dot_nn(ds, kr) * scale, 0.0)
        dk = dot_tn(ds, q_ref[:, h * NOPE : (h + 1) * NOPE]) * scale
        rope_sum = rope_sum + jnp.where(head == h, dot_tn(ds, qr) * scale, 0.0)
        dexp_parts += [dk.astype(BF16), dv.astype(BF16)]
    dexp = jnp.concatenate(dexp_parts, axis=1)
    dq_parts.append(turn(turned, cosine, -sine).astype(BF16))
    dq = dot_nt(jnp.concatenate(dq_parts, axis=1), regroup(BF16)).astype(BF16)

    early[1].wait()
    cpart = dot_nt(dexp, wexp[...])
    share = GROUP // TENSOR
    for i in range(TENSOR):
        r = slice(i * share, (i + 1) * share)
        cbuf[i, :, :LATENT] = cpart[r].astype(BF16)
        cbuf[i, :, LATENT:] = rope_sum[r].astype(BF16)
    for j, (to, frm) in enumerate(others):
        send(cbuf.at[to], cgot.at[t], c_s.at[j], c_r.at[j], "tensor", to)

    early[0].wait()
    for n in range(TENSOR):
        npart[n] = dot_nt(dq, wq[n * COLS : (n + 1) * COLS, :]).astype(BF16)
    n1, n2, n3, n4 = sum_stages(
        lambda owner: npart.at[owner],
        lambda j: npart[order[j]].astype(F32),
        GROUP, nsib, nhalf, nfull, n_s, n_r, send,
    )
    n1()
    forward_2(0)

    early[2].wait()
    for n in range(4):
        s = slice(n * 512, (n + 1) * 512)
        swq[:, s] = dot_tn(dq, normed[:, s]).astype(BF16)
    early[3].wait()
    gwexp = dot_tn(comp[...], dexp)
    for i in range(GROUPS):
        swexp[i] = gwexp[32 * i : 32 * (i + 1)].astype(BF16)
    run(expand_sum, 0)
    run(query_sum, 0)

    total = cbuf[t].astype(F32)
    for j, (to, frm) in enumerate(others):
        got(cgot.at[frm], c_s.at[j], c_r.at[j])
        total = total + cgot[frm].astype(F32)
    mine_rows = pl.ds(pl.multiple_of(t * share, share), share)
    dc = total[:, :LATENT]
    lat = lat_ref[mine_rows, :]
    linv = linv_ref[mine_rows, :]
    lu = dc * gain_row(lgain_ref)
    dot = jnp.sum(lu * lat, axis=1, keepdims=True)
    dlat[t, :, :LATENT] = (linv * lu - lat * (linv * linv * linv * dot * (1.0 / LATENT))).astype(BF16)
    both = total[:, LATENT:]
    both = both + pltpu.roll(both, 2 * ROPE - ROPE // 2, 1)
    both = jnp.where(lane_head((share, 2 * ROPE)) == 0, both, 0.0)
    dlat[t, :, LATENT:] = turn(both, cos_ref[mine_rows, :], -sin_ref[mine_rows, :]).astype(BF16)
    for j, (to, frm) in enumerate(others):
        send(dlat.at[t], dlat.at[t], dl_s.at[j], dl_r.at[j], "tensor", to)
    lgain_row = jnp.sum(dc * lat * linv, axis=0, keepdims=True)

    n2()
    forward_2(1)
    n3()
    chunks[0][2]()

    def undeal_1(value, high, ss, rs):
        high[0] = dot_tn(seat_of_row(seat_ref[...]), value).astype(BF16)
        hop_start(high.at[0], high.at[1], PADCAP, ss, rs, send_many)

    def undeal_2(high, low, ss, rs, ss_next, rs_next):
        hop_wait(high.at[1], PADCAP, ss, rs)
        low[0] = dot_tn(row_of_seat(seat_row_ref[...]), high[1]).astype(BF16)
        hop_start(low.at[0], low.at[1], GROUPS, ss_next, rs_next, send_many)

    def undeal_3(low, ss, rs):
        hop_wait(low.at[1], GROUPS, ss, rs)
        return dot_tn(by_sixteen(), low[1]).astype(BF16)

    for j, (to, frm) in enumerate(others):
        got(dlat.at[frm], dl_s.at[j], dl_r.at[j])
    for i in (5, 6, 7):
        early[i].wait()
    dl = dlat[...].reshape(GROUP, WIDE_LAT)
    latent_cols = dot_nn(dl, wl[...])
    dn = latent_cols + n4()
    xd = x_ref[...].astype(F32)
    inv = inv_ref[...]
    u = dn * own_gain(gain_ref, t)
    finish = sum_rows_start(u * xd, st_buf, st_s, st_r)
    run(out_sum, 1)
    run(expand_sum, 1)
    run(query_sum, 1)
    total = finish()
    chunks[1][2]()
    dx = (dmid_ref[...] + inv * u - xd * (inv * inv * inv * total * (1.0 / D))).astype(BF16)
    undeal_1(dx, xh, xa_s, xa_r)
    forward_4(0)
    early[4].wait()

    def combine(k, rows):
        gates = jnp.broadcast_to(gate_ref[k][:, None, :], (GROUPS, PADCAP, GROUP)).reshape(ROWS, GROUP)
        weight = place[k].astype(F32) * gates
        high = weight.astype(BF16)
        low = (weight - high.astype(F32)).astype(BF16)
        return dot_tn(high, rows) + dot_tn(low, rows)

    routed = mid_ref[...] + shout_ref[...]
    for k in range(EARLY):
        got(fback.at[k, pl.ds(0, OTHERS)], fb_s.at[k], fb_r.at[k])
        routed = routed + combine(k, fback[k])
    gm[...] = jnp.zeros(gm.shape, F32)
    gm[0:1] = jnp.sum(dn * xd * inv, axis=0, keepdims=True)
    gm[1:2] = ffn_ref[...]
    gm[2:3] = lgain_row[:, :COLS]
    gm[3:4] = lgain_row[:, COLS:]
    gin[e] = gm[...]
    send_many([(gm, gin.at[e], to) for to, frm in peers], gin.at[pl.ds(0, GROUPS - 1)], gm_s, gm_r, "expert")

    pick_rows = lax.broadcasted_iota(jnp.int32, (WIDE_LAT, 128), 0)
    pick_cols = lax.broadcasted_iota(jnp.int32, (WIDE_LAT, 128), 1)
    pick_own = jnp.where((pick_rows == pick_cols + t * SLICE) & (pick_cols < SLICE), 1.0, 0.0).astype(BF16)
    dl_own = dot_nn(dl, pick_own).astype(BF16)
    for n in range(4):
        s = slice(n * 512, (n + 1) * 512)
        swlat[:, s] = dot_tn(dl_own, normed[:, s])[:SLICE].astype(BF16)
    rwlat[e] = swlat[:, cols(e, 128)]
    targets = [(swlat.at[:, cols(to, 128)], rwlat.at[e], to) for to, frm in peers]
    send_many(targets, rwlat.at[pl.ds(0, GROUPS - 1)], w_s, w_r, "expert")

    forward_4(1)
    undeal_2(xh, xl, xa_s, xa_r, xb_s, xb_r)
    for k in range(late):
        got(fback.at[EARLY + k, pl.ds(0, OTHERS)], fb_s.at[EARLY + k], fb_r.at[EARLY + k])
        routed = routed + combine(EARLY + k, fback[EARLY + k])
    out = routed.astype(BF16)
    undeal_1(out, oh, oa_s, oa_r)
    dx_ref[...] = undeal_3(xl, xb_s, xb_r)

    got(gin.at[pl.ds(0, GROUPS - 1)], gm_s, gm_r)
    gains_ref[t] = jnp.sum(gin[...], axis=0)
    for j, (to, frm) in enumerate(others):
        send(gains_ref.at[t], gains_ref.at[t], gt_s.at[j], gt_r.at[j], "tensor", to)
    got(rwlat.at[pl.ds(0, GROUPS - 1)], w_s, w_r)
    lat_sum = rwlat[0].astype(F32)
    for i in range(1, GROUPS):
        lat_sum = lat_sum + rwlat[i].astype(F32)
    lowlat[...] = lat_sum.astype(BF16)
    gwlat_ref[t] = lowlat[...]
    for j, (to, frm) in enumerate(others):
        send(lowlat, gwlat_ref.at[t], wl_s.at[j], wl_r.at[j], "tensor", to)
    undeal_2(oh, ol, oa_s, oa_r, ob_s, ob_r)
    gwout_ref[...] = jnp.concatenate(run(out_sum, 2), axis=0)
    gwq_ref[...] = jnp.transpose(jnp.concatenate(run(query_sum, 2), axis=0))
    gwexp_ref[...] = jnp.concatenate(run(expand_sum, 2), axis=1)
    out_ref[...] = undeal_3(ol, ob_s, ob_r)
    for j, (to, frm) in enumerate(others):
        got(gains_ref.at[frm], gt_s.at[j], gt_r.at[j])
        got(gwlat_ref.at[frm], wl_s.at[j], wl_r.at[j])
    for c in sends:
        c.wait_send()


def back_step(small, large, cid):
    vmem = pltpu.VMEM

    def out(*shape, dtype=BF16):
        return jax.ShapeDtypeStruct(shape, dtype)

    late = LOCAL - EARLY
    pair = lambda n: [DMA((n,)), DMA((n,))]
    grid_pair = lambda m, n: [DMA((m, n)), DMA((m, n))]
    return pl.pallas_call(
        back_kernel,
        out_shape=(
            out(GROUP, COLS),
            out(GROUP, COLS),
            out(D // GROUPS, 2 * HEAD, dtype=F32),
            out(LATENT // GROUPS, 512, dtype=F32),
            out(2 * VDIM, D // GROUPS, dtype=F32),
            out(TENSOR, SLICE, D // GROUPS),
            out(TENSOR, 8, COLS, dtype=F32),
        ),
        in_specs=[VM] * len(small) + [ANY] * len(large),
        out_specs=(VM,) * 7,
        scratch_shapes=[
            vmem((GROUP, D), BF16),
            vmem((D, 2 * HEAD), BF16),
            vmem((LATENT, 512), BF16),
            vmem((GROUP, LATENT), BF16),
            vmem((WIDE_LAT, COLS), BF16),
            vmem((LOCAL, ROWS, GROUP), BF16),
            vmem((late, 4, ROWS, COLS), BF16),
            vmem((late, 4, ROWS, COLS), BF16),
            vmem((late, 2, ROWS // 2, COLS), BF16),
            vmem((late, 2, ROWS, COLS), BF16),
            vmem((late, ROWS, COLS), BF16),
            vmem((LOCAL, ROWS, COLS), BF16),
            vmem((TENSOR, GROUP, COLS), BF16),
            vmem((4, GROUP, COLS), BF16),
            vmem((2, GROUP // 2, COLS), BF16),
            vmem((2, GROUP, COLS), BF16),
            vmem((2 * HEAD, D), BF16),
            vmem((GROUPS, LATENT // GROUPS, 512), BF16),
            vmem((2 * VDIM, D), BF16),
            vmem((SLICE, D), BF16),
            vmem((GROUPS, SLICE, D // GROUPS), BF16),
            vmem((SLICE, D // GROUPS), BF16),
        ]
        + two_phase_scratch(2, HEAD, D // GROUPS)
        + two_phase_scratch(2, LATENT // GROUPS, 256)
        + two_phase_scratch(2, VDIM, D // GROUPS)
        + [
            vmem((TENSOR, GROUP // TENSOR, WIDE_LAT), BF16),
            vmem((TENSOR, GROUP // TENSOR, WIDE_LAT), BF16),
            vmem((TENSOR, GROUP // TENSOR, WIDE_LAT), BF16),
            vmem((8, COLS), F32),
            vmem((GROUPS, 8, COLS), F32),
            vmem((2, ROWS, COLS), BF16),
            vmem((2, ROWS, COLS), BF16),
            vmem((2, GROUP, COLS), BF16),
            vmem((2, GROUP, COLS), BF16),
        ]
        + sum_rows_scratch()
        + grid_pair(late, 8)
        + pair(LOCAL)
        + pair(8)
        + [DMA] * 2
        + pair(7)
        + pair(7)
        + [DMA] * 2
        + pair(7)
        + pair(7)
        + [DMA] * 8
        + [DMA((8,)), DMA((late, 4))],
        compiler_params=params(cid, 63),
        name="back_step",
    )(*small, *large)


def gather_stages(source, block, ss, rs, send):
    t, right, left, far, twin = x_peers()
    flip = twin - t

    def put(j, ref, to, src=None):
        send(ref if src is None else src, ref, ss.at[j], rs.at[j], "tensor", to)

    def arrived(j, ref):
        remote(ref, ref, ss.at[j], rs.at[j], "tensor", twin).wait_recv()

    def stage_1():
        put(0, block(t, None), right, source)
        put(1, block(t, None), left, source)
        put(4, block(t, None), twin, source)

    def stage_2():
        arrived(0, block(left, None))
        put(2, block(left, 0), right)
        put(5, block(left, None), twin)
        arrived(1, block(right, None))
        put(3, block(right, 1), left)
        put(6, block(right, None), twin)

    def stage_3():
        arrived(2, block(far, 0))
        put(7, block(far, 0), twin)
        arrived(3, block(far, 1))
        put(8, block(far, 1), twin)

    def stage_4():
        arrived(4, block(twin, None))
        arrived(5, block(left + flip, None))
        arrived(6, block(right + flip, None))
        arrived(7, block(far + flip, 0))
        arrived(8, block(far + flip, 1))

    return stage_1, stage_2, stage_3, stage_4


def column_blocks(ref, rows):
    def block(owner, part):
        r = pl.ds(0, rows) if part is None else pl.ds(part * (rows // 2), rows // 2)
        return ref.at[r, cols(owner, COLS)]

    return block


def gain_row(ref):
    return ref[...].astype(F32).reshape(1, ref.shape[0])


def own_gain(ref, t):
    whole = gain_row(ref)
    total = jnp.zeros((1, COLS), F32)
    for i in range(TENSOR):
        total = total + jnp.where(t == i, whole[:, i * COLS : (i + 1) * COLS], 0.0)
    return total


def iota(shape, dim):
    return lax.broadcasted_iota(jnp.int32, shape, dim)


def deal_in_kernel(lengths, order, group):
    n = lengths.shape[1]
    i, j = iota((n, n), 0), iota((n, n), 1)
    same, before = i == j, j < i

    def column(row):
        return jnp.sum(jnp.where(same, row, 0.0), axis=1, keepdims=True)

    def row(col):
        return jnp.sum(jnp.where(same, col, 0.0), axis=0, keepdims=True)

    def exclusive(values):
        return jnp.sum(jnp.where(before, values, 0.0), axis=1, keepdims=True)

    hit = column(order) == j.astype(F32)
    begins_col = exclusive(lengths)
    begins = row(begins_col)
    dealt_lengths = row(jnp.sum(jnp.where(hit, lengths, 0.0), axis=1, keepdims=True))
    dealt_col = exclusive(dealt_lengths)
    dealt = row(dealt_col)
    dealt_source_col = jnp.sum(jnp.where(hit, begins, 0.0), axis=1, keepdims=True)
    dealt_source = row(dealt_source_col)
    given = jnp.sum(jnp.where(hit, dealt_col, 0.0), axis=0, keepdims=True)
    given_col = column(given)

    def find(rows, lanes, starts, values):
        dim = 1 if lanes else 0
        shape = (GROUP, n) if lanes else (n, GROUP)
        place = jnp.sum(jnp.where(rows >= starts, 1.0, 0.0), axis=dim, keepdims=True) - 1.0
        on = iota(shape, dim).astype(F32) == place
        return place, jnp.sum(jnp.where(on, values, 0.0), axis=dim, keepdims=True)

    first = group * GROUP
    rows = (iota((GROUP, 1), 0) + first).astype(F32)
    rows_row = (iota((1, GROUP), 1) + first).astype(F32)
    which, start = find(rows, True, dealt, dealt)
    unused, shift = find(rows, True, dealt, dealt_source - dealt)
    which_row, shift_row = find(rows_row, False, dealt_col, dealt_source_col - dealt_col)
    source, source_row = rows + shift, rows_row + shift_row

    def rest(value):
        return value - GROUPS * jnp.floor(value * (1.0 / GROUPS))

    ahead = (rest(source) == rest(source_row)) & (source_row < source)
    rank = jnp.sum(jnp.where(ahead, 1.0, 0.0), axis=1, keepdims=True)
    seat = rest(source) * PADCAP + rank

    mine = (iota((GROUP, 1), 0) * GROUPS + group).astype(F32)
    mine_row = (iota((1, GROUP), 1) * GROUPS + group).astype(F32)
    unused, move = find(mine, True, begins, given - begins)
    unused, move_row = find(mine_row, False, begins_col, given_col - begins_col)
    to = jnp.floor((mine + move) * (1.0 / GROUP))
    to_row = jnp.floor((mine_row + move_row) * (1.0 / GROUP))
    ahead = (to == to_row) & (iota((GROUP, GROUP), 0) < iota((GROUP, GROUP), 1))
    rank = jnp.sum(jnp.where(ahead, 1.0, 0.0), axis=0, keepdims=True)
    seat_row = to_row * PADCAP + rank
    return rows - start, which, which_row, seat, seat_row


def front_kernel(
    tok_ref, cot_ref, len_ref, ord_ref, routes_ref, gates_ref, gain_ref, lgain_ref, fgain_ref,
    wq_hbm, wl_hbm, wexp_hbm, wout_hbm,
    xc_ref, dyc_ref, mid_ref, inv2_ref, ncols_ref, normed_ref, inv_ref, q_ref, exp_ref, kr_ref, comp_ref,
    lat_ref, linv_ref, probs_ref, mixed_ref, place_ref, gate_ref, seat_ref, seat_row_ref, cos_ref, sin_ref, dyfull, nfull,
    rown_hbm, grads_hbm,
    hop_a, hop_b, hop_c, hop_d, xfull, wq, wl, wexp, wout, wrope, apart, sib, half, full, gout, dbuf,
    st_buf, st_s, st_r,
    ha_s, ha_r, hb_s, hb_r, xg_s, xg_r, yg_s, yg_r, ng_s, ng_r, gg_s, gg_r, r_s, r_r, d_s, d_r, e_s, e_r, l_in, l_own, l_last,
):
    t, right, left, far, twin = x_peers()
    e, peers = expert_peers()
    greet(
        [("tensor", lax.rem(t + j, TENSOR)) for j in range(1, TENSOR)]
        + [("expert", to) for to, frm in peers]
    )
    sends = []

    def send(src, dst, ssem, rsem, axis, to):
        c = remote(src, dst, ssem, rsem, axis, to)
        c.start()
        sends.append(c)

    def send_many(targets, total, ssem, rsem, axis):
        for src, dst, to in targets:
            remote(src, dst, ssem, rsem, axis, to).start()
        sends.append(remote(total, total, ssem, rsem, axis, targets[0][2]))

    def got(ref, ssem, rsem):
        remote(ref, ref, ssem, rsem, "tensor", twin).wait_recv()

    def local(src, dst, sem):
        c = pltpu.make_async_copy(src, dst, sem)
        c.start()
        return c

    sixteen = by_sixteen()
    hop_a[:, :COLS] = dot_nn(sixteen, tok_ref[...]).astype(BF16)
    hop_a[:, COLS:] = dot_nn(sixteen, cot_ref[...]).astype(BF16)
    hop_start(hop_a, hop_b, GROUPS, ha_s, ha_r, send_many)
    early = [
        local(src, dst, l_in.at[i])
        for i, (src, dst) in enumerate([(wl_hbm, wl), (wq_hbm, wq), (wexp_hbm, wexp), (wout_hbm, wout)])
    ]

    offset, which, which_row, seat, seat_row = deal_in_kernel(
        len_ref[...].astype(F32), ord_ref[...].astype(F32), e
    )
    seat_ref[...] = seat
    seat_row_ref[...] = seat_row

    outward = row_of_seat(seat_row)
    hop_wait(hop_b, GROUPS, ha_s, ha_r)
    hop_c[...] = dot_nn(outward, hop_b[...]).astype(BF16)
    hop_start(hop_c, hop_d, PADCAP, hb_s, hb_r, send_many)
    hr = ROPE // 2
    lane = iota((GROUP, 2 * ROPE), 1)
    power = (lane & (hr - 1)).astype(F32) * (1.0 / hr)
    angle = offset * jnp.exp(power * (-math.log(10000.0)))
    cosine = jnp.cos(angle)
    sine = jnp.sin(angle)
    sine = jnp.where(lane < ROPE, -sine, sine)
    cos_ref[...] = cosine
    sin_ref[...] = sine

    number = iota((EXPERTS, 1), 0)
    expert = (number & 15) * LOCAL + (number >> 4)
    member = jnp.zeros((EXPERTS, GROUP), F32)
    gate_of = jnp.zeros((EXPERTS, GROUP), F32)
    for k in range(TOP):
        hit = routes_ref[k : k + 1, :] == expert
        member = member + jnp.where(hit, 1.0, 0.0)
        gate_of = gate_of + jnp.where(hit, gates_ref[k : k + 1, :], 0.0)
    earlier = jnp.where(iota((GROUP, GROUP), 0) < iota((GROUP, GROUP), 1), 1.0, 0.0).astype(BF16)
    count = dot_nn(member.astype(BF16), earlier)
    slot = jnp.where((member > 0.5) & (count < CAP - 0.5), count, -1.0)
    seats = iota((GROUPS, PADCAP, GROUP), 1).astype(F32)
    slot_gates = []
    for k in range(LOCAL):
        s = slice(k * GROUPS, (k + 1) * GROUPS)
        gate_ref[k] = gate_of[s]
        wide = jnp.broadcast_to(slot[s][:, None, :], (GROUPS, PADCAP, GROUP))
        on = jnp.where(wide == seats, 1.0, 0.0)
        place_ref[k] = on.reshape(ROWS, GROUP).astype(BF16)
        weight = on * jnp.broadcast_to(gate_of[s][:, None, :], (GROUPS, PADCAP, GROUP))
        slot_gates.append(jnp.sum(weight.reshape(ROWS, GROUP), axis=1, keepdims=True))
    early[0].wait()
    for i in range(4):
        row = LATENT + (i // 2) * hr
        wrope[i * hr : (i + 1) * hr] = wl[row : row + hr]
    inward = seat_of_row(seat)
    hop_wait(hop_d, PADCAP, hb_s, hb_r)

    xc_ref[...] = dot_nn(inward, hop_d[:, :COLS]).astype(BF16)
    xfull[:, cols(t, COLS)] = xc_ref[...]
    xg1, xg2, xg3, xg4 = gather_stages(xc_ref, column_blocks(xfull, GROUP), xg_s, xg_r, send)
    xg1()
    dyc_ref[...] = dot_nn(inward, hop_d[:, COLS:]).astype(BF16)
    dyfull[:, cols(t, COLS)] = dyc_ref[...]
    yg1, yg2, yg3, yg4 = gather_stages(dyc_ref, column_blocks(dyfull, GROUP), yg_s, yg_r, send)
    yg1()
    blocks = (t, far)

    def slot_gradients(b):
        for k in range(LOCAL):
            gout[b, k] = (slot_gates[k] * dot_nn(place_ref[k], dyfull[:, cols(blocks[b], COLS)])).astype(BF16)

    own_grads = {}

    def send_gradients(p, b):
        two = pl.ds(2 * p, 2)
        landed = grads_hbm.at[two, seat_rows(e), cols(blocks[b], COLS)]
        own_grads[p, b] = local(gout.at[b, two, seat_rows(e)], landed, l_own.at[p, b])
        targets = [(gout.at[b, two, seat_rows(to)], landed, to) for to, frm in peers]
        send_many(targets, gout.at[b, two, pl.ds(0, OTHERS)], d_s.at[p, b], d_r.at[p, b], "expert")

    slot_gradients(0)
    send_gradients(0, 0)
    send_gradients(1, 0)
    xg2()
    yg2()
    xg3()
    yg3()
    slot_gradients(1)
    send_gradients(0, 1)
    send_gradients(1, 1)
    xg4()

    def grad_block(k):
        return lambda owner: grads_hbm.at[k, :, cols(owner, COLS)]

    spread = [near_stages(grad_block(k), gg_s.at[k], gg_r.at[k], send) for k in range(LOCAL)]
    seen = set()

    def gradients(k, b):
        p = k // 2
        if (p, b) not in seen:
            seen.add((p, b))
            own_grads[p, b].wait()
            got(gout.at[b, pl.ds(2 * p, 2), pl.ds(0, OTHERS)], d_s.at[p, b], d_r.at[p, b])
        spread[k][b]()

    gradients(0, 0)

    xd = xfull[...].astype(F32)
    inv = lax.rsqrt(jnp.sum(xd * xd, axis=1, keepdims=True) * (1.0 / D) + EPS)
    inv_ref[...] = inv
    normed = (xd * inv * gain_row(gain_ref)).astype(BF16)
    normed_ref[...] = normed
    lat = dot_nt(normed, wl[:LATENT])
    lat_ref[...] = lat
    linv = lax.rsqrt(jnp.sum(lat * lat, axis=1, keepdims=True) * (1.0 / LATENT) + EPS)
    linv_ref[...] = linv
    kr = turn(dot_nt(normed, wrope[...]), cosine, sine).astype(BF16)
    kr_ref[...] = kr
    early[1].wait()
    pre = lax.dot_general(
        dot_nn(normed, wq[...]),
        regroup(F32),
        (((1,), (0,)), ((), ())),
        precision=lax.Precision.HIGHEST,
        preferred_element_type=F32,
    )
    q_ref[:, : 2 * NOPE] = pre[:, : 2 * NOPE].astype(BF16)
    qr = turn(pre[:, 2 * NOPE :], cosine, sine)
    q_ref[:, 2 * NOPE :] = qr.astype(BF16)
    comp = (lat * linv * gain_row(lgain_ref)).astype(BF16)
    comp_ref[...] = comp
    early[2].wait()
    expanded = dot_nn(comp, wexp[...]).astype(BF16)
    exp_ref[...] = expanded

    head = lane_head((GROUP, 2 * ROPE))
    allowed = (which == which_row) & (iota((GROUP, GROUP), 0) >= iota((GROUP, GROUP), 1))
    scale = HEAD ** (-0.5)
    for h in range(2):
        q = q_ref[:, h * NOPE : (h + 1) * NOPE]
        k = expanded[:, 256 * h : 256 * h + NOPE]
        v = expanded[:, 256 * h + NOPE : 256 * h + NOPE + VDIM]
        turned = jnp.where(head == h, qr, 0.0).astype(BF16)
        raw = (dot_nt(q, k) + dot_nt(turned, kr)) * scale
        scores = jnp.where(allowed, raw, -1e30)
        expo = jnp.exp(scores - jnp.max(scores, axis=1, keepdims=True))
        probs = expo / jnp.sum(expo, axis=1, keepdims=True)
        probs_ref[h] = probs
        mixed_ref[:, h * VDIM : (h + 1) * VDIM] = dot_nn(probs.astype(BF16), v).astype(BF16)
    mixed = mixed_ref[...]
    early[3].wait()
    for n in range(TENSOR):
        apart[n] = dot_nn(mixed, wout[:, n * COLS : (n + 1) * COLS]).astype(BF16)

    order = (far, right, left, t)
    r1, r2, r3, r4 = sum_stages(
        lambda owner: apart.at[owner],
        lambda j: apart[order[j]].astype(F32),
        GROUP, sib, half, full, r_s, r_r, send,
    )
    r1()
    r2()
    r3()
    gradients(1, 0)
    mid = xc_ref[...].astype(F32) + r4()
    mid_ref[...] = mid
    finish = sum_rows_start(mid * mid, st_buf, st_s, st_r)
    inv2 = lax.rsqrt(finish() * (1.0 / D) + EPS)
    inv2_ref[...] = inv2
    ncols_ref[...] = (mid * inv2 * own_gain(fgain_ref, t)).astype(BF16)
    nfull[:, cols(t, COLS)] = ncols_ref[...]
    ng1, ng2, ng3, ng4 = gather_stages(ncols_ref, column_blocks(nfull, GROUP), ng_s, ng_r, send)
    ng1()
    own_rows = {}

    def dispatch(b):
        for p in range(2):
            for k in (2 * p, 2 * p + 1):
                dbuf[b, k] = dot_nn(place_ref[k], nfull[:, cols(blocks[b], COLS)]).astype(BF16)
            two = pl.ds(2 * p, 2)
            landed = rown_hbm.at[b, two, seat_rows(e)]
            own_rows[p, b] = local(dbuf.at[b, two, seat_rows(e)], landed, l_last.at[p, b])
            targets = [(dbuf.at[b, two, seat_rows(to)], landed, to) for to, frm in peers]
            send_many(targets, dbuf.at[b, two, pl.ds(0, OTHERS)], e_s.at[p, b], e_r.at[p, b], "expert")

    dispatch(0)
    spread[0][2]()
    ng2()
    gradients(2, 0)
    ng3()
    dispatch(1)
    gradients(3, 0)
    gradients(0, 1)
    gradients(1, 1)
    spread[1][2]()
    gradients(2, 1)
    gradients(3, 1)
    spread[2][2]()
    yg4()
    ng4()
    spread[3][2]()
    for k in range(LOCAL):
        spread[k][3]()
    for p in range(2):
        for b in range(2):
            own_rows[p, b].wait()
            got(dbuf.at[b, pl.ds(2 * p, 2), pl.ds(0, OTHERS)], e_s.at[p, b], e_r.at[p, b])
    for c in sends:
        c.wait_send()


def front_step(small, large, cid):
    vmem = pltpu.VMEM

    def out(*shape, dtype=BF16):
        return jax.ShapeDtypeStruct(shape, dtype)

    def pair(*shape):
        return [DMA(shape), DMA(shape)]

    return pl.pallas_call(
        front_kernel,
        out_shape=(
            out(GROUP, COLS),
            out(GROUP, COLS),
            out(GROUP, COLS, dtype=F32),
            out(GROUP, 1, dtype=F32),
            out(GROUP, COLS),
            out(GROUP, D),
            out(GROUP, 1, dtype=F32),
            out(GROUP, 2 * HEAD),
            out(GROUP, 512),
            out(GROUP, 2 * ROPE),
            out(GROUP, LATENT),
            out(GROUP, LATENT, dtype=F32),
            out(GROUP, 1, dtype=F32),
            out(2, GROUP, GROUP, dtype=F32),
            out(GROUP, 2 * VDIM),
            out(LOCAL, ROWS, GROUP),
            out(LOCAL, GROUPS, GROUP, dtype=F32),
            out(GROUP, 1, dtype=F32),
            out(1, GROUP, dtype=F32),
            out(GROUP, 2 * ROPE, dtype=F32),
            out(GROUP, 2 * ROPE, dtype=F32),
            out(GROUP, D),
            out(GROUP, D),
            out(2, LOCAL, ROWS, COLS),
            out(LOCAL, ROWS, D),
        ),
        in_specs=[VM] * len(small) + [ANY] * len(large),
        out_specs=(VM,) * 23 + (ANY,) * 2,
        scratch_shapes=[
            vmem((GROUP, 2 * COLS), BF16),
            vmem((GROUP, 2 * COLS), BF16),
            vmem((ROWS, 2 * COLS), BF16),
            vmem((ROWS, 2 * COLS), BF16),
            vmem((GROUP, D), BF16),
            vmem((D, 2 * HEAD), BF16),
            vmem((LATENT + ROPE, D), BF16),
            vmem((LATENT, 512), BF16),
            vmem((2 * VDIM, D), BF16),
            vmem((2 * ROPE, D), BF16),
            vmem((TENSOR, GROUP, COLS), BF16),
            vmem((4, GROUP, COLS), BF16),
            vmem((2, GROUP // 2, COLS), BF16),
            vmem((2, GROUP, COLS), BF16),
            vmem((2, LOCAL, ROWS, COLS), BF16),
            vmem((2, LOCAL, ROWS, COLS), BF16),
        ]
        + sum_rows_scratch()
        + [DMA] * 4
        + pair(9)
        + pair(9)
        + pair(9)
        + pair(LOCAL, 6)
        + pair(8)
        + pair(2, 2)
        + pair(2, 2)
        + [DMA((4,)), DMA((2, 2)), DMA((2, 2))],
        compiler_params=params(cid, 60),
        name="front_step",
    )(*small, *large)


def finish_kernel(
    gg_ref, gu_ref, gd_ref, wsum_ref, out_in, dx_in, gwq_in, gwexp_in, gwout_in, gwlat_in, gains_in,
    ogg_ref, ogu_ref, ogd_ref, sg_ref, su_ref, sd_ref, out_ref, dx_ref, gwq_ref, gwexp_ref, gwout_ref, gwlat_ref,
    attn_ref, ffn_ref, lgain_ref,
):
    ogg_ref[...] = gg_ref[...].astype(F32)
    ogu_ref[...] = gu_ref[...].astype(F32)
    ogd_ref[...] = gd_ref[...].astype(F32)

    @pl.when((pl.program_id(0) == 0) & (pl.program_id(1) == 0))
    def small():
        e = lax.axis_index("expert")
        sg_ref[...] = wsum_ref[0]
        su_ref[...] = wsum_ref[1]
        sd_ref[...] = wsum_ref[2]
        out_ref[...] = out_in[...]
        dx_ref[...] = dx_in[...]
        gwq_ref[...] = gwq_in[...]
        gwexp_ref[...] = gwexp_in[...]
        gwout_ref[...] = gwout_in[...]
        lat = gwlat_in[...].astype(F32).reshape(WIDE_LAT, D // GROUPS)
        half = ROPE // 2
        gwlat_ref[: LATENT + half] = lat[: LATENT + half]
        gwlat_ref[LATENT + half :] = lat[LATENT + ROPE : LATENT + ROPE + half]
        own = gains_in[e // 2]
        side = lax.rem(e, 2) == 0
        attn_ref[...] = jnp.where(side, own[0:1, :128], own[0:1, 128:])
        ffn_ref[...] = jnp.where(side, own[1:2, :128], own[1:2, 128:])
        rows = jnp.sum(gains_in[...], axis=0)[2:4]
        row = jnp.where(e < 8, rows[0:1], rows[1:2])
        wanted = iota((COLS, LATENT // GROUPS), 1) + lax.rem(e, 8) * (LATENT // GROUPS)
        pick_own = jnp.where(iota((COLS, LATENT // GROUPS), 0) == wanted, 1.0, 0.0)
        lgain_ref[...] = lax.dot_general(
            row, pick_own, (((1,), (0,)), ((), ())),
            precision=lax.Precision.HIGHEST, preferred_element_type=F32,
        )


def finish_step(grads, rest):
    def out(*shape, dtype=F32):
        return jax.ShapeDtypeStruct(shape, dtype)

    hid = grads[0].shape[1]
    wide = rest[0].shape[1]
    block = pl.BlockSpec((1, hid, D), lambda i, j: (i, 0, j))

    def whole(shape):
        return pl.BlockSpec(shape, lambda i, j: (0,) * len(shape))

    outs = (
        out(wide, 128), out(wide, 128), out(wide, 128), out(GROUP, COLS, dtype=BF16), out(GROUP, COLS, dtype=BF16),
        out(128, 2 * HEAD), out(LATENT // GROUPS, 512), out(2 * VDIM, 128), out(LATENT + ROPE, 128),
        out(1, 128), out(1, 128), out(1, LATENT // GROUPS),
    )
    return pl.pallas_call(
        finish_kernel,
        grid=(LOCAL, 1),
        out_shape=(out(LOCAL, hid, D),) * 3 + outs,
        in_specs=[block] * 3 + [whole(a.shape) for a in rest],
        out_specs=(block,) * 3 + tuple(whole(o.shape) for o in outs),
        compiler_params=pltpu.CompilerParams(vmem_limit_bytes=63 * MIB),
        name="finish_step",
    )(*grads, *rest)


def per_device(
    tokens,
    cotangent,
    attn_gain,
    w_query,
    w_latent,
    latent_gain,
    w_expand,
    w_out,
    ffn_gain,
    shared_gate,
    shared_up,
    shared_down,
    expert_gate,
    expert_up,
    expert_down,
    seq_lengths,
    seq_order,
    routes,
    gate_weights,
):
    wlat_t = w_latent.T
    attn_row, ffn_row, lgain = attn_gain, ffn_gain, latent_gain

    (
        x_cols, dy_cols, middle, inv_two, normed_two_cols, normed, inv_one, query, expanded, key_rope, compressed,
        latent, inv_lat, probs, mixed, place, gate_of, seat, seat_row, cosine, sine, dy_full, normed_two, own_slots, grad_rows
    ) = front_step(
        (
            tokens,
            cotangent,
            seq_lengths.reshape(1, -1),
            seq_order.reshape(1, -1),
            routes.T,
            gate_weights.T,
            attn_row,
            lgain,
            ffn_row,
        ),
        (w_query, wlat_t, w_expand, w_out),
        1,
    )

    (
        part, grad_eg, grad_eu, grad_ed, shared_out, dmid, dgain_ffn, d_attn, unused, early_back, shared_weights
    ) = moe_step(
        place,
        own_slots,
        normed_two,
        dy_full,
        shared_gate.T,
        shared_up.T,
        shared_down,
        jnp.swapaxes(expert_gate, 1, 2),
        jnp.swapaxes(expert_up, 1, 2),
        expert_down,
        grad_rows,
        middle,
        inv_two,
        ffn_row,
        dy_cols,
        3,
    )
    output, input_grad, grad_wq, grad_wexp, grad_wout, grad_wlat, gains = back_step(
        (
            d_attn,
            mixed,
            w_out,
            query,
            expanded,
            key_rope,
            probs,
            cosine,
            sine,
            latent,
            inv_lat,
            lgain,
            x_cols,
            inv_one,
            attn_row,
            dmid,
            dgain_ffn,
            middle,
            shared_out,
            early_back,
            gate_of,
            seat,
            seat_row,
        ),
        (place, normed, w_query, w_expand, compressed, wlat_t, part),
        4,
    )
    (
        grad_eg, grad_eu, grad_ed, sg, su, sd, output, input_grad, grad_wq, grad_wexp, grad_wout, grad_wlat,
        attn_out, ffn_out, lgain_out
    ) = finish_step(
        (grad_eg, grad_eu, grad_ed),
        (shared_weights, output, input_grad, grad_wq, grad_wexp, grad_wout, grad_wlat, gains),
    )
    return (
        output,
        input_grad,
        attn_out[0],
        grad_wq,
        grad_wlat.T,
        lgain_out[0],
        grad_wexp,
        grad_wout,
        ffn_out[0],
        sg.T,
        su.T,
        sd,
        jnp.swapaxes(grad_eg, 1, 2),
        jnp.swapaxes(grad_eu, 1, 2),
        grad_ed,
    )


def solution(mesh):
    return jax.shard_map(
        per_device,
        mesh=mesh,
        in_specs=(
            P("expert", "tensor"),
            P("expert", "tensor"),
            P(),
            P(None, "tensor"),
            P(),
            P(),
            P(None, "tensor"),
            P("tensor", None),
            P(),
            P(None, "tensor"),
            P(None, "tensor"),
            P("tensor", None),
            P("expert", None, "tensor"),
            P("expert", None, "tensor"),
            P("expert", "tensor", None),
            P(),
            P(),
            P("expert", None),
            P("expert", None),
        ),
        out_specs=(
            P("expert", "tensor"),
            P("expert", "tensor"),
            P("expert"),
            P("expert", "tensor"),
            P("expert", None),
            P("expert"),
            P("expert", "tensor"),
            P("tensor", "expert"),
            P("expert"),
            P("expert", "tensor"),
            P("expert", "tensor"),
            P("tensor", "expert"),
            P("expert", None, "tensor"),
            P("expert", None, "tensor"),
            P("expert", "tensor", None),
        ),
        check_vma=False,
    )
```
